32 devices in a mesh: groups: 2 (over x), dp: 16 (over z, y, core).
Axes of the slice: x: 2, y: 2, z: 4, core: 2. Of those that a mesh axis runs over, the one named last changes fastest.
Arguments:
- latents: bfloat16 [64, 256, 2432], P(('groups', 'dp')), parts along dimension 0, may hold values from -6 to 6
- context: bfloat16 [32, 32, 2432], P('groups', 'dp'), parts along dimension 0, may hold values from -6 to 6
- lengths: int32 [32], P('groups'), parts along dimension 0, may hold values from 1 to 32, as said below
- winner_slot: int32 [32], P('groups'), parts along dimension 0, may hold values from 0 to 31, as said below
- loser_slot: int32 [32], P('groups'), parts along dimension 0, may hold values from 0 to 31, as said below
- image_mod: float32 [64, 2, 2432], P(('groups', 'dp')), parts along dimension 0, may hold values from -3 to 3
- context_mod: float32 [32, 2, 2432], P('groups'), parts along dimension 0, may hold values from -3 to 3
- w_q: bfloat16 [2432, 1216], P('dp'), may hold values from -0.125 to 0.125
- w_k: bfloat16 [2432, 1216], P('dp'), may hold values from -0.125 to 0.125
- w_v: bfloat16 [2432, 1216], P('dp'), may hold values from -0.125 to 0.125
- w_ck: bfloat16 [2432, 1216], P('dp'), may hold values from -0.125 to 0.125
- w_cv: bfloat16 [2432, 1216], P('dp'), may hold values from -0.125 to 0.125
Outputs:
- attended: bfloat16 [64, 256, 1216], P(('groups', 'dp')), parts along dimension 0
The draws below stay inside these ranges and needn't reach their ends.
There are 2 independent parts, one for each index of `groups`. The reference program is written for one: setup_inputs(seed, part) draws one part's arguments, and reference() takes and returns one part's arrays. A program takes and returns all parts, laid end to end along the dimension named above; an argument that names none is the same for every part. Nothing has to cross between parts.
Inputs may be any that keep to these rules, and one draw needn't show every extreme that they name: Each prompt is live for its first lengths[p] positions; some prompt has all 32 positions live. winner_slot and loser_slot together name every latent slot exactly once. winner_slot and loser_slot together name every latent slot exactly once.
All inputs are finite; a program needn't handle non-finite values.
Results may differ from the reference program's by a relative error of at most 0.0038.
Values may be sent and summed in bfloat16 or wider, within the bound.
No kernel may reach another device: no remote copies, remote signals or barrier semaphores. Data moves between devices by JAX's collectives and lax.ppermute only.
A program may use at most 128 MiB of HBM per device.

```python
import jax
import jax.numpy as jnp
from jax import lax

D = 2432
HEADS = 19
HEAD = 64
LAT_TOK = 256
PROMPTS = 16
CTX_LEN = 32
LATENTS = 32


def shuffled_slots(key):
    return jax.random.permutation(key, jnp.arange(2 * PROMPTS, dtype=jnp.int32))


def draw_winner_slot(key, part):
    shuffled = shuffled_slots(key)
    return shuffled[:PROMPTS]


def draw_loser_slot(key, part):
    shuffled = shuffled_slots(key)
    return shuffled[PROMPTS:]


def draw_lengths(key, part):
    key = jax.random.fold_in(key, 7)
    first_key, second_key = jax.random.split(key)
    drawn = jax.random.randint(first_key, (PROMPTS,), 1, CTX_LEN + 1, dtype=jnp.int32)
    chosen = jax.random.randint(second_key, (), 0, PROMPTS, dtype=jnp.int32)
    marker = jnp.arange(PROMPTS, dtype=jnp.int32) == chosen
    return jnp.where(marker, CTX_LEN, drawn).astype(jnp.int32)


def shard_levels(stream_key, extent, cuts, smallest, high):
    gain, own = 1.0, jax.random.fold_in(stream_key, 6)
    for dim, parts in cuts:
        draws = jnp.exp(jax.random.uniform(jax.random.fold_in(own, dim), (parts,), jnp.float32, smallest / len(cuts), high / len(cuts)))
        gain = gain * jnp.repeat(draws, extent[dim] // parts).reshape([-1 if axis == dim else 1 for axis in range(len(extent))])
    return gain


def centred(stream_key, dims, width, bound, pieces=(), kind=jnp.bfloat16):
    values = jax.random.normal(stream_key, dims, jnp.float32) * width
    if len(pieces) > 0:
        values = shard_levels(stream_key, dims, pieces, -0.22, 0.18) * values
    return jnp.clip(values, min=-bound, max=bound).astype(kind)


def setup_inputs(seed: int = 0, part: int = 0) -> dict:
    splits = jax.random.split(jax.random.key(seed), 13)
    part_keys = jax.random.split(jax.random.fold_in(splits[12], part), 13)
    return {
        "latents": centred(part_keys[0], (LATENTS, LAT_TOK, D), 1.0, 6.0, ((0, 16),)),
        "context": centred(part_keys[1], (PROMPTS, CTX_LEN, D), 1.0, 6.0, ((1, 16),)),
        "lengths": draw_lengths(jax.random.fold_in(jax.random.fold_in(splits[12], part), 71), part),
        "winner_slot": draw_winner_slot(jax.random.fold_in(jax.random.fold_in(splits[12], part), 71), part),
        "loser_slot": draw_loser_slot(jax.random.fold_in(jax.random.fold_in(splits[12], part), 71), part),
        "image_mod": centred(part_keys[5], (LATENTS, 2, D), 0.5, 3.0, ((0, 16),), jnp.float32),
        "context_mod": centred(part_keys[6], (PROMPTS, 2, D), 0.5, 3.0, (), jnp.float32),
        "w_q": centred(splits[7], (D, HEADS * HEAD), D ** -0.5, 0.125, ((0, 16),)),
        "w_k": centred(splits[8], (D, HEADS * HEAD), D ** -0.5, 0.125, ((0, 16),)),
        "w_v": centred(splits[9], (D, HEADS * HEAD), D ** -0.5, 0.125, ((0, 16),)),
        "w_ck": centred(splits[10], (D, HEADS * HEAD), D ** -0.5, 0.125, ((0, 16),)),
        "w_cv": centred(splits[11], (D, HEADS * HEAD), D ** -0.5, 0.125, ((0, 16),)),
    }


epsilon = 1e-06

def modulate(tokens, shifts, scales):
    values = tokens.astype(jnp.float32)
    average = lax.optimization_barrier(jnp.mean(values, axis=-1, keepdims=True))
    centered = values - average
    variance = lax.optimization_barrier(jnp.mean(centered * centered, axis=-1, keepdims=True))
    return (centered * lax.rsqrt(variance + epsilon) * (1.0 + scales) + shifts).astype(jnp.bfloat16)

def head_norm(projected, head_count):
    shaped = projected.reshape(projected.shape[:-1] + (head_count, -1))
    scaled = shaped * lax.rsqrt(lax.optimization_barrier(jnp.mean(shaped * shaped, axis=-1, keepdims=True)) + epsilon)
    return scaled.reshape(projected.shape).astype(jnp.bfloat16)

def slot_prompts(winner_slot, loser_slot):
    prompt_count = winner_slot.shape[0]
    slot_ids = jnp.arange(2 * prompt_count, dtype=jnp.int32)
    prompt_ids = jnp.arange(prompt_count, dtype=jnp.int32)
    matched = (winner_slot[None, :] == slot_ids[:, None]) | (loser_slot[None, :] == slot_ids[:, None])
    return lax.optimization_barrier(jnp.sum(jnp.where(matched, prompt_ids[None, :], 0), axis=1)).astype(jnp.int32)

def attend(queries, key_rows, value_rows, live_length, head_count):
    token_count, inner_width = queries.shape
    key_span = key_rows.shape[0]
    head_size = inner_width // head_count
    query_heads = queries.reshape(token_count, head_count, head_size).astype(jnp.float32)
    key_heads = key_rows.reshape(key_span, head_count, head_size).astype(jnp.float32)
    value_heads = value_rows.reshape(key_span, head_count, head_size).astype(jnp.float32)
    scores = jnp.einsum('qhd,khd->hqk', query_heads, key_heads) * (1.0 / jnp.sqrt(jnp.float32(head_size)))
    position = jnp.arange(key_span, dtype=jnp.int32)
    allowed = position < token_count + live_length
    raised = jnp.where(allowed[None, None, :], jnp.exp(scores), 0.0)
    weights = (raised / lax.optimization_barrier(jnp.sum(raised, axis=-1, keepdims=True))).astype(jnp.bfloat16)
    result = jnp.einsum('hqk,khd->qhd', weights.astype(jnp.float32), value_heads)
    return result.reshape(token_count, inner_width).astype(jnp.bfloat16)

def reference(latents, context, lengths, winner_slot, loser_slot, image_mod, context_mod, w_q, w_k, w_v, w_ck, w_cv):
    prompt_of = slot_prompts(winner_slot, loser_slot)

    def one_latent(bundle):
        tokens, modulation, prompt = bundle
        image = modulate(tokens, modulation[0], modulation[1])
        queries = head_norm(jnp.dot(image, w_q, preferred_element_type=jnp.float32), HEADS)
        image_keys = head_norm(jnp.dot(image, w_k, preferred_element_type=jnp.float32), HEADS)
        image_values = jnp.dot(image, w_v, preferred_element_type=jnp.float32).astype(jnp.bfloat16)
        prompt_rows = lax.dynamic_index_in_dim(context, prompt, 0, keepdims=False)
        prompt_mod = lax.dynamic_index_in_dim(context_mod, prompt, 0, keepdims=False)
        mixed = modulate(prompt_rows, prompt_mod[0], prompt_mod[1])
        prompt_keys = head_norm(jnp.dot(mixed, w_ck, preferred_element_type=jnp.float32), HEADS)
        prompt_values = jnp.dot(mixed, w_cv, preferred_element_type=jnp.float32).astype(jnp.bfloat16)
        live_length = lax.dynamic_index_in_dim(lengths, prompt, 0, keepdims=False)
        key_rows = jnp.concatenate([image_keys, prompt_keys], axis=0)
        value_rows = jnp.concatenate([image_values, prompt_values], axis=0)
        return attend(queries, key_rows, value_rows, live_length, HEADS)
    return lax.map(one_latent, (latents, image_mod, prompt_of))
```

```python
import jax
import jax.numpy as jnp
from jax import lax
from jax.sharding import PartitionSpec as P

HEADS = 19


epsilon = 1e-06


def modulate(tokens, shifts, scales):
    values = tokens.astype(jnp.float32)
    average = jnp.mean(values, axis=-1, keepdims=True)
    centered = values - average
    variance = jnp.mean(centered * centered, axis=-1, keepdims=True)
    return (centered * lax.rsqrt(variance + epsilon) * (1.0 + scales) + shifts).astype(jnp.bfloat16)


def head_norm(projected, head_count):
    shaped = projected.reshape(projected.shape[:-1] + (head_count, -1))
    scaled = shaped * lax.rsqrt(jnp.mean(shaped * shaped, axis=-1, keepdims=True) + epsilon)
    return scaled.reshape(projected.shape).astype(jnp.bfloat16)


def slot_prompts(winner_slot, loser_slot):
    prompt_count = winner_slot.shape[0]
    slot_ids = jnp.arange(2 * prompt_count, dtype=jnp.int32)
    prompt_ids = jnp.arange(prompt_count, dtype=jnp.int32)
    matched = (winner_slot[None, :] == slot_ids[:, None]) | (
        loser_slot[None, :] == slot_ids[:, None]
    )
    return jnp.sum(jnp.where(matched, prompt_ids[None, :], 0), axis=1)


def attend(queries, key_rows, value_rows, live_length, head_count):
    slot_count, token_count, inner_width = queries.shape
    key_span = key_rows.shape[1]
    head_size = inner_width // head_count
    query_heads = queries.reshape(slot_count, token_count, head_count, head_size)
    key_heads = key_rows.reshape(slot_count, key_span, head_count, head_size)
    value_heads = value_rows.reshape(slot_count, key_span, head_count, head_size)
    scores = jnp.einsum(
        "lqhd,lkhd->lhqk", query_heads, key_heads, preferred_element_type=jnp.float32
    )
    scores = scores * (1.0 / jnp.sqrt(jnp.float32(head_size)))
    position = jnp.arange(key_span, dtype=jnp.int32)
    allowed = position[None, :] < (token_count + live_length)[:, None]
    raised = jnp.where(allowed[:, None, None, :], jnp.exp(scores), 0.0)
    weights = (raised / jnp.sum(raised, axis=-1, keepdims=True)).astype(jnp.bfloat16)
    result = jnp.einsum("lhqk,lkhd->lqhd", weights, value_heads, preferred_element_type=jnp.float32)
    return result.reshape(slot_count, token_count, inner_width).astype(jnp.bfloat16)


def ring_order(groups, chips):
    if groups == 2:
        return list(range(0, chips, 2)) + list(range(1, chips, 2))[::-1]
    return list(range(chips))


def solution(mesh):
    groups, dp = mesh.shape["groups"], mesh.shape["dp"]
    chips = dp // 2
    ring = ring_order(groups, chips)
    place = [ring.index(chip) for chip in range(chips)]
    forward_pairs = [
        (2 * ring[i] + c, 2 * ring[(i + 1) % chips] + c) for i in range(chips) for c in range(2)
    ]
    backward_pairs = [(b, a) for a, b in forward_pairs]
    core_pairs = [(d, d ^ 1) for d in range(dp)]
    group_pairs = [(g, g ^ 1) for g in range(groups)]
    half_groups = [[2 * chip + c for chip in range(chips)] for c in range(2)]

    def forward(x):
        return lax.ppermute(x, "dp", forward_pairs)

    def backward(x):
        return lax.ppermute(x, "dp", backward_pairs)

    def swap_cores(x):
        return lax.ppermute(x, "dp", core_pairs)

    def swap_groups(x):
        return lax.ppermute(x, "groups", group_pairs)

    def ring_gather(block, far_forward):
        ahead = [block]
        behind = [block]
        reach_ahead = chips // 2 if far_forward else (chips - 1) // 2
        reach_behind = chips - 1 - reach_ahead
        for _ in range(reach_ahead):
            ahead.append(forward(ahead[-1]))
        for _ in range(reach_behind):
            behind.append(backward(behind[-1]))
        found = {o: ahead[o] for o in range(reach_ahead + 1)}
        for o in range(1, reach_behind + 1):
            found[chips - o] = behind[o]
        return [found[o] for o in range(chips)]

    def local(
        latents,
        context,
        lengths,
        winner_slot,
        loser_slot,
        image_mod,
        context_mod,
        w_q,
        w_k,
        w_v,
        w_ck,
        w_cv,
    ):
        slot_local, token_count, width = latents.shape
        prompt_count, spot_local, _ = context.shape
        depth, inner_width = w_q.shape
        me = lax.axis_index("dp")
        my_group = lax.axis_index("groups") % 2
        my_chip, my_core = me // 2, me % 2
        ring_table = jnp.array(ring, jnp.int32)
        my_place = jnp.array(place, jnp.int32)[my_chip]
        chip_at = ring_table[(my_place - jnp.arange(chips, dtype=jnp.int32)) % chips]

        own_mixed = modulate(context, context_mod[:, 0:1, :], context_mod[:, 1:2, :]).reshape(
            prompt_count * spot_local, width
        )
        mixed_blocks = ring_gather(own_mixed, True)

        span = 2 * inner_width // chips
        w_c = jnp.concatenate([w_ck, w_cv], axis=1)
        w_c = w_c.reshape(depth, chips, span).transpose(1, 0, 2)
        w_c = lax.all_to_all(w_c, "dp", 0, 0, axis_index_groups=half_groups, tiled=True)
        w_c_other = swap_cores(w_c)
        w_first = jnp.where(my_core == 0, w_c, w_c_other)
        w_second = jnp.where(my_core == 0, w_c_other, w_c)
        w_c = jnp.stack([w_first, w_second], axis=1).reshape(width, span)

        w_a = jnp.where(my_group == 0, w_q, w_k)
        a_blocks = ring_gather(w_a, True)
        v_blocks = ring_gather(w_v, False)
        b_blocks = [jnp.where(my_group == 0, w_k, w_q)] + [swap_groups(x) for x in a_blocks[1:]]

        image = modulate(latents, image_mod[:, 0:1, :], image_mod[:, 1:2, :]).reshape(
            slot_local * token_count, width
        )
        slabs = image.reshape(slot_local * token_count, dp, depth).transpose(1, 0, 2)

        order = [0]
        for o in range(1, chips // 2 + 1):
            order += [o] if 2 * o == chips else [o, chips - o]
        totals = [0.0, 0.0, 0.0]
        for o in order:
            chip = chip_at[o]
            mine = lax.dynamic_index_in_dim(slabs, 2 * chip + my_core, 0, keepdims=False)
            others = lax.dynamic_index_in_dim(slabs, 2 * chip + 1 - my_core, 0, keepdims=False)
            for i, blocks in enumerate((a_blocks, b_blocks, v_blocks)):
                totals[i] = (
                    totals[i]
                    + jnp.dot(mine, blocks[o], preferred_element_type=jnp.float32)
                    + jnp.dot(others, swap_cores(blocks[o]), preferred_element_type=jnp.float32)
                )
        pa, pb, pv = totals

        rows = jnp.concatenate(mixed_blocks, axis=0)
        projected = jnp.dot(rows, w_c, preferred_element_type=jnp.float32).astype(jnp.bfloat16)
        projected = projected.reshape(chips, prompt_count, spot_local, span)
        inverse = (my_place - jnp.array(place, jnp.int32)) % chips
        projected = jnp.take(projected, inverse, axis=0)
        prompt_of = slot_prompts(winner_slot, loser_slot)
        destined = prompt_of.reshape(-1, slot_local)
        outgoing = jnp.take(projected.transpose(1, 0, 2, 3), destined, axis=0)
        arrived = lax.all_to_all(outgoing, "dp", 0, 0, tiled=True)
        arrived = arrived.reshape(chips, 2, slot_local, chips, spot_local, span)
        arrived = arrived.transpose(2, 3, 1, 4, 0, 5).reshape(slot_local, -1, 2 * inner_width)

        my_prompts = lax.dynamic_slice_in_dim(prompt_of, me * slot_local, slot_local)
        live_length = jnp.take(lengths, my_prompts, axis=0)
        prompt_keys = head_norm(arrived[..., :inner_width].astype(jnp.float32), HEADS)
        prompt_values = arrived[..., inner_width:]
        pq = jnp.where(my_group == 0, pa, pb)
        pk = jnp.where(my_group == 0, pb, pa)
        queries = head_norm(pq, HEADS).reshape(slot_local, token_count, inner_width)
        image_keys = head_norm(pk, HEADS).reshape(slot_local, token_count, inner_width)
        image_values = pv.astype(jnp.bfloat16).reshape(slot_local, token_count, inner_width)
        key_rows = jnp.concatenate([image_keys, prompt_keys], axis=1)
        value_rows = jnp.concatenate([image_values, prompt_values], axis=1)
        return attend(queries, key_rows, value_rows, live_length, HEADS)

    placed = (
        P(("groups", "dp"), None, None),
        P("groups", "dp", None),
        P("groups"),
        P("groups"),
        P("groups"),
        P(("groups", "dp"), None, None),
        P("groups", None, None),
        P("dp", None),
        P("dp", None),
        P("dp", None),
        P("dp", None),
        P("dp", None),
    )
    return jax.shard_map(
        local,
        mesh=mesh,
        in_specs=placed,
        out_specs=P(("groups", "dp"), None, None),
        check_vma=False,
    )
```

```python
import jax
import jax.numpy as jnp
from jax import lax
from jax.sharding import PartitionSpec as P

HEADS = 19


epsilon = 1e-06


def modulate(tokens, shifts, scales):
    values = tokens.astype(jnp.float32)
    average = jnp.mean(values, axis=-1, keepdims=True)
    centered = values - average
    variance = jnp.mean(centered * centered, axis=-1, keepdims=True)
    return (centered * lax.rsqrt(variance + epsilon) * (1.0 + scales) + shifts).astype(jnp.bfloat16)


def head_norm(projected, head_count):
    shaped = projected.reshape(projected.shape[:-1] + (head_count, -1))
    scaled = shaped * lax.rsqrt(jnp.mean(shaped * shaped, axis=-1, keepdims=True) + epsilon)
    return scaled.reshape(projected.shape).astype(jnp.bfloat16)


def slot_prompts(winner_slot, loser_slot):
    prompt_count = winner_slot.shape[0]
    slot_ids = jnp.arange(2 * prompt_count, dtype=jnp.int32)
    prompt_ids = jnp.arange(prompt_count, dtype=jnp.int32)
    matched = (winner_slot[None, :] == slot_ids[:, None]) | (
        loser_slot[None, :] == slot_ids[:, None]
    )
    return jnp.sum(jnp.where(matched, prompt_ids[None, :], 0), axis=1)


def attend(queries, key_rows, value_rows, live_length, head_count):
    slot_count, token_count, inner_width = queries.shape
    key_span = key_rows.shape[1]
    head_size = inner_width // head_count
    query_heads = queries.reshape(slot_count, token_count, head_count, head_size)
    key_heads = key_rows.reshape(slot_count, key_span, head_count, head_size)
    value_heads = value_rows.reshape(slot_count, key_span, head_count, head_size)
    scores = jnp.einsum(
        "lqhd,lkhd->lhqk", query_heads, key_heads, preferred_element_type=jnp.float32
    )
    scores = scores * (1.0 / jnp.sqrt(jnp.float32(head_size)))
    position = jnp.arange(key_span, dtype=jnp.int32)
    allowed = position[None, :] < (token_count + live_length)[:, None]
    raised = jnp.where(allowed[:, None, None, :], jnp.exp(scores), 0.0)
    weights = (raised / jnp.sum(raised, axis=-1, keepdims=True)).astype(jnp.bfloat16)
    result = jnp.einsum("lhqk,lkhd->lqhd", weights, value_heads, preferred_element_type=jnp.float32)
    return result.reshape(slot_count, token_count, inner_width).astype(jnp.bfloat16)


def solution(mesh):
    groups, dp = mesh.shape["groups"], mesh.shape["dp"]
    chips = dp // 2
    core_pairs = [(d, d ^ 1) for d in range(dp)]
    group_pairs = [(g, g ^ 1) for g in range(groups)]
    half_groups = [[2 * chip + c for chip in range(chips)] for c in range(2)]

    def gather(x):
        return lax.all_gather(x, "dp", axis_index_groups=half_groups, axis=0, tiled=True)

    def swap_cores(x):
        return lax.ppermute(x, "dp", core_pairs)

    def swap_groups(x):
        return lax.ppermute(x, "groups", group_pairs)

    def local(
        latents,
        context,
        lengths,
        winner_slot,
        loser_slot,
        image_mod,
        context_mod,
        w_q,
        w_k,
        w_v,
        w_ck,
        w_cv,
    ):
        slot_local, token_count, width = latents.shape
        prompt_count, spot_local, _ = context.shape
        depth, inner_width = w_q.shape
        me = lax.axis_index("dp")
        my_group = lax.axis_index("groups") % 2
        my_core = me % 2
        head_size = inner_width // HEADS
        cut = (HEADS + 1) // 2 * head_size
        chunks = ((0, cut), (cut, inner_width))

        own_mixed = modulate(context, context_mod[:, 0:1, :], context_mod[:, 1:2, :]).reshape(
            prompt_count * spot_local, width
        )

        span = 2 * inner_width // chips
        w_c = jnp.concatenate([w_ck, w_cv], axis=1)
        w_c = w_c.reshape(depth, chips, span).transpose(1, 0, 2)
        w_c = lax.all_to_all(w_c, "dp", 0, 0, axis_index_groups=half_groups, tiled=True)
        w_c_other = swap_cores(w_c)
        w_first = jnp.where(my_core == 0, w_c, w_c_other)
        w_second = jnp.where(my_core == 0, w_c_other, w_c)
        w_c = jnp.stack([w_first, w_second], axis=1).reshape(width, span)

        w_a = jnp.where(my_group == 0, w_q, w_k)
        a_chunks = [gather(w_a[:, lo:hi]) for lo, hi in chunks]
        rows = gather(own_mixed)
        v_chunks = [gather(w_v[:, lo:hi]) for lo, hi in chunks]
        b_chunks = [swap_groups(x) for x in a_chunks]

        image = modulate(latents, image_mod[:, 0:1, :], image_mod[:, 1:2, :])
        image = image.reshape(slot_local * token_count, chips, 2, depth)
        halves = [image[:, :, c, :].reshape(slot_local * token_count, chips * depth) for c in range(2)]
        mine = jnp.where(my_core == 0, halves[0], halves[1])
        others = jnp.where(my_core == 0, halves[1], halves[0])

        def project(weights):
            return jnp.dot(mine, weights, preferred_element_type=jnp.float32) + jnp.dot(
                others, swap_cores(weights), preferred_element_type=jnp.float32
            )

        projected = jnp.dot(rows, w_c, preferred_element_type=jnp.float32).astype(jnp.bfloat16)
        projected = projected.reshape(chips, prompt_count, spot_local, span)
        prompt_of = slot_prompts(winner_slot, loser_slot)
        destined = prompt_of.reshape(-1, slot_local)
        outgoing = jnp.take(projected.transpose(1, 0, 2, 3), destined, axis=0)
        arrived = lax.all_to_all(outgoing, "dp", 0, 0, tiled=True)
        arrived = arrived.reshape(chips, 2, slot_local, chips, spot_local, span)
        arrived = arrived.transpose(2, 3, 1, 4, 0, 5).reshape(slot_local, -1, 2 * inner_width)

        my_prompts = lax.dynamic_slice_in_dim(prompt_of, me * slot_local, slot_local)
        live_length = jnp.take(lengths, my_prompts, axis=0)
        prompt_keys = head_norm(arrived[..., :inner_width].astype(jnp.float32), HEADS)
        prompt_values = arrived[..., inner_width:]
        results = []
        for (lo, hi), wa, wb, wv in zip(chunks, a_chunks, b_chunks, v_chunks):
            heads = (hi - lo) // head_size
            shape = (slot_local, token_count, hi - lo)
            na = head_norm(project(wa), heads).reshape(shape)
            nb = head_norm(project(wb), heads).reshape(shape)
            queries = jnp.where(my_group == 0, na, nb)
            image_keys = jnp.where(my_group == 0, nb, na)
            image_values = project(wv).astype(jnp.bfloat16).reshape(shape)
            key_rows = jnp.concatenate([image_keys, prompt_keys[..., lo:hi]], axis=1)
            value_rows = jnp.concatenate([image_values, prompt_values[..., lo:hi]], axis=1)
            results.append(attend(queries, key_rows, value_rows, live_length, heads))
        return jnp.concatenate(results, axis=-1)

    placed = (
        P(("groups", "dp"), None, None),
        P("groups", "dp", None),
        P("groups"),
        P("groups"),
        P("groups"),
        P(("groups", "dp"), None, None),
        P("groups", None, None),
        P("dp", None),
        P("dp", None),
        P("dp", None),
        P("dp", None),
        P("dp", None),
    )
    return jax.shard_map(
        local,
        mesh=mesh,
        in_specs=placed,
        out_specs=P(("groups", "dp"), None, None),
        check_vma=False,
    )
```

```python
import functools

import jax
import jax.numpy as jnp
from jax import lax
from jax.experimental import pallas as pl
from jax.experimental.pallas import tpu as pltpu
from jax.sharding import PartitionSpec as P

HEADS = 19
LANES = 128


epsilon = 1e-06


def modulate(tokens, shifts, scales):
    values = tokens.astype(jnp.float32)
    average = jnp.mean(values, axis=-1, keepdims=True)
    centered = values - average
    variance = jnp.mean(centered * centered, axis=-1, keepdims=True)
    return (centered * lax.rsqrt(variance + epsilon) * (1.0 + scales) + shifts).astype(jnp.bfloat16)


def slot_prompts(winner_slot, loser_slot):
    prompt_count = winner_slot.shape[0]
    slot_ids = jnp.arange(2 * prompt_count, dtype=jnp.int32)
    prompt_ids = jnp.arange(prompt_count, dtype=jnp.int32)
    matched = (winner_slot[None, :] == slot_ids[:, None]) | (
        loser_slot[None, :] == slot_ids[:, None]
    )
    return jnp.sum(jnp.where(matched, prompt_ids[None, :], 0), axis=1)


def attend_kernel(head_size, scalars, a_ref, b_ref, v_ref, pk_ref, pv_ref, out_ref):
    live = scalars[1 + pl.program_id(0)]
    even_group = scalars[0] == 0
    low = lax.broadcasted_iota(jnp.int32, (1, LANES), 1) < head_size

    def head_norm(x):
        squares = x * x
        first = jnp.sum(jnp.where(low, squares, 0.0), axis=-1, keepdims=True)
        second = jnp.sum(jnp.where(low, 0.0, squares), axis=-1, keepdims=True)
        scale = jnp.where(
            low,
            lax.rsqrt(first * (1.0 / head_size) + epsilon),
            lax.rsqrt(second * (1.0 / head_size) + epsilon),
        )
        return (x * scale).astype(jnp.bfloat16)

    a, b = a_ref[...], b_ref[...]
    queries = head_norm(jnp.where(even_group, a, b))
    keys = head_norm(jnp.where(even_group, b, a))
    values = v_ref[...].astype(jnp.bfloat16)
    prompt_keys = head_norm(pk_ref[0].astype(jnp.float32))
    prompt_values = pv_ref[0]
    span = prompt_keys.shape[0]
    allowed = lax.broadcasted_iota(jnp.int32, (1, span), 1) < live
    outs = []
    over_keys = (((1,), (1,)), ((), ()))
    for side in (low, jnp.logical_not(low)):
        q = jnp.where(side, queries, jnp.zeros_like(queries))
        s = lax.dot_general(q, keys, over_keys, preferred_element_type=jnp.float32)
        t = lax.dot_general(q, prompt_keys, over_keys, preferred_element_type=jnp.float32)
        s = jnp.exp(s * (1.0 / head_size**0.5))
        t = jnp.where(allowed, jnp.exp(t * (1.0 / head_size**0.5)), 0.0)
        total = jnp.sum(s, axis=-1, keepdims=True) + jnp.sum(t, axis=-1, keepdims=True)
        share = 1.0 / total
        outs.append(
            jnp.dot(
                (s * share).astype(jnp.bfloat16), values, preferred_element_type=jnp.float32
            )
            + jnp.dot(
                (t * share).astype(jnp.bfloat16), prompt_values, preferred_element_type=jnp.float32
            )
        )
    out_ref[...] = jnp.where(low, outs[0], outs[1]).astype(jnp.bfloat16)


def attend(scalars, av, b, prompt_keys, prompt_values, head_size, first, count, token_count):
    columns = b.shape[1]
    pairs = columns // LANES
    span = prompt_keys.shape[1]
    return pl.pallas_call(
        functools.partial(attend_kernel, head_size),
        grid_spec=pltpu.PrefetchScalarGridSpec(
            num_scalar_prefetch=1,
            grid=(count, pairs),
            in_specs=[
                pl.BlockSpec((token_count, LANES), lambda l, p, s: (first + l, p)),
                pl.BlockSpec((token_count, LANES), lambda l, p, s: (first + l, p)),
                pl.BlockSpec((token_count, LANES), lambda l, p, s: (first + l, pairs + p)),
                pl.BlockSpec((1, span, LANES), lambda l, p, s: (l, 0, p)),
                pl.BlockSpec((1, span, LANES), lambda l, p, s: (l, 0, p)),
            ],
            out_specs=pl.BlockSpec((token_count, LANES), lambda l, p, s: (l, p)),
        ),
        out_shape=jax.ShapeDtypeStruct((count * token_count, columns), jnp.bfloat16),
        cost_estimate=pl.CostEstimate(
            flops=4 * count * pairs * token_count * (token_count + span) * LANES,
            bytes_accessed=count * token_count * columns * 14,
            transcendentals=0,
        ),
    )(scalars, av, b, av, prompt_keys, prompt_values)


def modulate_kernel(chips, scalars, x_ref, mod_ref, out_ref):
    values = x_ref[0].astype(jnp.float32)
    average = jnp.mean(values, axis=-1, keepdims=True)
    centered = values - average
    variance = jnp.mean(centered * centered, axis=-1, keepdims=True)
    shift, scale = mod_ref[0, 0:1, :], mod_ref[0, 1:2, :]
    image = centered * lax.rsqrt(variance + epsilon) * (1.0 + scale) + shift
    image = image.astype(jnp.bfloat16)
    wide = image.shape[1] // chips
    for chip in range(chips):
        out_ref[scalars[chip]] = image[:, chip * wide : (chip + 1) * wide]


def modulate_image(slot_of_chip, latents, image_mod):
    slots, tokens, width = latents.shape
    chips = slot_of_chip.shape[0]
    wide = width // chips
    return pl.pallas_call(
        functools.partial(modulate_kernel, chips),
        grid_spec=pltpu.PrefetchScalarGridSpec(
            num_scalar_prefetch=1,
            grid=(slots,),
            in_specs=[
                pl.BlockSpec((1, tokens, width), lambda i, s: (i, 0, 0)),
                pl.BlockSpec((1, 2, width), lambda i, s: (i, 0, 0)),
            ],
            out_specs=pl.BlockSpec((chips, tokens, wide), lambda i, s: (0, i, 0)),
        ),
        out_shape=jax.ShapeDtypeStruct((chips, slots * tokens, wide), jnp.bfloat16),
        compiler_params=pltpu.CompilerParams(vmem_limit_bytes=24 * 2**20),
        cost_estimate=pl.CostEstimate(
            flops=0, bytes_accessed=4 * slots * tokens * width, transcendentals=0
        ),
    )(slot_of_chip, latents, image_mod)


def accumulate_kernel(count, has_total, tiles, *refs):
    own, other, panels = refs[:count], refs[count : 2 * count], refs[2 * count : 3 * count]
    out_ref = refs[-1]
    step = pl.program_id(0)

    def run(slabs):
        total = refs[3 * count][...] if has_total else None
        for slab, panel in zip(slabs, panels):
            product = jnp.dot(slab[0], panel[...], preferred_element_type=jnp.float32)
            total = product if total is None else total + product
        out_ref[...] = total

    pl.when(step < tiles)(lambda: run(own))
    pl.when(step >= tiles)(lambda: run(other))


def accumulate(total, own, other, places, panels):
    _, rows, wide = own.shape
    tile = min(rows, 256)
    tiles = rows // tile
    count, columns = len(places), panels[0].shape[1]
    in_specs = [
        pl.BlockSpec((1, tile, wide), lambda i, o=o: (o, jnp.minimum(i, tiles - 1), 0))
        for o in places
    ]
    in_specs += [
        pl.BlockSpec((1, tile, wide), lambda i, o=o: (o, jnp.maximum(i - tiles, 0), 0))
        for o in places
    ]
    in_specs += [pl.BlockSpec((wide, columns), lambda i: (0, 0)) for _ in places]
    operands = [own] * count + [other] * count + list(panels)
    aliases = {}
    if total is not None:
        in_specs.append(pl.BlockSpec((tile, columns), lambda i: (i, 0)))
        operands.append(total)
        aliases = {3 * count: 0}
    return pl.pallas_call(
        functools.partial(accumulate_kernel, count, total is not None, tiles),
        grid=(2 * tiles,),
        in_specs=in_specs,
        out_specs=pl.BlockSpec((tile, columns), lambda i: (i, 0)),
        out_shape=jax.ShapeDtypeStruct((2 * rows, columns), jnp.float32),
        input_output_aliases=aliases,
        compiler_params=pltpu.CompilerParams(vmem_limit_bytes=24 * 2**20),
        cost_estimate=pl.CostEstimate(
            flops=4 * rows * wide * columns * count,
            bytes_accessed=8 * rows * columns,
            transcendentals=0,
        ),
    )(*operands)


def ring_order(groups, chips):
    if groups == 2:
        return list(range(0, chips, 2)) + list(range(1, chips, 2))[::-1]
    return list(range(chips))


def solution(mesh):
    groups, dp = mesh.shape["groups"], mesh.shape["dp"]
    chips = dp // 2
    ring = ring_order(groups, chips)
    place = [ring.index(chip) for chip in range(chips)]
    forward_pairs = [
        (2 * ring[i] + c, 2 * ring[(i + 1) % chips] + c) for i in range(chips) for c in range(2)
    ]
    backward_pairs = [(b, a) for a, b in forward_pairs]
    core_pairs = [(d, d ^ 1) for d in range(dp)]
    group_pairs = [(g, g ^ 1) for g in range(groups)]
    half_groups = [[2 * chip + c for chip in range(chips)] for c in range(2)]

    def forward(x):
        return lax.ppermute(x, "dp", forward_pairs)

    def backward(x):
        return lax.ppermute(x, "dp", backward_pairs)

    def swap_cores(x):
        return lax.ppermute(x, "dp", core_pairs)

    def swap_groups(x):
        return lax.ppermute(x, "groups", group_pairs)

    def local(
        latents,
        context,
        lengths,
        winner_slot,
        loser_slot,
        image_mod,
        context_mod,
        w_q,
        w_k,
        w_v,
        w_ck,
        w_cv,
    ):
        slot_local, token_count, width = latents.shape
        prompt_count, spot_local, _ = context.shape
        depth, inner_width = w_q.shape
        head_size = inner_width // HEADS
        columns = (HEADS + 1) // 2 * head_size
        me = lax.axis_index("dp")
        my_group = lax.axis_index("groups") % 2
        my_chip, my_core = me // 2, me % 2
        my_place = jnp.array(place, jnp.int32)[my_chip]

        def side_columns(x, core):
            return jnp.where(core == 0, x[..., :columns], x[..., inner_width - columns :])

        w_a = jnp.where(my_group == 0, w_q, w_k)
        w_b = jnp.where(my_group == 0, w_k, w_q)
        keep = jnp.concatenate([side_columns(w, my_core) for w in (w_a, w_v, w_b)], axis=1)
        give = jnp.concatenate([side_columns(w, 1 - my_core) for w in (w_a, w_v, w_b)], axis=1)
        got = swap_cores(give)
        block = jnp.concatenate(
            [jnp.where(my_core == 0, keep, got), jnp.where(my_core == 0, got, keep)], axis=0
        )
        av, b_own = block[:, : 2 * columns], block[:, 2 * columns :]

        own_mixed = modulate(context, context_mod[:, 0:1, :], context_mod[:, 1:2, :]).reshape(
            prompt_count * spot_local, width
        )
        mixed = {0: own_mixed}
        ahead = behind = own_mixed
        for o in range(1, chips // 2 + 1):
            ahead = forward(ahead)
            mixed[o] = ahead
            if 2 * o < chips:
                behind = backward(behind)
                mixed[chips - o] = behind

        span = 2 * inner_width // chips
        w_c = jnp.concatenate([w_ck, w_cv], axis=1)
        w_c = w_c.reshape(depth, chips, span).transpose(1, 0, 2)
        w_c = lax.all_to_all(w_c, "dp", 0, 0, axis_index_groups=half_groups, tiled=True)
        w_c_other = swap_cores(w_c)
        w_first = jnp.where(my_core == 0, w_c, w_c_other)
        w_second = jnp.where(my_core == 0, w_c_other, w_c)
        w_c = jnp.stack([w_first, w_second], axis=1).reshape(width, span)

        inverse = (my_place - jnp.array(place, jnp.int32)) % chips
        own = modulate_image(inverse, latents, image_mod)
        other = swap_cores(own)

        group = max(1, chips // 8)
        total_av = accumulate(None, own, other, [0], [av])
        total_b = accumulate(None, own, other, [0], [b_own])
        waiting_av, waiting_b = [], []
        ahead = behind = av
        for o in range(1, chips // 2 + 1):
            if 2 * o == chips:
                a_far = forward(ahead[:, :columns])
                v_far = backward(behind[:, columns:])
                waiting_av.append((o, jnp.concatenate([a_far, v_far], axis=1)))
                waiting_b.append((o, swap_groups(a_far)))
            else:
                ahead, behind = forward(ahead), backward(behind)
                both = jnp.concatenate([ahead[:, :columns], behind[:, :columns]], axis=0)
                both = swap_groups(both)
                half = both.shape[0] // 2
                waiting_av += [(o, ahead), (chips - o, behind)]
                waiting_b += [(o, both[:half]), (chips - o, both[half:])]
            if o % group == 0:
                total_av = accumulate(total_av, own, other, *zip(*waiting_av))
                total_b = accumulate(total_b, own, other, *zip(*waiting_b))
                waiting_av, waiting_b = [], []

        rows = jnp.concatenate([mixed[o] for o in range(chips)], axis=0)
        projected = jnp.dot(rows, w_c, preferred_element_type=jnp.float32).astype(jnp.bfloat16)
        projected = projected.reshape(chips, prompt_count, spot_local, span)
        projected = jnp.take(projected, inverse, axis=0)
        prompt_of = slot_prompts(winner_slot, loser_slot)
        destined = prompt_of.reshape(-1, slot_local)
        outgoing = jnp.take(projected.transpose(1, 0, 2, 3), destined, axis=0)
        arrived = lax.all_to_all(outgoing, "dp", 0, 0, tiled=True)
        arrived = arrived.reshape(chips, 2, slot_local, chips, spot_local, span)
        arrived = arrived.transpose(2, 3, 1, 4, 0, 5).reshape(slot_local, -1, 2 * inner_width)
        arrived = jnp.concatenate([arrived, swap_cores(arrived)], axis=0)
        prompt_keys = side_columns(arrived[..., :inner_width], my_core)
        prompt_values = side_columns(arrived[..., inner_width:], my_core)

        live = jnp.take(lengths, prompt_of, axis=0)
        live_own = lax.dynamic_slice_in_dim(live, me * slot_local, slot_local)
        live_other = lax.dynamic_slice_in_dim(live, (me ^ 1) * slot_local, slot_local)
        flag = my_group.astype(jnp.int32).reshape(1)

        def run(live_part, first):
            return attend(
                jnp.concatenate([flag, live_part]),
                total_av,
                total_b,
                prompt_keys[first : first + slot_local],
                prompt_values[first : first + slot_local],
                head_size,
                first,
                slot_local,
                token_count,
            )

        theirs = swap_cores(run(live_other, slot_local))
        mine = run(live_own, 0)
        low = jnp.where(my_core == 0, mine, theirs)
        high = jnp.where(my_core == 0, theirs, mine)
        whole = jnp.concatenate([low, high[:, 2 * columns - inner_width :]], axis=1)
        return whole.reshape(slot_local, token_count, inner_width)

    placed = (
        P(("groups", "dp"), None, None),
        P("groups", "dp", None),
        P("groups"),
        P("groups"),
        P("groups"),
        P(("groups", "dp"), None, None),
        P("groups", None, None),
        P("dp", None),
        P("dp", None),
        P("dp", None),
        P("dp", None),
        P("dp", None),
    )
    return jax.shard_map(
        local,
        mesh=mesh,
        in_specs=placed,
        out_specs=P(("groups", "dp"), None, None),
        check_vma=False,
    )
```

```python
import functools

import jax
import jax.numpy as jnp
import numpy as np
from jax import lax
from jax.experimental import pallas as pl
from jax.experimental.pallas import tpu as pltpu
from jax.sharding import PartitionSpec as P

HEADS = 19
LANES = 128


epsilon = 1e-06


def params(mib):
    return pltpu.CompilerParams(vmem_limit_bytes=mib * 2**20)


def cost(flops, bytes_accessed):
    return pl.CostEstimate(flops=flops, bytes_accessed=bytes_accessed, transcendentals=0)


def layer_norm(values, shift, scale):
    average = jnp.mean(values, axis=-1, keepdims=True)
    centered = values - average
    variance = jnp.mean(centered * centered, axis=-1, keepdims=True)
    return (centered * lax.rsqrt(variance + epsilon) * (1.0 + scale) + shift).astype(jnp.bfloat16)


def head_pair_norm(x, head_size):
    low = lax.broadcasted_iota(jnp.int32, (1, LANES), 1) < head_size
    squares = x * x
    first = jnp.sum(jnp.where(low, squares, 0.0), axis=-1, keepdims=True)
    second = jnp.sum(jnp.where(low, 0.0, squares), axis=-1, keepdims=True)
    mean = jnp.where(low, first, second) * (1.0 / head_size)
    return (x * lax.rsqrt(mean + epsilon)).astype(jnp.bfloat16)


def split_kernel(columns, scalars, q_ref, k_ref, v_ref, keep_ref, give_ref):
    inner_width = q_ref.shape[1]

    def emit(parts, low_ref, high_ref):
        for i, part in enumerate(parts):
            at = slice(i * columns, (i + 1) * columns)
            low_ref[:, at] = part[:, :columns]
            high_ref[:, at] = part[:, inner_width - columns :]

    for group in range(2):
        parts = (q_ref, v_ref, k_ref) if group == 0 else (k_ref, v_ref, q_ref)
        for core in range(2):
            refs = (keep_ref, give_ref) if core == 0 else (give_ref, keep_ref)
            here = (scalars[0] == group) & (scalars[1] == core)
            pl.when(here)(functools.partial(emit, parts, *refs))


def split_weights(scalars, w_q, w_k, w_v, columns):
    depth = w_q.shape[0]
    whole = pl.BlockSpec(w_q.shape, lambda i, s: (0, 0))
    out = pl.BlockSpec((depth, 3 * columns), lambda i, s: (0, 0))
    shape = jax.ShapeDtypeStruct((depth, 3 * columns), jnp.bfloat16)
    return pl.pallas_call(
        functools.partial(split_kernel, columns),
        grid_spec=pltpu.PrefetchScalarGridSpec(
            num_scalar_prefetch=1, grid=(1,), in_specs=[whole] * 3, out_specs=[out] * 2
        ),
        out_shape=[shape] * 2,
        compiler_params=params(16),
        cost_estimate=cost(0, 12 * depth * 3 * columns),
    )(scalars, w_q, w_k, w_v)


def mixed_kernel(context_ref, mod_ref, out_ref):
    prompts, spots, _ = context_ref.shape
    shift, scale = mod_ref[:, 0, :], mod_ref[:, 1, :]
    for spot in range(spots):
        rows = context_ref[:, spot, :].astype(jnp.float32)
        out_ref[spot * prompts : (spot + 1) * prompts, :] = layer_norm(rows, shift, scale)


def mix_prompts(context, context_mod):
    prompts, spots, width = context.shape
    return pl.pallas_call(
        mixed_kernel,
        out_shape=jax.ShapeDtypeStruct((spots * prompts, width), jnp.bfloat16),
        compiler_params=params(16),
        cost_estimate=cost(0, 10 * prompts * spots * width),
    )(context.astype(jnp.float32), context_mod)


def image_kernel(chips, scalars, x_ref, mod_ref, own_ref, give_ref):
    image = layer_norm(x_ref[0].astype(jnp.float32), mod_ref[0, 0:1, :], mod_ref[0, 1:2, :])
    depth = image.shape[1] // (2 * chips)

    def emit(first_ref, second_ref):
        for chip in range(chips):
            start = 2 * chip * depth
            straight = image[:, start : start + 2 * depth]
            turned = jnp.concatenate([straight[:, depth:], straight[:, :depth]], axis=1)
            first_ref[scalars[2 + chip], :, : 2 * depth] = straight
            second_ref[scalars[2 + chip], :, : 2 * depth] = turned

    pl.when(scalars[1] == 0)(lambda: emit(own_ref, give_ref))
    pl.when(scalars[1] == 1)(lambda: emit(give_ref, own_ref))


def modulate_image(scalars, latents, image_mod, chips):
    slots, tokens, width = latents.shape
    wide = -(-width // chips // LANES) * LANES
    return pl.pallas_call(
        functools.partial(image_kernel, chips),
        grid_spec=pltpu.PrefetchScalarGridSpec(
            num_scalar_prefetch=1,
            grid=(slots,),
            in_specs=[
                pl.BlockSpec((1, tokens, width), lambda i, s: (i, 0, 0)),
                pl.BlockSpec((1, 2, width), lambda i, s: (i, 0, 0)),
            ],
            out_specs=[pl.BlockSpec((chips, tokens, wide), lambda i, s: (0, i, 0))] * 2,
        ),
        out_shape=[jax.ShapeDtypeStruct((chips, slots * tokens, wide), jnp.bfloat16)] * 2,
        compiler_params=params(32),
        cost_estimate=cost(0, 4 * slots * tokens * width),
    )(scalars, latents, image_mod)


def accumulate_kernel(count, has_total, *refs):
    own, other, panels = refs[:count], refs[count : 2 * count], refs[2 * count : 3 * count]
    out_ref = refs[-1]
    step = pl.program_id(0)

    def run(slabs):
        total = refs[3 * count][...] if has_total else None
        for slab, panel in zip(slabs, panels):
            features = slab[0, :, : panel.shape[0]]
            product = jnp.dot(features, panel[...], preferred_element_type=jnp.float32)
            total = product if total is None else total + product
        out_ref[...] = total

    pl.when(step == 0)(lambda: run(own))
    pl.when(step == 1)(lambda: run(other))


def accumulate(total, own, other, places, panels):
    _, rows, wide = own.shape
    count, (depth, columns) = len(places), panels[0].shape
    in_specs = [pl.BlockSpec((1, rows, wide), lambda i, o=o: (o, 0, 0)) for o in places] * 2
    in_specs += [pl.BlockSpec((depth, columns), lambda i: (0, 0)) for _ in places]
    operands = [own] * count + [other] * count + list(panels)
    aliases = {}
    if total is not None:
        in_specs.append(pl.BlockSpec((rows, columns), lambda i: (i, 0)))
        operands.append(total)
        aliases = {3 * count: 0}
    return pl.pallas_call(
        functools.partial(accumulate_kernel, count, total is not None),
        grid=(2,),
        in_specs=in_specs,
        out_specs=pl.BlockSpec((rows, columns), lambda i: (i, 0)),
        out_shape=jax.ShapeDtypeStruct((2 * rows, columns), jnp.float32),
        input_output_aliases=aliases,
        compiler_params=params(40),
        cost_estimate=cost(4 * rows * depth * columns * count, 8 * rows * columns),
    )(*operands)


def pick_kernel(far, ahead_ref, behind_ref, both_ref, *rest):
    rows = ahead_ref.shape[0]
    both_ref[:rows] = ahead_ref[...]
    both_ref[rows:] = behind_ref[...]


def pick(ahead, behind):
    rows, columns = ahead.shape[0], ahead.shape[1] // 2
    half = pl.BlockSpec((rows, columns), lambda i: (0, 0))
    return pl.pallas_call(
        functools.partial(pick_kernel, False),
        grid=(1,),
        in_specs=[half, half],
        out_specs=pl.BlockSpec((2 * rows, columns), lambda i: (0, 0)),
        out_shape=jax.ShapeDtypeStruct((2 * rows, columns), jnp.bfloat16),
        compiler_params=params(16),
        cost_estimate=cost(0, 8 * rows * columns),
    )(ahead, behind)


def cut_kernel(k_ref, v_ref, out_ref):
    chips, _, span = out_ref.shape
    half = chips // 2
    for chip in range(chips):
        source = k_ref if chip < half else v_ref
        start = (chip % half) * span
        out_ref[chip] = source[:, start : start + span]


def cut_prompt_weights(w_ck, w_cv, chips):
    depth, inner_width = w_ck.shape
    span = 2 * inner_width // chips
    return pl.pallas_call(
        cut_kernel,
        out_shape=jax.ShapeDtypeStruct((chips, depth, span), jnp.bfloat16),
        compiler_params=params(16),
        cost_estimate=cost(0, 8 * depth * inner_width),
    )(w_ck, w_cv)


def prompt_kernel(chips, scalars, *refs):
    blocks, weight_ref, out_ref = refs[:chips], refs[chips], refs[chips + 1]
    count = blocks[0].shape[0]
    rows = jnp.concatenate([block[...] for block in blocks], axis=0)
    product = jnp.dot(rows, weight_ref[...], preferred_element_type=jnp.float32)
    product = product.astype(jnp.bfloat16)
    for chip in range(chips):
        for o in range(chips):

            def store(chip=chip, o=o):
                out_ref[chip] = product[o * count : (o + 1) * count]

            pl.when(scalars[2 + chip] == o)(store)


def project_prompts(scalars, blocks, weight):
    chips = len(blocks)
    rows, span = blocks[0].shape[0], weight.shape[1]
    vmem = pl.BlockSpec(memory_space=pltpu.VMEM)
    return pl.pallas_call(
        functools.partial(prompt_kernel, chips),
        in_specs=[pl.BlockSpec(memory_space=pltpu.SMEM)] + [vmem] * (chips + 1),
        out_specs=vmem,
        out_shape=jax.ShapeDtypeStruct((chips, rows, span), jnp.bfloat16),
        compiler_params=params(56),
        cost_estimate=cost(2 * chips * rows * weight.shape[0] * span, 0),
    )(scalars, *blocks, weight)


def route_kernel(spots_here, prompts, winner_ref, loser_ref, rows_ref, out_ref):
    tile, count = out_ref.shape[0], rows_ref.shape[0]
    row = lax.broadcasted_iota(jnp.int32, (tile, 1), 0) + pl.program_id(0) * tile
    column = lax.broadcasted_iota(jnp.int32, (1, count), 1)
    slot = lax.div(row, spots_here)
    same_spot = lax.rem(row, spots_here) == lax.div(column, prompts)
    reads = (winner_ref[...] == slot) | (loser_ref[...] == slot)
    chosen = jnp.where(reads & same_spot, 1.0, 0.0).astype(jnp.bfloat16)
    out_ref[...] = jnp.dot(
        chosen, rows_ref[...], preferred_element_type=jnp.float32
    ).astype(jnp.bfloat16)


def route(projected, winner_slot, loser_slot, spots_here):
    count, span = projected.shape
    prompts = winner_slot.shape[0]
    total = 2 * prompts * spots_here
    tile = min(total, 512)
    row = pl.BlockSpec((1, count), lambda i: (0, 0))
    winners = jnp.tile(winner_slot, spots_here).reshape(1, count)
    losers = jnp.tile(loser_slot, spots_here).reshape(1, count)
    return pl.pallas_call(
        functools.partial(route_kernel, spots_here, prompts),
        grid=(total // tile,),
        in_specs=[row, row, pl.BlockSpec((count, span), lambda i: (0, 0))],
        out_specs=pl.BlockSpec((tile, span), lambda i: (i, 0)),
        out_shape=jax.ShapeDtypeStruct((total, span), jnp.bfloat16),
        compiler_params=params(56),
        cost_estimate=cost(2 * total * count * span, 2 * total * span),
    )(winners, losers, projected)


def finish_kernel(columns, head_size, scalars, own_ref, other_ref, keys_ref, values_ref):
    devices, rows, span = own_ref.shape
    slots = keys_ref.shape[0] // 2
    each = rows // slots
    inner_width = devices // 2 * span // 2

    def emit(start):
        for side, source in enumerate((own_ref, other_ref)):
            for slot in range(slots):
                at = slice(slot * each, (slot + 1) * each)
                for core in range(2):
                    parts = [source[2 * chip + core, at, :] for chip in range(devices // 2)]
                    whole = jnp.concatenate(parts, axis=1)
                    out = side * slots + slot
                    to = slice(core * each, (core + 1) * each)
                    keys = whole[:, start : start + columns].astype(jnp.float32)
                    for pair in range(columns // LANES):
                        lanes = slice(pair * LANES, (pair + 1) * LANES)
                        keys_ref[out, to, lanes] = head_pair_norm(keys[:, lanes], head_size)
                    first = inner_width + start
                    values_ref[out, to, :] = whole[:, first : first + columns]

    pl.when(scalars[1] == 0)(lambda: emit(0))
    pl.when(scalars[1] == 1)(lambda: emit(inner_width - columns))


def finish_prompts(scalars, own, other, columns, head_size, slots):
    devices, rows, _ = own.shape
    span = 2 * rows // slots
    vmem = pl.BlockSpec(memory_space=pltpu.VMEM)
    shape = jax.ShapeDtypeStruct((2 * slots, span, columns), jnp.bfloat16)
    return pl.pallas_call(
        functools.partial(finish_kernel, columns, head_size),
        in_specs=[pl.BlockSpec(memory_space=pltpu.SMEM), vmem, vmem],
        out_specs=[vmem, vmem],
        out_shape=[shape] * 2,
        compiler_params=params(32),
        cost_estimate=cost(0, 16 * slots * span * columns),
    )(scalars, own, other)


def attend_kernel(head_size, spots, scalars, live_ref, a_ref, b_ref, v_ref, pk_ref, pv_ref, out_ref):
    live = live_ref[pl.program_id(0)]
    even_group = scalars[0] == 0
    columns = b_ref.shape[1]
    span = pk_ref.shape[1]
    row = lax.broadcasted_iota(jnp.int32, (span, 1), 0)
    rest = lax.rem(row, span // 2)
    position = (2 * lax.div(rest, spots) + lax.div(row, span // 2)) * spots + lax.rem(rest, spots)
    allowed = position < live
    low = lax.broadcasted_iota(jnp.int32, (1, LANES), 1) < head_size
    over_lanes = (((1,), (1,)), ((), ()))
    over_rows = (((0,), (0,)), ((), ()))
    for pair in range(columns // LANES):
        lanes = slice(pair * LANES, (pair + 1) * LANES)
        a = head_pair_norm(a_ref[:, lanes], head_size)
        b = head_pair_norm(b_ref[:, lanes], head_size)
        queries = jnp.where(even_group, a, b)
        keys = jnp.where(even_group, b, a)
        values = v_ref[:, lanes].astype(jnp.bfloat16)
        prompt_keys = pk_ref[0, :, lanes]
        prompt_values = pv_ref[0, :, lanes]
        for head in range(2):
            side = low if head == 0 else jnp.logical_not(low)
            q = jnp.where(side, queries, jnp.zeros_like(queries))
            s = lax.dot_general(keys, q, over_lanes, preferred_element_type=jnp.float32)
            t = lax.dot_general(prompt_keys, q, over_lanes, preferred_element_type=jnp.float32)
            s = jnp.exp(s * (1.0 / head_size**0.5))
            t = jnp.where(allowed, jnp.exp(t * (1.0 / head_size**0.5)), 0.0)
            total = jnp.sum(s, axis=0, keepdims=True) + jnp.sum(t, axis=0, keepdims=True)
            out = lax.dot_general(
                values, s.astype(jnp.bfloat16), over_rows, preferred_element_type=jnp.float32
            ) + lax.dot_general(
                prompt_values, t.astype(jnp.bfloat16), over_rows, preferred_element_type=jnp.float32
            )
            rows = slice(head * head_size, (head + 1) * head_size)
            to = slice(pair * LANES + head * head_size, pair * LANES + (head + 1) * head_size)
            out_ref[0, to, :] = (out[rows] * (1.0 / total)).astype(jnp.bfloat16)


def attend(scalars, live, av, b, prompt_keys, prompt_values, head_size, spots, first, count):
    tokens = b.shape[0] // (2 * count)
    columns = b.shape[1]
    span = prompt_keys.shape[1]
    return pl.pallas_call(
        functools.partial(attend_kernel, head_size, spots),
        grid_spec=pltpu.PrefetchScalarGridSpec(
            num_scalar_prefetch=2,
            grid=(count,),
            in_specs=[
                pl.BlockSpec((tokens, columns), lambda l, s, t: (first + l, 0)),
                pl.BlockSpec((tokens, columns), lambda l, s, t: (first + l, 0)),
                pl.BlockSpec((tokens, columns), lambda l, s, t: (first + l, 1)),
                pl.BlockSpec((1, span, columns), lambda l, s, t: (first + l, 0, 0)),
                pl.BlockSpec((1, span, columns), lambda l, s, t: (first + l, 0, 0)),
            ],
            out_specs=pl.BlockSpec((1, columns, tokens), lambda l, s, t: (l, 0, 0)),
        ),
        out_shape=jax.ShapeDtypeStruct((count, columns, tokens), jnp.bfloat16),
        compiler_params=params(32),
        cost_estimate=cost(
            8 * count * tokens * (tokens + span) * columns, count * tokens * columns * 14
        ),
    )(scalars, live, av, b, av, prompt_keys, prompt_values)


def ring_order(groups, chips):
    if groups == 2:
        return list(range(0, chips, 2)) + list(range(1, chips, 2))[::-1]
    return list(range(chips))


def solution(mesh):
    groups, dp = mesh.shape["groups"], mesh.shape["dp"]
    chips = dp // 2
    ring = ring_order(groups, chips)
    place = [ring.index(chip) for chip in range(chips)]
    behind_by = np.array(
        [[(place[me] - place[chip]) % chips for chip in range(chips)] for me in range(chips)],
        np.int32,
    )
    forward_pairs = [
        (2 * ring[i] + c, 2 * ring[(i + 1) % chips] + c) for i in range(chips) for c in range(2)
    ]
    backward_pairs = [(b, a) for a, b in forward_pairs]
    core_pairs = [(d, d ^ 1) for d in range(dp)]
    group_pairs = [(g, g ^ 1) for g in range(groups)]
    half_groups = [[2 * chip + c for chip in range(chips)] for c in range(2)]

    def forward(x):
        return lax.ppermute(x, "dp", forward_pairs)

    def backward(x):
        return lax.ppermute(x, "dp", backward_pairs)

    def swap_cores(x):
        return lax.ppermute(x, "dp", core_pairs)

    def swap_groups(x):
        return lax.ppermute(x, "groups", group_pairs)

    def local(
        latents,
        context,
        lengths,
        winner_slot,
        loser_slot,
        image_mod,
        context_mod,
        w_q,
        w_k,
        w_v,
        w_ck,
        w_cv,
    ):
        slot_local, token_count, width = latents.shape
        prompt_count, spot_local, _ = context.shape
        depth, inner_width = w_q.shape
        head_size = inner_width // HEADS
        columns = (HEADS + 1) // 2 * head_size
        me = lax.axis_index("dp")
        my_group = lax.axis_index("groups") % 2
        my_chip, my_core = me // 2, me % 2
        places = lax.dynamic_index_in_dim(jnp.asarray(behind_by), my_chip, 0, keepdims=False)
        scalars = jnp.concatenate([jnp.stack([my_group, my_core]).astype(jnp.int32), places])

        keep, give = split_weights(scalars, w_q, w_k, w_v, columns)
        got = swap_cores(give)
        av = jnp.concatenate([keep[:, : 2 * columns], got[:, : 2 * columns]], axis=0)
        b_own = jnp.concatenate([keep[:, 2 * columns :], got[:, 2 * columns :]], axis=0)

        own, give = modulate_image(scalars, latents, image_mod, chips)
        other = swap_cores(give)

        own_mixed = mix_prompts(context, context_mod)
        mixed = {0: own_mixed}
        ahead = behind = own_mixed
        for o in range(1, chips // 2 + 1):
            ahead = forward(ahead)
            mixed[o] = ahead
            if 2 * o < chips:
                behind = backward(behind)
                mixed[chips - o] = behind

        w_c = cut_prompt_weights(w_ck, w_cv, chips)
        w_c = lax.all_to_all(w_c, "dp", 0, 0, axis_index_groups=half_groups, tiled=True)
        w_c_other = swap_cores(w_c)
        w_first = jnp.where(my_core == 0, w_c, w_c_other)
        w_second = jnp.where(my_core == 0, w_c_other, w_c)
        w_c = jnp.stack([w_first, w_second], axis=1).reshape(width, -1)

        total_av = total_b = None
        waiting_av, waiting_b = [(0, av)], [(0, b_own)]
        enough = max(1, 3 * chips // 8)
        ahead = behind = av
        for o in range(1, chips // 2 + 1):
            if 2 * o == chips:
                a_far = forward(ahead[:, :columns])
                v_far = backward(behind[:, columns:])
                waiting_av.append((o, jnp.concatenate([a_far, v_far], axis=1)))
                waiting_b.append((o, swap_groups(a_far)))
            else:
                ahead, behind = forward(ahead), backward(behind)
                both = swap_groups(pick(ahead, behind))
                half = both.shape[0] // 2
                waiting_av += [(o, ahead), (chips - o, behind)]
                waiting_b += [(o, both[:half]), (chips - o, both[half:])]
            if 2 * o == chips or len(waiting_av) >= enough:
                total_av = accumulate(total_av, own, other, *zip(*waiting_av))
                total_b = accumulate(total_b, own, other, *zip(*waiting_b))
                waiting_av, waiting_b = [], []

        blocks = [mixed[o] for o in range(chips)]
        projected = project_prompts(scalars, blocks, w_c).reshape(-1, w_c.shape[1])
        outgoing = route(projected, winner_slot, loser_slot, chips * spot_local)
        outgoing = outgoing.reshape(dp, -1, w_c.shape[1])
        arrived = lax.all_to_all(outgoing, "dp", 0, 0, tiled=True)
        prompt_keys, prompt_values = finish_prompts(
            scalars, arrived, swap_cores(arrived), columns, head_size, slot_local
        )

        here = jnp.arange(slot_local, dtype=jnp.int32)
        slots = jnp.concatenate([me * slot_local + here, (me ^ 1) * slot_local + here])
        reads = (winner_slot[None, :] == slots[:, None]) | (loser_slot[None, :] == slots[:, None])
        live = jnp.sum(jnp.where(reads, lengths[None, :], 0), axis=1)

        def run(first):
            return attend(
                scalars[:2],
                live[first : first + slot_local],
                total_av,
                total_b,
                prompt_keys,
                prompt_values,
                head_size,
                spot_local,
                first,
                slot_local,
            )

        theirs = swap_cores(run(slot_local))
        mine = run(0)
        low = jnp.where(my_core == 0, mine, theirs)
        high = jnp.where(my_core == 0, theirs, mine)
        whole = jnp.concatenate([low, high[:, 2 * columns - inner_width :]], axis=1)
        return whole.transpose(0, 2, 1)

    placed = (
        P(("groups", "dp"), None, None),
        P("groups", "dp", None),
        P("groups"),
        P("groups"),
        P("groups"),
        P(("groups", "dp"), None, None),
        P("groups", None, None),
        P("dp", None),
        P("dp", None),
        P("dp", None),
        P("dp", None),
        P("dp", None),
    )
    return jax.shard_map(
        local,
        mesh=mesh,
        in_specs=placed,
        out_specs=P(("groups", "dp"), None, None),
        check_vma=False,
    )
```

```python
import functools

import jax
import jax.numpy as jnp
import numpy as np
from jax import lax
from jax.experimental import pallas as pl
from jax.experimental.pallas import tpu as pltpu
from jax.sharding import PartitionSpec as P

HEADS = 19
LANES = 128


epsilon = 1e-06


def params(mib):
    return pltpu.CompilerParams(vmem_limit_bytes=mib * 2**20)


def cost(flops, bytes_accessed):
    return pl.CostEstimate(flops=flops, bytes_accessed=bytes_accessed, transcendentals=0)


def layer_norm(values, shift, scale):
    average = jnp.mean(values, axis=-1, keepdims=True)
    centered = values - average
    variance = jnp.mean(centered * centered, axis=-1, keepdims=True)
    return (centered * lax.rsqrt(variance + epsilon) * (1.0 + scale) + shift).astype(jnp.bfloat16)


def head_pair_norm(x, head_size):
    low = lax.broadcasted_iota(jnp.int32, (1, LANES), 1) < head_size
    squares = x * x
    first = jnp.sum(jnp.where(low, squares, 0.0), axis=-1, keepdims=True)
    second = jnp.sum(jnp.where(low, 0.0, squares), axis=-1, keepdims=True)
    mean = jnp.where(low, first, second) * (1.0 / head_size)
    return (x * lax.rsqrt(mean + epsilon)).astype(jnp.bfloat16)


def split_kernel(columns, scalars, q_ref, k_ref, v_ref, after_ref, keep_ref, give_ref):
    inner_width = q_ref.shape[1]

    def emit(parts, low_ref, high_ref):
        for i, part in enumerate(parts):
            at = slice(i * columns, (i + 1) * columns)
            low_ref[:, at] = part[:, :columns]
            high_ref[:, at] = part[:, inner_width - columns :]

    for group in range(2):
        parts = (q_ref, v_ref, k_ref) if group == 0 else (k_ref, v_ref, q_ref)
        for core in range(2):
            refs = (keep_ref, give_ref) if core == 0 else (give_ref, keep_ref)
            here = (scalars[0] == group) & (scalars[1] == core)
            pl.when(here)(functools.partial(emit, parts, *refs))


def split_weights(scalars, w_q, w_k, w_v, columns, after):
    depth = w_q.shape[0]
    whole = pl.BlockSpec(w_q.shape, lambda i, s: (0, 0))
    out = pl.BlockSpec((depth, 3 * columns), lambda i, s: (0, 0))
    shape = jax.ShapeDtypeStruct((depth, 3 * columns), jnp.bfloat16)
    return pl.pallas_call(
        functools.partial(split_kernel, columns),
        grid_spec=pltpu.PrefetchScalarGridSpec(
            num_scalar_prefetch=1,
            grid=(1,),
            in_specs=[whole] * 3 + [pl.BlockSpec(memory_space=pl.ANY)],
            out_specs=[out] * 2,
        ),
        out_shape=[shape] * 2,
        compiler_params=params(16),
        cost_estimate=cost(0, 12 * depth * 3 * columns),
    )(scalars, w_q, w_k, w_v, after)


def mixed_kernel(context_ref, mod_ref, out_ref):
    prompts, spots, _ = context_ref.shape
    shift, scale = mod_ref[:, 0, :], mod_ref[:, 1, :]
    for spot in range(spots):
        rows = context_ref[:, spot, :].astype(jnp.float32)
        out_ref[spot * prompts : (spot + 1) * prompts, :] = layer_norm(rows, shift, scale)


def mix_prompts(context, context_mod):
    prompts, spots, width = context.shape
    return pl.pallas_call(
        mixed_kernel,
        out_shape=jax.ShapeDtypeStruct((spots * prompts, width), jnp.bfloat16),
        compiler_params=params(16),
        cost_estimate=cost(0, 10 * prompts * spots * width),
    )(context.astype(jnp.float32), context_mod)


def image_kernel(chips, scalars, x_ref, mod_ref, after_ref, own_ref, give_ref):
    image = layer_norm(x_ref[0].astype(jnp.float32), mod_ref[0, 0:1, :], mod_ref[0, 1:2, :])
    depth = image.shape[1] // (2 * chips)

    def emit(first_ref, second_ref):
        for chip in range(chips):
            start = 2 * chip * depth
            straight = image[:, start : start + 2 * depth]
            turned = jnp.concatenate([straight[:, depth:], straight[:, :depth]], axis=1)
            first_ref[scalars[2 + chip], :, : 2 * depth] = straight
            second_ref[scalars[2 + chip], :, : 2 * depth] = turned

    pl.when(scalars[1] == 0)(lambda: emit(own_ref, give_ref))
    pl.when(scalars[1] == 1)(lambda: emit(give_ref, own_ref))


def modulate_image(scalars, latents, image_mod, chips, after):
    slots, tokens, width = latents.shape
    wide = -(-width // chips // LANES) * LANES
    return pl.pallas_call(
        functools.partial(image_kernel, chips),
        grid_spec=pltpu.PrefetchScalarGridSpec(
            num_scalar_prefetch=1,
            grid=(slots,),
            in_specs=[
                pl.BlockSpec((1, tokens, width), lambda i, s: (i, 0, 0)),
                pl.BlockSpec((1, 2, width), lambda i, s: (i, 0, 0)),
                pl.BlockSpec(memory_space=pl.ANY),
            ],
            out_specs=[pl.BlockSpec((chips, tokens, wide), lambda i, s: (0, i, 0))] * 2,
        ),
        out_shape=[jax.ShapeDtypeStruct((chips, slots * tokens, wide), jnp.bfloat16)] * 2,
        compiler_params=params(32),
        cost_estimate=cost(0, 4 * slots * tokens * width),
    )(scalars, latents, image_mod, after)


def accumulate_kernel(count, has_total, *refs):
    own, other, panels = refs[:count], refs[count : 2 * count], refs[2 * count : 3 * count]
    out_ref, token_ref = refs[-2:]
    step = pl.program_id(0)
    token_ref[...] = jnp.zeros_like(token_ref)

    def run(slabs):
        features = [slab[0, :, : panel.shape[0]] for slab, panel in zip(slabs, panels)]
        features = jnp.concatenate(features, axis=1)
        panel = jnp.concatenate([panel[...] for panel in panels], axis=0)
        product = jnp.dot(features, panel, preferred_element_type=jnp.float32)
        out_ref[...] = refs[3 * count][...] + product if has_total else product

    pl.when(step == 0)(lambda: run(own))
    pl.when(step == 1)(lambda: run(other))


def accumulate(total, own, other, places, panels):
    _, rows, wide = own.shape
    count, (depth, columns) = len(places), panels[0].shape
    in_specs = [pl.BlockSpec((1, rows, wide), lambda i, o=o: (o, 0, 0)) for o in places] * 2
    in_specs += [pl.BlockSpec((depth, columns), lambda i: (0, 0)) for _ in places]
    operands = [own] * count + [other] * count + list(panels)
    aliases = {}
    if total is not None:
        in_specs.append(pl.BlockSpec((rows, columns), lambda i: (i, 0)))
        operands.append(total)
        aliases = {3 * count: 0}
    return pl.pallas_call(
        functools.partial(accumulate_kernel, count, total is not None),
        grid=(2,),
        in_specs=in_specs,
        out_specs=[
            pl.BlockSpec((rows, columns), lambda i: (i, 0)),
            pl.BlockSpec((8, LANES), lambda i: (0, 0)),
        ],
        out_shape=[
            jax.ShapeDtypeStruct((2 * rows, columns), jnp.float32),
            jax.ShapeDtypeStruct((8, LANES), jnp.float32),
        ],
        input_output_aliases=aliases,
        compiler_params=params(36),
        cost_estimate=cost(4 * rows * depth * columns * count, 8 * rows * columns),
    )(*operands)


def pick_kernel(far, ahead_ref, behind_ref, *refs):
    outs = refs[-(1 + far * 2) :]
    rows, columns = ahead_ref.shape[0], ahead_ref.shape[1] // 2
    outs[0][:rows] = ahead_ref[:, :columns]
    outs[0][rows:] = behind_ref[:, :columns]
    if far:
        outs[1][...] = ahead_ref[:, :columns]
        outs[2][...] = behind_ref[:, columns:]


def pick(ahead, behind, far, tokens):
    rows, columns = ahead.shape[0], ahead.shape[1] // 2
    vmem = pl.BlockSpec(memory_space=pltpu.VMEM)
    shapes = [(2 * rows, columns)] + [(rows, columns)] * (2 * far)
    return pl.pallas_call(
        functools.partial(pick_kernel, far),
        in_specs=[vmem, vmem] + [pl.BlockSpec(memory_space=pl.ANY)] * len(tokens),
        out_specs=[vmem] * len(shapes),
        out_shape=[jax.ShapeDtypeStruct(shape, jnp.bfloat16) for shape in shapes],
        compiler_params=params(16),
        cost_estimate=cost(0, 8 * rows * columns),
    )(ahead, behind, *tokens)


def cut_kernel(k_ref, v_ref, after_ref, out_ref):
    chips, _, span = out_ref.shape
    half = chips // 2
    for chip in range(chips):
        source = k_ref if chip < half else v_ref
        start = (chip % half) * span
        out_ref[chip] = source[:, start : start + span]


def cut_prompt_weights(w_ck, w_cv, chips, after):
    depth, inner_width = w_ck.shape
    span = 2 * inner_width // chips
    vmem = pl.BlockSpec(memory_space=pltpu.VMEM)
    return pl.pallas_call(
        cut_kernel,
        in_specs=[vmem, vmem, pl.BlockSpec(memory_space=pl.ANY)],
        out_shape=jax.ShapeDtypeStruct((chips, depth, span), jnp.bfloat16),
        compiler_params=params(16),
        cost_estimate=cost(0, 8 * depth * inner_width),
    )(w_ck, w_cv, after)


def prompt_kernel(rows_ref, weight_ref, after_ref, out_ref):
    product = jnp.dot(rows_ref[...], weight_ref[...], preferred_element_type=jnp.float32)
    out_ref[...] = product.astype(jnp.bfloat16)


def project_prompts(rows, weight, after):
    count, (depth, span) = rows.shape[0], weight.shape
    tile = min(count, 512)
    return pl.pallas_call(
        prompt_kernel,
        grid=(count // tile,),
        in_specs=[
            pl.BlockSpec((tile, depth), lambda i: (i, 0)),
            pl.BlockSpec((depth, span), lambda i: (0, 0)),
            pl.BlockSpec(memory_space=pl.ANY),
        ],
        out_specs=pl.BlockSpec((tile, span), lambda i: (i, 0)),
        out_shape=jax.ShapeDtypeStruct((count, span), jnp.bfloat16),
        compiler_params=params(24),
        cost_estimate=cost(2 * count * depth * span, 2 * count * depth),
    )(rows, weight, after)


def route_kernel(spots_here, prompts, winner_ref, loser_ref, rows_ref, out_ref):
    tile, count = out_ref.shape[0], rows_ref.shape[0]
    row = lax.broadcasted_iota(jnp.int32, (tile, 1), 0) + pl.program_id(0) * tile
    column = lax.broadcasted_iota(jnp.int32, (1, count), 1)
    slot = lax.div(row, spots_here)
    same_spot = lax.rem(row, spots_here) == lax.div(column, prompts)
    reads = (winner_ref[...] == slot) | (loser_ref[...] == slot)
    chosen = jnp.where(reads & same_spot, 1.0, 0.0).astype(jnp.bfloat16)
    out_ref[...] = jnp.dot(
        chosen, rows_ref[...], preferred_element_type=jnp.float32
    ).astype(jnp.bfloat16)


def route(projected, winner_slot, loser_slot, spots_here):
    count, span = projected.shape
    prompts = winner_slot.shape[0]
    total = 2 * prompts * spots_here
    tile = min(total, 512)
    row = pl.BlockSpec((1, count), lambda i: (0, 0))
    winners = jnp.tile(winner_slot, spots_here).reshape(1, count)
    losers = jnp.tile(loser_slot, spots_here).reshape(1, count)
    return pl.pallas_call(
        functools.partial(route_kernel, spots_here, prompts),
        grid=(total // tile,),
        in_specs=[row, row, pl.BlockSpec((count, span), lambda i: (0, 0))],
        out_specs=pl.BlockSpec((tile, span), lambda i: (i, 0)),
        out_shape=jax.ShapeDtypeStruct((total, span), jnp.bfloat16),
        compiler_params=params(56),
        cost_estimate=cost(2 * total * count * span, 2 * total * span),
    )(winners, losers, projected)


def finish_kernel(columns, head_size, scalars, own_ref, other_ref, keys_ref, values_ref):
    devices, rows, span = own_ref.shape
    slots = keys_ref.shape[0] // 2
    each = rows // slots
    inner_width = devices // 2 * span // 2

    def emit(start):
        for side, source in enumerate((own_ref, other_ref)):
            for slot in range(slots):
                at = slice(slot * each, (slot + 1) * each)
                for core in range(2):
                    parts = [source[2 * chip + core, at, :] for chip in range(devices // 2)]
                    whole = jnp.concatenate(parts, axis=1)
                    out = side * slots + slot
                    to = slice(core * each, (core + 1) * each)
                    keys = whole[:, start : start + columns].astype(jnp.float32)
                    for pair in range(columns // LANES):
                        lanes = slice(pair * LANES, (pair + 1) * LANES)
                        keys_ref[out, to, lanes] = head_pair_norm(keys[:, lanes], head_size)
                    first = inner_width + start
                    values_ref[out, to, :] = whole[:, first : first + columns]

    pl.when(scalars[1] == 0)(lambda: emit(0))
    pl.when(scalars[1] == 1)(lambda: emit(inner_width - columns))


def finish_prompts(scalars, own, other, columns, head_size, slots):
    devices, rows, _ = own.shape
    span = 2 * rows // slots
    vmem = pl.BlockSpec(memory_space=pltpu.VMEM)
    shape = jax.ShapeDtypeStruct((2 * slots, span, columns), jnp.bfloat16)
    return pl.pallas_call(
        functools.partial(finish_kernel, columns, head_size),
        in_specs=[pl.BlockSpec(memory_space=pltpu.SMEM), vmem, vmem],
        out_specs=[vmem, vmem],
        out_shape=[shape] * 2,
        compiler_params=params(32),
        cost_estimate=cost(0, 16 * slots * span * columns),
    )(scalars, own, other)


def attend_kernel(head_size, spots, scalars, live_ref, a_ref, b_ref, v_ref, pk_ref, pv_ref, out_ref):
    live = live_ref[pl.program_id(0)]
    even_group = scalars[0] == 0
    columns = b_ref.shape[1]
    span = pk_ref.shape[1]
    row = lax.broadcasted_iota(jnp.int32, (span, 1), 0)
    rest = lax.rem(row, span // 2)
    position = (2 * lax.div(rest, spots) + lax.div(row, span // 2)) * spots + lax.rem(rest, spots)
    allowed = position < live
    low = lax.broadcasted_iota(jnp.int32, (1, LANES), 1) < head_size
    over_lanes = (((1,), (1,)), ((), ()))
    over_rows = (((0,), (0,)), ((), ()))
    for pair in range(columns // LANES):
        lanes = slice(pair * LANES, (pair + 1) * LANES)
        a = head_pair_norm(a_ref[:, lanes], head_size)
        b = head_pair_norm(b_ref[:, lanes], head_size)
        queries = jnp.where(even_group, a, b)
        keys = jnp.where(even_group, b, a)
        values = v_ref[:, lanes].astype(jnp.bfloat16)
        prompt_keys = pk_ref[0, :, lanes]
        prompt_values = pv_ref[0, :, lanes]
        for head in range(2):
            side = low if head == 0 else jnp.logical_not(low)
            q = jnp.where(side, queries, jnp.zeros_like(queries))
            s = lax.dot_general(keys, q, over_lanes, preferred_element_type=jnp.float32)
            t = lax.dot_general(prompt_keys, q, over_lanes, preferred_element_type=jnp.float32)
            s = jnp.exp(s * (1.0 / head_size**0.5))
            t = jnp.where(allowed, jnp.exp(t * (1.0 / head_size**0.5)), 0.0)
            total = jnp.sum(s, axis=0, keepdims=True) + jnp.sum(t, axis=0, keepdims=True)
            out = lax.dot_general(
                values, s.astype(jnp.bfloat16), over_rows, preferred_element_type=jnp.float32
            ) + lax.dot_general(
                prompt_values, t.astype(jnp.bfloat16), over_rows, preferred_element_type=jnp.float32
            )
            rows = slice(head * head_size, (head + 1) * head_size)
            to = slice(pair * LANES + head * head_size, pair * LANES + (head + 1) * head_size)
            out_ref[0, to, :] = (out[rows] * (1.0 / total)).astype(jnp.bfloat16)


def attend(scalars, live, av, b, prompt_keys, prompt_values, head_size, spots, first, count):
    tokens = b.shape[0] // (2 * count)
    columns = b.shape[1]
    span = prompt_keys.shape[1]
    return pl.pallas_call(
        functools.partial(attend_kernel, head_size, spots),
        grid_spec=pltpu.PrefetchScalarGridSpec(
            num_scalar_prefetch=2,
            grid=(count,),
            in_specs=[
                pl.BlockSpec((tokens, columns), lambda l, s, t: (first + l, 0)),
                pl.BlockSpec((tokens, columns), lambda l, s, t: (first + l, 0)),
                pl.BlockSpec((tokens, columns), lambda l, s, t: (first + l, 1)),
                pl.BlockSpec((1, span, columns), lambda l, s, t: (first + l, 0, 0)),
                pl.BlockSpec((1, span, columns), lambda l, s, t: (first + l, 0, 0)),
            ],
            out_specs=pl.BlockSpec((1, columns, tokens), lambda l, s, t: (l, 0, 0)),
        ),
        out_shape=jax.ShapeDtypeStruct((count, columns, tokens), jnp.bfloat16),
        compiler_params=params(32),
        cost_estimate=cost(
            8 * count * tokens * (tokens + span) * columns, count * tokens * columns * 14
        ),
    )(scalars, live, av, b, av, prompt_keys, prompt_values)


def ring_order(groups, chips):
    if groups == 2:
        return list(range(0, chips, 2)) + list(range(1, chips, 2))[::-1]
    return list(range(chips))


def solution(mesh):
    groups, dp = mesh.shape["groups"], mesh.shape["dp"]
    chips = dp // 2
    ring = ring_order(groups, chips)
    place = [ring.index(chip) for chip in range(chips)]
    behind_by = np.array(
        [[(place[me] - place[chip]) % chips for chip in range(chips)] for me in range(chips)],
        np.int32,
    )
    forward_pairs = [
        (2 * ring[i] + c, 2 * ring[(i + 1) % chips] + c) for i in range(chips) for c in range(2)
    ]
    backward_pairs = [(b, a) for a, b in forward_pairs]
    core_pairs = [(d, d ^ 1) for d in range(dp)]
    group_pairs = [(g, g ^ 1) for g in range(groups)]
    half_groups = [[2 * chip + c for chip in range(chips)] for c in range(2)]

    def forward(x):
        return lax.ppermute(x, "dp", forward_pairs)

    def backward(x):
        return lax.ppermute(x, "dp", backward_pairs)

    def swap_cores(x):
        return lax.ppermute(x, "dp", core_pairs)

    def swap_groups(x):
        return lax.ppermute(x, "groups", group_pairs)

    def local(
        latents,
        context,
        lengths,
        winner_slot,
        loser_slot,
        image_mod,
        context_mod,
        w_q,
        w_k,
        w_v,
        w_ck,
        w_cv,
    ):
        slot_local, token_count, width = latents.shape
        prompt_count, spot_local, _ = context.shape
        depth, inner_width = w_q.shape
        head_size = inner_width // HEADS
        columns = (HEADS + 1) // 2 * head_size
        me = lax.axis_index("dp")
        my_group = lax.axis_index("groups") % 2
        my_chip, my_core = me // 2, me % 2
        places = lax.dynamic_index_in_dim(jnp.asarray(behind_by), my_chip, 0, keepdims=False)
        scalars = jnp.concatenate([jnp.stack([my_group, my_core]).astype(jnp.int32), places])

        mixed = mix_prompts(context, context_mod)
        rows = lax.all_gather(
            mixed,
            "dp",
            axis_index_groups=half_groups,
            axis=0,
            tiled=True,
        )

        keep, give = split_weights(scalars, w_q, w_k, w_v, columns, mixed)
        got = swap_cores(give)
        av = jnp.concatenate([keep[:, : 2 * columns], got[:, : 2 * columns]], axis=0)
        b_own = jnp.concatenate([keep[:, 2 * columns :], got[:, 2 * columns :]], axis=0)

        own, give = modulate_image(scalars, latents, image_mod, chips, av)
        other = swap_cores(give)

        w_c = cut_prompt_weights(w_ck, w_cv, chips, av)
        w_c = lax.all_to_all(w_c, "dp", 0, 0, axis_index_groups=half_groups, tiled=True)
        w_c_other = swap_cores(w_c)
        w_first = jnp.where(my_core == 0, w_c, w_c_other)
        w_second = jnp.where(my_core == 0, w_c_other, w_c)
        w_c = jnp.stack([w_first, w_second], axis=1).reshape(width, -1)

        total_av = total_b = None
        waiting_av, waiting_b, swapped = [(0, av)], [(0, b_own)], []
        enough = max(1, chips // 8)
        tokens = []
        ahead = behind = av
        for o in range(1, chips // 2):
            ahead, behind = forward(ahead), backward(behind)
            after = ahead
            last = 2 * o + 2 == chips
            picked = pick(ahead, behind, last, tokens)
            tokens = []
            if len(swapped) >= enough or last:
                waiting_b += swapped
                swapped = []
                total_b, token = accumulate(total_b, own, other, *zip(*waiting_b))
                tokens.append(token)
                waiting_b = []
            both = swap_groups(picked[0])
            half = both.shape[0] // 2
            swapped += [(o, both[:half]), (chips - o, both[half:])]
            waiting_av += [(o, ahead), (chips - o, behind)]
            if len(waiting_av) >= 2 * enough or last:
                total_av, token = accumulate(total_av, own, other, *zip(*waiting_av))
                tokens.append(token)
                waiting_av = []
        a_far, v_far = forward(picked[1]), backward(picked[2])
        b_far = swap_groups(a_far)
        total_b, _ = accumulate(total_b, own, other, *zip(*swapped))
        total_av, _ = accumulate(
            total_av, own, other, [chips // 2], [jnp.concatenate([a_far, v_far], axis=1)]
        )
        total_b, _ = accumulate(total_b, own, other, [chips // 2], [b_far])

        projected = project_prompts(rows, w_c, after)
        outgoing = route(projected, winner_slot, loser_slot, chips * spot_local)
        outgoing = outgoing.reshape(dp, -1, w_c.shape[1])
        arrived = lax.all_to_all(outgoing, "dp", 0, 0, tiled=True)
        prompt_keys, prompt_values = finish_prompts(
            scalars, arrived, swap_cores(arrived), columns, head_size, slot_local
        )

        here = jnp.arange(slot_local, dtype=jnp.int32)
        slots = jnp.concatenate([me * slot_local + here, (me ^ 1) * slot_local + here])
        reads = (winner_slot[None, :] == slots[:, None]) | (loser_slot[None, :] == slots[:, None])
        live = jnp.sum(jnp.where(reads, lengths[None, :], 0), axis=1)

        def run(first):
            return attend(
                scalars[:2],
                live[first : first + slot_local],
                total_av,
                total_b,
                prompt_keys,
                prompt_values,
                head_size,
                spot_local,
                first,
                slot_local,
            )

        theirs = swap_cores(run(slot_local))
        mine = run(0)
        low = jnp.where(my_core == 0, mine, theirs)
        high = jnp.where(my_core == 0, theirs, mine)
        whole = jnp.concatenate([low, high[:, 2 * columns - inner_width :]], axis=1)
        return whole.transpose(0, 2, 1)

    placed = (
        P(("groups", "dp"), None, None),
        P("groups", "dp", None),
        P("groups"),
        P("groups"),
        P("groups"),
        P(("groups", "dp"), None, None),
        P("groups", None, None),
        P("dp", None),
        P("dp", None),
        P("dp", None),
        P("dp", None),
        P("dp", None),
    )
    return jax.shard_map(
        local,
        mesh=mesh,
        in_specs=placed,
        out_specs=P(("groups", "dp"), None, None),
        check_vma=False,
    )
```

```python
import functools

import jax
import jax.numpy as jnp
import numpy as np
from jax import lax
from jax.experimental import pallas as pl
from jax.experimental.pallas import tpu as pltpu
from jax.sharding import PartitionSpec as P

HEADS = 19
LANES = 128


epsilon = 1e-06


def params(mib):
    return pltpu.CompilerParams(vmem_limit_bytes=mib * 2**20)


def cost():
    return pl.CostEstimate(flops=1, bytes_accessed=1, transcendentals=0)


def layer_norm(values, shift, scale):
    average = jnp.mean(values, axis=-1, keepdims=True)
    centered = values - average
    variance = jnp.mean(centered * centered, axis=-1, keepdims=True)
    return (centered * lax.rsqrt(variance + epsilon) * (1.0 + scale) + shift).astype(jnp.bfloat16)


def head_pair_norm(x, head_size):
    low = lax.broadcasted_iota(jnp.int32, (1, LANES), 1) < head_size
    squares = x * x
    first = jnp.sum(jnp.where(low, squares, 0.0), axis=-1, keepdims=True)
    second = jnp.sum(jnp.where(low, 0.0, squares), axis=-1, keepdims=True)
    mean = jnp.where(low, first, second) * (1.0 / head_size)
    return (x * lax.rsqrt(mean + epsilon)).astype(jnp.bfloat16)


def split_kernel(columns, scalars, q_ref, k_ref, v_ref, after_ref, keep_ref, give_ref):
    inner_width = q_ref.shape[1]

    def emit(parts, low_ref, high_ref):
        for i, part in enumerate(parts):
            at = slice(i * columns, (i + 1) * columns)
            low_ref[:, at] = part[:, :columns]
            high_ref[:, at] = part[:, inner_width - columns :]

    for group in range(2):
        parts = (q_ref, v_ref, k_ref) if group == 0 else (k_ref, v_ref, q_ref)
        for core in range(2):
            refs = (keep_ref, give_ref) if core == 0 else (give_ref, keep_ref)
            here = (scalars[0] == group) & (scalars[1] == core)
            pl.when(here)(functools.partial(emit, parts, *refs))


def split_weights(scalars, w_q, w_k, w_v, columns, after):
    depth = w_q.shape[0]
    whole = pl.BlockSpec(w_q.shape, lambda i, s: (0, 0))
    out = pl.BlockSpec((depth, 3 * columns), lambda i, s: (0, 0))
    shape = jax.ShapeDtypeStruct((depth, 3 * columns), jnp.bfloat16)
    return pl.pallas_call(
        functools.partial(split_kernel, columns),
        grid_spec=pltpu.PrefetchScalarGridSpec(
            num_scalar_prefetch=1,
            grid=(1,),
            in_specs=[whole] * 3 + [pl.BlockSpec(memory_space=pl.ANY)],
            out_specs=[out] * 2,
        ),
        out_shape=[shape] * 2,
        compiler_params=params(16),
        cost_estimate=cost(),
    )(scalars, w_q, w_k, w_v, after)


def mixed_kernel(context_ref, mod_ref, out_ref):
    prompts, spots, _ = context_ref.shape
    shift, scale = mod_ref[:, 0, :], mod_ref[:, 1, :]
    for spot in range(spots):
        rows = context_ref[:, spot, :].astype(jnp.float32)
        out_ref[spot * prompts : (spot + 1) * prompts, :] = layer_norm(rows, shift, scale)


def mix_prompts(context, context_mod):
    prompts, spots, width = context.shape
    return pl.pallas_call(
        mixed_kernel,
        out_shape=jax.ShapeDtypeStruct((spots * prompts, width), jnp.bfloat16),
        compiler_params=params(16),
        cost_estimate=cost(),
    )(context.astype(jnp.float32), context_mod)


def image_kernel(chips, scalars, x_ref, mod_ref, after_ref, own_ref, give_ref):
    image = layer_norm(x_ref[0].astype(jnp.float32), mod_ref[0, 0:1, :], mod_ref[0, 1:2, :])
    depth = image.shape[1] // (2 * chips)

    def emit(first_ref, second_ref):
        for chip in range(chips):
            start = 2 * chip * depth
            straight = image[:, start : start + 2 * depth]
            turned = jnp.concatenate([straight[:, depth:], straight[:, :depth]], axis=1)
            first_ref[scalars[2 + chip], :, : 2 * depth] = straight
            second_ref[scalars[2 + chip], :, : 2 * depth] = turned

    pl.when(scalars[1] == 0)(lambda: emit(own_ref, give_ref))
    pl.when(scalars[1] == 1)(lambda: emit(give_ref, own_ref))


def modulate_image(scalars, latents, image_mod, chips, after):
    slots, tokens, width = latents.shape
    wide = -(-width // chips // LANES) * LANES
    return pl.pallas_call(
        functools.partial(image_kernel, chips),
        grid_spec=pltpu.PrefetchScalarGridSpec(
            num_scalar_prefetch=1,
            grid=(slots,),
            in_specs=[
                pl.BlockSpec((1, tokens, width), lambda i, s: (i, 0, 0)),
                pl.BlockSpec((1, 2, width), lambda i, s: (i, 0, 0)),
                pl.BlockSpec(memory_space=pl.ANY),
            ],
            out_specs=[pl.BlockSpec((chips, tokens, wide), lambda i, s: (0, i, 0))] * 2,
        ),
        out_shape=[jax.ShapeDtypeStruct((chips, slots * tokens, wide), jnp.bfloat16)] * 2,
        compiler_params=params(32),
        cost_estimate=cost(),
    )(scalars, latents, image_mod, after)


def accumulate_kernel(count, has_total, *refs):
    own, other, panels = refs[:count], refs[count : 2 * count], refs[2 * count : 3 * count]
    out_ref, token_ref = refs[-2:]
    step = pl.program_id(0)
    token_ref[...] = jnp.zeros_like(token_ref)

    def run(slabs):
        features = [slab[0, :, : panel.shape[0]] for slab, panel in zip(slabs, panels)]
        features = jnp.concatenate(features, axis=1)
        panel = jnp.concatenate([panel[...] for panel in panels], axis=0)
        product = jnp.dot(features, panel, preferred_element_type=jnp.float32)
        out_ref[...] = refs[3 * count][...] + product if has_total else product

    pl.when(step == 0)(lambda: run(own))
    pl.when(step == 1)(lambda: run(other))


def accumulate(total, own, other, places, panels):
    _, rows, wide = own.shape
    count, (depth, columns) = len(places), panels[0].shape
    in_specs = [pl.BlockSpec((1, rows, wide), lambda i, o=o: (o, 0, 0)) for o in places] * 2
    in_specs += [pl.BlockSpec((depth, columns), lambda i: (0, 0)) for _ in places]
    operands = [own] * count + [other] * count + list(panels)
    aliases = {}
    if total is not None:
        in_specs.append(pl.BlockSpec((rows, columns), lambda i: (i, 0)))
        operands.append(total)
        aliases = {3 * count: 0}
    return pl.pallas_call(
        functools.partial(accumulate_kernel, count, total is not None),
        grid=(2,),
        in_specs=in_specs,
        out_specs=[
            pl.BlockSpec((rows, columns), lambda i: (i, 0)),
            pl.BlockSpec((8, LANES), lambda i: (0, 0)),
        ],
        out_shape=[
            jax.ShapeDtypeStruct((2 * rows, columns), jnp.float32),
            jax.ShapeDtypeStruct((8, LANES), jnp.float32),
        ],
        input_output_aliases=aliases,
        compiler_params=params(36),
        cost_estimate=cost(),
    )(*operands)


def meet(first, second, others):
    anywhere = pl.BlockSpec(memory_space=pl.ANY)
    return pl.pallas_call(
        lambda *refs: None,
        in_specs=[anywhere] * (2 + len(others)),
        out_specs=[anywhere] * 2,
        out_shape=[jax.ShapeDtypeStruct(x.shape, x.dtype) for x in (first, second)],
        input_output_aliases={0: 0, 1: 1},
        cost_estimate=cost(),
    )(first, second, *others)


def pick_kernel(far, ahead_ref, behind_ref, *outs):
    rows, columns = ahead_ref.shape[0], ahead_ref.shape[1] // 2
    outs[0][:rows] = ahead_ref[:, :columns]
    outs[0][rows:] = behind_ref[:, :columns]
    if far:
        outs[1][...] = ahead_ref[:, :columns]
        outs[2][...] = behind_ref[:, columns:]


def pick(ahead, behind, far):
    rows, columns = ahead.shape[0], ahead.shape[1] // 2
    vmem = pl.BlockSpec(memory_space=pltpu.VMEM)
    shapes = [(2 * rows, columns)] + [(rows, columns)] * (2 * far)
    return pl.pallas_call(
        functools.partial(pick_kernel, far),
        in_specs=[vmem, vmem],
        out_specs=[vmem] * len(shapes),
        out_shape=[jax.ShapeDtypeStruct(shape, jnp.bfloat16) for shape in shapes],
        compiler_params=params(16),
        cost_estimate=cost(),
    )(ahead, behind)


def cut_kernel(k_ref, v_ref, after_ref, out_ref):
    chips, _, span = out_ref.shape
    half = chips // 2
    for chip in range(chips):
        source = k_ref if chip < half else v_ref
        start = (chip % half) * span
        out_ref[chip] = source[:, start : start + span]


def cut_prompt_weights(w_ck, w_cv, chips, after):
    depth, inner_width = w_ck.shape
    span = 2 * inner_width // chips
    vmem = pl.BlockSpec(memory_space=pltpu.VMEM)
    return pl.pallas_call(
        cut_kernel,
        in_specs=[vmem, vmem, pl.BlockSpec(memory_space=pl.ANY)],
        out_shape=jax.ShapeDtypeStruct((chips, depth, span), jnp.bfloat16),
        compiler_params=params(16),
        cost_estimate=cost(),
    )(w_ck, w_cv, after)


def prompt_kernel(rows_ref, weight_ref, after_ref, out_ref):
    product = jnp.dot(rows_ref[...], weight_ref[...], preferred_element_type=jnp.float32)
    out_ref[...] = product.astype(jnp.bfloat16)


def project_prompts(rows, weight, after):
    count, (depth, span) = rows.shape[0], weight.shape
    tile = min(count, 512)
    return pl.pallas_call(
        prompt_kernel,
        grid=(count // tile,),
        in_specs=[
            pl.BlockSpec((tile, depth), lambda i: (i, 0)),
            pl.BlockSpec((depth, span), lambda i: (0, 0)),
            pl.BlockSpec(memory_space=pl.ANY),
        ],
        out_specs=pl.BlockSpec((tile, span), lambda i: (i, 0)),
        out_shape=jax.ShapeDtypeStruct((count, span), jnp.bfloat16),
        compiler_params=params(24),
        cost_estimate=cost(),
    )(rows, weight, after)


def route_kernel(spots_here, prompts, winner_ref, loser_ref, rows_ref, out_ref):
    tile, count = out_ref.shape[0], rows_ref.shape[0]
    row = lax.broadcasted_iota(jnp.int32, (tile, 1), 0) + pl.program_id(0) * tile
    column = lax.broadcasted_iota(jnp.int32, (1, count), 1)
    slot = lax.div(row, spots_here)
    same_spot = lax.rem(row, spots_here) == lax.div(column, prompts)
    reads = (winner_ref[...] == slot) | (loser_ref[...] == slot)
    chosen = jnp.where(reads & same_spot, 1.0, 0.0).astype(jnp.bfloat16)
    out_ref[...] = jnp.dot(
        chosen, rows_ref[...], preferred_element_type=jnp.float32
    ).astype(jnp.bfloat16)


def route(projected, winner_slot, loser_slot, spots_here):
    count, span = projected.shape
    prompts = winner_slot.shape[0]
    total = 2 * prompts * spots_here
    tile = min(total, 512)
    row = pl.BlockSpec((1, count), lambda i: (0, 0))
    winners = jnp.tile(winner_slot, spots_here).reshape(1, count)
    losers = jnp.tile(loser_slot, spots_here).reshape(1, count)
    return pl.pallas_call(
        functools.partial(route_kernel, spots_here, prompts),
        grid=(total // tile,),
        in_specs=[row, row, pl.BlockSpec((count, span), lambda i: (0, 0))],
        out_specs=pl.BlockSpec((tile, span), lambda i: (i, 0)),
        out_shape=jax.ShapeDtypeStruct((total, span), jnp.bfloat16),
        compiler_params=params(56),
        cost_estimate=cost(),
    )(winners, losers, projected)


def finish_kernel(columns, head_size, scalars, own_ref, other_ref, keys_ref, values_ref):
    devices, rows, span = own_ref.shape
    slots = keys_ref.shape[0] // 2
    each = rows // slots
    inner_width = devices // 2 * span // 2

    def emit(start):
        for side, source in enumerate((own_ref, other_ref)):
            for slot in range(slots):
                at = slice(slot * each, (slot + 1) * each)
                for core in range(2):
                    parts = [source[2 * chip + core, at, :] for chip in range(devices // 2)]
                    whole = jnp.concatenate(parts, axis=1)
                    out = side * slots + slot
                    to = slice(core * each, (core + 1) * each)
                    keys = whole[:, start : start + columns].astype(jnp.float32)
                    for pair in range(columns // LANES):
                        lanes = slice(pair * LANES, (pair + 1) * LANES)
                        keys_ref[out, to, lanes] = head_pair_norm(keys[:, lanes], head_size)
                    first = inner_width + start
                    values_ref[out, to, :] = whole[:, first : first + columns]

    pl.when(scalars[1] == 0)(lambda: emit(0))
    pl.when(scalars[1] == 1)(lambda: emit(inner_width - columns))


def finish_prompts(scalars, own, other, columns, head_size, slots):
    devices, rows, _ = own.shape
    span = 2 * rows // slots
    vmem = pl.BlockSpec(memory_space=pltpu.VMEM)
    shape = jax.ShapeDtypeStruct((2 * slots, span, columns), jnp.bfloat16)
    return pl.pallas_call(
        functools.partial(finish_kernel, columns, head_size),
        in_specs=[pl.BlockSpec(memory_space=pltpu.SMEM), vmem, vmem],
        out_specs=[vmem, vmem],
        out_shape=[shape] * 2,
        compiler_params=params(32),
        cost_estimate=cost(),
    )(scalars, own, other)


def attend_kernel(head_size, spots, scalars, live_ref, a_ref, b_ref, v_ref, pk_ref, pv_ref, out_ref):
    live = live_ref[pl.program_id(0)]
    even_group = scalars[0] == 0
    columns = b_ref.shape[1]
    span = pk_ref.shape[1]
    row = lax.broadcasted_iota(jnp.int32, (span, 1), 0)
    rest = lax.rem(row, span // 2)
    position = (2 * lax.div(rest, spots) + lax.div(row, span // 2)) * spots + lax.rem(rest, spots)
    allowed = position < live
    low = lax.broadcasted_iota(jnp.int32, (1, LANES), 1) < head_size
    over_lanes = (((1,), (1,)), ((), ()))
    over_rows = (((0,), (0,)), ((), ()))
    for pair in range(columns // LANES):
        lanes = slice(pair * LANES, (pair + 1) * LANES)
        a = head_pair_norm(a_ref[:, lanes], head_size)
        b = head_pair_norm(b_ref[:, lanes], head_size)
        queries = jnp.where(even_group, a, b)
        keys = jnp.where(even_group, b, a)
        values = v_ref[:, lanes].astype(jnp.bfloat16)
        prompt_keys = pk_ref[0, :, lanes]
        prompt_values = pv_ref[0, :, lanes]
        for head in range(2):
            side = low if head == 0 else jnp.logical_not(low)
            q = jnp.where(side, queries, jnp.zeros_like(queries))
            s = lax.dot_general(keys, q, over_lanes, preferred_element_type=jnp.float32)
            t = lax.dot_general(prompt_keys, q, over_lanes, preferred_element_type=jnp.float32)
            s = jnp.exp(s * (1.0 / head_size**0.5))
            t = jnp.where(allowed, jnp.exp(t * (1.0 / head_size**0.5)), 0.0)
            total = jnp.sum(s, axis=0, keepdims=True) + jnp.sum(t, axis=0, keepdims=True)
            out = lax.dot_general(
                values, s.astype(jnp.bfloat16), over_rows, preferred_element_type=jnp.float32
            ) + lax.dot_general(
                prompt_values, t.astype(jnp.bfloat16), over_rows, preferred_element_type=jnp.float32
            )
            rows = slice(head * head_size, (head + 1) * head_size)
            to = slice(pair * LANES + head * head_size, pair * LANES + (head + 1) * head_size)
            out_ref[0, to, :] = (out[rows] * (1.0 / total)).astype(jnp.bfloat16)


def attend(scalars, live, av, b, prompt_keys, prompt_values, head_size, spots, first, count):
    tokens = b.shape[0] // (2 * count)
    columns = b.shape[1]
    span = prompt_keys.shape[1]
    return pl.pallas_call(
        functools.partial(attend_kernel, head_size, spots),
        grid_spec=pltpu.PrefetchScalarGridSpec(
            num_scalar_prefetch=2,
            grid=(count,),
            in_specs=[
                pl.BlockSpec((tokens, columns), lambda l, s, t: (first + l, 0)),
                pl.BlockSpec((tokens, columns), lambda l, s, t: (first + l, 0)),
                pl.BlockSpec((tokens, columns), lambda l, s, t: (first + l, 1)),
                pl.BlockSpec((1, span, columns), lambda l, s, t: (first + l, 0, 0)),
                pl.BlockSpec((1, span, columns), lambda l, s, t: (first + l, 0, 0)),
            ],
            out_specs=pl.BlockSpec((1, columns, tokens), lambda l, s, t: (l, 0, 0)),
        ),
        out_shape=jax.ShapeDtypeStruct((count, columns, tokens), jnp.bfloat16),
        compiler_params=params(32),
        cost_estimate=cost(),
    )(scalars, live, av, b, av, prompt_keys, prompt_values)


def ring_order(groups, chips):
    if groups == 2:
        return list(range(0, chips, 2)) + list(range(1, chips, 2))[::-1]
    return list(range(chips))


def solution(mesh):
    groups, dp = mesh.shape["groups"], mesh.shape["dp"]
    chips = dp // 2
    ring = ring_order(groups, chips)
    place = [ring.index(chip) for chip in range(chips)]
    behind_by = np.array(
        [[(place[me] - place[chip]) % chips for chip in range(chips)] for me in range(chips)],
        np.int32,
    )
    forward_pairs = [
        (2 * ring[i] + c, 2 * ring[(i + 1) % chips] + c) for i in range(chips) for c in range(2)
    ]
    backward_pairs = [(b, a) for a, b in forward_pairs]
    core_pairs = [(d, d ^ 1) for d in range(dp)]
    group_pairs = [(g, g ^ 1) for g in range(groups)]
    half_groups = [[2 * chip + c for chip in range(chips)] for c in range(2)]

    def forward(x):
        return lax.ppermute(x, "dp", forward_pairs)

    def backward(x):
        return lax.ppermute(x, "dp", backward_pairs)

    def swap_cores(x):
        return lax.ppermute(x, "dp", core_pairs)

    def swap_groups(x):
        return lax.ppermute(x, "groups", group_pairs)

    def local(
        latents,
        context,
        lengths,
        winner_slot,
        loser_slot,
        image_mod,
        context_mod,
        w_q,
        w_k,
        w_v,
        w_ck,
        w_cv,
    ):
        slot_local, token_count, width = latents.shape
        prompt_count, spot_local, _ = context.shape
        depth, inner_width = w_q.shape
        head_size = inner_width // HEADS
        columns = (HEADS + 1) // 2 * head_size
        me = lax.axis_index("dp")
        my_group = lax.axis_index("groups") % 2
        my_chip, my_core = me // 2, me % 2
        places = lax.dynamic_index_in_dim(jnp.asarray(behind_by), my_chip, 0, keepdims=False)
        scalars = jnp.concatenate([jnp.stack([my_group, my_core]).astype(jnp.int32), places])

        mixed = mix_prompts(context, context_mod)
        rows = lax.all_gather(
            mixed,
            "dp",
            axis_index_groups=half_groups,
            axis=0,
            tiled=True,
        )

        keep, give = split_weights(scalars, w_q, w_k, w_v, columns, mixed)
        got = swap_cores(give)
        av = jnp.concatenate([keep[:, : 2 * columns], got[:, : 2 * columns]], axis=0)
        b_own = jnp.concatenate([keep[:, 2 * columns :], got[:, 2 * columns :]], axis=0)

        own, give = modulate_image(scalars, latents, image_mod, chips, av)
        other = swap_cores(give)

        total_av = total_b = None
        waiting_av, waiting_b, swapped = [(0, av)], [(0, b_own)], []
        enough = max(1, chips // 8)
        tokens = [own]
        first = None
        ahead = behind = av
        for o in range(1, chips // 2):
            ahead, behind = meet(forward(ahead), backward(behind), tokens)
            first = ahead if first is None else first
            last = 2 * o + 2 == chips
            picked = pick(ahead, behind, last)
            tokens = []
            if len(swapped) >= enough or last:
                waiting_b += swapped
                swapped = []
                total_b, token = accumulate(total_b, own, other, *zip(*waiting_b))
                tokens.append(token)
                waiting_b = []
            both = swap_groups(picked[0])
            half = both.shape[0] // 2
            swapped += [(o, both[:half]), (chips - o, both[half:])]
            waiting_av += [(o, ahead), (chips - o, behind)]
            if len(waiting_av) >= 2 * enough or last:
                total_av, token = accumulate(total_av, own, other, *zip(*waiting_av))
                tokens.append(token)
                waiting_av = []
        a_far, v_far = meet(forward(picked[1]), backward(picked[2]), tokens)
        b_far = swap_groups(a_far)
        total_b, _ = accumulate(total_b, own, other, *zip(*swapped))
        total_av, _ = accumulate(
            total_av, own, other, [chips // 2], [jnp.concatenate([a_far, v_far], axis=1)]
        )
        total_b, _ = accumulate(total_b, own, other, [chips // 2], [b_far])

        w_c = cut_prompt_weights(w_ck, w_cv, chips, first)
        w_c = lax.all_to_all(w_c, "dp", 0, 0, axis_index_groups=half_groups, tiled=True)
        w_c_other = swap_cores(w_c)
        w_first = jnp.where(my_core == 0, w_c, w_c_other)
        w_second = jnp.where(my_core == 0, w_c_other, w_c)
        w_c = jnp.stack([w_first, w_second], axis=1).reshape(width, -1)

        projected = project_prompts(rows, w_c, ahead)
        outgoing = route(projected, winner_slot, loser_slot, chips * spot_local)
        outgoing = outgoing.reshape(dp, -1, w_c.shape[1])
        arrived = lax.all_to_all(outgoing, "dp", 0, 0, tiled=True)
        prompt_keys, prompt_values = finish_prompts(
            scalars, arrived, swap_cores(arrived), columns, head_size, slot_local
        )

        here = jnp.arange(slot_local, dtype=jnp.int32)
        slots = jnp.concatenate([me * slot_local + here, (me ^ 1) * slot_local + here])
        reads = (winner_slot[None, :] == slots[:, None]) | (loser_slot[None, :] == slots[:, None])
        live = jnp.sum(jnp.where(reads, lengths[None, :], 0), axis=1)

        def run(first):
            return attend(
                scalars[:2],
                live[first : first + slot_local],
                total_av,
                total_b,
                prompt_keys,
                prompt_values,
                head_size,
                spot_local,
                first,
                slot_local,
            )

        theirs = swap_cores(run(slot_local))
        mine = run(0)
        low = jnp.where(my_core == 0, mine, theirs)
        high = jnp.where(my_core == 0, theirs, mine)
        whole = jnp.concatenate([low, high[:, 2 * columns - inner_width :]], axis=1)
        return whole.transpose(0, 2, 1)

    placed = (
        P(("groups", "dp"), None, None),
        P("groups", "dp", None),
        P("groups"),
        P("groups"),
        P("groups"),
        P(("groups", "dp"), None, None),
        P("groups", None, None),
        P("dp", None),
        P("dp", None),
        P("dp", None),
        P("dp", None),
        P("dp", None),
    )
    return jax.shard_map(
        local,
        mesh=mesh,
        in_specs=placed,
        out_specs=P(("groups", "dp"), None, None),
        check_vma=False,
    )
```

```python
import functools

import jax
import jax.numpy as jnp
import numpy as np
from jax import lax
from jax.experimental import pallas as pl
from jax.experimental.pallas import tpu as pltpu
from jax.sharding import PartitionSpec as P

HEADS = 19
LANES = 128


epsilon = 1e-06


def params(mib):
    return pltpu.CompilerParams(vmem_limit_bytes=mib * 2**20)


def cost():
    return pl.CostEstimate(flops=1, bytes_accessed=1, transcendentals=0)


def layer_norm(values, shift, scale):
    average = jnp.mean(values, axis=-1, keepdims=True)
    centered = values - average
    variance = jnp.mean(centered * centered, axis=-1, keepdims=True)
    return (centered * lax.rsqrt(variance + epsilon) * (1.0 + scale) + shift).astype(jnp.bfloat16)


def head_pair_norm(x, head_size):
    row = lax.broadcasted_iota(jnp.int32, (LANES, LANES), 0) < head_size
    column = lax.broadcasted_iota(jnp.int32, (LANES, LANES), 1) < head_size
    ones = jnp.where(row == column, 1.0, 0.0).astype(jnp.bfloat16)
    squares = x * x
    high = squares.astype(jnp.bfloat16)
    rest = (squares - high.astype(jnp.float32)).astype(jnp.bfloat16)
    total = jnp.dot(high, ones, preferred_element_type=jnp.float32) + jnp.dot(
        rest, ones, preferred_element_type=jnp.float32
    )
    return (x * lax.rsqrt(total * (1.0 / head_size) + epsilon)).astype(jnp.bfloat16)


def vmem():
    return pl.BlockSpec(memory_space=pltpu.VMEM)


def smem():
    return pl.BlockSpec(memory_space=pltpu.SMEM)


def split_kernel(columns, scalars, q_ref, k_ref, v_ref, keep_ref, give_ref):
    inner_width = q_ref.shape[1]

    def emit(parts, low_ref, high_ref):
        for i, part in enumerate(parts):
            at = slice(i * columns, (i + 1) * columns)
            low_ref[:, at] = part[:, :columns]
            high_ref[:, at] = part[:, inner_width - columns :]

    for group in range(2):
        parts = (q_ref, v_ref, k_ref) if group == 0 else (k_ref, v_ref, q_ref)
        for core in range(2):
            refs = (keep_ref, give_ref) if core == 0 else (give_ref, keep_ref)
            here = (scalars[0] == group) & (scalars[1] == core)
            pl.when(here)(functools.partial(emit, parts, *refs))


def split_weights(scalars, w_q, w_k, w_v, columns):
    shape = jax.ShapeDtypeStruct((w_q.shape[0], 3 * columns), jnp.bfloat16)
    return pl.pallas_call(
        functools.partial(split_kernel, columns),
        in_specs=[smem()] + [vmem()] * 3,
        out_specs=[vmem()] * 2,
        out_shape=[shape] * 2,
        compiler_params=params(8),
        cost_estimate=cost(),
    )(scalars, w_q, w_k, w_v)


def mixed_kernel(chips, context_ref, mod_ref, out_ref):
    prompts, spots, width = context_ref.shape
    depth = width // (2 * chips)
    shift, scale = mod_ref[:, 0, :], mod_ref[:, 1, :]
    values = context_ref[...].astype(jnp.float32)
    for spot in range(spots):
        rows = layer_norm(values[:, spot, :], shift, scale)
        for core in range(2):
            parts = [
                rows[:, (2 * chip + core) * depth : (2 * chip + core + 1) * depth]
                for chip in range(chips)
            ]
            at = (core * spots + spot) * prompts
            parts.append(jnp.zeros((prompts, out_ref.shape[1] - width // 2), jnp.bfloat16))
            out_ref[at : at + prompts, :] = jnp.concatenate(parts, axis=1)


def mix_prompts(context, context_mod, chips, columns):
    prompts, spots, width = context.shape
    return pl.pallas_call(
        functools.partial(mixed_kernel, chips),
        in_specs=[vmem()] * 2,
        out_specs=vmem(),
        out_shape=jax.ShapeDtypeStruct((2 * spots * prompts, columns), jnp.bfloat16),
        compiler_params=params(16),
        cost_estimate=cost(),
    )(context, context_mod)


def image_kernel(chips, scalars, x_ref, mod_ref, after_ref, own_ref, give_ref):
    image = layer_norm(x_ref[0].astype(jnp.float32), mod_ref[0, 0:1, :], mod_ref[0, 1:2, :])
    depth = image.shape[1] // (2 * chips)

    def emit(first_ref, second_ref):
        for chip in range(chips):
            start = 2 * chip * depth
            straight = image[:, start : start + 2 * depth]
            turned = jnp.concatenate([straight[:, depth:], straight[:, :depth]], axis=1)
            first_ref[scalars[2 + chip], :, : 2 * depth] = straight
            second_ref[scalars[2 + chip], :, : 2 * depth] = turned

    pl.when(scalars[1] == 0)(lambda: emit(own_ref, give_ref))
    pl.when(scalars[1] == 1)(lambda: emit(give_ref, own_ref))


def modulate_image(scalars, latents, image_mod, chips, after):
    slots, tokens, width = latents.shape
    wide = -(-width // chips // LANES) * LANES
    return pl.pallas_call(
        functools.partial(image_kernel, chips),
        grid_spec=pltpu.PrefetchScalarGridSpec(
            num_scalar_prefetch=1,
            grid=(slots,),
            in_specs=[
                pl.BlockSpec((1, tokens, width), lambda i, s: (i, 0, 0)),
                pl.BlockSpec((1, 2, width), lambda i, s: (i, 0, 0)),
                pl.BlockSpec(memory_space=pl.ANY),
            ],
            out_specs=[pl.BlockSpec((chips, tokens, wide), lambda i, s: (0, i, 0))] * 2,
        ),
        out_shape=[jax.ShapeDtypeStruct((chips, slots * tokens, wide), jnp.bfloat16)] * 2,
        compiler_params=params(32),
        cost_estimate=cost(),
    )(scalars, latents, image_mod, after)


def product_kernel(depth, av_places, b_places, first, *refs):
    own_ref, other_ref = refs[:2]
    panels = refs[2 : 2 + len(av_places)]
    at = 2 + len(av_places)
    pieces = refs[at : at + len(b_places) // 2 + 2 * first]
    out_av, out_b, token_ref = refs[-3:]
    totals = (None, None) if first else refs[-5:-3]
    rows = own_ref.shape[1]
    columns = out_av.shape[1]
    token_ref[...] = jnp.zeros_like(token_ref)

    def product(slab, places, panel):
        features = jnp.concatenate([slab[o, :, :depth] for o in places], axis=1)
        return jnp.dot(features, panel, preferred_element_type=jnp.float32)

    for side, slab in enumerate((own_ref, other_ref)):
        to = slice(side * rows, (side + 1) * rows)
        if av_places:
            panel = jnp.concatenate([panel[:depth] for panel in panels], axis=0)
            sums = product(slab, av_places, panel)
            out_av[to] = sums if first else totals[0][to] + sums
        elif totals[0] is not out_av:
            out_av[to] = totals[0][to]
        panel = jnp.concatenate([piece[...] for piece in pieces[2 * first :]], axis=0)
        sums = product(slab, b_places, panel)
        if first:
            features = slab[0, :, :depth]
            half = depth // 2
            for own, part in zip((slice(0, half), slice(half, depth)), pieces):
                sums = sums + jnp.dot(
                    features[:, own], part[:, columns:], preferred_element_type=jnp.float32
                )
            out_b[to] = sums
        else:
            out_b[to] = totals[1][to] + sums


def accumulate(depth, totals, own, other, av_items, b_items):
    first = totals is None
    rows, columns = own.shape[1], 2 * b_items[0][1].shape[1]
    if first:
        columns = 2 * b_items[0][1].shape[1] // 3
    av_places = [o for places, _ in av_items for o in places]
    b_places = [o for places, _ in b_items for o in places]
    operands = [own, other] + [x for _, x in av_items] + [x for _, x in b_items]
    aliases = {}
    if not first:
        aliases = {len(operands): 0, len(operands) + 1: 1}
        operands += list(totals)
    out = pl.pallas_call(
        functools.partial(product_kernel, depth, av_places, b_places, first),
        in_specs=[vmem()] * len(operands),
        out_specs=[vmem()] * 3,
        out_shape=[
            jax.ShapeDtypeStruct((2 * rows, columns), jnp.float32),
            jax.ShapeDtypeStruct((2 * rows, columns // 2), jnp.float32),
            jax.ShapeDtypeStruct((8, LANES), jnp.float32),
        ],
        input_output_aliases=aliases,
        compiler_params=params(24),
        cost_estimate=cost(),
    )(*operands)
    return out[:2], out[2]


def meet(first, second, others):
    return pl.pallas_call(
        lambda *refs: None,
        in_specs=[pl.BlockSpec(memory_space=pl.ANY)] * (2 + len(others)),
        out_specs=[pl.BlockSpec(memory_space=pl.ANY)] * 2,
        out_shape=[jax.ShapeDtypeStruct(x.shape, x.dtype) for x in (first, second)],
        input_output_aliases={0: 0, 1: 1},
        compiler_params=params(4),
        cost_estimate=cost(),
    )(first, second, *others)


def pick_kernel(rows, ahead_ref, behind_ref, *outs):
    columns = ahead_ref.shape[1] // 2
    outs[0][:rows] = ahead_ref[:rows, :columns]
    outs[0][rows:] = behind_ref[:rows, :columns]
    if len(outs) > 1:
        outs[1][...] = ahead_ref[:rows, :columns]
        outs[2][...] = behind_ref[:rows, columns:]
        outs[3][...] = ahead_ref[rows:]


def pick(rows, ahead, behind, last):
    columns = ahead.shape[1] // 2
    shapes = [(2 * rows, columns)]
    if last:
        shapes += [(rows, columns)] * 2 + [(ahead.shape[0] - rows, 2 * columns)]
    return pl.pallas_call(
        functools.partial(pick_kernel, rows),
        in_specs=[vmem()] * 2,
        out_specs=[vmem()] * len(shapes),
        out_shape=[jax.ShapeDtypeStruct(shape, jnp.bfloat16) for shape in shapes],
        compiler_params=params(8),
        cost_estimate=cost(),
    )(ahead, behind)


def cut_kernel(k_ref, v_ref, after_ref, out_ref):
    chips, _, span = out_ref.shape
    half = chips // 2
    for chip in range(chips):
        source = k_ref if chip < half else v_ref
        start = (chip % half) * span
        out_ref[chip] = source[:, start : start + span]


def cut_prompt_weights(w_ck, w_cv, chips, after):
    depth, inner_width = w_ck.shape
    span = 2 * inner_width // chips
    return pl.pallas_call(
        cut_kernel,
        in_specs=[vmem(), vmem(), pl.BlockSpec(memory_space=pl.ANY)],
        out_specs=vmem(),
        out_shape=jax.ShapeDtypeStruct((chips, depth, span), jnp.bfloat16),
        compiler_params=params(8),
        cost_estimate=cost(),
    )(w_ck, w_cv, after)


def prompt_kernel(starts, scalars, *refs):
    chips = len(starts)
    blocks, (own_ref, other_ref, out_ref, held_ref) = refs[:chips], refs[chips:]
    depth = own_ref.shape[0]
    half = out_ref.shape[1]
    parts = [
        jnp.concatenate(
            [
                block[start + core * half : start + (core + 1) * half, :depth]
                for start, block in zip(starts, blocks)
            ],
            axis=0,
        )
        for core in range(2)
    ]

    def emit(first, second):
        product = jnp.dot(parts[0], first[...], preferred_element_type=jnp.float32) + jnp.dot(
            parts[1], second[...], preferred_element_type=jnp.float32
        )
        held_ref[...] = product.astype(jnp.bfloat16).reshape(held_ref.shape)

    pl.when(scalars[1] == 0)(lambda: emit(own_ref, other_ref))
    pl.when(scalars[1] == 1)(lambda: emit(other_ref, own_ref))
    for chip in range(chips):
        out_ref[chip] = held_ref[scalars[2 + chip]]


def project_prompts(scalars, blocks, starts, w_own, w_other):
    chips, span = len(blocks), w_own.shape[1]
    half = (blocks[0].shape[0] - starts[0]) // 2
    if blocks[0].shape[0] * chips > 4096:
        depth = w_own.shape[0]
        straight = scalars[1] == 0
        weights = [jnp.where(straight, w_own, w_other), jnp.where(straight, w_other, w_own)]
        product = 0.0
        for core, weight in enumerate(weights):
            rows = [
                x[start + core * half : start + (core + 1) * half, :depth]
                for start, x in zip(starts, blocks)
            ]
            rows = jnp.concatenate(rows, axis=0)
            product = product + jnp.dot(rows, weight, preferred_element_type=jnp.float32)
        product = product.astype(jnp.bfloat16).reshape(chips, half, span)
        return jnp.take(product, scalars[2:], axis=0)
    return pl.pallas_call(
        functools.partial(prompt_kernel, starts),
        in_specs=[smem()] + [vmem()] * (chips + 2),
        out_specs=vmem(),
        out_shape=jax.ShapeDtypeStruct((chips, half, span), jnp.bfloat16),
        scratch_shapes=[pltpu.VMEM((chips, half, span), jnp.bfloat16)],
        compiler_params=params(16),
        cost_estimate=cost(),
    )(scalars, *blocks, w_own, w_other)


def route_kernel(spots_here, winner_ref, loser_ref, rows_ref, out_ref):
    tile, count = out_ref.shape[0], rows_ref.shape[0]
    prompts = winner_ref.shape[1]
    row = lax.broadcasted_iota(jnp.int32, (tile, 1), 0) + pl.program_id(0) * tile
    slot = lax.div(row, spots_here)
    reads = (winner_ref[...] == slot) | (loser_ref[...] == slot)
    column = lax.broadcasted_iota(jnp.int32, (prompts, count), 1)
    prompt = lax.broadcasted_iota(jnp.int32, (prompts, count), 0)
    spread = jnp.where(lax.rem(column, prompts) == prompt, 1.0, 0.0).astype(jnp.bfloat16)
    reads = jnp.where(reads, 1.0, 0.0).astype(jnp.bfloat16)
    reads = jnp.dot(reads, spread, preferred_element_type=jnp.float32)
    same_spot = lax.rem(row, spots_here) == lax.div(column[0:1], prompts)
    chosen = jnp.where(same_spot, reads, 0.0).astype(jnp.bfloat16)
    out_ref[...] = jnp.dot(
        chosen, rows_ref[...], preferred_element_type=jnp.float32
    ).astype(jnp.bfloat16)


def route(projected, winner_slot, loser_slot, spots_here):
    count, span = projected.shape
    prompts = winner_slot.shape[0]
    total = 2 * prompts * spots_here
    tile = min(total, 512)
    row = pl.BlockSpec((1, prompts), lambda i: (0, 0))
    return pl.pallas_call(
        functools.partial(route_kernel, spots_here),
        grid=(total // tile,),
        in_specs=[row, row, pl.BlockSpec((count, span), lambda i: (0, 0))],
        out_specs=pl.BlockSpec((tile, span), lambda i: (i, 0)),
        out_shape=jax.ShapeDtypeStruct((total, span), jnp.bfloat16),
        compiler_params=params(32 if count > 1024 else 8),
        cost_estimate=cost(),
    )(winner_slot.reshape(1, prompts), loser_slot.reshape(1, prompts), projected)


def finish_kernel(columns, head_size, scalars, own_ref, other_ref, keys_ref, values_ref):
    devices, rows, span = own_ref.shape
    slots = keys_ref.shape[0] // 2
    each = rows // slots
    inner_width = devices // 2 * span // 2

    def emit(start):
        for side, source in enumerate((own_ref, other_ref)):
            for slot in range(slots):
                at = slice(slot * each, (slot + 1) * each)
                for core in range(2):
                    parts = [source[2 * chip + core, at, :] for chip in range(devices // 2)]
                    whole = jnp.concatenate(parts, axis=1)
                    out = side * slots + slot
                    to = slice(core * each, (core + 1) * each)
                    keys = whole[:, start : start + columns].astype(jnp.float32)
                    for pair in range(columns // LANES):
                        lanes = slice(pair * LANES, (pair + 1) * LANES)
                        keys_ref[out, to, lanes] = head_pair_norm(keys[:, lanes], head_size)
                    first = inner_width + start
                    values_ref[out, to, :] = whole[:, first : first + columns]

    pl.when(scalars[1] == 0)(lambda: emit(0))
    pl.when(scalars[1] == 1)(lambda: emit(inner_width - columns))


def finish_prompts(scalars, own, other, columns, head_size, slots):
    devices, rows, _ = own.shape
    span = 2 * rows // slots
    shape = jax.ShapeDtypeStruct((2 * slots, span, columns), jnp.bfloat16)
    return pl.pallas_call(
        functools.partial(finish_kernel, columns, head_size),
        in_specs=[smem(), vmem(), vmem()],
        out_specs=[vmem()] * 2,
        out_shape=[shape] * 2,
        compiler_params=params(16),
        cost_estimate=cost(),
    )(scalars, own, other)


def attend_kernel(
    head_size,
    spots,
    scalars,
    winner,
    loser,
    lengths,
    av_ref,
    b_ref,
    slab_ref,
    far_ref,
    pk_ref,
    pv_ref,
    out_ref,
):
    step = pl.program_id(0)
    even_group = scalars[0] == 0
    _, columns, tokens = out_ref.shape
    far_place = slab_ref.shape[0] // 2
    depth = far_ref.shape[0]
    slot = scalars[4] + step

    def count(p, live):
        hit = (winner[p] == slot) | (loser[p] == slot)
        return live + jnp.where(hit, lengths[p], 0)

    live = lax.fori_loop(0, winner.shape[0], count, jnp.int32(0))
    span = pk_ref.shape[1]
    row = lax.broadcasted_iota(jnp.int32, (span, 1), 0)
    rest = lax.rem(row, span // 2)
    position = (2 * lax.div(rest, spots) + lax.div(row, span // 2)) * spots + lax.rem(rest, spots)
    allowed = position < live
    low = lax.broadcasted_iota(jnp.int32, (1, LANES), 1) < head_size
    over_lanes = (((1,), (1,)), ((), ()))
    over_rows = (((0,), (0,)), ((), ()))
    scale = 1.4426950408889634 / head_size**0.5
    here = pl.ds(pl.multiple_of(scalars[1] + step * tokens, tokens), tokens)
    slab_rows = pl.ds(pl.multiple_of(step * tokens, tokens), tokens)
    block = scalars[3] + step
    features = slab_ref[far_place, slab_rows, :][:, :depth]
    last = jnp.dot(features, far_ref[...], preferred_element_type=jnp.float32)
    for pair in range(columns // LANES):
        lanes = slice(pair * LANES, (pair + 1) * LANES)
        a = head_pair_norm(av_ref[here, lanes], head_size)
        b = head_pair_norm(b_ref[here, lanes] + last[:, lanes], head_size)
        queries = jnp.where(even_group, a, b)
        keys = jnp.where(even_group, b, a)
        values = av_ref[here, columns + pair * LANES : columns + (pair + 1) * LANES]
        values = values.astype(jnp.bfloat16)
        prompt_keys = pk_ref[block, :, lanes]
        prompt_values = pv_ref[block, :, lanes]
        for head in range(2):
            side = low if head == 0 else jnp.logical_not(low)
            q = jnp.where(side, queries, jnp.zeros_like(queries))
            s = lax.dot_general(keys, q, over_lanes, preferred_element_type=jnp.float32)
            t = lax.dot_general(prompt_keys, q, over_lanes, preferred_element_type=jnp.float32)
            s = jnp.exp2(s * scale)
            t = jnp.where(allowed, jnp.exp2(t * scale), 0.0)
            total = jnp.sum(s, axis=0, keepdims=True) + jnp.sum(t, axis=0, keepdims=True)
            out = lax.dot_general(
                values, s.astype(jnp.bfloat16), over_rows, preferred_element_type=jnp.float32
            ) + lax.dot_general(
                prompt_values, t.astype(jnp.bfloat16), over_rows, preferred_element_type=jnp.float32
            )
            rows = slice(head * head_size, (head + 1) * head_size)
            to = slice(pair * LANES + head * head_size, pair * LANES + (head + 1) * head_size)
            out_ref[0, to, :] = (out[rows] * (1.0 / total)).astype(jnp.bfloat16)


def attend(numbers, routes, totals, slab, far, prompt_keys, prompt_values, head_size, spots, count):
    av, b = totals
    tokens = b.shape[0] // (2 * count)
    columns = b.shape[1]
    return pl.pallas_call(
        functools.partial(attend_kernel, head_size, spots),
        grid=(count,),
        in_specs=[smem()] * 4 + [vmem()] * 6,
        out_specs=pl.BlockSpec((1, columns, tokens), lambda l: (l, 0, 0)),
        out_shape=jax.ShapeDtypeStruct((count, columns, tokens), jnp.bfloat16),
        compiler_params=params(16),
        cost_estimate=cost(),
    )(numbers, *routes, av, b, slab, far, prompt_keys, prompt_values)


def ring_order(groups, chips):
    if groups == 2:
        return list(range(0, chips, 2)) + list(range(1, chips, 2))[::-1]
    return list(range(chips))


def solution(mesh):
    groups, dp = mesh.shape["groups"], mesh.shape["dp"]
    chips = dp // 2
    ring = ring_order(groups, chips)
    place = [ring.index(chip) for chip in range(chips)]
    behind_by = np.array(
        [[(place[me] - place[chip]) % chips for chip in range(chips)] for me in range(chips)],
        np.int32,
    )
    forward_pairs = [
        (2 * ring[i] + c, 2 * ring[(i + 1) % chips] + c) for i in range(chips) for c in range(2)
    ]
    backward_pairs = [(b, a) for a, b in forward_pairs]
    core_pairs = [(d, d ^ 1) for d in range(dp)]
    group_pairs = [(g, g ^ 1) for g in range(groups)]
    half_groups = [[2 * chip + c for chip in range(chips)] for c in range(2)]

    def forward(x):
        return lax.ppermute(x, "dp", forward_pairs)

    def backward(x):
        return lax.ppermute(x, "dp", backward_pairs)

    def swap_cores(x):
        return lax.ppermute(x, "dp", core_pairs)

    def swap_groups(x):
        return lax.ppermute(x, "groups", group_pairs)

    def local(
        latents,
        context,
        lengths,
        winner_slot,
        loser_slot,
        image_mod,
        context_mod,
        w_q,
        w_k,
        w_v,
        w_ck,
        w_cv,
    ):
        slot_local, token_count, width = latents.shape
        prompt_count, spot_local, _ = context.shape
        depth, inner_width = w_q.shape
        head_size = inner_width // HEADS
        columns = (HEADS + 1) // 2 * head_size
        me = lax.axis_index("dp")
        my_group = lax.axis_index("groups") % 2
        my_chip, my_core = me // 2, me % 2
        places = lax.dynamic_index_in_dim(jnp.asarray(behind_by), my_chip, 0, keepdims=False)
        scalars = jnp.concatenate([jnp.stack([my_group, my_core]).astype(jnp.int32), places])

        keep, give = split_weights(scalars, w_q, w_k, w_v, columns)
        got = swap_cores(give)
        mixed = mix_prompts(context, context_mod, chips, 2 * columns)
        av = jnp.concatenate([keep[:, : 2 * columns], got[:, : 2 * columns], mixed], axis=0)

        w_c = cut_prompt_weights(w_ck, w_cv, chips, av)
        w_c = lax.all_to_all(w_c, "dp", 0, 0, axis_index_groups=half_groups, tiled=True)
        w_c_other = swap_cores(w_c).reshape(width // 2, -1)
        w_c = w_c.reshape(width // 2, -1)

        totals = own = other = None
        enough = max(1, chips // 8)
        tokens, waiting_av, waiting_b = [], [((0,), av)], []
        ahead = behind = av
        blocks = {0: (av, 2 * depth)}
        for o in range(1, chips // 2):
            ahead, behind = meet(forward(ahead), backward(behind), tokens)
            tokens = []
            last = 2 * o + 2 == chips
            picked = pick(2 * depth, ahead, behind, last)
            if own is None:
                own, give = modulate_image(scalars, latents, image_mod, chips, ahead)
                other = swap_cores(give)
                tokens.append(own)
            waiting_av += [((o,), ahead), ((chips - o,), behind)]
            blocks[o], blocks[chips - o] = (ahead, 2 * depth), (behind, 2 * depth)
            if totals is None and o > enough:
                totals, token = accumulate(
                    2 * depth, None, own, other, waiting_av, [((), keep), ((), got)] + waiting_b
                )
                tokens.append(token)
                waiting_av, waiting_b = [], []
            elif totals is not None and (len(waiting_b) >= enough or last):
                totals, token = accumulate(2 * depth, totals, own, other, waiting_av, waiting_b)
                tokens.append(token)
                waiting_av, waiting_b = [], []
            waiting_b.append(((o, chips - o), swap_groups(picked[0])))
        a_far, v_far = meet(forward(picked[1]), backward(picked[2]), tokens)
        b_far = swap_groups(a_far)
        blocks[chips // 2] = (forward(picked[3]), 0)
        waiting_av.append(((chips // 2,), jnp.concatenate([a_far, v_far], axis=1)))
        totals, _ = accumulate(2 * depth, totals, own, other, waiting_av, waiting_b)

        blocks, starts = zip(*[blocks[o] for o in range(chips)])
        projected = project_prompts(scalars, blocks, starts, w_c, w_c_other)
        projected = projected.reshape(-1, projected.shape[2])
        outgoing = route(projected, winner_slot, loser_slot, chips * spot_local)
        outgoing = outgoing.reshape(dp, -1, outgoing.shape[1])
        arrived = lax.all_to_all(outgoing, "dp", 0, 0, tiled=True)
        prompt_keys, prompt_values = finish_prompts(
            scalars, arrived, swap_cores(arrived), columns, head_size, slot_local
        )

        routes = (winner_slot, loser_slot, lengths)

        def run(side, slab):
            first_row = side * slot_local * token_count
            slot = (me ^ side) * slot_local
            numbers = jnp.stack([my_group, first_row, 0, side * slot_local, slot])
            return attend(
                numbers.astype(jnp.int32),
                routes,
                totals,
                slab,
                b_far,
                prompt_keys,
                prompt_values,
                head_size,
                spot_local,
                slot_local,
            )

        theirs = swap_cores(run(1, other))
        mine = run(0, own)
        low = jnp.where(my_core == 0, mine, theirs)
        high = jnp.where(my_core == 0, theirs, mine)
        whole = jnp.concatenate([low, high[:, 2 * columns - inner_width :]], axis=1)
        return whole.transpose(0, 2, 1)

    placed = (
        P(("groups", "dp"), None, None),
        P("groups", "dp", None),
        P("groups"),
        P("groups"),
        P("groups"),
        P(("groups", "dp"), None, None),
        P("groups", None, None),
        P("dp", None),
        P("dp", None),
        P("dp", None),
        P("dp", None),
        P("dp", None),
    )
    return jax.shard_map(
        local,
        mesh=mesh,
        in_specs=placed,
        out_specs=P(("groups", "dp"), None, None),
        check_vma=False,
    )
```

```python
import functools

import jax
import jax.numpy as jnp
import numpy as np
from jax import lax
from jax.experimental import pallas as pl
from jax.experimental.pallas import tpu as pltpu
from jax.sharding import PartitionSpec as P

HEADS = 19
LANES = 128


epsilon = 1e-06


def params(mib):
    return pltpu.CompilerParams(vmem_limit_bytes=mib * 2**20)


def cost(flops=1):
    return pl.CostEstimate(flops=flops, bytes_accessed=1, transcendentals=0)


def anywhere():
    return pl.BlockSpec(memory_space=pl.ANY)


def layer_norm(values, shift, scale):
    average = jnp.mean(values, axis=-1, keepdims=True)
    centered = values - average
    variance = jnp.mean(centered * centered, axis=-1, keepdims=True)
    return (centered * lax.rsqrt(variance + epsilon) * (1.0 + scale) + shift).astype(jnp.bfloat16)


def head_pair_norm(x, head_size):
    low = lax.broadcasted_iota(jnp.int32, (1, LANES), 1) < head_size
    squares = x * x
    first = jnp.sum(jnp.where(low, squares, 0.0), axis=-1, keepdims=True)
    second = jnp.sum(jnp.where(low, 0.0, squares), axis=-1, keepdims=True)
    first = lax.rsqrt(first * (1.0 / head_size) + epsilon)
    second = lax.rsqrt(second * (1.0 / head_size) + epsilon)
    return (x * jnp.where(low, first, second)).astype(jnp.bfloat16)


def vmem():
    return pl.BlockSpec(memory_space=pltpu.VMEM)


def smem():
    return pl.BlockSpec(memory_space=pltpu.SMEM)


def split_kernel(columns, scalars, q_ref, k_ref, v_ref, keep_ref, give_ref):
    inner_width = q_ref.shape[1]

    def emit(parts, low_ref, high_ref):
        for i, part in enumerate(parts):
            at = slice(i * columns, (i + 1) * columns)
            low_ref[:, at] = part[:, :columns]
            high_ref[:, at] = part[:, inner_width - columns :]

    for group in range(2):
        parts = (q_ref, v_ref, k_ref) if group == 0 else (k_ref, v_ref, q_ref)
        for core in range(2):
            refs = (keep_ref, give_ref) if core == 0 else (give_ref, keep_ref)
            here = (scalars[0] == group) & (scalars[1] == core)
            pl.when(here)(functools.partial(emit, parts, *refs))


def split_weights(scalars, w_q, w_k, w_v, columns):
    shape = jax.ShapeDtypeStruct((w_q.shape[0], 3 * columns), jnp.bfloat16)
    return pl.pallas_call(
        functools.partial(split_kernel, columns),
        in_specs=[smem()] + [vmem()] * 3,
        out_specs=[vmem()] * 2,
        out_shape=[shape] * 2,
        compiler_params=params(8),
        cost_estimate=cost(),
    )(scalars, w_q, w_k, w_v)


def mixed_kernel(chips, context_ref, mod_ref, out_ref):
    prompts, spots, width = context_ref.shape
    depth = width // (2 * chips)
    shift, scale = mod_ref[:, 0, :], mod_ref[:, 1, :]
    values = context_ref[...].astype(jnp.float32)
    for spot in range(spots):
        rows = layer_norm(values[:, spot, :], shift, scale)
        for core in range(2):
            parts = [
                rows[:, (2 * chip + core) * depth : (2 * chip + core + 1) * depth]
                for chip in range(chips)
            ]
            at = (core * spots + spot) * prompts
            parts.append(jnp.zeros((prompts, out_ref.shape[1] - width // 2), jnp.bfloat16))
            out_ref[at : at + prompts, :] = jnp.concatenate(parts, axis=1)


def mix_prompts(context, context_mod, chips, columns):
    prompts, spots, width = context.shape
    return pl.pallas_call(
        functools.partial(mixed_kernel, chips),
        in_specs=[vmem()] * 2,
        out_specs=vmem(),
        out_shape=jax.ShapeDtypeStruct((2 * spots * prompts, columns), jnp.bfloat16),
        compiler_params=params(16),
        cost_estimate=cost(),
    )(context, context_mod)


def image_kernel(chips, scalars, x_ref, mod_ref, after_ref, own_ref, *give_refs):
    image = layer_norm(x_ref[0].astype(jnp.float32), mod_ref[0, 0:1, :], mod_ref[0, 1:2, :])
    depth = image.shape[1] // (2 * chips)
    step = pl.program_id(0)

    def emit(first_ref, second_ref):
        for chip in range(chips):
            start = 2 * chip * depth
            straight = image[:, start : start + 2 * depth]
            turned = jnp.concatenate([straight[:, depth:], straight[:, :depth]], axis=1)
            first_ref[scalars[2 + chip], :, : 2 * depth] = straight
            second_ref[scalars[2 + chip], :, : 2 * depth] = turned

    for slot, give_ref in enumerate(give_refs):
        here = step == slot
        pl.when(here & (scalars[1] == 0))(functools.partial(emit, own_ref, give_ref))
        pl.when(here & (scalars[1] == 1))(functools.partial(emit, give_ref, own_ref))


def modulate_image(scalars, latents, image_mod, chips, after):
    slots, tokens, width = latents.shape
    wide = -(-width // chips // LANES) * LANES
    block = (chips, tokens, wide)
    return pl.pallas_call(
        functools.partial(image_kernel, chips),
        grid_spec=pltpu.PrefetchScalarGridSpec(
            num_scalar_prefetch=1,
            grid=(slots,),
            in_specs=[
                pl.BlockSpec((1, tokens, width), lambda i, s: (i, 0, 0)),
                pl.BlockSpec((1, 2, width), lambda i, s: (i, 0, 0)),
                anywhere(),
            ],
            out_specs=[pl.BlockSpec(block, lambda i, s: (0, i, 0))]
            + [pl.BlockSpec(block, lambda i, s: (0, 0, 0))] * slots,
        ),
        out_shape=[jax.ShapeDtypeStruct((chips, slots * tokens, wide), jnp.bfloat16)]
        + [jax.ShapeDtypeStruct(block, jnp.bfloat16)] * slots,
        compiler_params=params(32),
        cost_estimate=cost(),
    )(scalars, latents, image_mod, after)


def take_rows(slab, o, depth):
    return jnp.concatenate([part[o, :, :depth] for part in slab], axis=0)


def product_kernel(slots, depth, av_places, b_places, first, *refs):
    slabs, refs = refs[:slots], refs[slots:]
    panels = refs[: len(av_places)]
    at = len(av_places)
    pieces = refs[at : at + len(b_places) // 2 + 2 * first]
    out_av, out_b, token_ref = refs[-3:]
    totals = (None, None) if first else refs[-5:-3]
    rows = slabs[0].shape[1]
    columns = out_av.shape[1]
    token_ref[...] = jnp.zeros_like(token_ref)

    def product(slab, places, panel):
        features = jnp.concatenate([take_rows(slab, o, depth) for o in places], axis=1)
        return jnp.dot(features, panel, preferred_element_type=jnp.float32)

    for side, slab in enumerate((slabs[:1], slabs[1:])):
        to = slice(side * rows, (side + 1) * rows)
        if av_places:
            panel = jnp.concatenate([panel[:depth] for panel in panels], axis=0)
            sums = product(slab, av_places, panel)
            out_av[to] = sums if first else totals[0][to] + sums
        elif totals[0] is not out_av:
            out_av[to] = totals[0][to]
        panel = jnp.concatenate([piece[...] for piece in pieces[2 * first :]], axis=0)
        sums = product(slab, b_places, panel)
        if first:
            features = take_rows(slab, 0, depth)
            half = depth // 2
            for own, part in zip((slice(0, half), slice(half, depth)), pieces):
                sums = sums + jnp.dot(
                    features[:, own], part[:, columns:], preferred_element_type=jnp.float32
                )
            out_b[to] = sums
        else:
            out_b[to] = totals[1][to] + sums


def accumulate(depth, totals, slabs, av_items, b_items):
    first = totals is None
    slabs = slabs[0] + slabs[1]
    rows, columns = slabs[0].shape[1], 2 * b_items[0][1].shape[1]
    if first:
        columns = 2 * b_items[0][1].shape[1] // 3
    av_places = [o for places, _ in av_items for o in places]
    b_places = [o for places, _ in b_items for o in places]
    operands = slabs + [x for _, x in av_items] + [x for _, x in b_items]
    aliases = {}
    if not first:
        aliases = {len(operands): 0, len(operands) + 1: 1}
        operands += list(totals)
    out = pl.pallas_call(
        functools.partial(product_kernel, len(slabs), depth, av_places, b_places, first),
        in_specs=[vmem()] * len(operands),
        out_specs=[vmem()] * 3,
        out_shape=[
            jax.ShapeDtypeStruct((2 * rows, columns), jnp.float32),
            jax.ShapeDtypeStruct((2 * rows, columns // 2), jnp.float32),
            jax.ShapeDtypeStruct((8, LANES), jnp.float32),
        ],
        input_output_aliases=aliases,
        compiler_params=params(20),
        cost_estimate=cost(4 * 10**10),
    )(*operands)
    return out[:2], out[2]


def last_kernel(slots, depth, head_size, av_places, b_places, *refs):
    slabs, refs = refs[:slots], refs[slots:]
    count = len(av_places) - 1
    panels, (a_far, v_far) = refs[:count], refs[count : count + 2]
    swapped = refs[count + 2 : count + 2 + len(b_places) // 2]
    total_av, total_b, out_a, out_v, out_b, out_far = refs[-6:]
    rows, columns = slabs[0].shape[1], out_a.shape[1]

    def product(slab, places, panel):
        features = jnp.concatenate([take_rows(slab, o, depth) for o in places], axis=1)
        return jnp.dot(features, panel, preferred_element_type=jnp.float32)

    for side, slab in enumerate((slabs[:1], slabs[1:])):
        to = slice(side * rows, (side + 1) * rows)
        for half, far in enumerate((a_far, v_far)):
            lanes = slice(half * columns, (half + 1) * columns)
            parts = [panel[:depth, lanes] for panel in panels] + [far[...]]
            sums = total_av[to, lanes] + product(slab, av_places, jnp.concatenate(parts, axis=0))
            if half == 1:
                out_v[to] = sums.astype(jnp.bfloat16)
                continue
            for pair in range(columns // LANES):
                at = slice(pair * LANES, (pair + 1) * LANES)
                out_a[to, at] = head_pair_norm(sums[:, at], head_size)
        panel = jnp.concatenate([piece[...] for piece in swapped], axis=0)
        out_b[to] = total_b[to] + product(slab, b_places, panel)
        out_far[to, :depth] = take_rows(slab, av_places[-1], depth)


def last_products(depth, head_size, totals, slabs, av_items, far_items, b_items):
    slabs = slabs[0] + slabs[1]
    rows, columns = 2 * slabs[0].shape[1], totals[1].shape[1]
    av_places = [o for places, _ in av_items for o in places] + [far_items[0]]
    b_places = [o for places, _ in b_items for o in places]
    operands = slabs + [x for _, x in av_items] + list(far_items[1:])
    operands += [x for _, x in b_items] + list(totals)
    return pl.pallas_call(
        functools.partial(last_kernel, len(slabs), depth, head_size, av_places, b_places),
        in_specs=[vmem()] * len(operands),
        out_specs=[vmem()] * 4,
        out_shape=[
            jax.ShapeDtypeStruct((rows, columns), jnp.bfloat16),
            jax.ShapeDtypeStruct((rows, columns), jnp.bfloat16),
            jax.ShapeDtypeStruct((rows, columns), jnp.float32),
            jax.ShapeDtypeStruct((rows, slabs[0].shape[2]), jnp.bfloat16),
        ],
        compiler_params=params(20),
        cost_estimate=cost(4 * 10**10),
    )(*operands)


def meet(first, second, others):
    return pl.pallas_call(
        lambda *refs: None,
        in_specs=[anywhere()] * (2 + len(others)),
        out_specs=[anywhere()] * 2,
        out_shape=[jax.ShapeDtypeStruct(x.shape, x.dtype) for x in (first, second)],
        input_output_aliases={0: 0, 1: 1},
        compiler_params=params(4),
        cost_estimate=cost(),
    )(first, second, *others)


def pick_kernel(rows, ahead_ref, behind_ref, *outs):
    columns = outs[0].shape[1]
    outs[0][:rows] = ahead_ref[:rows, :columns]
    outs[0][rows:] = behind_ref[:rows, :columns]
    if len(outs) > 1:
        outs[1][...] = ahead_ref[:rows, :columns]
        outs[2][...] = behind_ref[:rows, columns:]


def pick(rows, ahead, behind, last):
    columns = ahead.shape[1] // 2
    shapes = [(2 * rows, columns)] + [(rows, columns)] * (2 * last)
    return pl.pallas_call(
        functools.partial(pick_kernel, rows),
        grid=(1,),
        in_specs=[pl.BlockSpec(x.shape, lambda i: (0, 0)) for x in (ahead, behind)],
        out_specs=[pl.BlockSpec(shape, lambda i: (0, 0)) for shape in shapes],
        out_shape=[jax.ShapeDtypeStruct(shape, jnp.bfloat16) for shape in shapes],
        compiler_params=params(12),
        cost_estimate=cost(),
    )(ahead, behind)


def cut_kernel(k_ref, v_ref, after_ref, out_ref):
    chips, _, span = out_ref.shape
    half = chips // 2
    for chip in range(chips):
        source = k_ref if chip < half else v_ref
        start = (chip % half) * span
        out_ref[chip] = source[:, start : start + span]


def cut_prompt_weights(w_ck, w_cv, chips, after):
    depth, inner_width = w_ck.shape
    span = 2 * inner_width // chips
    return pl.pallas_call(
        cut_kernel,
        in_specs=[vmem(), vmem(), anywhere()],
        out_specs=vmem(),
        out_shape=jax.ShapeDtypeStruct((chips, depth, span), jnp.bfloat16),
        compiler_params=params(8),
        cost_estimate=cost(),
    )(w_ck, w_cv, after)


def prompt_kernel(starts, scalars, *refs):
    chips = len(starts)
    blocks, (own_ref, other_ref, out_ref, held_ref) = refs[:chips], refs[chips:]
    depth = own_ref.shape[0]
    half = out_ref.shape[1]
    parts = [
        jnp.concatenate(
            [
                block[start + core * half : start + (core + 1) * half, :depth]
                for start, block in zip(starts, blocks)
            ],
            axis=0,
        )
        for core in range(2)
    ]

    def emit(first, second):
        product = jnp.dot(parts[0], first[...], preferred_element_type=jnp.float32) + jnp.dot(
            parts[1], second[...], preferred_element_type=jnp.float32
        )
        held_ref[...] = product.astype(jnp.bfloat16).reshape(held_ref.shape)

    pl.when(scalars[1] == 0)(lambda: emit(own_ref, other_ref))
    pl.when(scalars[1] == 1)(lambda: emit(other_ref, own_ref))
    for chip in range(chips):
        out_ref[chip] = held_ref[scalars[2 + chip]]


def project_prompts(scalars, blocks, starts, w_own, w_other):
    chips, span = len(blocks), w_own.shape[1]
    half = (blocks[0].shape[0] - starts[0]) // 2
    if blocks[0].shape[0] * chips > 4096:
        depth = w_own.shape[0]
        straight = scalars[1] == 0
        weights = [jnp.where(straight, w_own, w_other), jnp.where(straight, w_other, w_own)]
        product = 0.0
        for core, weight in enumerate(weights):
            rows = [
                x[start + core * half : start + (core + 1) * half, :depth]
                for start, x in zip(starts, blocks)
            ]
            rows = jnp.concatenate(rows, axis=0)
            product = product + jnp.dot(rows, weight, preferred_element_type=jnp.float32)
        product = product.astype(jnp.bfloat16).reshape(chips, half, span)
        return jnp.take(product, scalars[2:], axis=0)
    return pl.pallas_call(
        functools.partial(prompt_kernel, starts),
        in_specs=[smem()] + [vmem()] * (chips + 2),
        out_specs=vmem(),
        out_shape=jax.ShapeDtypeStruct((chips, half, span), jnp.bfloat16),
        scratch_shapes=[pltpu.VMEM((chips, half, span), jnp.bfloat16)],
        compiler_params=params(16),
        cost_estimate=cost(),
    )(scalars, *blocks, w_own, w_other)


def route_kernel(spots_here, winner_ref, loser_ref, rows_ref, out_ref):
    tile, count = out_ref.shape[0], rows_ref.shape[0]
    prompts = winner_ref.shape[1]
    row = lax.broadcasted_iota(jnp.int32, (tile, 1), 0) + pl.program_id(0) * tile
    slot = lax.div(row, spots_here)
    reads = (winner_ref[...] == slot) | (loser_ref[...] == slot)
    column = lax.broadcasted_iota(jnp.int32, (prompts, count), 1)
    prompt = lax.broadcasted_iota(jnp.int32, (prompts, count), 0)
    spread = jnp.where(lax.rem(column, prompts) == prompt, 1.0, 0.0).astype(jnp.bfloat16)
    reads = jnp.where(reads, 1.0, 0.0).astype(jnp.bfloat16)
    reads = jnp.dot(reads, spread, preferred_element_type=jnp.float32)
    same_spot = lax.rem(row, spots_here) == lax.div(column[0:1], prompts)
    chosen = jnp.where(same_spot, reads, 0.0).astype(jnp.bfloat16)
    out_ref[...] = jnp.dot(
        chosen, rows_ref[...], preferred_element_type=jnp.float32
    ).astype(jnp.bfloat16)


def route(projected, winner_slot, loser_slot, spots_here):
    count, span = projected.shape
    prompts = winner_slot.shape[0]
    total = 2 * prompts * spots_here
    tile = min(total, 512)
    row = pl.BlockSpec((1, prompts), lambda i: (0, 0))
    return pl.pallas_call(
        functools.partial(route_kernel, spots_here),
        grid=(total // tile,),
        in_specs=[row, row, pl.BlockSpec((count, span), lambda i: (0, 0))],
        out_specs=pl.BlockSpec((tile, span), lambda i: (i, 0)),
        out_shape=jax.ShapeDtypeStruct((total, span), jnp.bfloat16),
        compiler_params=params(32 if count > 1024 else 8),
        cost_estimate=cost(),
    )(winner_slot.reshape(1, prompts), loser_slot.reshape(1, prompts), projected)


def finish_kernel(columns, head_size, scalars, own_ref, other_ref, keys_ref, values_ref):
    devices, rows, span = own_ref.shape
    slots = keys_ref.shape[0] // 2
    each = rows // slots
    inner_width = devices // 2 * span // 2

    def emit(start):
        for side, source in enumerate((own_ref, other_ref)):
            for slot in range(slots):
                at = slice(slot * each, (slot + 1) * each)
                for core in range(2):
                    parts = [source[2 * chip + core, at, :] for chip in range(devices // 2)]
                    whole = jnp.concatenate(parts, axis=1)
                    out = side * slots + slot
                    to = slice(core * each, (core + 1) * each)
                    keys = whole[:, start : start + columns].astype(jnp.float32)
                    for pair in range(columns // LANES):
                        lanes = slice(pair * LANES, (pair + 1) * LANES)
                        keys_ref[out, to, lanes] = head_pair_norm(keys[:, lanes], head_size)
                    first = inner_width + start
                    values_ref[out, to, :] = whole[:, first : first + columns]

    pl.when(scalars[1] == 0)(lambda: emit(0))
    pl.when(scalars[1] == 1)(lambda: emit(inner_width - columns))


def finish_prompts(scalars, own, other, columns, head_size, slots):
    devices, rows, _ = own.shape
    span = 2 * rows // slots
    shape = jax.ShapeDtypeStruct((2 * slots, span, columns), jnp.bfloat16)
    return pl.pallas_call(
        functools.partial(finish_kernel, columns, head_size),
        in_specs=[smem(), vmem(), vmem()],
        out_specs=[vmem()] * 2,
        out_shape=[shape] * 2,
        compiler_params=params(16),
        cost_estimate=cost(),
    )(scalars, own, other)


def attend_kernel(
    head_size,
    spots,
    scalars,
    winner,
    loser,
    lengths,
    a_ref,
    v_ref,
    b_ref,
    features_ref,
    far_ref,
    pk_ref,
    pv_ref,
    out_ref,
):
    step = pl.program_id(0)
    even_group = scalars[0] == 0
    _, columns, tokens = out_ref.shape
    depth = far_ref.shape[0]
    slot = scalars[4] + step

    def count(p, live):
        hit = (winner[p] == slot) | (loser[p] == slot)
        return live + jnp.where(hit, lengths[p], 0)

    live = lax.fori_loop(0, winner.shape[0], count, jnp.int32(0))
    span = pk_ref.shape[1]
    row = lax.broadcasted_iota(jnp.int32, (span, 1), 0)
    rest = lax.rem(row, span // 2)
    position = (2 * lax.div(rest, spots) + lax.div(row, span // 2)) * spots + lax.rem(rest, spots)
    allowed = position < live
    low = lax.broadcasted_iota(jnp.int32, (1, LANES), 1) < head_size
    over_lanes = (((1,), (1,)), ((), ()))
    over_rows = (((0,), (0,)), ((), ()))
    scale = 1.4426950408889634 / head_size**0.5
    here = pl.ds(pl.multiple_of(scalars[1] + step * tokens, tokens), tokens)
    block = scalars[3] + step
    features = features_ref[here, :][:, :depth]
    last = jnp.dot(features, far_ref[...], preferred_element_type=jnp.float32)
    for pair in range(columns // LANES):
        lanes = slice(pair * LANES, (pair + 1) * LANES)
        a = a_ref[here, lanes]
        b = head_pair_norm(b_ref[here, lanes] + last[:, lanes], head_size)
        queries = jnp.where(even_group, a, b)
        keys = jnp.where(even_group, b, a)
        values = v_ref[here, lanes]
        prompt_keys = pk_ref[block, :, lanes]
        prompt_values = pv_ref[block, :, lanes]
        for head in range(2):
            side = low if head == 0 else jnp.logical_not(low)
            q = jnp.where(side, queries, jnp.zeros_like(queries))
            s = lax.dot_general(keys, q, over_lanes, preferred_element_type=jnp.float32)
            t = lax.dot_general(prompt_keys, q, over_lanes, preferred_element_type=jnp.float32)
            s = jnp.exp2(s * scale)
            t = jnp.where(allowed, jnp.exp2(t * scale), 0.0)
            total = jnp.sum(s, axis=0, keepdims=True) + jnp.sum(t, axis=0, keepdims=True)
            out = lax.dot_general(
                values, s.astype(jnp.bfloat16), over_rows, preferred_element_type=jnp.float32
            ) + lax.dot_general(
                prompt_values, t.astype(jnp.bfloat16), over_rows, preferred_element_type=jnp.float32
            )
            rows = slice(head * head_size, (head + 1) * head_size)
            to = slice(pair * LANES + head * head_size, pair * LANES + (head + 1) * head_size)
            out_ref[0, to, :] = (out[rows] * (1.0 / total)).astype(jnp.bfloat16)


def attend(numbers, routes, rows, far, prompt_keys, prompt_values, head_size, spots, count):
    tokens = rows[0].shape[0] // (2 * count)
    columns = rows[0].shape[1]
    return pl.pallas_call(
        functools.partial(attend_kernel, head_size, spots),
        grid=(count,),
        in_specs=[smem()] * 4 + [vmem()] * 7,
        out_specs=pl.BlockSpec((1, columns, tokens), lambda l: (l, 0, 0)),
        out_shape=jax.ShapeDtypeStruct((count, columns, tokens), jnp.bfloat16),
        compiler_params=params(16),
        cost_estimate=cost(),
    )(numbers, *routes, *rows, far, prompt_keys, prompt_values)


def ring_order(groups, chips):
    if groups == 2:
        return list(range(0, chips, 2)) + list(range(1, chips, 2))[::-1]
    return list(range(chips))


def solution(mesh):
    groups, dp = mesh.shape["groups"], mesh.shape["dp"]
    chips = dp // 2
    ring = ring_order(groups, chips)
    place = [ring.index(chip) for chip in range(chips)]
    behind_by = np.array(
        [[(place[me] - place[chip]) % chips for chip in range(chips)] for me in range(chips)],
        np.int32,
    )
    forward_pairs = [
        (2 * ring[i] + c, 2 * ring[(i + 1) % chips] + c) for i in range(chips) for c in range(2)
    ]
    backward_pairs = [(b, a) for a, b in forward_pairs]
    core_pairs = [(d, d ^ 1) for d in range(dp)]
    group_pairs = [(g, g ^ 1) for g in range(groups)]
    half_groups = [[2 * chip + c for chip in range(chips)] for c in range(2)]

    def forward(x):
        return lax.ppermute(x, "dp", forward_pairs)

    def backward(x):
        return lax.ppermute(x, "dp", backward_pairs)

    def swap_cores(x):
        return lax.ppermute(x, "dp", core_pairs)

    def swap_groups(x):
        return lax.ppermute(x, "groups", group_pairs)

    def local(
        latents,
        context,
        lengths,
        winner_slot,
        loser_slot,
        image_mod,
        context_mod,
        w_q,
        w_k,
        w_v,
        w_ck,
        w_cv,
    ):
        slot_local, token_count, width = latents.shape
        prompt_count, spot_local, _ = context.shape
        depth, inner_width = w_q.shape
        head_size = inner_width // HEADS
        columns = (HEADS + 1) // 2 * head_size
        me = lax.axis_index("dp")
        my_group = lax.axis_index("groups") % 2
        my_chip, my_core = me // 2, me % 2
        places = lax.dynamic_index_in_dim(jnp.asarray(behind_by), my_chip, 0, keepdims=False)
        scalars = jnp.concatenate([jnp.stack([my_group, my_core]).astype(jnp.int32), places])

        keep, give = split_weights(scalars, w_q, w_k, w_v, columns)
        got = swap_cores(give)
        mixed = mix_prompts(context, context_mod, chips, 2 * columns)
        own_av = [keep[:, : 2 * columns], got[:, : 2 * columns]]
        ahead = jnp.concatenate(own_av + [forward(mixed)], axis=0)
        behind = jnp.concatenate(own_av + [backward(mixed)], axis=0)

        own, *give = modulate_image(scalars, latents, image_mod, chips, ahead)
        slabs = [[own], [swap_cores(x) for x in give]]

        w_c = cut_prompt_weights(w_ck, w_cv, chips, ahead)
        w_c = lax.all_to_all(w_c, "dp", 0, 0, axis_index_groups=half_groups, tiled=True)

        totals = None
        enough = max(1, chips // 8)
        tokens, waiting_av, waiting_b = [], [((0,), ahead)], []
        blocks = {0: (mixed, 0), 1: (ahead, 2 * depth), chips - 1: (behind, 2 * depth)}
        for o in range(1, chips // 2):
            ahead, behind = meet(forward(ahead), backward(behind), tokens)
            tokens = []
            last = 2 * o + 2 == chips
            picked = pick(2 * depth, ahead, behind, last)
            waiting_av += [((o,), ahead), ((chips - o,), behind)]
            blocks.setdefault(o + 1, (ahead, 2 * depth))
            blocks.setdefault(chips - o - 1, (behind, 2 * depth))
            if totals is None and o > enough:
                totals, token = accumulate(
                    2 * depth, None, slabs, waiting_av, [((), keep), ((), got)] + waiting_b
                )
                tokens.append(token)
                waiting_av, waiting_b = [], []
                w_c, _ = meet(w_c, token, [])
            elif totals is not None and len(waiting_b) > 2 * enough:
                totals, token = accumulate(2 * depth, totals, slabs, waiting_av, waiting_b)
                tokens.append(token)
                waiting_av, waiting_b = [], []
            waiting_b.append(((o, chips - o), swap_groups(picked[0])))
        a_far, v_far = meet(
            forward(picked[1]), backward(picked[2]), tokens + [x for _, x in waiting_b[:-1]]
        )
        b_far = swap_groups(a_far)
        done_rows = last_products(
            2 * depth,
            head_size,
            totals,
            slabs,
            waiting_av,
            (chips // 2, a_far, v_far),
            waiting_b,
        )
        w_c_other = swap_cores(w_c).reshape(width // 2, -1)
        w_c = w_c.reshape(width // 2, -1)

        blocks, starts = zip(*[blocks[o] for o in range(chips)])
        projected = project_prompts(scalars, blocks, starts, w_c, w_c_other)
        projected = projected.reshape(-1, projected.shape[2])
        outgoing = route(projected, winner_slot, loser_slot, chips * spot_local)
        outgoing = outgoing.reshape(dp, -1, outgoing.shape[1])
        arrived = lax.all_to_all(outgoing, "dp", 0, 0, tiled=True)
        prompt_keys, prompt_values = finish_prompts(
            scalars, arrived, swap_cores(arrived), columns, head_size, slot_local
        )

        routes = (winner_slot, loser_slot, lengths)

        def run(side):
            first_row = side * slot_local * token_count
            slot = (me ^ side) * slot_local
            numbers = jnp.stack([my_group, first_row, 0, side * slot_local, slot])
            return attend(
                numbers.astype(jnp.int32),
                routes,
                done_rows,
                b_far,
                prompt_keys,
                prompt_values,
                head_size,
                spot_local,
                slot_local,
            )

        theirs = swap_cores(run(1))
        mine = run(0)
        low = jnp.where(my_core == 0, mine, theirs)
        high = jnp.where(my_core == 0, theirs, mine)
        whole = jnp.concatenate([low, high[:, 2 * columns - inner_width :]], axis=1)
        return whole.transpose(0, 2, 1)

    placed = (
        P(("groups", "dp"), None, None),
        P("groups", "dp", None),
        P("groups"),
        P("groups"),
        P("groups"),
        P(("groups", "dp"), None, None),
        P("groups", None, None),
        P("dp", None),
        P("dp", None),
        P("dp", None),
        P("dp", None),
        P("dp", None),
    )
    return jax.shard_map(
        local,
        mesh=mesh,
        in_specs=placed,
        out_specs=P(("groups", "dp"), None, None),
        check_vma=False,
    )
```

```python
import functools

import jax
import jax.numpy as jnp
import numpy as np
from jax import lax
from jax.experimental import pallas as pl
from jax.experimental.pallas import tpu as pltpu
from jax.sharding import PartitionSpec as P

HEADS = 19
LANES = 128


epsilon = 1e-06


def params(mib):
    return pltpu.CompilerParams(vmem_limit_bytes=mib * 2**20)


def cost(flops=1):
    return pl.CostEstimate(flops=flops, bytes_accessed=1, transcendentals=0)


def anywhere():
    return pl.BlockSpec(memory_space=pl.ANY)


def layer_norm(values, shift, scale):
    average = jnp.mean(values, axis=-1, keepdims=True)
    centered = values - average
    variance = jnp.mean(centered * centered, axis=-1, keepdims=True)
    return (centered * lax.rsqrt(variance + epsilon) * (1.0 + scale) + shift).astype(jnp.bfloat16)


def head_pair_norm(x, head_size):
    low = lax.broadcasted_iota(jnp.int32, (1, LANES), 1) < head_size
    squares = x * x
    first = jnp.sum(jnp.where(low, squares, 0.0), axis=-1, keepdims=True)
    second = jnp.sum(jnp.where(low, 0.0, squares), axis=-1, keepdims=True)
    first = lax.rsqrt(first * (1.0 / head_size) + epsilon)
    second = lax.rsqrt(second * (1.0 / head_size) + epsilon)
    return (x * jnp.where(low, first, second)).astype(jnp.bfloat16)


def vmem():
    return pl.BlockSpec(memory_space=pltpu.VMEM)


def smem():
    return pl.BlockSpec(memory_space=pltpu.SMEM)


def split_kernel(columns, scalars, q_ref, k_ref, v_ref, keep_ref, give_ref):
    inner_width = q_ref.shape[1]

    def emit(parts, low_ref, high_ref):
        for i, part in enumerate(parts):
            at = slice(i * columns, (i + 1) * columns)
            low_ref[:, at] = part[:, :columns]
            high_ref[:, at] = part[:, inner_width - columns :]

    for group in range(2):
        parts = (q_ref, v_ref, k_ref) if group == 0 else (k_ref, v_ref, q_ref)
        for core in range(2):
            refs = (keep_ref, give_ref) if core == 0 else (give_ref, keep_ref)
            here = (scalars[0] == group) & (scalars[1] == core)
            pl.when(here)(functools.partial(emit, parts, *refs))


def split_weights(scalars, w_q, w_k, w_v, columns):
    depth, inner_width = w_q.shape
    shape = jax.ShapeDtypeStruct((depth, 3 * columns), jnp.bfloat16)
    whole = pl.BlockSpec((depth, inner_width), lambda i, s: (0, 0))
    out = pl.BlockSpec((depth, 3 * columns), lambda i, s: (0, 0))
    return pl.pallas_call(
        functools.partial(split_kernel, columns),
        grid_spec=pltpu.PrefetchScalarGridSpec(
            num_scalar_prefetch=1, grid=(1,), in_specs=[whole] * 3, out_specs=[out] * 2
        ),
        out_shape=[shape] * 2,
        compiler_params=params(56),
        cost_estimate=cost(),
    )(scalars, w_q, w_k, w_v)


def mixed_kernel(chips, context_ref, mod_ref, out_ref):
    prompts, spots, width = context_ref.shape
    depth = width // (2 * chips)
    shift, scale = mod_ref[:, 0, :], mod_ref[:, 1, :]
    values = context_ref[...].astype(jnp.float32)
    for spot in range(spots):
        rows = layer_norm(values[:, spot, :], shift, scale)
        for core in range(2):
            parts = [
                rows[:, (2 * chip + core) * depth : (2 * chip + core + 1) * depth]
                for chip in range(chips)
            ]
            at = (core * spots + spot) * prompts
            out_ref[at : at + prompts, :] = jnp.concatenate(parts, axis=1)


def mix_prompts(context, context_mod, chips, half_width):
    prompts, spots, width = context.shape
    return pl.pallas_call(
        functools.partial(mixed_kernel, chips),
        in_specs=[vmem()] * 2,
        out_specs=vmem(),
        out_shape=jax.ShapeDtypeStruct((2 * spots * prompts, half_width), jnp.bfloat16),
        compiler_params=params(16),
        cost_estimate=cost(),
    )(context, context_mod)


def image_kernel(chips, scalars, x_ref, mod_ref, after_ref, own_ref, give_ref):
    image = layer_norm(x_ref[0].astype(jnp.float32), mod_ref[0, 0:1, :], mod_ref[0, 1:2, :])
    depth = image.shape[1] // (2 * chips)

    def emit(first_ref, second_ref):
        for chip in range(chips):
            start = 2 * chip * depth
            straight = image[:, start : start + 2 * depth]
            turned = jnp.concatenate([straight[:, depth:], straight[:, :depth]], axis=1)
            first_ref[scalars[2 + chip], :, : 2 * depth] = straight
            second_ref[scalars[2 + chip], :, : 2 * depth] = turned

    pl.when(scalars[1] == 0)(lambda: emit(own_ref, give_ref))
    pl.when(scalars[1] == 1)(lambda: emit(give_ref, own_ref))


def modulate_image(scalars, latents, image_mod, chips, after):
    slots, tokens, width = latents.shape
    wide = -(-width // chips // LANES) * LANES
    block = (chips, tokens, wide)
    return pl.pallas_call(
        functools.partial(image_kernel, chips),
        grid_spec=pltpu.PrefetchScalarGridSpec(
            num_scalar_prefetch=1,
            grid=(slots,),
            in_specs=[
                pl.BlockSpec((1, tokens, width), lambda i, s: (i, 0, 0)),
                pl.BlockSpec((1, 2, width), lambda i, s: (i, 0, 0)),
                anywhere(),
            ],
            out_specs=[pl.BlockSpec(block, lambda i, s: (0, i, 0))] * 2,
        ),
        out_shape=[jax.ShapeDtypeStruct((chips, slots * tokens, wide), jnp.bfloat16)] * 2,
        compiler_params=params(32),
        cost_estimate=cost(),
    )(scalars, latents, image_mod, after)


def take_rows(slab, o, depth):
    return jnp.concatenate([part[o, :, :depth] for part in slab], axis=0)


def product_kernel(slots, depth, av_places, b_places, first, *refs):
    slabs, refs = refs[:slots], refs[slots:]
    panels = refs[: len(av_places)]
    at = len(av_places)
    pieces = refs[at : at + len(b_places) // 2 + 2 * first]
    out_av, out_b, token_ref = refs[-3:]
    totals = (None, None) if first else refs[-5:-3]
    rows = slabs[0].shape[1]
    columns = out_av.shape[1]
    token_ref[...] = jnp.zeros_like(token_ref)

    def product(slab, places, panel):
        features = jnp.concatenate([take_rows(slab, o, depth) for o in places], axis=1)
        return jnp.dot(features, panel, preferred_element_type=jnp.float32)

    for side, slab in enumerate((slabs[:1], slabs[1:])):
        to = slice(side * rows, (side + 1) * rows)
        if av_places:
            panel = jnp.concatenate([panel[:depth] for panel in panels], axis=0)
            sums = product(slab, av_places, panel)
            out_av[to] = sums if first else totals[0][to] + sums
        elif totals[0] is not out_av:
            out_av[to] = totals[0][to]
        panel = jnp.concatenate([piece[...] for piece in pieces[2 * first :]], axis=0)
        sums = product(slab, b_places, panel)
        if first:
            features = take_rows(slab, 0, depth)
            half = depth // 2
            for own, part in zip((slice(0, half), slice(half, depth)), pieces):
                sums = sums + jnp.dot(
                    features[:, own], part[:, columns:], preferred_element_type=jnp.float32
                )
            out_b[to] = sums
        else:
            out_b[to] = totals[1][to] + sums


def accumulate(depth, totals, slabs, av_items, b_items):
    first = totals is None
    slabs = slabs[0] + slabs[1]
    rows, columns = slabs[0].shape[1], 2 * b_items[0][1].shape[1]
    if first:
        columns = 2 * b_items[0][1].shape[1] // 3
    av_places = [o for places, _ in av_items for o in places]
    b_places = [o for places, _ in b_items for o in places]
    operands = slabs + [x for _, x in av_items] + [x for _, x in b_items]
    aliases = {}
    if not first:
        aliases = {len(operands): 0, len(operands) + 1: 1}
        operands += list(totals)
    out = pl.pallas_call(
        functools.partial(product_kernel, len(slabs), depth, av_places, b_places, first),
        in_specs=[vmem()] * len(operands),
        out_specs=[vmem()] * 3,
        out_shape=[
            jax.ShapeDtypeStruct((2 * rows, columns), jnp.float32),
            jax.ShapeDtypeStruct((2 * rows, columns // 2), jnp.float32),
            jax.ShapeDtypeStruct((8, LANES), jnp.float32),
        ],
        input_output_aliases=aliases,
        compiler_params=params(20),
        cost_estimate=cost(4 * 10**10),
    )(*operands)
    return out[:2], out[2]


def last_kernel(slots, depth, head_size, av_places, b_places, *refs):
    slabs, refs = refs[:slots], refs[slots:]
    count = len(av_places) - 1
    panels, (a_far, v_far) = refs[:count], refs[count : count + 2]
    swapped = refs[count + 2 : count + 2 + len(b_places) // 2]
    total_av, total_b, out_a, out_v, out_b, out_far = refs[-6:]
    rows, columns = slabs[0].shape[1], out_a.shape[1]

    def product(slab, places, panel):
        features = jnp.concatenate([take_rows(slab, o, depth) for o in places], axis=1)
        return jnp.dot(features, panel, preferred_element_type=jnp.float32)

    for side, slab in enumerate((slabs[:1], slabs[1:])):
        to = slice(side * rows, (side + 1) * rows)
        for half, far in enumerate((a_far, v_far)):
            lanes = slice(half * columns, (half + 1) * columns)
            parts = [panel[:depth, lanes] for panel in panels] + [far[...]]
            sums = total_av[to, lanes] + product(slab, av_places, jnp.concatenate(parts, axis=0))
            if half == 1:
                out_v[to] = sums.astype(jnp.bfloat16)
                continue
            for pair in range(columns // LANES):
                at = slice(pair * LANES, (pair + 1) * LANES)
                out_a[to, at] = head_pair_norm(sums[:, at], head_size)
        panel = jnp.concatenate([piece[...] for piece in swapped], axis=0)
        out_b[to] = total_b[to] + product(slab, b_places, panel)
        out_far[to, :depth] = take_rows(slab, av_places[-1], depth)


def last_products(depth, head_size, totals, slabs, av_items, far_items, b_items):
    slabs = slabs[0] + slabs[1]
    rows, columns = 2 * slabs[0].shape[1], totals[1].shape[1]
    av_places = [o for places, _ in av_items for o in places] + [far_items[0]]
    b_places = [o for places, _ in b_items for o in places]
    operands = slabs + [x for _, x in av_items] + list(far_items[1:])
    operands += [x for _, x in b_items] + list(totals)
    return pl.pallas_call(
        functools.partial(last_kernel, len(slabs), depth, head_size, av_places, b_places),
        in_specs=[vmem()] * len(operands),
        out_specs=[vmem()] * 4,
        out_shape=[
            jax.ShapeDtypeStruct((rows, columns), jnp.bfloat16),
            jax.ShapeDtypeStruct((rows, columns), jnp.bfloat16),
            jax.ShapeDtypeStruct((rows, columns), jnp.float32),
            jax.ShapeDtypeStruct((rows, slabs[0].shape[2]), jnp.bfloat16),
        ],
        compiler_params=params(20),
        cost_estimate=cost(4 * 10**10),
    )(*operands)


def meet(arrays, others):
    return pl.pallas_call(
        lambda *refs: None,
        in_specs=[anywhere()] * (len(arrays) + len(others)),
        out_specs=[anywhere()] * len(arrays),
        out_shape=[jax.ShapeDtypeStruct(x.shape, x.dtype) for x in arrays],
        input_output_aliases={i: i for i in range(len(arrays))},
        compiler_params=params(4),
        cost_estimate=cost(),
    )(*arrays, *others)


def pick_kernel(rows, ahead_ref, behind_ref, *outs):
    columns = outs[0].shape[1]
    outs[0][:rows] = ahead_ref[:, :columns]
    outs[0][rows:] = behind_ref[:, :columns]
    if len(outs) > 1:
        outs[1][...] = ahead_ref[:, :columns]
        outs[2][...] = behind_ref[:, columns:]


def pick(ahead, behind, last):
    rows, columns = ahead.shape[0], ahead.shape[1] // 2
    shapes = [(2 * rows, columns)] + [(rows, columns)] * (2 * last)
    widths = (columns, 2 * columns if last else columns)
    return pl.pallas_call(
        functools.partial(pick_kernel, rows),
        grid=(1,),
        in_specs=[pl.BlockSpec((rows, wide), lambda i: (0, 0)) for wide in widths],
        out_specs=[pl.BlockSpec(shape, lambda i: (0, 0)) for shape in shapes],
        out_shape=[jax.ShapeDtypeStruct(shape, jnp.bfloat16) for shape in shapes],
        compiler_params=params(12),
        cost_estimate=cost(),
    )(ahead, behind)


def join_kernel(scalars, mine_ref, theirs_ref, out_ref):
    columns = mine_ref.shape[1]
    shared = 2 * columns - out_ref.shape[1]

    def emit(low, high):
        out_ref[:, :columns] = low[...]
        out_ref[:, columns:] = high[:, shared:]

    pl.when(scalars[1] == 0)(lambda: emit(mine_ref, theirs_ref))
    pl.when(scalars[1] == 1)(lambda: emit(theirs_ref, mine_ref))


def join(scalars, mine, theirs, inner_width):
    slots, _, tokens = mine.shape
    return pl.pallas_call(
        join_kernel,
        in_specs=[smem(), vmem(), vmem()],
        out_specs=vmem(),
        out_shape=jax.ShapeDtypeStruct((slots, inner_width, tokens), jnp.bfloat16),
        compiler_params=params(8),
        cost_estimate=cost(),
    )(scalars, mine, theirs)


def cut_kernel(k_ref, v_ref, after_ref, out_ref):
    chips, _, span = out_ref.shape
    half = chips // 2
    for chip in range(chips):
        source = k_ref if chip < half else v_ref
        start = (chip % half) * span
        out_ref[chip] = source[:, start : start + span]


def cut_prompt_weights(w_ck, w_cv, chips, after):
    depth, inner_width = w_ck.shape
    span = 2 * inner_width // chips
    return pl.pallas_call(
        cut_kernel,
        in_specs=[vmem(), vmem(), anywhere()],
        out_specs=vmem(),
        out_shape=jax.ShapeDtypeStruct((chips, depth, span), jnp.bfloat16),
        compiler_params=params(8),
        cost_estimate=cost(),
    )(w_ck, w_cv, after)


def prompt_kernel(starts, scalars, *refs):
    chips = len(starts)
    blocks, (own_ref, other_ref, out_ref, held_ref) = refs[:chips], refs[chips:]
    depth = own_ref.shape[0]
    half = out_ref.shape[1]
    parts = [
        jnp.concatenate(
            [
                block[start + core * half : start + (core + 1) * half, :depth]
                for start, block in zip(starts, blocks)
            ],
            axis=0,
        )
        for core in range(2)
    ]

    def emit(first, second):
        product = jnp.dot(parts[0], first[...], preferred_element_type=jnp.float32) + jnp.dot(
            parts[1], second[...], preferred_element_type=jnp.float32
        )
        held_ref[...] = product.astype(jnp.bfloat16).reshape(held_ref.shape)

    pl.when(scalars[1] == 0)(lambda: emit(own_ref, other_ref))
    pl.when(scalars[1] == 1)(lambda: emit(other_ref, own_ref))
    for chip in range(chips):
        out_ref[chip] = held_ref[scalars[2 + chip]]


def project_prompts(scalars, blocks, starts, w_own, w_other):
    chips, span = len(blocks), w_own.shape[1]
    half = (blocks[0].shape[0] - starts[0]) // 2
    if blocks[0].shape[0] * chips > 4096:
        depth = w_own.shape[0]
        straight = scalars[1] == 0
        weights = [jnp.where(straight, w_own, w_other), jnp.where(straight, w_other, w_own)]
        product = 0.0
        for core, weight in enumerate(weights):
            rows = [
                x[start + core * half : start + (core + 1) * half, :depth]
                for start, x in zip(starts, blocks)
            ]
            rows = jnp.concatenate(rows, axis=0)
            product = product + jnp.dot(rows, weight, preferred_element_type=jnp.float32)
        product = product.astype(jnp.bfloat16).reshape(chips, half, span)
        return jnp.take(product, scalars[2 : 2 + chips], axis=0)
    return pl.pallas_call(
        functools.partial(prompt_kernel, starts),
        in_specs=[smem()] + [vmem()] * (chips + 2),
        out_specs=vmem(),
        out_shape=jax.ShapeDtypeStruct((chips, half, span), jnp.bfloat16),
        scratch_shapes=[pltpu.VMEM((chips, half, span), jnp.bfloat16)],
        compiler_params=params(16),
        cost_estimate=cost(),
    )(scalars, *blocks, w_own, w_other)


def route_kernel(spots_here, winner_ref, loser_ref, rows_ref, out_ref):
    tile, count = out_ref.shape[0], rows_ref.shape[0]
    prompts = winner_ref.shape[1]
    row = lax.broadcasted_iota(jnp.int32, (tile, 1), 0) + pl.program_id(0) * tile
    slot = lax.div(row, spots_here)
    reads = (winner_ref[...] == slot) | (loser_ref[...] == slot)
    column = lax.broadcasted_iota(jnp.int32, (prompts, count), 1)
    prompt = lax.broadcasted_iota(jnp.int32, (prompts, count), 0)
    spread = jnp.where(lax.rem(column, prompts) == prompt, 1.0, 0.0).astype(jnp.bfloat16)
    reads = jnp.where(reads, 1.0, 0.0).astype(jnp.bfloat16)
    reads = jnp.dot(reads, spread, preferred_element_type=jnp.float32)
    same_spot = lax.rem(row, spots_here) == lax.div(column[0:1], prompts)
    chosen = jnp.where(same_spot, reads, 0.0).astype(jnp.bfloat16)
    out_ref[...] = jnp.dot(
        chosen, rows_ref[...], preferred_element_type=jnp.float32
    ).astype(jnp.bfloat16)


def route(projected, winner_slot, loser_slot, spots_here):
    count, span = projected.shape
    prompts = winner_slot.shape[0]
    total = 2 * prompts * spots_here
    tile = min(total, 512)
    row = pl.BlockSpec((1, prompts), lambda i: (0, 0))
    return pl.pallas_call(
        functools.partial(route_kernel, spots_here),
        grid=(total // tile,),
        in_specs=[row, row, pl.BlockSpec((count, span), lambda i: (0, 0))],
        out_specs=pl.BlockSpec((tile, span), lambda i: (i, 0)),
        out_shape=jax.ShapeDtypeStruct((total, span), jnp.bfloat16),
        compiler_params=params(32 if count > 1024 else 8),
        cost_estimate=cost(),
    )(winner_slot.reshape(1, prompts), loser_slot.reshape(1, prompts), projected)


def finish_kernel(columns, head_size, scalars, own_ref, other_ref, keys_ref, values_ref):
    devices, rows, span = own_ref.shape
    slots = keys_ref.shape[0] // 2
    each = rows // slots
    inner_width = devices // 2 * span // 2

    def emit(start):
        for side, source in enumerate((own_ref, other_ref)):
            for slot in range(slots):
                at = slice(slot * each, (slot + 1) * each)
                for core in range(2):
                    parts = [source[2 * chip + core, at, :] for chip in range(devices // 2)]
                    whole = jnp.concatenate(parts, axis=1)
                    out = side * slots + slot
                    to = slice(core * each, (core + 1) * each)
                    keys = whole[:, start : start + columns].astype(jnp.float32)
                    for pair in range(columns // LANES):
                        lanes = slice(pair * LANES, (pair + 1) * LANES)
                        keys_ref[out, to, lanes] = head_pair_norm(keys[:, lanes], head_size)
                    first = inner_width + start
                    values_ref[out, to, :] = whole[:, first : first + columns]

    pl.when(scalars[1] == 0)(lambda: emit(0))
    pl.when(scalars[1] == 1)(lambda: emit(inner_width - columns))


def finish_prompts(scalars, own, other, columns, head_size, slots):
    devices, rows, _ = own.shape
    span = 2 * rows // slots
    shape = jax.ShapeDtypeStruct((2 * slots, span, columns), jnp.bfloat16)
    return pl.pallas_call(
        functools.partial(finish_kernel, columns, head_size),
        in_specs=[smem(), vmem(), vmem()],
        out_specs=[vmem()] * 2,
        out_shape=[shape] * 2,
        compiler_params=params(16),
        cost_estimate=cost(),
    )(scalars, own, other)


def attend_kernel(
    head_size,
    spots,
    side,
    scalars,
    winner,
    loser,
    lengths,
    a_ref,
    v_ref,
    b_ref,
    features_ref,
    far_ref,
    pk_ref,
    pv_ref,
    out_ref,
):
    step = pl.program_id(0)
    count_here = pl.num_programs(0)
    even_group = scalars[0] == 0
    _, columns, tokens = out_ref.shape
    depth = far_ref.shape[0]
    owner = scalars[scalars.shape[0] - 2 + side]
    slot = owner + step

    def count(p, live):
        hit = (winner[p] == slot) | (loser[p] == slot)
        return live + jnp.where(hit, lengths[p], 0)

    live = lax.fori_loop(0, winner.shape[0], count, jnp.int32(0))
    span = pk_ref.shape[1]
    row = lax.broadcasted_iota(jnp.int32, (span, 1), 0)
    rest = lax.rem(row, span // 2)
    position = (2 * lax.div(rest, spots) + lax.div(row, span // 2)) * spots + lax.rem(rest, spots)
    allowed = position < live
    low = lax.broadcasted_iota(jnp.int32, (1, LANES), 1) < head_size
    over_lanes = (((1,), (1,)), ((), ()))
    over_rows = (((0,), (0,)), ((), ()))
    scale = 1.4426950408889634 / head_size**0.5
    here = pl.ds(pl.multiple_of((side * count_here + step) * tokens, tokens), tokens)
    block = side * count_here + step
    features = features_ref[here, :][:, :depth]
    for pair in range(columns // LANES):
        lanes = slice(pair * LANES, (pair + 1) * LANES)
        a = a_ref[here, lanes]
        last = jnp.dot(features, far_ref[:, lanes], preferred_element_type=jnp.float32)
        b = head_pair_norm(b_ref[here, lanes] + last, head_size)
        queries = jnp.where(even_group, a, b)
        keys = jnp.where(even_group, b, a)
        values = v_ref[here, lanes]
        prompt_keys = pk_ref[block, :, lanes]
        prompt_values = pv_ref[block, :, lanes]
        for head in range(2):
            side = low if head == 0 else jnp.logical_not(low)
            q = jnp.where(side, queries, jnp.zeros_like(queries))
            s = lax.dot_general(keys, q, over_lanes, preferred_element_type=jnp.float32)
            t = lax.dot_general(prompt_keys, q, over_lanes, preferred_element_type=jnp.float32)
            s = jnp.exp2(s * scale)
            t = jnp.where(allowed, jnp.exp2(t * scale), 0.0)
            total = jnp.sum(s, axis=0, keepdims=True) + jnp.sum(t, axis=0, keepdims=True)
            out = lax.dot_general(
                values, s.astype(jnp.bfloat16), over_rows, preferred_element_type=jnp.float32
            ) + lax.dot_general(
                prompt_values, t.astype(jnp.bfloat16), over_rows, preferred_element_type=jnp.float32
            )
            rows = slice(head * head_size, (head + 1) * head_size)
            to = slice(pair * LANES + head * head_size, pair * LANES + (head + 1) * head_size)
            out_ref[0, to, :] = (out[rows] * (1.0 / total)).astype(jnp.bfloat16)


def attend(side, scalars, routes, rows, far, prompt_keys, prompt_values, head_size, spots, count):
    tokens = rows[0].shape[0] // (2 * count)
    columns = rows[0].shape[1]
    return pl.pallas_call(
        functools.partial(attend_kernel, head_size, spots, side),
        grid=(count,),
        in_specs=[smem()] * 4 + [vmem()] * 7,
        out_specs=pl.BlockSpec((1, columns, tokens), lambda l: (l, 0, 0)),
        out_shape=jax.ShapeDtypeStruct((count, columns, tokens), jnp.bfloat16),
        compiler_params=params(16),
        cost_estimate=cost(),
    )(scalars, *routes, *rows, far, prompt_keys, prompt_values)


def ring_order(groups, chips):
    if groups == 2:
        return list(range(0, chips, 2)) + list(range(1, chips, 2))[::-1]
    return list(range(chips))


def solution(mesh):
    groups, dp = mesh.shape["groups"], mesh.shape["dp"]
    chips = dp // 2
    ring = ring_order(groups, chips)
    place = [ring.index(chip) for chip in range(chips)]
    behind_by = np.array(
        [[(place[me] - place[chip]) % chips for chip in range(chips)] for me in range(chips)],
        np.int32,
    )
    forward_pairs = [
        (2 * ring[i] + c, 2 * ring[(i + 1) % chips] + c) for i in range(chips) for c in range(2)
    ]
    backward_pairs = [(b, a) for a, b in forward_pairs]
    core_pairs = [(d, d ^ 1) for d in range(dp)]
    group_pairs = [(g, g ^ 1) for g in range(groups)]
    half_groups = [[2 * chip + c for chip in range(chips)] for c in range(2)]

    def forward(x):
        return lax.ppermute(x, "dp", forward_pairs)

    def backward(x):
        return lax.ppermute(x, "dp", backward_pairs)

    def swap_cores(x):
        return lax.ppermute(x, "dp", core_pairs)

    def swap_groups(x):
        return lax.ppermute(x, "groups", group_pairs)

    def local(
        latents,
        context,
        lengths,
        winner_slot,
        loser_slot,
        image_mod,
        context_mod,
        w_q,
        w_k,
        w_v,
        w_ck,
        w_cv,
    ):
        slot_local, token_count, width = latents.shape
        prompt_count, spot_local, _ = context.shape
        depth, inner_width = w_q.shape
        head_size = inner_width // HEADS
        columns = (HEADS + 1) // 2 * head_size
        me = lax.axis_index("dp")
        my_group = lax.axis_index("groups") % 2
        my_chip, my_core = me // 2, me % 2
        places = lax.dynamic_index_in_dim(jnp.asarray(behind_by), my_chip, 0, keepdims=False)
        first = [my_group, my_core]
        last = [me * slot_local, (me ^ 1) * slot_local]
        scalars = jnp.concatenate([jnp.stack(first), places, jnp.stack(last)]).astype(jnp.int32)

        keep, give = split_weights(scalars, w_q, w_k, w_v, columns)
        got = swap_cores(give)
        av = jnp.concatenate([keep[:, : 2 * columns], got[:, : 2 * columns]], axis=0)

        own_mixed = mix_prompts(context, context_mod, chips, width // 2)
        mixed = {0: own_mixed}
        sent = [own_mixed, own_mixed]
        hops = []
        for o in range(1, chips // 2 + 1):
            sent[0] = mixed[o] = forward(sent[0])
            if 2 * o < chips:
                sent[1] = mixed[chips - o] = backward(sent[1])
            hops.append([mixed[o], mixed[chips - o]])

        own, *give = modulate_image(scalars, latents, image_mod, chips, av)

        w_c = cut_prompt_weights(w_ck, w_cv, chips, keep)
        w_c = lax.all_to_all(w_c, "dp", 0, 0, axis_index_groups=half_groups, tiled=True)

        w_c_other = swap_cores(w_c).reshape(width // 2, -1)
        w_c = w_c.reshape(width // 2, -1)

        totals = None
        enough = max(1, chips // 8)
        tokens, waiting_av, waiting_b = [w_c, w_c_other], [((0,), av)], []
        ahead = behind = av
        for o in range(1, chips // 2):
            here = [x for hop in hops[2 * o - 2 : 2 * o] for x in hop]
            ahead, behind = meet([forward(ahead), backward(behind)], tokens + here)
            if 4 * o == chips:
                slabs = [[own], [swap_cores(x) for x in meet(give, [ahead])]]
            tokens = []
            last = 2 * o + 2 == chips
            picked = pick(ahead, behind, last)
            waiting_av += [((o,), ahead), ((chips - o,), behind)]
            if len(waiting_b) > 3 * enough or (last and totals is None):
                totals, token = accumulate(
                    2 * depth,
                    totals,
                    slabs,
                    waiting_av,
                    ([((), keep), ((), got)] if totals is None else []) + waiting_b,
                )
                tokens.append(token)
                waiting_av, waiting_b = [], []
            waiting_b.append(((o, chips - o), swap_groups(picked[0])))
            if not last:
                tokens.append(waiting_b[-1][1])
        a_far, v_far = meet([forward(picked[1]), backward(picked[2])], tokens)
        b_far = swap_groups(a_far)
        done_rows = last_products(
            2 * depth,
            head_size,
            totals,
            slabs,
            waiting_av,
            (chips // 2, a_far, v_far),
            waiting_b,
        )

        blocks, starts = [mixed[o] for o in range(chips)], [0] * chips
        projected = project_prompts(scalars, blocks, starts, w_c, w_c_other)
        projected = projected.reshape(-1, projected.shape[2])
        outgoing = route(projected, winner_slot, loser_slot, chips * spot_local)
        outgoing = outgoing.reshape(dp, -1, outgoing.shape[1])
        arrived = lax.all_to_all(outgoing, "dp", 0, 0, tiled=True)
        prompt_keys, prompt_values = finish_prompts(
            scalars, arrived, swap_cores(arrived), columns, head_size, slot_local
        )

        routes = (winner_slot, loser_slot, lengths)

        def run(side):
            return attend(
                side,
                scalars,
                routes,
                done_rows,
                b_far,
                prompt_keys,
                prompt_values,
                head_size,
                spot_local,
                slot_local,
            )

        theirs = swap_cores(run(1))
        mine = run(0)
        return join(scalars, mine, theirs, inner_width).transpose(0, 2, 1)

    placed = (
        P(("groups", "dp"), None, None),
        P("groups", "dp", None),
        P("groups"),
        P("groups"),
        P("groups"),
        P(("groups", "dp"), None, None),
        P("groups", None, None),
        P("dp", None),
        P("dp", None),
        P("dp", None),
        P("dp", None),
        P("dp", None),
    )
    return jax.shard_map(
        local,
        mesh=mesh,
        in_specs=placed,
        out_specs=P(("groups", "dp"), None, None),
        check_vma=False,
    )
```

```python
import functools

import jax
import jax.numpy as jnp
import numpy as np
from jax import lax
from jax.experimental import pallas as pl
from jax.experimental.pallas import tpu as pltpu
from jax.sharding import PartitionSpec as P

HEADS = 19
LANES = 128


epsilon = 1e-06


def params(mib):
    return pltpu.CompilerParams(vmem_limit_bytes=mib * 2**20)


def cost(flops=1):
    return pl.CostEstimate(flops=flops, bytes_accessed=1, transcendentals=0)


def anywhere():
    return pl.BlockSpec(memory_space=pl.ANY)


def layer_norm(values, shift, scale):
    average = jnp.mean(values, axis=-1, keepdims=True)
    centered = values - average
    variance = jnp.mean(centered * centered, axis=-1, keepdims=True)
    return (centered * lax.rsqrt(variance + epsilon) * (1.0 + scale) + shift).astype(jnp.bfloat16)


def head_pair_norm(x, head_size):
    low = lax.broadcasted_iota(jnp.int32, (1, LANES), 1) < head_size
    squares = x * x
    first = jnp.sum(jnp.where(low, squares, 0.0), axis=-1, keepdims=True)
    second = jnp.sum(jnp.where(low, 0.0, squares), axis=-1, keepdims=True)
    first = lax.rsqrt(first * (1.0 / head_size) + epsilon)
    second = lax.rsqrt(second * (1.0 / head_size) + epsilon)
    return (x * jnp.where(low, first, second)).astype(jnp.bfloat16)


def vmem():
    return pl.BlockSpec(memory_space=pltpu.VMEM)


def smem():
    return pl.BlockSpec(memory_space=pltpu.SMEM)


def split_kernel(columns, scalars, q_ref, k_ref, v_ref, keep_ref, give_ref):
    inner_width = q_ref.shape[1]

    def emit(parts, low_ref, high_ref):
        for i, part in enumerate(parts):
            at = slice(i * columns, (i + 1) * columns)
            low_ref[:, at] = part[:, :columns]
            high_ref[:, at] = part[:, inner_width - columns :]

    for group in range(2):
        parts = (q_ref, v_ref, k_ref) if group == 0 else (k_ref, v_ref, q_ref)
        for core in range(2):
            refs = (keep_ref, give_ref) if core == 0 else (give_ref, keep_ref)
            here = (scalars[0] == group) & (scalars[1] == core)
            pl.when(here)(functools.partial(emit, parts, *refs))


def split_weights(scalars, w_q, w_k, w_v, columns):
    depth, inner_width = w_q.shape
    shape = jax.ShapeDtypeStruct((depth, 3 * columns), jnp.bfloat16)
    whole = pl.BlockSpec((depth, inner_width), lambda i, s: (0, 0))
    out = pl.BlockSpec((depth, 3 * columns), lambda i, s: (0, 0))
    return pl.pallas_call(
        functools.partial(split_kernel, columns),
        grid_spec=pltpu.PrefetchScalarGridSpec(
            num_scalar_prefetch=1, grid=(1,), in_specs=[whole] * 3, out_specs=[out] * 2
        ),
        out_shape=[shape] * 2,
        compiler_params=params(56),
        cost_estimate=cost(),
    )(scalars, w_q, w_k, w_v)


def mixed_kernel(chips, context_ref, mod_ref, out_ref):
    prompts, spots, width = context_ref.shape
    depth = width // (2 * chips)
    shift, scale = mod_ref[:, 0, :], mod_ref[:, 1, :]
    values = context_ref[...].astype(jnp.float32)
    for spot in range(spots):
        rows = layer_norm(values[:, spot, :], shift, scale)
        for core in range(2):
            parts = [
                rows[:, (2 * chip + core) * depth : (2 * chip + core + 1) * depth]
                for chip in range(chips)
            ]
            at = (core * spots + spot) * prompts
            parts.append(jnp.zeros((prompts, out_ref.shape[1] - width // 2), jnp.bfloat16))
            out_ref[at : at + prompts, :] = jnp.concatenate(parts, axis=1)


def mix_prompts(context, context_mod, chips, columns):
    prompts, spots, width = context.shape
    return pl.pallas_call(
        functools.partial(mixed_kernel, chips),
        in_specs=[vmem()] * 2,
        out_specs=vmem(),
        out_shape=jax.ShapeDtypeStruct((2 * spots * prompts, columns), jnp.bfloat16),
        compiler_params=params(16),
        cost_estimate=cost(),
    )(context, context_mod)


def image_kernel(chips, scalars, x_ref, mod_ref, after_ref, own_ref, give_ref):
    image = layer_norm(x_ref[0].astype(jnp.float32), mod_ref[0, 0:1, :], mod_ref[0, 1:2, :])
    depth = image.shape[1] // (2 * chips)

    def emit(first_ref, second_ref):
        for chip in range(chips):
            start = 2 * chip * depth
            straight = image[:, start : start + 2 * depth]
            turned = jnp.concatenate([straight[:, depth:], straight[:, :depth]], axis=1)
            first_ref[scalars[2 + chip], :, : 2 * depth] = straight
            second_ref[scalars[2 + chip], :, : 2 * depth] = turned

    pl.when(scalars[1] == 0)(lambda: emit(own_ref, give_ref))
    pl.when(scalars[1] == 1)(lambda: emit(give_ref, own_ref))


def modulate_image(scalars, latents, image_mod, chips, after):
    slots, tokens, width = latents.shape
    wide = -(-width // chips // LANES) * LANES
    block = (chips, tokens, wide)
    return pl.pallas_call(
        functools.partial(image_kernel, chips),
        grid_spec=pltpu.PrefetchScalarGridSpec(
            num_scalar_prefetch=1,
            grid=(slots,),
            in_specs=[
                pl.BlockSpec((1, tokens, width), lambda i, s: (i, 0, 0)),
                pl.BlockSpec((1, 2, width), lambda i, s: (i, 0, 0)),
                anywhere(),
            ],
            out_specs=[pl.BlockSpec(block, lambda i, s: (0, i, 0))] * 2,
        ),
        out_shape=[jax.ShapeDtypeStruct((chips, slots * tokens, wide), jnp.bfloat16)] * 2,
        compiler_params=params(32),
        cost_estimate=cost(),
    )(scalars, latents, image_mod, after)


def take_rows(slab, o, depth):
    return jnp.concatenate([part[o, :, :depth] for part in slab], axis=0)


def product_kernel(slots, depth, av_places, b_places, first, *refs):
    slabs, refs = refs[:slots], refs[slots:]
    panels = refs[: len(av_places)]
    at = len(av_places)
    pieces = refs[at : at + len(b_places) // 2 + 2 * first]
    out_av, out_b, token_ref = refs[-3:]
    totals = (None, None) if first else refs[-5:-3]
    rows = slabs[0].shape[1]
    columns = out_av.shape[1]
    token_ref[...] = jnp.zeros_like(token_ref)

    def product(slab, places, panel):
        features = jnp.concatenate([take_rows(slab, o, depth) for o in places], axis=1)
        return jnp.dot(features, panel, preferred_element_type=jnp.float32)

    for side, slab in enumerate((slabs[:1], slabs[1:])):
        to = slice(side * rows, (side + 1) * rows)
        if av_places:
            panel = jnp.concatenate([panel[:depth] for panel in panels], axis=0)
            sums = product(slab, av_places, panel)
            out_av[to] = sums if first else totals[0][to] + sums
        elif totals[0] is not out_av:
            out_av[to] = totals[0][to]
        sums = 0.0
        if b_places:
            panel = jnp.concatenate([piece[...] for piece in pieces[2 * first :]], axis=0)
            sums = product(slab, b_places, panel)
        if first:
            features = take_rows(slab, 0, depth)
            half = depth // 2
            for own, part in zip((slice(0, half), slice(half, depth)), pieces):
                sums = sums + jnp.dot(
                    features[:, own], part[:, columns:], preferred_element_type=jnp.float32
                )
            out_b[to] = sums
        else:
            out_b[to] = totals[1][to] + sums


def accumulate(depth, totals, slabs, av_items, b_items):
    first = totals is None
    slabs = slabs[0] + slabs[1]
    rows, columns = slabs[0].shape[1], 2 * b_items[0][1].shape[1]
    if first:
        columns = 2 * b_items[0][1].shape[1] // 3
    av_places = [o for places, _ in av_items for o in places]
    b_places = [o for places, _ in b_items for o in places]
    operands = slabs + [x for _, x in av_items] + [x for _, x in b_items]
    aliases = {}
    if not first:
        aliases = {len(operands): 0, len(operands) + 1: 1}
        operands += list(totals)
    out = pl.pallas_call(
        functools.partial(product_kernel, len(slabs), depth, av_places, b_places, first),
        in_specs=[vmem()] * len(operands),
        out_specs=[vmem()] * 3,
        out_shape=[
            jax.ShapeDtypeStruct((2 * rows, columns), jnp.float32),
            jax.ShapeDtypeStruct((2 * rows, columns // 2), jnp.float32),
            jax.ShapeDtypeStruct((8, LANES), jnp.float32),
        ],
        input_output_aliases=aliases,
        compiler_params=params(20),
        cost_estimate=cost(4 * 10**10),
    )(*operands)
    return out[:2], out[2]


def last_kernel(slots, depth, head_size, av_places, b_places, *refs):
    slabs, refs = refs[:slots], refs[slots:]
    count = len(av_places) - 1
    panels, (a_far, v_far) = refs[:count], refs[count : count + 2]
    swapped = refs[count + 2 : count + 2 + len(b_places) // 2]
    total_av, total_b, out_a, out_v, out_b, out_far = refs[-6:]
    rows, columns = slabs[0].shape[1], out_a.shape[1]

    def product(slab, places, panel):
        features = jnp.concatenate([take_rows(slab, o, depth) for o in places], axis=1)
        return jnp.dot(features, panel, preferred_element_type=jnp.float32)

    for side, slab in enumerate((slabs[:1], slabs[1:])):
        to = slice(side * rows, (side + 1) * rows)
        for half, far in enumerate((a_far, v_far)):
            lanes = slice(half * columns, (half + 1) * columns)
            parts = [panel[:depth, lanes] for panel in panels] + [far[...]]
            sums = total_av[to, lanes] + product(slab, av_places, jnp.concatenate(parts, axis=0))
            if half == 1:
                out_v[to] = sums.astype(jnp.bfloat16)
                continue
            for pair in range(columns // LANES):
                at = slice(pair * LANES, (pair + 1) * LANES)
                out_a[to, at] = head_pair_norm(sums[:, at], head_size)
        panel = jnp.concatenate([piece[...] for piece in swapped], axis=0)
        out_b[to] = total_b[to] + product(slab, b_places, panel)
        out_far[to, :depth] = take_rows(slab, av_places[-1], depth)


def last_products(depth, head_size, totals, slabs, av_items, far_items, b_items):
    slabs = slabs[0] + slabs[1]
    rows, columns = 2 * slabs[0].shape[1], totals[1].shape[1]
    av_places = [o for places, _ in av_items for o in places] + [far_items[0]]
    b_places = [o for places, _ in b_items for o in places]
    operands = slabs + [x for _, x in av_items] + list(far_items[1:])
    operands += [x for _, x in b_items] + list(totals)
    return pl.pallas_call(
        functools.partial(last_kernel, len(slabs), depth, head_size, av_places, b_places),
        in_specs=[vmem()] * len(operands),
        out_specs=[vmem()] * 4,
        out_shape=[
            jax.ShapeDtypeStruct((rows, columns), jnp.bfloat16),
            jax.ShapeDtypeStruct((rows, columns), jnp.bfloat16),
            jax.ShapeDtypeStruct((rows, columns), jnp.float32),
            jax.ShapeDtypeStruct((rows, slabs[0].shape[2]), jnp.bfloat16),
        ],
        compiler_params=params(20),
        cost_estimate=cost(4 * 10**10),
    )(*operands)


def close_kernel(head_size, total_ref, features_ref, far_ref, out_ref):
    features = features_ref[:, : far_ref.shape[0]]
    sums = jnp.dot(features, far_ref[...], preferred_element_type=jnp.float32) + total_ref[...]
    for pair in range(out_ref.shape[1] // LANES):
        lanes = slice(pair * LANES, (pair + 1) * LANES)
        out_ref[:, lanes] = head_pair_norm(sums[:, lanes], head_size)


def close(total, features, far, head_size):
    return pl.pallas_call(
        functools.partial(close_kernel, head_size),
        in_specs=[vmem()] * 3,
        out_specs=vmem(),
        out_shape=jax.ShapeDtypeStruct(total.shape, jnp.bfloat16),
        compiler_params=params(16),
        cost_estimate=cost(),
    )(total, features, far)


def meet(arrays, others):
    return pl.pallas_call(
        lambda *refs: None,
        in_specs=[anywhere()] * (len(arrays) + len(others)),
        out_specs=[anywhere()] * len(arrays),
        out_shape=[jax.ShapeDtypeStruct(x.shape, x.dtype) for x in arrays],
        input_output_aliases={i: i for i in range(len(arrays))},
        compiler_params=params(4),
        cost_estimate=cost(),
    )(*arrays, *others)


def pick_kernel(rows, ahead_ref, behind_ref, *outs):
    columns = outs[0].shape[1]
    outs[0][:rows] = ahead_ref[:rows, :columns]
    outs[0][rows:] = behind_ref[:rows, :columns]
    if len(outs) > 1:
        outs[1][...] = ahead_ref[:rows, :columns]
        outs[2][...] = behind_ref[:rows, columns:]


def pick(rows, ahead, behind, last):
    height, columns = ahead.shape[0], ahead.shape[1] // 2
    shapes = [(2 * rows, columns)] + [(rows, columns)] * (2 * last)
    widths = (columns, 2 * columns if last else columns)
    return pl.pallas_call(
        functools.partial(pick_kernel, rows),
        grid=(1,),
        in_specs=[pl.BlockSpec((height, wide), lambda i: (0, 0)) for wide in widths],
        out_specs=[pl.BlockSpec(shape, lambda i: (0, 0)) for shape in shapes],
        out_shape=[jax.ShapeDtypeStruct(shape, jnp.bfloat16) for shape in shapes],
        compiler_params=params(12),
        cost_estimate=cost(),
    )(ahead, behind)


def join_kernel(scalars, mine_ref, theirs_ref, out_ref):
    columns = mine_ref.shape[1]
    shared = 2 * columns - out_ref.shape[1]

    def emit(low, high):
        out_ref[:, :columns] = low[...]
        out_ref[:, columns:] = high[:, shared:]

    pl.when(scalars[1] == 0)(lambda: emit(mine_ref, theirs_ref))
    pl.when(scalars[1] == 1)(lambda: emit(theirs_ref, mine_ref))


def join(scalars, mine, theirs, inner_width):
    slots, _, tokens = mine.shape
    return pl.pallas_call(
        join_kernel,
        in_specs=[smem(), vmem(), vmem()],
        out_specs=vmem(),
        out_shape=jax.ShapeDtypeStruct((slots, inner_width, tokens), jnp.bfloat16),
        compiler_params=params(8),
        cost_estimate=cost(),
    )(scalars, mine, theirs)


def cut_kernel(k_ref, v_ref, after_ref, out_ref):
    chips, _, span = out_ref.shape
    half = chips // 2
    for chip in range(chips):
        source = k_ref if chip < half else v_ref
        start = (chip % half) * span
        out_ref[chip] = source[:, start : start + span]


def cut_prompt_weights(w_ck, w_cv, chips, after):
    depth, inner_width = w_ck.shape
    span = 2 * inner_width // chips
    return pl.pallas_call(
        cut_kernel,
        in_specs=[vmem(), vmem(), anywhere()],
        out_specs=vmem(),
        out_shape=jax.ShapeDtypeStruct((chips, depth, span), jnp.bfloat16),
        compiler_params=params(8),
        cost_estimate=cost(),
    )(w_ck, w_cv, after)


def prompt_kernel(starts, scalars, after_ref, *refs):
    chips = len(starts)
    blocks, (own_ref, other_ref, out_ref, held_ref) = refs[:chips], refs[chips:]
    depth = own_ref.shape[0]
    half = out_ref.shape[1]
    parts = [
        jnp.concatenate(
            [
                block[start + core * half : start + (core + 1) * half, :depth]
                for start, block in zip(starts, blocks)
            ],
            axis=0,
        )
        for core in range(2)
    ]

    def emit(first, second):
        product = jnp.dot(parts[0], first[...], preferred_element_type=jnp.float32) + jnp.dot(
            parts[1], second[...], preferred_element_type=jnp.float32
        )
        held_ref[...] = product.astype(jnp.bfloat16).reshape(held_ref.shape)

    pl.when(scalars[1] == 0)(lambda: emit(own_ref, other_ref))
    pl.when(scalars[1] == 1)(lambda: emit(other_ref, own_ref))
    for chip in range(chips):
        out_ref[chip] = held_ref[scalars[2 + chip]]


def project_prompts(scalars, blocks, starts, w_own, w_other, after):
    chips, span = len(blocks), w_own.shape[1]
    half = (blocks[0].shape[0] - starts[0]) // 2
    if blocks[0].shape[0] * chips > 4096:
        depth = w_own.shape[0]
        straight = scalars[1] == 0
        weights = [jnp.where(straight, w_own, w_other), jnp.where(straight, w_other, w_own)]
        product = 0.0
        for core, weight in enumerate(weights):
            rows = [
                x[start + core * half : start + (core + 1) * half, :depth]
                for start, x in zip(starts, blocks)
            ]
            rows = jnp.concatenate(rows, axis=0)
            product = product + jnp.dot(rows, weight, preferred_element_type=jnp.float32)
        product = product.astype(jnp.bfloat16).reshape(chips, half, span)
        return jnp.take(product, scalars[2 : 2 + chips], axis=0)
    return pl.pallas_call(
        functools.partial(prompt_kernel, starts),
        in_specs=[smem(), anywhere()] + [vmem()] * (chips + 2),
        out_specs=vmem(),
        out_shape=jax.ShapeDtypeStruct((chips, half, span), jnp.bfloat16),
        scratch_shapes=[pltpu.VMEM((chips, half, span), jnp.bfloat16)],
        compiler_params=params(16),
        cost_estimate=cost(),
    )(scalars, after, *blocks, w_own, w_other)


def route_kernel(spots_here, winner_ref, loser_ref, rows_ref, out_ref):
    tile, count = out_ref.shape[0], rows_ref.shape[0]
    prompts = winner_ref.shape[1]
    row = lax.broadcasted_iota(jnp.int32, (tile, 1), 0) + pl.program_id(0) * tile
    slot = lax.div(row, spots_here)
    reads = (winner_ref[...] == slot) | (loser_ref[...] == slot)
    column = lax.broadcasted_iota(jnp.int32, (prompts, count), 1)
    prompt = lax.broadcasted_iota(jnp.int32, (prompts, count), 0)
    spread = jnp.where(lax.rem(column, prompts) == prompt, 1.0, 0.0).astype(jnp.bfloat16)
    reads = jnp.where(reads, 1.0, 0.0).astype(jnp.bfloat16)
    reads = jnp.dot(reads, spread, preferred_element_type=jnp.float32)
    same_spot = lax.rem(row, spots_here) == lax.div(column[0:1], prompts)
    chosen = jnp.where(same_spot, reads, 0.0).astype(jnp.bfloat16)
    out_ref[...] = jnp.dot(
        chosen, rows_ref[...], preferred_element_type=jnp.float32
    ).astype(jnp.bfloat16)


def route(projected, winner_slot, loser_slot, spots_here):
    count, span = projected.shape
    prompts = winner_slot.shape[0]
    total = 2 * prompts * spots_here
    tile = min(total, 512)
    row = pl.BlockSpec((1, prompts), lambda i: (0, 0))
    return pl.pallas_call(
        functools.partial(route_kernel, spots_here),
        grid=(total // tile,),
        in_specs=[row, row, pl.BlockSpec((count, span), lambda i: (0, 0))],
        out_specs=pl.BlockSpec((tile, span), lambda i: (i, 0)),
        out_shape=jax.ShapeDtypeStruct((total, span), jnp.bfloat16),
        compiler_params=params(32 if count > 1024 else 8),
        cost_estimate=cost(),
    )(winner_slot.reshape(1, prompts), loser_slot.reshape(1, prompts), projected)


def finish_kernel(columns, head_size, scalars, own_ref, other_ref, keys_ref, values_ref):
    devices, rows, span = own_ref.shape
    slots = keys_ref.shape[0] // 2
    each = rows // slots
    inner_width = devices // 2 * span // 2

    def emit(start):
        for side, source in enumerate((own_ref, other_ref)):
            for slot in range(slots):
                at = slice(slot * each, (slot + 1) * each)
                for core in range(2):
                    parts = [source[2 * chip + core, at, :] for chip in range(devices // 2)]
                    whole = jnp.concatenate(parts, axis=1)
                    out = side * slots + slot
                    to = slice(core * each, (core + 1) * each)
                    keys = whole[:, start : start + columns].astype(jnp.float32)
                    for pair in range(columns // LANES):
                        lanes = slice(pair * LANES, (pair + 1) * LANES)
                        keys_ref[out, to, lanes] = head_pair_norm(keys[:, lanes], head_size)
                    first = inner_width + start
                    values_ref[out, to, :] = whole[:, first : first + columns]

    pl.when(scalars[1] == 0)(lambda: emit(0))
    pl.when(scalars[1] == 1)(lambda: emit(inner_width - columns))


def finish_prompts(scalars, own, other, columns, head_size, slots):
    devices, rows, _ = own.shape
    span = 2 * rows // slots
    shape = jax.ShapeDtypeStruct((2 * slots, span, columns), jnp.bfloat16)
    return pl.pallas_call(
        functools.partial(finish_kernel, columns, head_size),
        in_specs=[smem(), vmem(), vmem()],
        out_specs=[vmem()] * 2,
        out_shape=[shape] * 2,
        compiler_params=params(16),
        cost_estimate=cost(),
    )(scalars, own, other)


def attend_kernel(
    head_size,
    spots,
    side,
    scalars,
    winner,
    loser,
    lengths,
    a_ref,
    v_ref,
    b_ref,
    pk_ref,
    pv_ref,
    out_ref,
):
    step = pl.program_id(0)
    count_here = pl.num_programs(0)
    even_group = scalars[0] == 0
    _, columns, tokens = out_ref.shape
    owner = scalars[scalars.shape[0] - 2 + side]
    slot = owner + step

    def count(p, live):
        hit = (winner[p] == slot) | (loser[p] == slot)
        return live + jnp.where(hit, lengths[p], 0)

    live = lax.fori_loop(0, winner.shape[0], count, jnp.int32(0))
    span = pk_ref.shape[1]
    row = lax.broadcasted_iota(jnp.int32, (span, 1), 0)
    rest = lax.rem(row, span // 2)
    position = (2 * lax.div(rest, spots) + lax.div(row, span // 2)) * spots + lax.rem(rest, spots)
    allowed = position < live
    low = lax.broadcasted_iota(jnp.int32, (1, LANES), 1) < head_size
    over_lanes = (((1,), (1,)), ((), ()))
    over_rows = (((0,), (0,)), ((), ()))
    scale = 1.4426950408889634 / head_size**0.5
    here = pl.ds(pl.multiple_of((side * count_here + step) * tokens, tokens), tokens)
    block = side * count_here + step
    for pair in range(columns // LANES):
        lanes = slice(pair * LANES, (pair + 1) * LANES)
        a = a_ref[here, lanes]
        b = b_ref[here, lanes]
        queries = jnp.where(even_group, a, b)
        keys = jnp.where(even_group, b, a)
        values = v_ref[here, lanes]
        prompt_keys = pk_ref[block, :, lanes]
        prompt_values = pv_ref[block, :, lanes]
        for head in range(2):
            side = low if head == 0 else jnp.logical_not(low)
            q = jnp.where(side, queries, jnp.zeros_like(queries))
            s = lax.dot_general(keys, q, over_lanes, preferred_element_type=jnp.float32)
            t = lax.dot_general(prompt_keys, q, over_lanes, preferred_element_type=jnp.float32)
            s = jnp.exp2(s * scale)
            t = jnp.where(allowed, jnp.exp2(t * scale), 0.0)
            total = jnp.sum(s, axis=0, keepdims=True) + jnp.sum(t, axis=0, keepdims=True)
            out = lax.dot_general(
                values, s.astype(jnp.bfloat16), over_rows, preferred_element_type=jnp.float32
            ) + lax.dot_general(
                prompt_values, t.astype(jnp.bfloat16), over_rows, preferred_element_type=jnp.float32
            )
            rows = slice(head * head_size, (head + 1) * head_size)
            to = slice(pair * LANES + head * head_size, pair * LANES + (head + 1) * head_size)
            out_ref[0, to, :] = (out[rows] * (1.0 / total)).astype(jnp.bfloat16)


def attend(side, scalars, routes, rows, prompt_keys, prompt_values, head_size, spots, count):
    tokens = rows[0].shape[0] // (2 * count)
    columns = rows[0].shape[1]
    return pl.pallas_call(
        functools.partial(attend_kernel, head_size, spots, side),
        grid=(count,),
        in_specs=[smem()] * 4 + [vmem()] * 5,
        out_specs=pl.BlockSpec((1, columns, tokens), lambda l: (l, 0, 0)),
        out_shape=jax.ShapeDtypeStruct((count, columns, tokens), jnp.bfloat16),
        compiler_params=params(16),
        cost_estimate=cost(),
    )(scalars, *routes, *rows, prompt_keys, prompt_values)


def ring_order(groups, chips):
    if groups == 2:
        return list(range(0, chips, 2)) + list(range(1, chips, 2))[::-1]
    return list(range(chips))


def solution(mesh):
    groups, dp = mesh.shape["groups"], mesh.shape["dp"]
    chips = dp // 2
    ring = ring_order(groups, chips)
    place = [ring.index(chip) for chip in range(chips)]
    behind_by = np.array(
        [[(place[me] - place[chip]) % chips for chip in range(chips)] for me in range(chips)],
        np.int32,
    )
    forward_pairs = [
        (2 * ring[i] + c, 2 * ring[(i + 1) % chips] + c) for i in range(chips) for c in range(2)
    ]
    backward_pairs = [(b, a) for a, b in forward_pairs]
    core_pairs = [(d, d ^ 1) for d in range(dp)]
    group_pairs = [(g, g ^ 1) for g in range(groups)]
    half_groups = [[2 * chip + c for chip in range(chips)] for c in range(2)]

    def forward(x):
        return lax.ppermute(x, "dp", forward_pairs)

    def backward(x):
        return lax.ppermute(x, "dp", backward_pairs)

    def swap_cores(x):
        return lax.ppermute(x, "dp", core_pairs)

    def swap_groups(x):
        return lax.ppermute(x, "groups", group_pairs)

    def local(
        latents,
        context,
        lengths,
        winner_slot,
        loser_slot,
        image_mod,
        context_mod,
        w_q,
        w_k,
        w_v,
        w_ck,
        w_cv,
    ):
        slot_local, token_count, width = latents.shape
        prompt_count, spot_local, _ = context.shape
        depth, inner_width = w_q.shape
        head_size = inner_width // HEADS
        columns = (HEADS + 1) // 2 * head_size
        me = lax.axis_index("dp")
        my_group = lax.axis_index("groups") % 2
        my_chip, my_core = me // 2, me % 2
        places = lax.dynamic_index_in_dim(jnp.asarray(behind_by), my_chip, 0, keepdims=False)
        first = [my_group, my_core]
        last = [me * slot_local, (me ^ 1) * slot_local]
        scalars = jnp.concatenate([jnp.stack(first), places, jnp.stack(last)]).astype(jnp.int32)

        keep, give = split_weights(scalars, w_q, w_k, w_v, columns)
        got = swap_cores(give)
        own_mixed = mix_prompts(context, context_mod, chips, 2 * columns)
        once = [forward(own_mixed), backward(own_mixed)]
        twice = [forward(once[0]), backward(once[1])]
        mixed = {0: (own_mixed, 0)}
        for o, arrived in ((1, once), (2, twice)):
            mixed.setdefault(o % chips, (arrived[0], 0))
            mixed.setdefault(-o % chips, (arrived[1], 0))
        own_av = [keep[:, : 2 * columns], got[:, : 2 * columns]]
        ahead, behind = [jnp.concatenate(own_av + [x], axis=0) for x in twice]

        own, *give = modulate_image(scalars, latents, image_mod, chips, ahead)

        w_c = cut_prompt_weights(w_ck, w_cv, chips, own_mixed)
        w_c = lax.all_to_all(w_c, "dp", 0, 0, axis_index_groups=half_groups, tiled=True)

        totals = None
        enough = max(1, chips // 8)
        tokens, waiting_av, waiting_b = [w_c], [((0,), ahead)], []
        for o in range(1, chips // 2):
            ahead, behind = meet([forward(ahead), backward(behind)], tokens)
            mixed.setdefault((o + 2) % chips, (ahead, 2 * depth))
            mixed.setdefault((-o - 2) % chips, (behind, 2 * depth))
            if o == 1:
                (w_c,) = meet([w_c], [ahead])
                w_parts = [x.reshape(width // 2, -1) for x in (w_c, swap_cores(w_c))]
            if 4 * o == chips:
                slabs = [[own], [swap_cores(x) for x in meet(give, [ahead])]]
            tokens = []
            if 2 * o + 4 == chips:
                blocks, starts = zip(*[mixed[o] for o in range(chips)])
                projected = project_prompts(scalars, blocks, starts, *w_parts, slabs[1][0])
                projected = projected.reshape(-1, projected.shape[2])
                outgoing = route(projected, winner_slot, loser_slot, chips * spot_local)
                outgoing = outgoing.reshape(dp, -1, outgoing.shape[1])
            last = 2 * o + 2 == chips
            picked = pick(2 * depth, ahead, behind, last)
            waiting_av += [((o,), ahead), ((chips - o,), behind)]
            if len(waiting_b) > 3 * enough or (last and totals is None):
                first = totals is None
                items = [((), keep), ((), got)] if first else waiting_b
                totals, token = accumulate(2 * depth, totals, slabs, waiting_av, items)
                tokens.append(token)
                waiting_av, waiting_b = [], waiting_b if first else []
            waiting_b.append(((o, chips - o), swap_groups(picked[0])))
            if not last:
                tokens.append(waiting_b[-1][1])
            if 2 * o + 4 == chips:
                tokens.append(outgoing)
        a_far, v_far = meet([forward(picked[1]), backward(picked[2])], tokens)
        b_far = swap_groups(a_far)
        rows_a, rows_v, rows_b, features = last_products(
            2 * depth,
            head_size,
            totals,
            slabs,
            waiting_av,
            (chips // 2, a_far, v_far),
            waiting_b,
        )

        done_rows = (rows_a, rows_v, close(rows_b, features, b_far, head_size))

        (arrived,) = meet([lax.all_to_all(outgoing, "dp", 0, 0, tiled=True)], [ahead])
        prompt_keys, prompt_values = finish_prompts(
            scalars, arrived, swap_cores(arrived), columns, head_size, slot_local
        )

        routes = (winner_slot, loser_slot, lengths)

        def run(side):
            return attend(
                side,
                scalars,
                routes,
                done_rows,
                prompt_keys,
                prompt_values,
                head_size,
                spot_local,
                slot_local,
            )

        theirs = swap_cores(run(1))
        mine = run(0)
        return join(scalars, mine, theirs, inner_width).transpose(0, 2, 1)

    placed = (
        P(("groups", "dp"), None, None),
        P("groups", "dp", None),
        P("groups"),
        P("groups"),
        P("groups"),
        P(("groups", "dp"), None, None),
        P("groups", None, None),
        P("dp", None),
        P("dp", None),
        P("dp", None),
        P("dp", None),
        P("dp", None),
    )
    return jax.shard_map(
        local,
        mesh=mesh,
        in_specs=placed,
        out_specs=P(("groups", "dp"), None, None),
        check_vma=False,
    )
```

```python
import functools

import jax
import jax.numpy as jnp
import numpy as np
from jax import lax
from jax.experimental import pallas as pl
from jax.experimental.pallas import tpu as pltpu
from jax.sharding import PartitionSpec as P

HEADS = 19
LANES = 128


epsilon = 1e-06


def params(mib):
    return pltpu.CompilerParams(vmem_limit_bytes=mib * 2**20)


def cost(flops=1):
    return pl.CostEstimate(flops=flops, bytes_accessed=1, transcendentals=0)


def anywhere():
    return pl.BlockSpec(memory_space=pl.ANY)


def layer_norm(values, shift, scale):
    average = jnp.mean(values, axis=-1, keepdims=True)
    centered = values - average
    variance = jnp.mean(centered * centered, axis=-1, keepdims=True)
    return (centered * lax.rsqrt(variance + epsilon) * (1.0 + scale) + shift).astype(jnp.bfloat16)


def head_pair_norm(x, head_size):
    low = lax.broadcasted_iota(jnp.int32, (1, LANES), 1) < head_size
    squares = x * x
    first = jnp.sum(jnp.where(low, squares, 0.0), axis=-1, keepdims=True)
    second = jnp.sum(jnp.where(low, 0.0, squares), axis=-1, keepdims=True)
    first = lax.rsqrt(first * (1.0 / head_size) + epsilon)
    second = lax.rsqrt(second * (1.0 / head_size) + epsilon)
    return (x * jnp.where(low, first, second)).astype(jnp.bfloat16)


def vmem():
    return pl.BlockSpec(memory_space=pltpu.VMEM)


def smem():
    return pl.BlockSpec(memory_space=pltpu.SMEM)


def split_kernel(columns, scalars, q_ref, k_ref, v_ref, after_ref, keep_ref, give_ref):
    inner_width = q_ref.shape[1]

    def emit(parts, low_ref, high_ref):
        for i, part in enumerate(parts):
            at = slice(i * columns, (i + 1) * columns)
            low_ref[:, at] = part[:, :columns]
            high_ref[:, at] = part[:, inner_width - columns :]

    for group in range(2):
        parts = (q_ref, v_ref, k_ref) if group == 0 else (k_ref, v_ref, q_ref)
        for core in range(2):
            refs = (keep_ref, give_ref) if core == 0 else (give_ref, keep_ref)
            here = (scalars[0] == group) & (scalars[1] == core)
            pl.when(here)(functools.partial(emit, parts, *refs))


def split_weights(scalars, w_q, w_k, w_v, columns, after):
    depth, inner_width = w_q.shape
    shape = jax.ShapeDtypeStruct((depth, 3 * columns), jnp.bfloat16)
    whole = pl.BlockSpec((depth, inner_width), lambda i, s: (0, 0))
    out = pl.BlockSpec((depth, 3 * columns), lambda i, s: (0, 0))
    return pl.pallas_call(
        functools.partial(split_kernel, columns),
        grid_spec=pltpu.PrefetchScalarGridSpec(
            num_scalar_prefetch=1,
            grid=(1,),
            in_specs=[whole] * 3 + [anywhere()],
            out_specs=[out] * 2,
        ),
        out_shape=[shape] * 2,
        compiler_params=params(56),
        cost_estimate=cost(),
    )(scalars, w_q, w_k, w_v, after)


def mixed_kernel(chips, context_ref, mod_ref, out_ref):
    prompts, spots, width = context_ref.shape
    depth = width // (2 * chips)
    shift, scale = mod_ref[:, 0, :], mod_ref[:, 1, :]
    values = context_ref[...].astype(jnp.float32)
    for spot in range(spots):
        rows = layer_norm(values[:, spot, :], shift, scale)
        for core in range(2):
            parts = [
                rows[:, (2 * chip + core) * depth : (2 * chip + core + 1) * depth]
                for chip in range(chips)
            ]
            at = (core * spots + spot) * prompts
            parts.append(jnp.zeros((prompts, out_ref.shape[1] - width // 2), jnp.bfloat16))
            out_ref[at : at + prompts, :] = jnp.concatenate(parts, axis=1)


def mix_prompts(context, context_mod, chips, columns):
    prompts, spots, width = context.shape
    return pl.pallas_call(
        functools.partial(mixed_kernel, chips),
        grid=(1,),
        in_specs=[pl.BlockSpec(x.shape, lambda i: (0, 0, 0)) for x in (context, context_mod)],
        out_specs=pl.BlockSpec((2 * spots * prompts, columns), lambda i: (0, 0)),
        out_shape=jax.ShapeDtypeStruct((2 * spots * prompts, columns), jnp.bfloat16),
        compiler_params=params(56),
        cost_estimate=cost(),
    )(context, context_mod)


def image_kernel(chips, scalars, x_ref, mod_ref, after_ref, own_ref, give_ref):
    image = layer_norm(x_ref[0].astype(jnp.float32), mod_ref[0, 0:1, :], mod_ref[0, 1:2, :])
    depth = image.shape[1] // (2 * chips)

    def emit(first_ref, second_ref):
        for chip in range(chips):
            start = 2 * chip * depth
            straight = image[:, start : start + 2 * depth]
            turned = jnp.concatenate([straight[:, depth:], straight[:, :depth]], axis=1)
            first_ref[scalars[2 + chip], :, : 2 * depth] = straight
            second_ref[scalars[2 + chip], :, : 2 * depth] = turned

    pl.when(scalars[1] == 0)(lambda: emit(own_ref, give_ref))
    pl.when(scalars[1] == 1)(lambda: emit(give_ref, own_ref))


def modulate_image(scalars, latents, image_mod, chips, after):
    slots, tokens, width = latents.shape
    wide = -(-width // chips // LANES) * LANES
    block = (chips, tokens, wide)
    return pl.pallas_call(
        functools.partial(image_kernel, chips),
        grid_spec=pltpu.PrefetchScalarGridSpec(
            num_scalar_prefetch=1,
            grid=(slots,),
            in_specs=[
                pl.BlockSpec((1, tokens, width), lambda i, s: (i, 0, 0)),
                pl.BlockSpec((1, 2, width), lambda i, s: (i, 0, 0)),
                anywhere(),
            ],
            out_specs=[pl.BlockSpec(block, lambda i, s: (0, i, 0))] * 2,
        ),
        out_shape=[jax.ShapeDtypeStruct((chips, slots * tokens, wide), jnp.bfloat16)] * 2,
        compiler_params=params(32),
        cost_estimate=cost(),
    )(scalars, latents, image_mod, after)


def take_rows(slab, o, depth):
    return jnp.concatenate([part[o, :, :depth] for part in slab], axis=0)


def product_kernel(slots, depth, av_places, b_places, first, others, *refs):
    slabs, refs = refs[:slots], refs[slots:]
    panels = refs[: len(av_places)]
    at = len(av_places)
    pieces = refs[at : at + len(b_places) // 2 + 2 * first]
    out_av, out_b, token_ref = refs[-3:]
    totals = (None, None) if first else refs[-5 - others : -3 - others]
    rows = slabs[0].shape[1]
    columns = out_av.shape[1]
    token_ref[...] = jnp.zeros_like(token_ref)

    def product(slab, places, panel):
        features = jnp.concatenate([take_rows(slab, o, depth) for o in places], axis=1)
        return jnp.dot(features, panel, preferred_element_type=jnp.float32)

    for side, slab in enumerate((slabs[:1], slabs[1:])):
        to = slice(side * rows, (side + 1) * rows)
        if av_places:
            panel = jnp.concatenate([panel[:depth] for panel in panels], axis=0)
            sums = product(slab, av_places, panel)
            out_av[to] = sums if first else totals[0][to] + sums
        elif totals[0] is not out_av:
            out_av[to] = totals[0][to]
        sums = 0.0
        if b_places:
            panel = jnp.concatenate([piece[...] for piece in pieces[2 * first :]], axis=0)
            sums = product(slab, b_places, panel)
        if first:
            features = take_rows(slab, 0, depth)
            half = depth // 2
            for own, part in zip((slice(0, half), slice(half, depth)), pieces):
                sums = sums + jnp.dot(
                    features[:, own], part[:, columns:], preferred_element_type=jnp.float32
                )
            out_b[to] = sums
        else:
            out_b[to] = totals[1][to] + sums


def accumulate(depth, totals, slabs, av_items, b_items, others=()):
    first = totals is None
    slabs = slabs[0] + slabs[1]
    rows, columns = slabs[0].shape[1], 2 * b_items[0][1].shape[1]
    if first:
        columns = 2 * b_items[0][1].shape[1] // 3
    av_places = [o for places, _ in av_items for o in places]
    b_places = [o for places, _ in b_items for o in places]
    operands = slabs + [x for _, x in av_items] + [x for _, x in b_items]
    aliases = {}
    if not first:
        aliases = {len(operands): 0, len(operands) + 1: 1}
        operands += list(totals)
    in_specs = [vmem()] * len(operands) + [anywhere()] * len(others)
    out = pl.pallas_call(
        functools.partial(
            product_kernel, len(slabs), depth, av_places, b_places, first, len(others)
        ),
        in_specs=in_specs,
        out_specs=[vmem()] * 3,
        out_shape=[
            jax.ShapeDtypeStruct((2 * rows, columns), jnp.float32),
            jax.ShapeDtypeStruct((2 * rows, columns // 2), jnp.float32),
            jax.ShapeDtypeStruct((8, LANES), jnp.float32),
        ],
        input_output_aliases=aliases,
        compiler_params=params(20),
        cost_estimate=cost(4 * 10**10),
    )(*operands, *others)
    return out[:2], out[2]


def last_kernel(slots, depth, head_size, av_places, b_places, pieces, *refs):
    slabs, refs = refs[:slots], refs[slots:]
    count = len(av_places) - 1
    panels, (a_far, v_far) = refs[:count], refs[count : count + 2]
    swapped = refs[count + 2 : count + 2 + pieces]
    total_av, total_b, out_a, out_v, out_b, out_far = refs[-6:]
    rows, columns = slabs[0].shape[1], out_a.shape[1]

    def product(slab, places, panel):
        features = jnp.concatenate([take_rows(slab, o, depth) for o in places], axis=1)
        return jnp.dot(features, panel, preferred_element_type=jnp.float32)

    for side, slab in enumerate((slabs[:1], slabs[1:])):
        to = slice(side * rows, (side + 1) * rows)
        for half, far in enumerate((a_far, v_far)):
            lanes = slice(half * columns, (half + 1) * columns)
            parts = [panel[:depth, lanes] for panel in panels] + [far[...]]
            sums = total_av[to, lanes] + product(slab, av_places, jnp.concatenate(parts, axis=0))
            if half == 1:
                out_v[to] = sums.astype(jnp.bfloat16)
                continue
            for pair in range(columns // LANES):
                at = slice(pair * LANES, (pair + 1) * LANES)
                out_a[to, at] = head_pair_norm(sums[:, at], head_size)
        panel = jnp.concatenate([piece[...] for piece in swapped], axis=0)
        out_b[to] = total_b[to] + product(slab, b_places, panel)
        out_far[to, :depth] = take_rows(slab, av_places[-1], depth)


def last_products(depth, head_size, totals, slabs, av_items, far_items, b_items):
    slabs = slabs[0] + slabs[1]
    rows, columns = 2 * slabs[0].shape[1], totals[1].shape[1]
    av_places = [o for places, _ in av_items for o in places] + [far_items[0]]
    b_places = [o for places, _ in b_items for o in places]
    operands = slabs + [x for _, x in av_items] + list(far_items[1:])
    operands += [x for _, x in b_items] + list(totals)
    return pl.pallas_call(
        functools.partial(
            last_kernel, len(slabs), depth, head_size, av_places, b_places, len(b_items)
        ),
        in_specs=[vmem()] * len(operands),
        out_specs=[vmem()] * 4,
        out_shape=[
            jax.ShapeDtypeStruct((rows, columns), jnp.bfloat16),
            jax.ShapeDtypeStruct((rows, columns), jnp.bfloat16),
            jax.ShapeDtypeStruct((rows, columns), jnp.float32),
            jax.ShapeDtypeStruct((rows, slabs[0].shape[2]), jnp.bfloat16),
        ],
        compiler_params=params(20),
        cost_estimate=cost(4 * 10**10),
    )(*operands)


def close_kernel(head_size, total_ref, features_ref, far_ref, out_ref):
    features = features_ref[:, : far_ref.shape[0]]
    sums = jnp.dot(features, far_ref[...], preferred_element_type=jnp.float32) + total_ref[...]
    for pair in range(out_ref.shape[1] // LANES):
        lanes = slice(pair * LANES, (pair + 1) * LANES)
        out_ref[:, lanes] = head_pair_norm(sums[:, lanes], head_size)


def close(total, features, far, head_size):
    return pl.pallas_call(
        functools.partial(close_kernel, head_size),
        in_specs=[vmem()] * 3,
        out_specs=vmem(),
        out_shape=jax.ShapeDtypeStruct(total.shape, jnp.bfloat16),
        compiler_params=params(16),
        cost_estimate=cost(),
    )(total, features, far)


def meet(arrays, others):
    return pl.pallas_call(
        lambda *refs: None,
        in_specs=[anywhere()] * (len(arrays) + len(others)),
        out_specs=[anywhere()] * len(arrays),
        out_shape=[jax.ShapeDtypeStruct(x.shape, x.dtype) for x in arrays],
        input_output_aliases={i: i for i in range(len(arrays))},
        compiler_params=params(4),
        cost_estimate=cost(),
    )(*arrays, *others)


def pick_kernel(ahead_ref, behind_ref, out_ref):
    rows, columns = out_ref.shape[0] // 2, out_ref.shape[1]
    out_ref[:rows] = ahead_ref[:rows]
    out_ref[rows:] = behind_ref[:rows]


def pick(rows, ahead, behind):
    height, columns = ahead.shape[0], ahead.shape[1] // 2
    return pl.pallas_call(
        pick_kernel,
        grid=(1,),
        in_specs=[pl.BlockSpec((height, columns), lambda i: (0, 0))] * 2,
        out_specs=pl.BlockSpec((2 * rows, columns), lambda i: (0, 0)),
        out_shape=jax.ShapeDtypeStruct((2 * rows, columns), jnp.bfloat16),
        compiler_params=params(12),
        cost_estimate=cost(),
    )(ahead, behind)


def pick_last_kernel(ahead_ref, behind_ref, swapped_ref, a_ref, v_ref, ahead_b_ref, behind_b_ref):
    rows = a_ref.shape[0]
    a_ref[...] = ahead_ref[:rows]
    v_ref[...] = behind_ref[:rows]
    ahead_b_ref[...] = swapped_ref[:rows]
    behind_b_ref[...] = swapped_ref[rows:]


def pick_last(rows, ahead, behind, swapped):
    height, columns = ahead.shape[0], ahead.shape[1] // 2
    shape = (rows, columns)
    return pl.pallas_call(
        pick_last_kernel,
        grid=(1,),
        in_specs=[
            pl.BlockSpec((height, columns), lambda i: (0, 0)),
            pl.BlockSpec((height, columns), lambda i: (0, 1)),
            pl.BlockSpec((2 * rows, columns), lambda i: (0, 0)),
        ],
        out_specs=[pl.BlockSpec(shape, lambda i: (0, 0))] * 4,
        out_shape=[jax.ShapeDtypeStruct(shape, jnp.bfloat16)] * 4,
        compiler_params=params(12),
        cost_estimate=cost(),
    )(ahead, behind, swapped)


def join_kernel(scalars, mine_ref, theirs_ref, out_ref):
    columns = mine_ref.shape[1]
    shared = 2 * columns - out_ref.shape[1]

    def emit(low, high):
        out_ref[:, :columns] = low[...]
        out_ref[:, columns:] = high[:, shared:]

    pl.when(scalars[1] == 0)(lambda: emit(mine_ref, theirs_ref))
    pl.when(scalars[1] == 1)(lambda: emit(theirs_ref, mine_ref))


def join(scalars, mine, theirs, inner_width):
    slots, _, tokens = mine.shape
    return pl.pallas_call(
        join_kernel,
        in_specs=[smem(), vmem(), vmem()],
        out_specs=vmem(),
        out_shape=jax.ShapeDtypeStruct((slots, inner_width, tokens), jnp.bfloat16),
        compiler_params=params(8),
        cost_estimate=cost(),
    )(scalars, mine, theirs)


def cut_kernel(k_ref, v_ref, after_ref, out_ref):
    chips, _, span = out_ref.shape
    half = chips // 2
    for chip in range(chips):
        source = k_ref if chip < half else v_ref
        start = (chip % half) * span
        out_ref[chip] = source[:, start : start + span]


def cut_prompt_weights(w_ck, w_cv, chips, after):
    depth, inner_width = w_ck.shape
    span = 2 * inner_width // chips
    return pl.pallas_call(
        cut_kernel,
        grid=(1,),
        in_specs=[pl.BlockSpec(w_ck.shape, lambda i: (0, 0))] * 2 + [anywhere()],
        out_specs=pl.BlockSpec((chips, depth, span), lambda i: (0, 0, 0)),
        out_shape=jax.ShapeDtypeStruct((chips, depth, span), jnp.bfloat16),
        compiler_params=params(56),
        cost_estimate=cost(),
    )(w_ck, w_cv, after)


def prompt_kernel(starts, scalars, after_ref, *refs):
    chips = len(starts)
    blocks, (own_ref, other_ref, out_ref, held_ref) = refs[:chips], refs[chips:]
    depth = own_ref.shape[0]
    half = out_ref.shape[1]
    parts = [
        jnp.concatenate(
            [
                block[start + core * half : start + (core + 1) * half, :depth]
                for start, block in zip(starts, blocks)
            ],
            axis=0,
        )
        for core in range(2)
    ]

    def emit(first, second):
        product = jnp.dot(parts[0], first[...], preferred_element_type=jnp.float32) + jnp.dot(
            parts[1], second[...], preferred_element_type=jnp.float32
        )
        held_ref[...] = product.astype(jnp.bfloat16).reshape(held_ref.shape)

    pl.when(scalars[1] == 0)(lambda: emit(own_ref, other_ref))
    pl.when(scalars[1] == 1)(lambda: emit(other_ref, own_ref))
    for chip in range(chips):
        out_ref[chip] = held_ref[scalars[2 + chip]]


def project_prompts(scalars, blocks, starts, w_own, w_other, after):
    chips, span = len(blocks), w_own.shape[1]
    half = (blocks[0].shape[0] - starts[0]) // 2
    if blocks[0].shape[0] * chips > 4096:
        depth = w_own.shape[0]
        straight = scalars[1] == 0
        weights = [jnp.where(straight, w_own, w_other), jnp.where(straight, w_other, w_own)]
        product = 0.0
        for core, weight in enumerate(weights):
            rows = [
                x[start + core * half : start + (core + 1) * half, :depth]
                for start, x in zip(starts, blocks)
            ]
            rows = jnp.concatenate(rows, axis=0)
            product = product + jnp.dot(rows, weight, preferred_element_type=jnp.float32)
        product = product.astype(jnp.bfloat16).reshape(chips, half, span)
        return jnp.take(product, scalars[2 : 2 + chips], axis=0)
    return pl.pallas_call(
        functools.partial(prompt_kernel, starts),
        in_specs=[smem(), anywhere()] + [vmem()] * (chips + 2),
        out_specs=vmem(),
        out_shape=jax.ShapeDtypeStruct((chips, half, span), jnp.bfloat16),
        scratch_shapes=[pltpu.VMEM((chips, half, span), jnp.bfloat16)],
        compiler_params=params(16),
        cost_estimate=cost(),
    )(scalars, after, *blocks, w_own, w_other)


def route_kernel(spots_here, winner_ref, loser_ref, rows_ref, out_ref):
    tile, count = out_ref.shape[0], rows_ref.shape[0]
    prompts = winner_ref.shape[1]
    row = lax.broadcasted_iota(jnp.int32, (tile, 1), 0) + pl.program_id(0) * tile
    slot = lax.div(row, spots_here)
    reads = (winner_ref[...] == slot) | (loser_ref[...] == slot)
    column = lax.broadcasted_iota(jnp.int32, (prompts, count), 1)
    prompt = lax.broadcasted_iota(jnp.int32, (prompts, count), 0)
    spread = jnp.where(lax.rem(column, prompts) == prompt, 1.0, 0.0).astype(jnp.bfloat16)
    reads = jnp.where(reads, 1.0, 0.0).astype(jnp.bfloat16)
    reads = jnp.dot(reads, spread, preferred_element_type=jnp.float32)
    same_spot = lax.rem(row, spots_here) == lax.div(column[0:1], prompts)
    chosen = jnp.where(same_spot, reads, 0.0).astype(jnp.bfloat16)
    out_ref[...] = jnp.dot(
        chosen, rows_ref[...], preferred_element_type=jnp.float32
    ).astype(jnp.bfloat16)


def route(projected, winner_slot, loser_slot, spots_here):
    count, span = projected.shape
    prompts = winner_slot.shape[0]
    total = 2 * prompts * spots_here
    tile = min(total, 512)
    row = pl.BlockSpec((1, prompts), lambda i: (0, 0))
    return pl.pallas_call(
        functools.partial(route_kernel, spots_here),
        grid=(total // tile,),
        in_specs=[row, row, pl.BlockSpec((count, span), lambda i: (0, 0))],
        out_specs=pl.BlockSpec((tile, span), lambda i: (i, 0)),
        out_shape=jax.ShapeDtypeStruct((total, span), jnp.bfloat16),
        compiler_params=params(32 if count > 1024 else 8),
        cost_estimate=cost(),
    )(winner_slot.reshape(1, prompts), loser_slot.reshape(1, prompts), projected)


def finish_kernel(columns, head_size, scalars, own_ref, other_ref, keys_ref, values_ref):
    devices, rows, span = own_ref.shape
    slots = keys_ref.shape[0] // 2
    each = rows // slots
    inner_width = devices // 2 * span // 2

    def emit(start):
        for side, source in enumerate((own_ref, other_ref)):
            for slot in range(slots):
                at = slice(slot * each, (slot + 1) * each)
                for core in range(2):
                    parts = [source[2 * chip + core, at, :] for chip in range(devices // 2)]
                    whole = jnp.concatenate(parts, axis=1)
                    out = side * slots + slot
                    to = slice(core * each, (core + 1) * each)
                    keys = whole[:, start : start + columns].astype(jnp.float32)
                    for pair in range(columns // LANES):
                        lanes = slice(pair * LANES, (pair + 1) * LANES)
                        keys_ref[out, to, lanes] = head_pair_norm(keys[:, lanes], head_size)
                    first = inner_width + start
                    values_ref[out, to, :] = whole[:, first : first + columns]

    pl.when(scalars[1] == 0)(lambda: emit(0))
    pl.when(scalars[1] == 1)(lambda: emit(inner_width - columns))


def finish_prompts(scalars, own, other, columns, head_size, slots):
    devices, rows, _ = own.shape
    span = 2 * rows // slots
    shape = jax.ShapeDtypeStruct((2 * slots, span, columns), jnp.bfloat16)
    return pl.pallas_call(
        functools.partial(finish_kernel, columns, head_size),
        in_specs=[smem(), vmem(), vmem()],
        out_specs=[vmem()] * 2,
        out_shape=[shape] * 2,
        compiler_params=params(16),
        cost_estimate=cost(),
    )(scalars, own, other)


def attend_kernel(
    head_size,
    spots,
    side,
    scalars,
    winner,
    loser,
    lengths,
    a_ref,
    v_ref,
    b_ref,
    pk_ref,
    pv_ref,
    out_ref,
):
    step = pl.program_id(0)
    count_here = pl.num_programs(0)
    even_group = scalars[0] == 0
    _, columns, tokens = out_ref.shape
    owner = scalars[scalars.shape[0] - 2 + side]
    slot = owner + step

    def count(p, live):
        hit = (winner[p] == slot) | (loser[p] == slot)
        return live + jnp.where(hit, lengths[p], 0)

    live = lax.fori_loop(0, winner.shape[0], count, jnp.int32(0))
    span = pk_ref.shape[1]
    row = lax.broadcasted_iota(jnp.int32, (span, 1), 0)
    rest = lax.rem(row, span // 2)
    position = (2 * lax.div(rest, spots) + lax.div(row, span // 2)) * spots + lax.rem(rest, spots)
    allowed = position < live
    low = lax.broadcasted_iota(jnp.int32, (1, LANES), 1) < head_size
    over_lanes = (((1,), (1,)), ((), ()))
    over_rows = (((0,), (0,)), ((), ()))
    scale = 1.4426950408889634 / head_size**0.5
    here = pl.ds(pl.multiple_of((side * count_here + step) * tokens, tokens), tokens)
    block = side * count_here + step
    for pair in range(columns // LANES):
        lanes = slice(pair * LANES, (pair + 1) * LANES)
        a = a_ref[here, lanes]
        b = b_ref[here, lanes]
        queries = jnp.where(even_group, a, b)
        keys = jnp.where(even_group, b, a)
        values = v_ref[here, lanes]
        prompt_keys = pk_ref[block, :, lanes]
        prompt_values = pv_ref[block, :, lanes]
        for head in range(2):
            side = low if head == 0 else jnp.logical_not(low)
            q = jnp.where(side, queries, jnp.zeros_like(queries))
            s = lax.dot_general(keys, q, over_lanes, preferred_element_type=jnp.float32)
            t = lax.dot_general(prompt_keys, q, over_lanes, preferred_element_type=jnp.float32)
            s = jnp.exp2(s * scale)
            t = jnp.where(allowed, jnp.exp2(t * scale), 0.0)
            total = jnp.sum(s, axis=0, keepdims=True) + jnp.sum(t, axis=0, keepdims=True)
            out = lax.dot_general(
                values, s.astype(jnp.bfloat16), over_rows, preferred_element_type=jnp.float32
            ) + lax.dot_general(
                prompt_values, t.astype(jnp.bfloat16), over_rows, preferred_element_type=jnp.float32
            )
            rows = slice(head * head_size, (head + 1) * head_size)
            to = slice(pair * LANES + head * head_size, pair * LANES + (head + 1) * head_size)
            out_ref[0, to, :] = (out[rows] * (1.0 / total)).astype(jnp.bfloat16)


def attend(side, scalars, routes, rows, prompt_keys, prompt_values, head_size, spots, count):
    tokens = rows[0].shape[0] // (2 * count)
    columns = rows[0].shape[1]
    return pl.pallas_call(
        functools.partial(attend_kernel, head_size, spots, side),
        grid=(count,),
        in_specs=[smem()] * 4 + [vmem()] * 5,
        out_specs=pl.BlockSpec((1, columns, tokens), lambda l: (l, 0, 0)),
        out_shape=jax.ShapeDtypeStruct((count, columns, tokens), jnp.bfloat16),
        compiler_params=params(16),
        cost_estimate=cost(),
    )(scalars, *routes, *rows, prompt_keys, prompt_values)


def ring_order(groups, chips):
    if groups == 2:
        return list(range(0, chips, 2)) + list(range(1, chips, 2))[::-1]
    return list(range(chips))


def solution(mesh):
    groups, dp = mesh.shape["groups"], mesh.shape["dp"]
    chips = dp // 2
    ring = ring_order(groups, chips)
    place = [ring.index(chip) for chip in range(chips)]
    behind_by = np.array(
        [[(place[me] - place[chip]) % chips for chip in range(chips)] for me in range(chips)],
        np.int32,
    )
    forward_pairs = [
        (2 * ring[i] + c, 2 * ring[(i + 1) % chips] + c) for i in range(chips) for c in range(2)
    ]
    backward_pairs = [(b, a) for a, b in forward_pairs]
    core_pairs = [(d, d ^ 1) for d in range(dp)]
    group_pairs = [(g, g ^ 1) for g in range(groups)]
    half_groups = [[2 * chip + c for chip in range(chips)] for c in range(2)]

    def forward(x):
        return lax.ppermute(x, "dp", forward_pairs)

    def backward(x):
        return lax.ppermute(x, "dp", backward_pairs)

    def swap_cores(x):
        return lax.ppermute(x, "dp", core_pairs)

    def swap_groups(x):
        return lax.ppermute(x, "groups", group_pairs)

    def local(
        latents,
        context,
        lengths,
        winner_slot,
        loser_slot,
        image_mod,
        context_mod,
        w_q,
        w_k,
        w_v,
        w_ck,
        w_cv,
    ):
        slot_local, token_count, width = latents.shape
        prompt_count, spot_local, _ = context.shape
        depth, inner_width = w_q.shape
        head_size = inner_width // HEADS
        columns = (HEADS + 1) // 2 * head_size
        me = lax.axis_index("dp")
        my_group = lax.axis_index("groups") % 2
        my_chip, my_core = me // 2, me % 2
        places = lax.dynamic_index_in_dim(jnp.asarray(behind_by), my_chip, 0, keepdims=False)
        first = [my_group, my_core]
        last = [me * slot_local, (me ^ 1) * slot_local]
        scalars = jnp.concatenate([jnp.stack(first), places, jnp.stack(last)]).astype(jnp.int32)

        own_mixed = mix_prompts(context, context_mod, chips, 2 * columns)
        once = [forward(own_mixed), backward(own_mixed)]
        twice = [forward(once[0]), backward(once[1])]
        mixed = {0: (own_mixed, 0)}
        for o, arrived in ((1, once), (2, twice)):
            mixed.setdefault(o % chips, (arrived[0], 0))
            mixed.setdefault(-o % chips, (arrived[1], 0))
        keep, give = split_weights(scalars, w_q, w_k, w_v, columns, own_mixed)
        got = swap_cores(give)
        own_av = [keep[:, : 2 * columns], got[:, : 2 * columns]]
        ahead, behind = [jnp.concatenate(own_av + [x], axis=0) for x in twice]

        own, *give = modulate_image(scalars, latents, image_mod, chips, ahead)

        w_c = cut_prompt_weights(w_ck, w_cv, chips, own_mixed)
        w_c = lax.all_to_all(w_c, "dp", 0, 0, axis_index_groups=half_groups, tiled=True)

        totals = None
        enough = max(1, chips // 8)
        tokens, waiting_av, waiting_b = [w_c], [((0,), ahead)], []
        for o in range(1, chips // 2):
            ahead, behind = meet([forward(ahead), backward(behind)], tokens)
            mixed.setdefault((o + 2) % chips, (ahead, 2 * depth))
            mixed.setdefault((-o - 2) % chips, (behind, 2 * depth))
            if o == 1:
                (w_c,) = meet([w_c], [ahead])
                w_parts = [x.reshape(width // 2, -1) for x in (w_c, swap_cores(w_c))]
            if 4 * o == chips:
                slabs = [[own], [swap_cores(x) for x in meet(give, [ahead])]]
            tokens = []
            if 2 * o + 4 == chips:
                blocks, starts = zip(*[mixed[o] for o in range(chips)])
                projected = project_prompts(scalars, blocks, starts, *w_parts, slabs[1][0])
                projected = projected.reshape(-1, projected.shape[2])
                outgoing = route(projected, winner_slot, loser_slot, chips * spot_local)
                outgoing = outgoing.reshape(dp, -1, outgoing.shape[1])
                (arrived,) = [lax.all_to_all(outgoing, "dp", 0, 0, tiled=True)]
            last = 2 * o + 2 == chips
            waiting_av += [((o,), ahead), ((chips - o,), behind)]
            if last:
                (arrived,) = meet([arrived], [ahead])
                picked = pick_last(2 * depth, ahead, behind, waiting_b[-1][1])
            else:
                swapped = swap_groups(pick(2 * depth, ahead, behind))
            if len(waiting_b) > 3 * enough or (last and totals is None):
                first = totals is None
                items = [((), keep), ((), got)] if first else waiting_b
                totals, token = accumulate(
                    2 * depth, totals, slabs, waiting_av, items, [arrived] if last else []
                )
                tokens.append(token)
                waiting_av, waiting_b = [], waiting_b if first else []
            if not last:
                waiting_b.append(((o, chips - o), swapped))
                tokens.append(swapped)
            if 2 * o + 4 == chips:
                tokens.append(outgoing)
        a_far, v_far = meet([forward(picked[0]), backward(picked[1])], tokens)
        o = chips // 2 - 1
        waiting_b += [((o,), forward(picked[2])), ((chips - o,), backward(picked[3]))]
        b_far = swap_groups(a_far)
        rows_a, rows_v, rows_b, features = last_products(
            2 * depth,
            head_size,
            totals,
            slabs,
            waiting_av,
            (chips // 2, a_far, v_far),
            waiting_b,
        )

        done_rows = (rows_a, rows_v, close(rows_b, features, b_far, head_size))

        prompt_keys, prompt_values = finish_prompts(
            scalars, arrived, swap_cores(arrived), columns, head_size, slot_local
        )

        routes = (winner_slot, loser_slot, lengths)

        def run(side):
            return attend(
                side,
                scalars,
                routes,
                done_rows,
                prompt_keys,
                prompt_values,
                head_size,
                spot_local,
                slot_local,
            )

        theirs = swap_cores(run(1))
        mine = run(0)
        return join(scalars, mine, theirs, inner_width).transpose(0, 2, 1)

    placed = (
        P(("groups", "dp"), None, None),
        P("groups", "dp", None),
        P("groups"),
        P("groups"),
        P("groups"),
        P(("groups", "dp"), None, None),
        P("groups", None, None),
        P("dp", None),
        P("dp", None),
        P("dp", None),
        P("dp", None),
        P("dp", None),
    )
    return jax.shard_map(
        local,
        mesh=mesh,
        in_specs=placed,
        out_specs=P(("groups", "dp"), None, None),
        check_vma=False,
    )
```

```python
import functools

import jax
import jax.numpy as jnp
import numpy as np
from jax import lax
from jax.experimental import pallas as pl
from jax.experimental.pallas import tpu as pltpu
from jax.sharding import PartitionSpec as P

HEADS = 19
LANES = 128


epsilon = 1e-06


def params(mib):
    return pltpu.CompilerParams(vmem_limit_bytes=mib * 2**20)


def cost(flops=1):
    return pl.CostEstimate(flops=flops, bytes_accessed=1, transcendentals=0)


def anywhere():
    return pl.BlockSpec(memory_space=pl.ANY)


def layer_norm(values, shift, scale):
    average = jnp.mean(values, axis=-1, keepdims=True)
    centered = values - average
    variance = jnp.mean(centered * centered, axis=-1, keepdims=True)
    return (centered * lax.rsqrt(variance + epsilon) * (1.0 + scale) + shift).astype(jnp.bfloat16)


def head_pair_norm(x, head_size):
    low = lax.broadcasted_iota(jnp.int32, (1, LANES), 1) < head_size
    squares = x * x
    first = jnp.sum(jnp.where(low, squares, 0.0), axis=-1, keepdims=True)
    second = jnp.sum(jnp.where(low, 0.0, squares), axis=-1, keepdims=True)
    first = lax.rsqrt(first * (1.0 / head_size) + epsilon)
    second = lax.rsqrt(second * (1.0 / head_size) + epsilon)
    return (x * jnp.where(low, first, second)).astype(jnp.bfloat16)


def vmem():
    return pl.BlockSpec(memory_space=pltpu.VMEM)


def smem():
    return pl.BlockSpec(memory_space=pltpu.SMEM)


def split_kernel(columns, scalars, q_ref, k_ref, v_ref, after_ref, keep_ref, give_ref):
    inner_width = q_ref.shape[1]

    def emit(parts, low_ref, high_ref):
        for i, part in enumerate(parts):
            at = slice(i * columns, (i + 1) * columns)
            low_ref[:, at] = part[:, :columns]
            high_ref[:, at] = part[:, inner_width - columns :]

    for group in range(2):
        parts = (q_ref, v_ref, k_ref) if group == 0 else (k_ref, v_ref, q_ref)
        for core in range(2):
            refs = (keep_ref, give_ref) if core == 0 else (give_ref, keep_ref)
            here = (scalars[0] == group) & (scalars[1] == core)
            pl.when(here)(functools.partial(emit, parts, *refs))


def split_weights(scalars, w_q, w_k, w_v, columns, after):
    depth, inner_width = w_q.shape
    shape = jax.ShapeDtypeStruct((depth, 3 * columns), jnp.bfloat16)
    whole = pl.BlockSpec((depth, inner_width), lambda i, s: (0, 0))
    out = pl.BlockSpec((depth, 3 * columns), lambda i, s: (0, 0))
    return pl.pallas_call(
        functools.partial(split_kernel, columns),
        grid_spec=pltpu.PrefetchScalarGridSpec(
            num_scalar_prefetch=1,
            grid=(1,),
            in_specs=[whole] * 3 + [anywhere()],
            out_specs=[out] * 2,
        ),
        out_shape=[shape] * 2,
        compiler_params=params(56),
        cost_estimate=cost(),
    )(scalars, w_q, w_k, w_v, after)


def mixed_kernel(chips, context_ref, mod_ref, out_ref):
    prompts, spots, width = context_ref.shape
    depth = width // (2 * chips)
    shift, scale = mod_ref[:, 0, :], mod_ref[:, 1, :]
    values = context_ref[...].astype(jnp.float32)
    for spot in range(spots):
        rows = layer_norm(values[:, spot, :], shift, scale)
        for core in range(2):
            parts = [
                rows[:, (2 * chip + core) * depth : (2 * chip + core + 1) * depth]
                for chip in range(chips)
            ]
            at = (core * spots + spot) * prompts
            parts.append(jnp.zeros((prompts, out_ref.shape[1] - width // 2), jnp.bfloat16))
            out_ref[at : at + prompts, :] = jnp.concatenate(parts, axis=1)


def mix_prompts(context, context_mod, chips, columns):
    prompts, spots, width = context.shape
    return pl.pallas_call(
        functools.partial(mixed_kernel, chips),
        grid=(1,),
        in_specs=[pl.BlockSpec(x.shape, lambda i: (0, 0, 0)) for x in (context, context_mod)],
        out_specs=pl.BlockSpec((2 * spots * prompts, columns), lambda i: (0, 0)),
        out_shape=jax.ShapeDtypeStruct((2 * spots * prompts, columns), jnp.bfloat16),
        compiler_params=params(56),
        cost_estimate=cost(),
    )(context, context_mod)


def image_kernel(chips, scalars, x_ref, mod_ref, after_ref, own_ref, give_ref):
    image = layer_norm(x_ref[0].astype(jnp.float32), mod_ref[0, 0:1, :], mod_ref[0, 1:2, :])
    depth = image.shape[1] // (2 * chips)

    def emit(first_ref, second_ref):
        for chip in range(chips):
            start = 2 * chip * depth
            straight = image[:, start : start + 2 * depth]
            turned = jnp.concatenate([straight[:, depth:], straight[:, :depth]], axis=1)
            first_ref[scalars[2 + chip], :, : 2 * depth] = straight
            second_ref[scalars[2 + chip], :, : 2 * depth] = turned

    pl.when(scalars[1] == 0)(lambda: emit(own_ref, give_ref))
    pl.when(scalars[1] == 1)(lambda: emit(give_ref, own_ref))


def modulate_image(scalars, latents, image_mod, chips, after):
    slots, tokens, width = latents.shape
    wide = -(-width // chips // LANES) * LANES
    block = (chips, tokens, wide)
    return pl.pallas_call(
        functools.partial(image_kernel, chips),
        grid_spec=pltpu.PrefetchScalarGridSpec(
            num_scalar_prefetch=1,
            grid=(slots,),
            in_specs=[
                pl.BlockSpec((1, tokens, width), lambda i, s: (i, 0, 0)),
                pl.BlockSpec((1, 2, width), lambda i, s: (i, 0, 0)),
                anywhere(),
            ],
            out_specs=[pl.BlockSpec(block, lambda i, s: (0, i, 0))] * 2,
        ),
        out_shape=[jax.ShapeDtypeStruct((chips, slots * tokens, wide), jnp.bfloat16)] * 2,
        compiler_params=params(32),
        cost_estimate=cost(),
    )(scalars, latents, image_mod, after)


def take_rows(slab, o, depth):
    return jnp.concatenate([part[o, :, :depth] for part in slab], axis=0)


def product_kernel(slots, depth, av_places, b_places, first, others, *refs):
    slabs, refs = refs[:slots], refs[slots:]
    panels = refs[: len(av_places)]
    at = len(av_places)
    pieces = refs[at : at + len(b_places) // 2 + 2 * first]
    out_av, out_b, token_ref = refs[-3:]
    totals = (None, None) if first else refs[-5 - others : -3 - others]
    rows = slabs[0].shape[1]
    columns = out_av.shape[1]
    token_ref[...] = jnp.zeros_like(token_ref)

    def product(slab, places, panel):
        features = jnp.concatenate([take_rows(slab, o, depth) for o in places], axis=1)
        return jnp.dot(features, panel, preferred_element_type=jnp.float32)

    for side, slab in enumerate((slabs[:1], slabs[1:])):
        to = slice(side * rows, (side + 1) * rows)
        if av_places:
            panel = jnp.concatenate([panel[:depth] for panel in panels], axis=0)
            sums = product(slab, av_places, panel)
            out_av[to] = sums if first else totals[0][to] + sums
        elif totals[0] is not out_av:
            out_av[to] = totals[0][to]
        sums = 0.0
        if b_places:
            panel = jnp.concatenate([piece[...] for piece in pieces[2 * first :]], axis=0)
            sums = product(slab, b_places, panel)
        if first:
            features = take_rows(slab, 0, depth)
            half = depth // 2
            for own, part in zip((slice(0, half), slice(half, depth)), pieces):
                sums = sums + jnp.dot(
                    features[:, own], part[:, columns:], preferred_element_type=jnp.float32
                )
            out_b[to] = sums
        else:
            out_b[to] = totals[1][to] + sums


def accumulate(depth, totals, slabs, av_items, b_items, others=()):
    first = totals is None
    slabs = slabs[0] + slabs[1]
    rows, columns = slabs[0].shape[1], 2 * b_items[0][1].shape[1]
    if first:
        columns = 2 * b_items[0][1].shape[1] // 3
    av_places = [o for places, _ in av_items for o in places]
    b_places = [o for places, _ in b_items for o in places]
    operands = slabs + [x for _, x in av_items] + [x for _, x in b_items]
    aliases = {}
    if not first:
        aliases = {len(operands): 0, len(operands) + 1: 1}
        operands += list(totals)
    in_specs = [vmem()] * len(operands) + [anywhere()] * len(others)
    out = pl.pallas_call(
        functools.partial(
            product_kernel, len(slabs), depth, av_places, b_places, first, len(others)
        ),
        in_specs=in_specs,
        out_specs=[vmem()] * 3,
        out_shape=[
            jax.ShapeDtypeStruct((2 * rows, columns), jnp.float32),
            jax.ShapeDtypeStruct((2 * rows, columns // 2), jnp.float32),
            jax.ShapeDtypeStruct((8, LANES), jnp.float32),
        ],
        input_output_aliases=aliases,
        compiler_params=params(20),
        cost_estimate=cost(4 * 10**10),
    )(*operands, *others)
    return out[:2], out[2]


def last_kernel(slots, depth, head_size, av_places, b_places, pieces, *refs):
    slabs, refs = refs[:slots], refs[slots:]
    count = len(av_places) - 1
    panels, (a_far, v_far) = refs[:count], refs[count : count + 2]
    swapped = refs[count + 2 : count + 2 + pieces]
    total_av, total_b, out_a, out_v, out_b, out_far = refs[-6:]
    rows, columns = slabs[0].shape[1], out_a.shape[1]

    def product(slab, places, panel):
        features = jnp.concatenate([take_rows(slab, o, depth) for o in places], axis=1)
        return jnp.dot(features, panel, preferred_element_type=jnp.float32)

    for side, slab in enumerate((slabs[:1], slabs[1:])):
        to = slice(side * rows, (side + 1) * rows)
        for half, far in enumerate((a_far, v_far)):
            lanes = slice(half * columns, (half + 1) * columns)
            parts = [panel[:depth, lanes] for panel in panels] + [far[...]]
            sums = total_av[to, lanes] + product(slab, av_places, jnp.concatenate(parts, axis=0))
            if half == 1:
                out_v[to] = sums.astype(jnp.bfloat16)
                continue
            for pair in range(columns // LANES):
                at = slice(pair * LANES, (pair + 1) * LANES)
                out_a[to, at] = head_pair_norm(sums[:, at], head_size)
        panel = jnp.concatenate([piece[...] for piece in swapped], axis=0)
        out_b[to] = total_b[to] + product(slab, b_places, panel)
        out_far[to, :depth] = take_rows(slab, av_places[-1], depth)


def last_products(depth, head_size, totals, slabs, av_items, far_items, b_items):
    slabs = slabs[0] + slabs[1]
    rows, columns = 2 * slabs[0].shape[1], totals[1].shape[1]
    av_places = [o for places, _ in av_items for o in places] + [far_items[0]]
    b_places = [o for places, _ in b_items for o in places]
    operands = slabs + [x for _, x in av_items] + list(far_items[1:])
    operands += [x for _, x in b_items] + list(totals)
    return pl.pallas_call(
        functools.partial(
            last_kernel, len(slabs), depth, head_size, av_places, b_places, len(b_items)
        ),
        in_specs=[vmem()] * len(operands),
        out_specs=[vmem()] * 4,
        out_shape=[
            jax.ShapeDtypeStruct((rows, columns), jnp.bfloat16),
            jax.ShapeDtypeStruct((rows, columns), jnp.bfloat16),
            jax.ShapeDtypeStruct((rows, columns), jnp.float32),
            jax.ShapeDtypeStruct((rows, slabs[0].shape[2]), jnp.bfloat16),
        ],
        compiler_params=params(20),
        cost_estimate=cost(4 * 10**10),
    )(*operands)


def close_kernel(head_size, total_ref, features_ref, far_ref, out_ref):
    features = features_ref[:, : far_ref.shape[0]]
    sums = jnp.dot(features, far_ref[...], preferred_element_type=jnp.float32) + total_ref[...]
    for pair in range(out_ref.shape[1] // LANES):
        lanes = slice(pair * LANES, (pair + 1) * LANES)
        out_ref[:, lanes] = head_pair_norm(sums[:, lanes], head_size)


def close(total, features, far, head_size):
    return pl.pallas_call(
        functools.partial(close_kernel, head_size),
        in_specs=[vmem()] * 3,
        out_specs=vmem(),
        out_shape=jax.ShapeDtypeStruct(total.shape, jnp.bfloat16),
        compiler_params=params(16),
        cost_estimate=cost(),
    )(total, features, far)


def meet(arrays, others):
    return pl.pallas_call(
        lambda *refs: None,
        in_specs=[anywhere()] * (len(arrays) + len(others)),
        out_specs=[anywhere()] * len(arrays),
        out_shape=[jax.ShapeDtypeStruct(x.shape, x.dtype) for x in arrays],
        input_output_aliases={i: i for i in range(len(arrays))},
        compiler_params=params(4),
        cost_estimate=cost(),
    )(*arrays, *others)


def pick_kernel(ahead_ref, behind_ref, out_ref):
    rows, columns = out_ref.shape[0] // 2, out_ref.shape[1]
    out_ref[:rows] = ahead_ref[:rows]
    out_ref[rows:] = behind_ref[:rows]


def pick(rows, ahead, behind):
    height, columns = ahead.shape[0], ahead.shape[1] // 2
    return pl.pallas_call(
        pick_kernel,
        grid=(1,),
        in_specs=[pl.BlockSpec((height, columns), lambda i: (0, 0))] * 2,
        out_specs=pl.BlockSpec((2 * rows, columns), lambda i: (0, 0)),
        out_shape=jax.ShapeDtypeStruct((2 * rows, columns), jnp.bfloat16),
        compiler_params=params(12),
        cost_estimate=cost(),
    )(ahead, behind)


def pick_last_kernel(ahead_ref, behind_ref, swapped_ref, a_ref, v_ref, ahead_b_ref, behind_b_ref):
    rows = a_ref.shape[0]
    a_ref[...] = ahead_ref[:rows]
    v_ref[...] = behind_ref[:rows]
    ahead_b_ref[...] = swapped_ref[:rows]
    behind_b_ref[...] = swapped_ref[rows:]


def pick_last(rows, ahead, behind, swapped):
    height, columns = ahead.shape[0], ahead.shape[1] // 2
    shape = (rows, columns)
    return pl.pallas_call(
        pick_last_kernel,
        grid=(1,),
        in_specs=[
            pl.BlockSpec((height, columns), lambda i: (0, 0)),
            pl.BlockSpec((height, columns), lambda i: (0, 1)),
            pl.BlockSpec((2 * rows, columns), lambda i: (0, 0)),
        ],
        out_specs=[pl.BlockSpec(shape, lambda i: (0, 0))] * 4,
        out_shape=[jax.ShapeDtypeStruct(shape, jnp.bfloat16)] * 4,
        compiler_params=params(12),
        cost_estimate=cost(),
    )(ahead, behind, swapped)


def join_kernel(scalars, mine_ref, theirs_ref, out_ref):
    columns = mine_ref.shape[1]
    shared = 2 * columns - out_ref.shape[1]

    def emit(low, high):
        out_ref[:, :columns] = low[...]
        out_ref[:, columns:] = high[:, shared:]

    pl.when(scalars[1] == 0)(lambda: emit(mine_ref, theirs_ref))
    pl.when(scalars[1] == 1)(lambda: emit(theirs_ref, mine_ref))


def join(scalars, mine, theirs, inner_width):
    slots, _, tokens = mine.shape
    return pl.pallas_call(
        join_kernel,
        in_specs=[smem(), vmem(), vmem()],
        out_specs=vmem(),
        out_shape=jax.ShapeDtypeStruct((slots, inner_width, tokens), jnp.bfloat16),
        compiler_params=params(8),
        cost_estimate=cost(),
    )(scalars, mine, theirs)


def cut_kernel(k_ref, v_ref, after_ref, out_ref):
    chips, _, span = out_ref.shape
    half = chips // 2
    for chip in range(chips):
        source = k_ref if chip < half else v_ref
        start = (chip % half) * span
        out_ref[chip] = source[:, start : start + span]


def cut_prompt_weights(w_ck, w_cv, chips, after):
    depth, inner_width = w_ck.shape
    span = 2 * inner_width // chips
    return pl.pallas_call(
        cut_kernel,
        grid=(1,),
        in_specs=[pl.BlockSpec(w_ck.shape, lambda i: (0, 0))] * 2 + [anywhere()],
        out_specs=pl.BlockSpec((chips, depth, span), lambda i: (0, 0, 0)),
        out_shape=jax.ShapeDtypeStruct((chips, depth, span), jnp.bfloat16),
        compiler_params=params(56),
        cost_estimate=cost(),
    )(w_ck, w_cv, after)


def prompt_kernel(starts, scalars, after_ref, *refs):
    chips = len(starts)
    blocks, (own_ref, other_ref, out_ref, held_ref) = refs[:chips], refs[chips:]
    depth = own_ref.shape[0]
    half = out_ref.shape[1]
    parts = [
        jnp.concatenate(
            [
                block[start + core * half : start + (core + 1) * half, :depth]
                for start, block in zip(starts, blocks)
            ],
            axis=0,
        )
        for core in range(2)
    ]

    def emit(first, second):
        product = jnp.dot(parts[0], first[...], preferred_element_type=jnp.float32) + jnp.dot(
            parts[1], second[...], preferred_element_type=jnp.float32
        )
        held_ref[...] = product.astype(jnp.bfloat16).reshape(held_ref.shape)

    pl.when(scalars[1] == 0)(lambda: emit(own_ref, other_ref))
    pl.when(scalars[1] == 1)(lambda: emit(other_ref, own_ref))
    for chip in range(chips):
        out_ref[chip] = held_ref[scalars[2 + chip]]


def project_prompts(scalars, blocks, starts, w_own, w_other, after):
    chips, span = len(blocks), w_own.shape[1]
    half = (blocks[0].shape[0] - starts[0]) // 2
    if blocks[0].shape[0] * chips > 4096:
        depth = w_own.shape[0]
        straight = scalars[1] == 0
        weights = [jnp.where(straight, w_own, w_other), jnp.where(straight, w_other, w_own)]
        product = 0.0
        for core, weight in enumerate(weights):
            rows = [
                x[start + core * half : start + (core + 1) * half, :depth]
                for start, x in zip(starts, blocks)
            ]
            rows = jnp.concatenate(rows, axis=0)
            product = product + jnp.dot(rows, weight, preferred_element_type=jnp.float32)
        product = product.astype(jnp.bfloat16).reshape(chips, half, span)
        return jnp.take(product, scalars[2 : 2 + chips], axis=0)
    return pl.pallas_call(
        functools.partial(prompt_kernel, starts),
        in_specs=[smem(), anywhere()] + [vmem()] * (chips + 2),
        out_specs=vmem(),
        out_shape=jax.ShapeDtypeStruct((chips, half, span), jnp.bfloat16),
        scratch_shapes=[pltpu.VMEM((chips, half, span), jnp.bfloat16)],
        compiler_params=params(16),
        cost_estimate=cost(),
    )(scalars, after, *blocks, w_own, w_other)


def route_kernel(spots_here, winner_ref, loser_ref, rows_ref, out_ref):
    tile, count = out_ref.shape[0], rows_ref.shape[0]
    prompts = winner_ref.shape[1]
    row = lax.broadcasted_iota(jnp.int32, (tile, 1), 0) + pl.program_id(0) * tile
    slot = lax.div(row, spots_here)
    reads = (winner_ref[...] == slot) | (loser_ref[...] == slot)
    column = lax.broadcasted_iota(jnp.int32, (prompts, count), 1)
    prompt = lax.broadcasted_iota(jnp.int32, (prompts, count), 0)
    spread = jnp.where(lax.rem(column, prompts) == prompt, 1.0, 0.0).astype(jnp.bfloat16)
    reads = jnp.where(reads, 1.0, 0.0).astype(jnp.bfloat16)
    reads = jnp.dot(reads, spread, preferred_element_type=jnp.float32)
    same_spot = lax.rem(row, spots_here) == lax.div(column[0:1], prompts)
    chosen = jnp.where(same_spot, reads, 0.0).astype(jnp.bfloat16)
    out_ref[...] = jnp.dot(
        chosen, rows_ref[...], preferred_element_type=jnp.float32
    ).astype(jnp.bfloat16)


def route(projected, winner_slot, loser_slot, spots_here):
    count, span = projected.shape
    prompts = winner_slot.shape[0]
    total = 2 * prompts * spots_here
    tile = min(total, 512)
    row = pl.BlockSpec((1, prompts), lambda i: (0, 0))
    return pl.pallas_call(
        functools.partial(route_kernel, spots_here),
        grid=(total // tile,),
        in_specs=[row, row, pl.BlockSpec((count, span), lambda i: (0, 0))],
        out_specs=pl.BlockSpec((tile, span), lambda i: (i, 0)),
        out_shape=jax.ShapeDtypeStruct((total, span), jnp.bfloat16),
        compiler_params=params(32 if count > 1024 else 8),
        cost_estimate=cost(),
    )(winner_slot.reshape(1, prompts), loser_slot.reshape(1, prompts), projected)


def finish_kernel(columns, head_size, scalars, own_ref, other_ref, keys_ref, values_ref):
    devices, rows, span = own_ref.shape
    slots = keys_ref.shape[0] // 2
    each = rows // slots
    inner_width = devices // 2 * span // 2

    def emit(start):
        for side, source in enumerate((own_ref, other_ref)):
            for slot in range(slots):
                at = slice(slot * each, (slot + 1) * each)
                for core in range(2):
                    parts = [source[2 * chip + core, at, :] for chip in range(devices // 2)]
                    whole = jnp.concatenate(parts, axis=1)
                    out = side * slots + slot
                    to = slice(core * each, (core + 1) * each)
                    keys = whole[:, start : start + columns].astype(jnp.float32)
                    for pair in range(columns // LANES):
                        lanes = slice(pair * LANES, (pair + 1) * LANES)
                        keys_ref[out, to, lanes] = head_pair_norm(keys[:, lanes], head_size)
                    first = inner_width + start
                    values_ref[out, to, :] = whole[:, first : first + columns]

    pl.when(scalars[1] == 0)(lambda: emit(0))
    pl.when(scalars[1] == 1)(lambda: emit(inner_width - columns))


def finish_prompts(scalars, own, other, columns, head_size, slots):
    devices, rows, _ = own.shape
    span = 2 * rows // slots
    shape = jax.ShapeDtypeStruct((2 * slots, span, columns), jnp.bfloat16)
    return pl.pallas_call(
        functools.partial(finish_kernel, columns, head_size),
        in_specs=[smem(), vmem(), vmem()],
        out_specs=[vmem()] * 2,
        out_shape=[shape] * 2,
        compiler_params=params(16),
        cost_estimate=cost(),
    )(scalars, own, other)


def attend_kernel(
    head_size,
    spots,
    side,
    scalars,
    winner,
    loser,
    lengths,
    a_ref,
    v_ref,
    b_ref,
    pk_ref,
    pv_ref,
    out_ref,
):
    step = pl.program_id(0)
    count_here = pl.num_programs(0)
    even_group = scalars[0] == 0
    _, columns, tokens = out_ref.shape
    owner = scalars[scalars.shape[0] - 2 + side]
    slot = owner + step

    def count(p, live):
        hit = (winner[p] == slot) | (loser[p] == slot)
        return live + jnp.where(hit, lengths[p], 0)

    live = lax.fori_loop(0, winner.shape[0], count, jnp.int32(0))
    span = pk_ref.shape[1]
    row = lax.broadcasted_iota(jnp.int32, (span, 1), 0)
    rest = lax.rem(row, span // 2)
    position = (2 * lax.div(rest, spots) + lax.div(row, span // 2)) * spots + lax.rem(rest, spots)
    allowed = position < live
    low = lax.broadcasted_iota(jnp.int32, (1, LANES), 1) < head_size
    over_lanes = (((1,), (1,)), ((), ()))
    over_rows = (((0,), (0,)), ((), ()))
    scale = 1.4426950408889634 / head_size**0.5
    here = pl.ds(pl.multiple_of((side * count_here + step) * tokens, tokens), tokens)
    block = side * count_here + step
    for pair in range(columns // LANES):
        lanes = slice(pair * LANES, (pair + 1) * LANES)
        a = a_ref[here, lanes]
        b = b_ref[here, lanes]
        queries = jnp.where(even_group, a, b)
        keys = jnp.where(even_group, b, a)
        values = v_ref[here, lanes]
        prompt_keys = pk_ref[block, :, lanes]
        prompt_values = pv_ref[block, :, lanes]
        for head in range(2):
            side = low if head == 0 else jnp.logical_not(low)
            q = jnp.where(side, queries, jnp.zeros_like(queries))
            s = lax.dot_general(keys, q, over_lanes, preferred_element_type=jnp.float32)
            t = lax.dot_general(prompt_keys, q, over_lanes, preferred_element_type=jnp.float32)
            s = jnp.exp2(s * scale)
            t = jnp.where(allowed, jnp.exp2(t * scale), 0.0)
            total = jnp.sum(s, axis=0, keepdims=True) + jnp.sum(t, axis=0, keepdims=True)
            out = lax.dot_general(
                values, s.astype(jnp.bfloat16), over_rows, preferred_element_type=jnp.float32
            ) + lax.dot_general(
                prompt_values, t.astype(jnp.bfloat16), over_rows, preferred_element_type=jnp.float32
            )
            rows = slice(head * head_size, (head + 1) * head_size)
            to = slice(pair * LANES + head * head_size, pair * LANES + (head + 1) * head_size)
            out_ref[0, to, :] = (out[rows] * (1.0 / total)).astype(jnp.bfloat16)


def attend(side, scalars, routes, rows, prompt_keys, prompt_values, head_size, spots, count):
    tokens = rows[0].shape[0] // (2 * count)
    columns = rows[0].shape[1]
    return pl.pallas_call(
        functools.partial(attend_kernel, head_size, spots, side),
        grid=(count,),
        in_specs=[smem()] * 4 + [vmem()] * 5,
        out_specs=pl.BlockSpec((1, columns, tokens), lambda l: (l, 0, 0)),
        out_shape=jax.ShapeDtypeStruct((count, columns, tokens), jnp.bfloat16),
        compiler_params=params(16),
        cost_estimate=cost(),
    )(scalars, *routes, *rows, prompt_keys, prompt_values)


def ring_order(groups, chips):
    if groups == 2:
        return list(range(0, chips, 2)) + list(range(1, chips, 2))[::-1]
    return list(range(chips))


def solution(mesh):
    groups, dp = mesh.shape["groups"], mesh.shape["dp"]
    chips = dp // 2
    ring = ring_order(groups, chips)
    place = [ring.index(chip) for chip in range(chips)]
    behind_by = np.array(
        [[(place[me] - place[chip]) % chips for chip in range(chips)] for me in range(chips)],
        np.int32,
    )
    forward_pairs = [
        (2 * ring[i] + c, 2 * ring[(i + 1) % chips] + c) for i in range(chips) for c in range(2)
    ]
    backward_pairs = [(b, a) for a, b in forward_pairs]
    core_pairs = [(d, d ^ 1) for d in range(dp)]
    group_pairs = [(g, g ^ 1) for g in range(groups)]
    half_groups = [[2 * chip + c for chip in range(chips)] for c in range(2)]

    def forward(x):
        return lax.ppermute(x, "dp", forward_pairs)

    def backward(x):
        return lax.ppermute(x, "dp", backward_pairs)

    def swap_cores(x):
        return lax.ppermute(x, "dp", core_pairs)

    def swap_groups(x):
        return lax.ppermute(x, "groups", group_pairs)

    def local(
        latents,
        context,
        lengths,
        winner_slot,
        loser_slot,
        image_mod,
        context_mod,
        w_q,
        w_k,
        w_v,
        w_ck,
        w_cv,
    ):
        slot_local, token_count, width = latents.shape
        prompt_count, spot_local, _ = context.shape
        depth, inner_width = w_q.shape
        head_size = inner_width // HEADS
        columns = (HEADS + 1) // 2 * head_size
        me = lax.axis_index("dp")
        my_group = lax.axis_index("groups") % 2
        my_chip, my_core = me // 2, me % 2
        places = lax.dynamic_index_in_dim(jnp.asarray(behind_by), my_chip, 0, keepdims=False)
        first = [my_group, my_core]
        last = [me * slot_local, (me ^ 1) * slot_local]
        scalars = jnp.concatenate([jnp.stack(first), places, jnp.stack(last)]).astype(jnp.int32)

        own_mixed = mix_prompts(context, context_mod, chips, 2 * columns)
        w_cut = cut_prompt_weights(w_ck, w_cv, chips, own_mixed)
        w_c = lax.all_to_all(w_cut, "dp", 0, 0, axis_index_groups=half_groups, tiled=True)
        once = [forward(own_mixed), backward(own_mixed)]
        twice = [forward(once[0]), backward(once[1])]
        mixed = {0: (own_mixed, 0)}
        for o, arrived in ((1, once), (2, twice)):
            mixed.setdefault(o % chips, (arrived[0], 0))
            mixed.setdefault(-o % chips, (arrived[1], 0))
        keep, give = split_weights(scalars, w_q, w_k, w_v, columns, w_cut)
        got = swap_cores(give)
        own_av = [keep[:, : 2 * columns], got[:, : 2 * columns]]
        ahead, behind = [jnp.concatenate(own_av + [x], axis=0) for x in twice]

        own, *give = modulate_image(scalars, latents, image_mod, chips, ahead)

        totals = None
        enough = max(1, chips // 8)
        tokens, waiting_av, waiting_b = [w_c], [((0,), ahead)], []
        for o in range(1, chips // 2):
            ahead, behind = meet([forward(ahead), backward(behind)], tokens)
            mixed.setdefault((o + 2) % chips, (ahead, 2 * depth))
            mixed.setdefault((-o - 2) % chips, (behind, 2 * depth))
            if o == 1:
                (w_c,) = meet([w_c], [ahead])
                w_parts = [x.reshape(width // 2, -1) for x in (w_c, swap_cores(w_c))]
            if 4 * o == chips:
                slabs = [[own], [swap_cores(x) for x in meet(give, [ahead])]]
            tokens = []
            if 2 * o + 4 == chips:
                blocks, starts = zip(*[mixed[o] for o in range(chips)])
                projected = project_prompts(scalars, blocks, starts, *w_parts, slabs[1][0])
                projected = projected.reshape(-1, projected.shape[2])
                outgoing = route(projected, winner_slot, loser_slot, chips * spot_local)
                outgoing = outgoing.reshape(dp, -1, outgoing.shape[1])
                arrived = lax.all_to_all(outgoing, "dp", 0, 0, tiled=True)
            last = 2 * o + 2 == chips
            waiting_av += [((o,), ahead), ((chips - o,), behind)]
            if last:
                picked = pick_last(2 * depth, ahead, behind, waiting_b[-1][1])
            else:
                swapped = swap_groups(pick(2 * depth, ahead, behind))
            if len(waiting_b) > 3 * enough or (last and totals is None):
                first = totals is None
                items = [((), keep), ((), got)] if first else waiting_b
                totals, token = accumulate(
                    2 * depth, totals, slabs, waiting_av, items, [arrived] if last else []
                )
                tokens.append(token)
                waiting_av, waiting_b = [], waiting_b if first else []
            if not last:
                waiting_b.append(((o, chips - o), swapped))
                tokens.append(swapped)
            if 2 * o + 4 == chips:
                tokens.append(arrived)
        a_far, v_far = meet([forward(picked[0]), backward(picked[1])], tokens)
        o = chips // 2 - 1
        waiting_b += [((o,), forward(picked[2])), ((chips - o,), backward(picked[3]))]
        b_far = swap_groups(a_far)
        rows_a, rows_v, rows_b, features = last_products(
            2 * depth,
            head_size,
            totals,
            slabs,
            waiting_av,
            (chips // 2, a_far, v_far),
            waiting_b,
        )

        done_rows = (rows_a, rows_v, close(rows_b, features, b_far, head_size))

        prompt_keys, prompt_values = finish_prompts(
            scalars, arrived, swap_cores(arrived), columns, head_size, slot_local
        )

        routes = (winner_slot, loser_slot, lengths)

        def run(side):
            return attend(
                side,
                scalars,
                routes,
                done_rows,
                prompt_keys,
                prompt_values,
                head_size,
                spot_local,
                slot_local,
            )

        theirs = swap_cores(run(1))
        mine = run(0)
        return join(scalars, mine, theirs, inner_width).transpose(0, 2, 1)

    placed = (
        P(("groups", "dp"), None, None),
        P("groups", "dp", None),
        P("groups"),
        P("groups"),
        P("groups"),
        P(("groups", "dp"), None, None),
        P("groups", None, None),
        P("dp", None),
        P("dp", None),
        P("dp", None),
        P("dp", None),
        P("dp", None),
    )
    return jax.shard_map(
        local,
        mesh=mesh,
        in_specs=placed,
        out_specs=P(("groups", "dp"), None, None),
        check_vma=False,
    )
```

```python
import functools

import jax
import jax.numpy as jnp
import numpy as np
from jax import lax
from jax.experimental import pallas as pl
from jax.experimental.pallas import tpu as pltpu
from jax.sharding import PartitionSpec as P

HEADS = 19
LANES = 128


epsilon = 1e-06


def params(mib):
    return pltpu.CompilerParams(vmem_limit_bytes=mib * 2**20)


def cost(flops=1):
    return pl.CostEstimate(flops=flops, bytes_accessed=1, transcendentals=0)


def anywhere():
    return pl.BlockSpec(memory_space=pl.ANY)


def layer_norm(values, shift, scale):
    average = jnp.mean(values, axis=-1, keepdims=True)
    centered = values - average
    variance = jnp.mean(centered * centered, axis=-1, keepdims=True)
    return (centered * lax.rsqrt(variance + epsilon) * (1.0 + scale) + shift).astype(jnp.bfloat16)


def head_pair_norm(x, head_size):
    low = lax.broadcasted_iota(jnp.int32, (1, LANES), 1) < head_size
    squares = x * x
    first = jnp.sum(jnp.where(low, squares, 0.0), axis=-1, keepdims=True)
    second = jnp.sum(jnp.where(low, 0.0, squares), axis=-1, keepdims=True)
    first = lax.rsqrt(first * (1.0 / head_size) + epsilon)
    second = lax.rsqrt(second * (1.0 / head_size) + epsilon)
    return (x * jnp.where(low, first, second)).astype(jnp.bfloat16)


def vmem():
    return pl.BlockSpec(memory_space=pltpu.VMEM)


def smem():
    return pl.BlockSpec(memory_space=pltpu.SMEM)


def split_kernel(columns, scalars, q_ref, k_ref, v_ref, after_ref, keep_ref, give_ref):
    inner_width = q_ref.shape[1]

    def emit(parts, low_ref, high_ref):
        for i, part in enumerate(parts):
            at = slice(i * columns, (i + 1) * columns)
            low_ref[:, at] = part[:, :columns]
            high_ref[:, at] = part[:, inner_width - columns :]

    for group in range(2):
        parts = (q_ref, v_ref, k_ref) if group == 0 else (k_ref, v_ref, q_ref)
        for core in range(2):
            refs = (keep_ref, give_ref) if core == 0 else (give_ref, keep_ref)
            here = (scalars[0] == group) & (scalars[1] == core)
            pl.when(here)(functools.partial(emit, parts, *refs))


def split_weights(scalars, w_q, w_k, w_v, columns, after):
    depth, inner_width = w_q.shape
    shape = jax.ShapeDtypeStruct((depth, 3 * columns), jnp.bfloat16)
    whole = pl.BlockSpec((depth, inner_width), lambda i, s: (0, 0))
    out = pl.BlockSpec((depth, 3 * columns), lambda i, s: (0, 0))
    return pl.pallas_call(
        functools.partial(split_kernel, columns),
        grid_spec=pltpu.PrefetchScalarGridSpec(
            num_scalar_prefetch=1,
            grid=(1,),
            in_specs=[whole] * 3 + [anywhere()],
            out_specs=[out] * 2,
        ),
        out_shape=[shape] * 2,
        compiler_params=params(56),
        cost_estimate=cost(),
    )(scalars, w_q, w_k, w_v, after)


def mixed_kernel(chips, context_ref, mod_ref, out_ref):
    prompts, spots, width = context_ref.shape
    depth = width // (2 * chips)
    shift, scale = mod_ref[:, 0, :], mod_ref[:, 1, :]
    values = context_ref[...].astype(jnp.float32)
    for spot in range(spots):
        rows = layer_norm(values[:, spot, :], shift, scale)
        for core in range(2):
            parts = [
                rows[:, (2 * chip + core) * depth : (2 * chip + core + 1) * depth]
                for chip in range(chips)
            ]
            at = (core * spots + spot) * prompts
            parts.append(jnp.zeros((prompts, out_ref.shape[1] - width // 2), jnp.bfloat16))
            out_ref[at : at + prompts, :] = jnp.concatenate(parts, axis=1)


def mix_prompts(context, context_mod, chips, columns):
    prompts, spots, width = context.shape
    return pl.pallas_call(
        functools.partial(mixed_kernel, chips),
        grid=(1,),
        in_specs=[pl.BlockSpec(x.shape, lambda i: (0, 0, 0)) for x in (context, context_mod)],
        out_specs=pl.BlockSpec((2 * spots * prompts, columns), lambda i: (0, 0)),
        out_shape=jax.ShapeDtypeStruct((2 * spots * prompts, columns), jnp.bfloat16),
        compiler_params=params(56),
        cost_estimate=cost(),
    )(context, context_mod)


def image_kernel(chips, scalars, x_ref, mod_ref, after_ref, own_ref, give_ref):
    image = layer_norm(x_ref[0].astype(jnp.float32), mod_ref[0, 0:1, :], mod_ref[0, 1:2, :])
    depth = image.shape[1] // (2 * chips)

    def emit(first_ref, second_ref):
        for chip in range(chips):
            start = 2 * chip * depth
            straight = image[:, start : start + 2 * depth]
            turned = jnp.concatenate([straight[:, depth:], straight[:, :depth]], axis=1)
            first_ref[scalars[2 + chip], :, : 2 * depth] = straight
            second_ref[scalars[2 + chip], :, : 2 * depth] = turned

    pl.when(scalars[1] == 0)(lambda: emit(own_ref, give_ref))
    pl.when(scalars[1] == 1)(lambda: emit(give_ref, own_ref))


def modulate_image(scalars, latents, image_mod, chips, after):
    slots, tokens, width = latents.shape
    wide = -(-width // chips // LANES) * LANES
    block = (chips, tokens, wide)
    return pl.pallas_call(
        functools.partial(image_kernel, chips),
        grid_spec=pltpu.PrefetchScalarGridSpec(
            num_scalar_prefetch=1,
            grid=(slots,),
            in_specs=[
                pl.BlockSpec((1, tokens, width), lambda i, s: (i, 0, 0)),
                pl.BlockSpec((1, 2, width), lambda i, s: (i, 0, 0)),
                anywhere(),
            ],
            out_specs=[pl.BlockSpec(block, lambda i, s: (0, i, 0))] * 2,
        ),
        out_shape=[jax.ShapeDtypeStruct((chips, slots * tokens, wide), jnp.bfloat16)] * 2,
        compiler_params=params(32),
        cost_estimate=cost(),
    )(scalars, latents, image_mod, after)


def take_rows(slab, o, depth):
    return jnp.concatenate([part[o, :, :depth] for part in slab], axis=0)


def product_kernel(slots, depth, av_places, b_places, first, others, *refs):
    slabs, refs = refs[:slots], refs[slots:]
    panels = refs[: len(av_places)]
    at = len(av_places)
    pieces = refs[at : at + len(b_places) // 2 + 2 * first]
    out_av, out_b, token_ref = refs[-3:]
    totals = (None, None) if first else refs[-5 - others : -3 - others]
    rows = slabs[0].shape[1]
    columns = out_av.shape[1]
    token_ref[...] = jnp.zeros_like(token_ref)

    def product(slab, places, panel):
        features = jnp.concatenate([take_rows(slab, o, depth) for o in places], axis=1)
        return jnp.dot(features, panel, preferred_element_type=jnp.float32)

    for side, slab in enumerate((slabs[:1], slabs[1:])):
        to = slice(side * rows, (side + 1) * rows)
        if av_places:
            panel = jnp.concatenate([panel[:depth] for panel in panels], axis=0)
            sums = product(slab, av_places, panel)
            out_av[to] = sums if first else totals[0][to] + sums
        elif totals[0] is not out_av:
            out_av[to] = totals[0][to]
        sums = 0.0
        if b_places:
            panel = jnp.concatenate([piece[...] for piece in pieces[2 * first :]], axis=0)
            sums = product(slab, b_places, panel)
        if first:
            features = take_rows(slab, 0, depth)
            half = depth // 2
            for own, part in zip((slice(0, half), slice(half, depth)), pieces):
                sums = sums + jnp.dot(
                    features[:, own], part[:, columns:], preferred_element_type=jnp.float32
                )
            out_b[to] = sums
        else:
            out_b[to] = totals[1][to] + sums


def accumulate(depth, totals, slabs, av_items, b_items, others=()):
    first = totals is None
    slabs = slabs[0] + slabs[1]
    rows, columns = slabs[0].shape[1], 2 * b_items[0][1].shape[1]
    if first:
        columns = 2 * b_items[0][1].shape[1] // 3
    av_places = [o for places, _ in av_items for o in places]
    b_places = [o for places, _ in b_items for o in places]
    operands = slabs + [x for _, x in av_items] + [x for _, x in b_items]
    aliases = {}
    if not first:
        aliases = {len(operands): 0, len(operands) + 1: 1}
        operands += list(totals)
    in_specs = [vmem()] * len(operands) + [anywhere()] * len(others)
    out = pl.pallas_call(
        functools.partial(
            product_kernel, len(slabs), depth, av_places, b_places, first, len(others)
        ),
        in_specs=in_specs,
        out_specs=[vmem()] * 3,
        out_shape=[
            jax.ShapeDtypeStruct((2 * rows, columns), jnp.float32),
            jax.ShapeDtypeStruct((2 * rows, columns // 2), jnp.float32),
            jax.ShapeDtypeStruct((8, LANES), jnp.float32),
        ],
        input_output_aliases=aliases,
        compiler_params=params(20),
        cost_estimate=cost(4 * 10**10),
    )(*operands, *others)
    return out[:2], out[2]


def last_kernel(slots, depth, head_size, av_places, b_places, pieces, *refs):
    slabs, refs = refs[:slots], refs[slots:]
    count = len(av_places) - 1
    panels, (a_far, v_far) = refs[:count], refs[count : count + 2]
    swapped = refs[count + 2 : count + 2 + pieces]
    total_av, total_b, out_a, out_v, out_b, out_far = refs[-6:]
    rows, columns = slabs[0].shape[1], out_a.shape[1]

    def product(slab, places, panel):
        features = jnp.concatenate([take_rows(slab, o, depth) for o in places], axis=1)
        return jnp.dot(features, panel, preferred_element_type=jnp.float32)

    for side, slab in enumerate((slabs[:1], slabs[1:])):
        to = slice(side * rows, (side + 1) * rows)
        for half, far in enumerate((a_far, v_far)):
            lanes = slice(half * columns, (half + 1) * columns)
            parts = [panel[:depth, lanes] for panel in panels] + [far[...]]
            sums = total_av[to, lanes] + product(slab, av_places, jnp.concatenate(parts, axis=0))
            if half == 1:
                out_v[to] = sums.astype(jnp.bfloat16)
                continue
            for pair in range(columns // LANES):
                at = slice(pair * LANES, (pair + 1) * LANES)
                out_a[to, at] = head_pair_norm(sums[:, at], head_size)
        panel = jnp.concatenate([piece[...] for piece in swapped], axis=0)
        out_b[to] = total_b[to] + product(slab, b_places, panel)
        out_far[to, :depth] = take_rows(slab, av_places[-1], depth)


def last_products(depth, head_size, totals, slabs, av_items, far_items, b_items):
    slabs = slabs[0] + slabs[1]
    rows, columns = 2 * slabs[0].shape[1], totals[1].shape[1]
    av_places = [o for places, _ in av_items for o in places] + [far_items[0]]
    b_places = [o for places, _ in b_items for o in places]
    operands = slabs + [x for _, x in av_items] + list(far_items[1:])
    operands += [x for _, x in b_items] + list(totals)
    return pl.pallas_call(
        functools.partial(
            last_kernel, len(slabs), depth, head_size, av_places, b_places, len(b_items)
        ),
        in_specs=[vmem()] * len(operands),
        out_specs=[vmem()] * 4,
        out_shape=[
            jax.ShapeDtypeStruct((rows, columns), jnp.bfloat16),
            jax.ShapeDtypeStruct((rows, columns), jnp.bfloat16),
            jax.ShapeDtypeStruct((rows, columns), jnp.float32),
            jax.ShapeDtypeStruct((rows, slabs[0].shape[2]), jnp.bfloat16),
        ],
        compiler_params=params(20),
        cost_estimate=cost(4 * 10**10),
    )(*operands)


def close_kernel(head_size, total_ref, features_ref, far_ref, out_ref):
    features = features_ref[:, : far_ref.shape[0]]
    sums = jnp.dot(features, far_ref[...], preferred_element_type=jnp.float32) + total_ref[...]
    for pair in range(out_ref.shape[1] // LANES):
        lanes = slice(pair * LANES, (pair + 1) * LANES)
        out_ref[:, lanes] = head_pair_norm(sums[:, lanes], head_size)


def close(total, features, far, head_size):
    return pl.pallas_call(
        functools.partial(close_kernel, head_size),
        in_specs=[vmem()] * 3,
        out_specs=vmem(),
        out_shape=jax.ShapeDtypeStruct(total.shape, jnp.bfloat16),
        compiler_params=params(16),
        cost_estimate=cost(),
    )(total, features, far)


def meet(arrays, others):
    return pl.pallas_call(
        lambda *refs: None,
        in_specs=[anywhere()] * (len(arrays) + len(others)),
        out_specs=[anywhere()] * len(arrays),
        out_shape=[jax.ShapeDtypeStruct(x.shape, x.dtype) for x in arrays],
        input_output_aliases={i: i for i in range(len(arrays))},
        compiler_params=params(4),
        cost_estimate=cost(),
    )(*arrays, *others)


def pick_kernel(ahead_ref, behind_ref, out_ref):
    rows, columns = out_ref.shape[0] // 2, out_ref.shape[1]
    out_ref[:rows] = ahead_ref[:rows]
    out_ref[rows:] = behind_ref[:rows]


def pick(rows, ahead, behind):
    height, columns = ahead.shape[0], ahead.shape[1] // 2
    return pl.pallas_call(
        pick_kernel,
        grid=(1,),
        in_specs=[pl.BlockSpec((height, columns), lambda i: (0, 0))] * 2,
        out_specs=pl.BlockSpec((2 * rows, columns), lambda i: (0, 0)),
        out_shape=jax.ShapeDtypeStruct((2 * rows, columns), jnp.bfloat16),
        compiler_params=params(12),
        cost_estimate=cost(),
    )(ahead, behind)


def pick_last_kernel(ahead_ref, behind_ref, swapped_ref, a_ref, v_ref, ahead_b_ref, behind_b_ref):
    rows = a_ref.shape[0]
    a_ref[...] = ahead_ref[:rows]
    v_ref[...] = behind_ref[:rows]
    ahead_b_ref[...] = swapped_ref[:rows]
    behind_b_ref[...] = swapped_ref[rows:]


def pick_last(rows, ahead, behind, swapped):
    height, columns = ahead.shape[0], ahead.shape[1] // 2
    shape = (rows, columns)
    return pl.pallas_call(
        pick_last_kernel,
        grid=(1,),
        in_specs=[
            pl.BlockSpec((height, columns), lambda i: (0, 0)),
            pl.BlockSpec((height, columns), lambda i: (0, 1)),
            pl.BlockSpec((2 * rows, columns), lambda i: (0, 0)),
        ],
        out_specs=[pl.BlockSpec(shape, lambda i: (0, 0))] * 4,
        out_shape=[jax.ShapeDtypeStruct(shape, jnp.bfloat16)] * 4,
        compiler_params=params(12),
        cost_estimate=cost(),
    )(ahead, behind, swapped)


def join_kernel(scalars, mine_ref, theirs_ref, out_ref):
    columns = mine_ref.shape[1]
    shared = 2 * columns - out_ref.shape[1]

    def emit(low, high):
        out_ref[:, :columns] = low[...]
        out_ref[:, columns:] = high[:, shared:]

    pl.when(scalars[1] == 0)(lambda: emit(mine_ref, theirs_ref))
    pl.when(scalars[1] == 1)(lambda: emit(theirs_ref, mine_ref))


def join(scalars, mine, theirs, inner_width):
    slots, _, tokens = mine.shape
    return pl.pallas_call(
        join_kernel,
        in_specs=[smem(), vmem(), vmem()],
        out_specs=vmem(),
        out_shape=jax.ShapeDtypeStruct((slots, inner_width, tokens), jnp.bfloat16),
        compiler_params=params(8),
        cost_estimate=cost(),
    )(scalars, mine, theirs)


def cut_kernel(k_ref, v_ref, after_ref, out_ref):
    chips, _, span = out_ref.shape
    half = chips // 2
    for chip in range(chips):
        source = k_ref if chip < half else v_ref
        start = (chip % half) * span
        out_ref[chip] = source[:, start : start + span]


def cut_prompt_weights(w_ck, w_cv, chips, after):
    depth, inner_width = w_ck.shape
    span = 2 * inner_width // chips
    return pl.pallas_call(
        cut_kernel,
        grid=(1,),
        in_specs=[pl.BlockSpec(w_ck.shape, lambda i: (0, 0))] * 2 + [anywhere()],
        out_specs=pl.BlockSpec((chips, depth, span), lambda i: (0, 0, 0)),
        out_shape=jax.ShapeDtypeStruct((chips, depth, span), jnp.bfloat16),
        compiler_params=params(56),
        cost_estimate=cost(),
    )(w_ck, w_cv, after)


def prompt_kernel(starts, scalars, after_ref, *refs):
    chips = len(starts)
    blocks, (own_ref, other_ref, out_ref, held_ref) = refs[:chips], refs[chips:]
    depth = own_ref.shape[0]
    half = out_ref.shape[1]
    parts = [
        jnp.concatenate(
            [
                block[start + core * half : start + (core + 1) * half, :depth]
                for start, block in zip(starts, blocks)
            ],
            axis=0,
        )
        for core in range(2)
    ]

    def emit(first, second):
        product = jnp.dot(parts[0], first[...], preferred_element_type=jnp.float32) + jnp.dot(
            parts[1], second[...], preferred_element_type=jnp.float32
        )
        held_ref[...] = product.astype(jnp.bfloat16).reshape(held_ref.shape)

    pl.when(scalars[1] == 0)(lambda: emit(own_ref, other_ref))
    pl.when(scalars[1] == 1)(lambda: emit(other_ref, own_ref))
    for chip in range(chips):
        out_ref[chip] = held_ref[scalars[2 + chip]]


def project_prompts(scalars, blocks, starts, w_own, w_other, after):
    chips, span = len(blocks), w_own.shape[1]
    half = (blocks[0].shape[0] - starts[0]) // 2
    if blocks[0].shape[0] * chips > 4096:
        depth = w_own.shape[0]
        straight = scalars[1] == 0
        weights = [jnp.where(straight, w_own, w_other), jnp.where(straight, w_other, w_own)]
        product = 0.0
        for core, weight in enumerate(weights):
            rows = [
                x[start + core * half : start + (core + 1) * half, :depth]
                for start, x in zip(starts, blocks)
            ]
            rows = jnp.concatenate(rows, axis=0)
            product = product + jnp.dot(rows, weight, preferred_element_type=jnp.float32)
        product = product.astype(jnp.bfloat16).reshape(chips, half, span)
        return jnp.take(product, scalars[2 : 2 + chips], axis=0)
    return pl.pallas_call(
        functools.partial(prompt_kernel, starts),
        in_specs=[smem(), anywhere()] + [vmem()] * (chips + 2),
        out_specs=vmem(),
        out_shape=jax.ShapeDtypeStruct((chips, half, span), jnp.bfloat16),
        scratch_shapes=[pltpu.VMEM((chips, half, span), jnp.bfloat16)],
        compiler_params=params(16),
        cost_estimate=cost(4 * 10**10),
    )(scalars, after, *blocks, w_own, w_other)


def route_kernel(spots_here, winner_ref, loser_ref, rows_ref, out_ref):
    tile, count = out_ref.shape[0], rows_ref.shape[0]
    prompts = winner_ref.shape[1]
    row = lax.broadcasted_iota(jnp.int32, (tile, 1), 0) + pl.program_id(0) * tile
    slot = lax.div(row, spots_here)
    reads = (winner_ref[...] == slot) | (loser_ref[...] == slot)
    column = lax.broadcasted_iota(jnp.int32, (prompts, count), 1)
    prompt = lax.broadcasted_iota(jnp.int32, (prompts, count), 0)
    spread = jnp.where(lax.rem(column, prompts) == prompt, 1.0, 0.0).astype(jnp.bfloat16)
    reads = jnp.where(reads, 1.0, 0.0).astype(jnp.bfloat16)
    reads = jnp.dot(reads, spread, preferred_element_type=jnp.float32)
    same_spot = lax.rem(row, spots_here) == lax.div(column[0:1], prompts)
    chosen = jnp.where(same_spot, reads, 0.0).astype(jnp.bfloat16)
    out_ref[...] = jnp.dot(
        chosen, rows_ref[...], preferred_element_type=jnp.float32
    ).astype(jnp.bfloat16)


def route(projected, winner_slot, loser_slot, spots_here):
    count, span = projected.shape
    prompts = winner_slot.shape[0]
    total = 2 * prompts * spots_here
    tile = min(total, 512)
    row = pl.BlockSpec((1, prompts), lambda i: (0, 0))
    return pl.pallas_call(
        functools.partial(route_kernel, spots_here),
        grid=(total // tile,),
        in_specs=[row, row, pl.BlockSpec((count, span), lambda i: (0, 0))],
        out_specs=pl.BlockSpec((tile, span), lambda i: (i, 0)),
        out_shape=jax.ShapeDtypeStruct((total, span), jnp.bfloat16),
        compiler_params=params(32 if count > 1024 else 8),
        cost_estimate=cost(),
    )(winner_slot.reshape(1, prompts), loser_slot.reshape(1, prompts), projected)


def finish_kernel(columns, head_size, scalars, own_ref, other_ref, keys_ref, values_ref):
    devices, rows, span = own_ref.shape
    slots = keys_ref.shape[0] // 2
    each = rows // slots
    inner_width = devices // 2 * span // 2

    def emit(start):
        for side, source in enumerate((own_ref, other_ref)):
            for slot in range(slots):
                at = slice(slot * each, (slot + 1) * each)
                for core in range(2):
                    parts = [source[2 * chip + core, at, :] for chip in range(devices // 2)]
                    whole = jnp.concatenate(parts, axis=1)
                    out = side * slots + slot
                    to = slice(core * each, (core + 1) * each)
                    keys = whole[:, start : start + columns].astype(jnp.float32)
                    for pair in range(columns // LANES):
                        lanes = slice(pair * LANES, (pair + 1) * LANES)
                        keys_ref[out, to, lanes] = head_pair_norm(keys[:, lanes], head_size)
                    first = inner_width + start
                    values_ref[out, to, :] = whole[:, first : first + columns]

    pl.when(scalars[1] == 0)(lambda: emit(0))
    pl.when(scalars[1] == 1)(lambda: emit(inner_width - columns))


def finish_prompts(scalars, own, other, columns, head_size, slots):
    devices, rows, _ = own.shape
    span = 2 * rows // slots
    shape = jax.ShapeDtypeStruct((2 * slots, span, columns), jnp.bfloat16)
    return pl.pallas_call(
        functools.partial(finish_kernel, columns, head_size),
        in_specs=[smem(), vmem(), vmem()],
        out_specs=[vmem()] * 2,
        out_shape=[shape] * 2,
        compiler_params=params(16),
        cost_estimate=cost(),
    )(scalars, own, other)


def attend_kernel(
    head_size,
    spots,
    side,
    scalars,
    winner,
    loser,
    lengths,
    a_ref,
    v_ref,
    b_ref,
    pk_ref,
    pv_ref,
    out_ref,
):
    step = pl.program_id(0)
    count_here = pl.num_programs(0)
    even_group = scalars[0] == 0
    _, columns, tokens = out_ref.shape
    owner = scalars[scalars.shape[0] - 2 + side]
    slot = owner + step

    def count(p, live):
        hit = (winner[p] == slot) | (loser[p] == slot)
        return live + jnp.where(hit, lengths[p], 0)

    live = lax.fori_loop(0, winner.shape[0], count, jnp.int32(0))
    span = pk_ref.shape[1]
    row = lax.broadcasted_iota(jnp.int32, (span, 1), 0)
    rest = lax.rem(row, span // 2)
    position = (2 * lax.div(rest, spots) + lax.div(row, span // 2)) * spots + lax.rem(rest, spots)
    allowed = position < live
    low = lax.broadcasted_iota(jnp.int32, (1, LANES), 1) < head_size
    over_lanes = (((1,), (1,)), ((), ()))
    over_rows = (((0,), (0,)), ((), ()))
    scale = 1.4426950408889634 / head_size**0.5
    here = pl.ds(pl.multiple_of((side * count_here + step) * tokens, tokens), tokens)
    block = side * count_here + step
    for pair in range(columns // LANES):
        lanes = slice(pair * LANES, (pair + 1) * LANES)
        a = a_ref[here, lanes]
        b = b_ref[here, lanes]
        queries = jnp.where(even_group, a, b)
        keys = jnp.where(even_group, b, a)
        values = v_ref[here, lanes]
        prompt_keys = pk_ref[block, :, lanes]
        prompt_values = pv_ref[block, :, lanes]
        for head in range(2):
            side = low if head == 0 else jnp.logical_not(low)
            q = jnp.where(side, queries, jnp.zeros_like(queries))
            s = lax.dot_general(keys, q, over_lanes, preferred_element_type=jnp.float32)
            t = lax.dot_general(prompt_keys, q, over_lanes, preferred_element_type=jnp.float32)
            s = jnp.exp2(s * scale)
            t = jnp.where(allowed, jnp.exp2(t * scale), 0.0)
            total = jnp.sum(s, axis=0, keepdims=True) + jnp.sum(t, axis=0, keepdims=True)
            out = lax.dot_general(
                values, s.astype(jnp.bfloat16), over_rows, preferred_element_type=jnp.float32
            ) + lax.dot_general(
                prompt_values, t.astype(jnp.bfloat16), over_rows, preferred_element_type=jnp.float32
            )
            rows = slice(head * head_size, (head + 1) * head_size)
            to = slice(pair * LANES + head * head_size, pair * LANES + (head + 1) * head_size)
            out_ref[0, to, :] = (out[rows] * (1.0 / total)).astype(jnp.bfloat16)


def attend(side, scalars, routes, rows, prompt_keys, prompt_values, head_size, spots, count):
    tokens = rows[0].shape[0] // (2 * count)
    columns = rows[0].shape[1]
    return pl.pallas_call(
        functools.partial(attend_kernel, head_size, spots, side),
        grid=(count,),
        in_specs=[smem()] * 4 + [vmem()] * 5,
        out_specs=pl.BlockSpec((1, columns, tokens), lambda l: (l, 0, 0)),
        out_shape=jax.ShapeDtypeStruct((count, columns, tokens), jnp.bfloat16),
        compiler_params=params(16),
        cost_estimate=cost(),
    )(scalars, *routes, *rows, prompt_keys, prompt_values)


def ring_order(groups, chips):
    if groups == 2:
        return list(range(0, chips, 2)) + list(range(1, chips, 2))[::-1]
    return list(range(chips))


def solution(mesh):
    groups, dp = mesh.shape["groups"], mesh.shape["dp"]
    chips = dp // 2
    ring = ring_order(groups, chips)
    place = [ring.index(chip) for chip in range(chips)]
    behind_by = np.array(
        [[(place[me] - place[chip]) % chips for chip in range(chips)] for me in range(chips)],
        np.int32,
    )
    forward_pairs = [
        (2 * ring[i] + c, 2 * ring[(i + 1) % chips] + c) for i in range(chips) for c in range(2)
    ]
    backward_pairs = [(b, a) for a, b in forward_pairs]
    core_pairs = [(d, d ^ 1) for d in range(dp)]
    group_pairs = [(g, g ^ 1) for g in range(groups)]
    half_groups = [[2 * chip + c for chip in range(chips)] for c in range(2)]

    def forward(x):
        return lax.ppermute(x, "dp", forward_pairs)

    def backward(x):
        return lax.ppermute(x, "dp", backward_pairs)

    def swap_cores(x):
        return lax.ppermute(x, "dp", core_pairs)

    def swap_groups(x):
        return lax.ppermute(x, "groups", group_pairs)

    def local(
        latents,
        context,
        lengths,
        winner_slot,
        loser_slot,
        image_mod,
        context_mod,
        w_q,
        w_k,
        w_v,
        w_ck,
        w_cv,
    ):
        slot_local, token_count, width = latents.shape
        prompt_count, spot_local, _ = context.shape
        depth, inner_width = w_q.shape
        head_size = inner_width // HEADS
        columns = (HEADS + 1) // 2 * head_size
        me = lax.axis_index("dp")
        my_group = lax.axis_index("groups") % 2
        my_chip, my_core = me // 2, me % 2
        places = lax.dynamic_index_in_dim(jnp.asarray(behind_by), my_chip, 0, keepdims=False)
        first = [my_group, my_core]
        last = [me * slot_local, (me ^ 1) * slot_local]
        scalars = jnp.concatenate([jnp.stack(first), places, jnp.stack(last)]).astype(jnp.int32)

        w_cut = cut_prompt_weights(w_ck, w_cv, chips, w_q)
        w_c = lax.all_to_all(w_cut, "dp", 0, 0, axis_index_groups=half_groups, tiled=True)
        own_mixed = mix_prompts(context, context_mod, chips, 2 * columns)
        (own_mixed,) = meet([own_mixed], [w_c])
        mixed = {0: (own_mixed, 0)}
        once = [forward(own_mixed), backward(own_mixed)]
        mixed.setdefault(1 % chips, (once[0], 0))
        mixed.setdefault(-1 % chips, (once[1], 0))
        keep, give = split_weights(scalars, w_q, w_k, w_v, columns, w_cut)
        got = swap_cores(give)
        own_av = [keep[:, : 2 * columns], got[:, : 2 * columns]]
        ahead, behind = [jnp.concatenate(own_av + [x], axis=0) for x in once]

        own, *give = modulate_image(scalars, latents, image_mod, chips, ahead)

        totals = None
        enough = max(1, chips // 8)
        tokens, waiting_av, waiting_b = [], [((0,), ahead)], []
        for o in range(1, chips // 2):
            ahead, behind = meet([forward(ahead), backward(behind)], tokens)
            mixed.setdefault((o + 1) % chips, (ahead, 2 * depth))
            mixed.setdefault((-o - 1) % chips, (behind, 2 * depth))
            if o == 1:
                (w_c,) = meet([w_c], [ahead])
                w_parts = [x.reshape(width // 2, -1) for x in (w_c, swap_cores(w_c))]
            if 4 * o == chips:
                slabs = [[own], [swap_cores(x) for x in meet(give, [ahead])]]
            tokens = []
            if 2 * o + 2 == chips:
                blocks, starts = zip(*[mixed[o] for o in range(chips)])
                projected = project_prompts(scalars, blocks, starts, *w_parts, slabs[1][0])
                projected = projected.reshape(-1, projected.shape[2])
                outgoing = route(projected, winner_slot, loser_slot, chips * spot_local)
                outgoing = outgoing.reshape(dp, -1, outgoing.shape[1])
                arrived = lax.all_to_all(outgoing, "dp", 0, 0, tiled=True)
            last = 2 * o + 2 == chips
            waiting_av += [((o,), ahead), ((chips - o,), behind)]
            if last:
                picked = pick_last(2 * depth, ahead, behind, waiting_b[-1][1])
            else:
                swapped = swap_groups(pick(2 * depth, ahead, behind))
            if len(waiting_b) > 3 * enough or (last and totals is None):
                first = totals is None
                items = [((), keep), ((), got)] if first else waiting_b
                totals, token = accumulate(
                    2 * depth, totals, slabs, waiting_av, items, [outgoing] if last else []
                )
                tokens.append(token)
                waiting_av, waiting_b = [], waiting_b if first else []
            if not last:
                waiting_b.append(((o, chips - o), swapped))
                tokens.append(swapped)
        a_far, v_far = meet([forward(picked[0]), backward(picked[1])], tokens)
        o = chips // 2 - 1
        waiting_b += [((o,), forward(picked[2])), ((chips - o,), backward(picked[3]))]
        b_far = swap_groups(a_far)
        rows_a, rows_v, rows_b, features = last_products(
            2 * depth,
            head_size,
            totals,
            slabs,
            waiting_av,
            (chips // 2, a_far, v_far),
            waiting_b,
        )

        (arrived,) = meet([arrived], [rows_v])
        done_rows = (rows_a, rows_v, close(rows_b, features, b_far, head_size))

        prompt_keys, prompt_values = finish_prompts(
            scalars, arrived, swap_cores(arrived), columns, head_size, slot_local
        )

        routes = (winner_slot, loser_slot, lengths)

        def run(side):
            return attend(
                side,
                scalars,
                routes,
                done_rows,
                prompt_keys,
                prompt_values,
                head_size,
                spot_local,
                slot_local,
            )

        theirs = swap_cores(run(1))
        mine = run(0)
        return join(scalars, mine, theirs, inner_width).transpose(0, 2, 1)

    placed = (
        P(("groups", "dp"), None, None),
        P("groups", "dp", None),
        P("groups"),
        P("groups"),
        P("groups"),
        P(("groups", "dp"), None, None),
        P("groups", None, None),
        P("dp", None),
        P("dp", None),
        P("dp", None),
        P("dp", None),
        P("dp", None),
    )
    return jax.shard_map(
        local,
        mesh=mesh,
        in_specs=placed,
        out_specs=P(("groups", "dp"), None, None),
        check_vma=False,
    )
```

```python
import functools

import jax
import jax.numpy as jnp
import numpy as np
from jax import lax
from jax.experimental import pallas as pl
from jax.experimental.pallas import tpu as pltpu
from jax.sharding import PartitionSpec as P

HEADS = 19
LANES = 128


epsilon = 1e-06


def params(mib):
    return pltpu.CompilerParams(vmem_limit_bytes=mib * 2**20)


def cost(flops=1):
    return pl.CostEstimate(flops=flops, bytes_accessed=1, transcendentals=0)


def anywhere():
    return pl.BlockSpec(memory_space=pl.ANY)


def layer_norm(values, shift, scale):
    average = jnp.mean(values, axis=-1, keepdims=True)
    centered = values - average
    variance = jnp.mean(centered * centered, axis=-1, keepdims=True)
    return (centered * lax.rsqrt(variance + epsilon) * (1.0 + scale) + shift).astype(jnp.bfloat16)


def head_pair_norm(x, head_size):
    low = lax.broadcasted_iota(jnp.int32, (1, LANES), 1) < head_size
    squares = x * x
    first = jnp.sum(jnp.where(low, squares, 0.0), axis=-1, keepdims=True)
    second = jnp.sum(jnp.where(low, 0.0, squares), axis=-1, keepdims=True)
    first = lax.rsqrt(first * (1.0 / head_size) + epsilon)
    second = lax.rsqrt(second * (1.0 / head_size) + epsilon)
    return (x * jnp.where(low, first, second)).astype(jnp.bfloat16)


def vmem():
    return pl.BlockSpec(memory_space=pltpu.VMEM)


def smem():
    return pl.BlockSpec(memory_space=pltpu.SMEM)


def split_kernel(columns, scalars, q_ref, k_ref, v_ref, after_ref, keep_ref, give_ref):
    inner_width = q_ref.shape[1]

    def emit(parts, low_ref, high_ref):
        for i, part in enumerate(parts):
            at = slice(i * columns, (i + 1) * columns)
            low_ref[:, at] = part[:, :columns]
            high_ref[:, at] = part[:, inner_width - columns :]

    for group in range(2):
        parts = (q_ref, v_ref, k_ref) if group == 0 else (k_ref, v_ref, q_ref)
        for core in range(2):
            refs = (keep_ref, give_ref) if core == 0 else (give_ref, keep_ref)
            here = (scalars[0] == group) & (scalars[1] == core)
            pl.when(here)(functools.partial(emit, parts, *refs))


def split_weights(scalars, w_q, w_k, w_v, columns, after):
    depth, inner_width = w_q.shape
    shape = jax.ShapeDtypeStruct((depth, 3 * columns), jnp.bfloat16)
    whole = pl.BlockSpec((depth, inner_width), lambda i, s: (0, 0))
    out = pl.BlockSpec((depth, 3 * columns), lambda i, s: (0, 0))
    return pl.pallas_call(
        functools.partial(split_kernel, columns),
        grid_spec=pltpu.PrefetchScalarGridSpec(
            num_scalar_prefetch=1,
            grid=(1,),
            in_specs=[whole] * 3 + [anywhere()],
            out_specs=[out] * 2,
        ),
        out_shape=[shape] * 2,
        compiler_params=params(56),
        cost_estimate=cost(),
    )(scalars, w_q, w_k, w_v, after)


def mixed_kernel(chips, context_ref, mod_ref, out_ref):
    prompts, spots, width = context_ref.shape
    depth = width // (2 * chips)
    shift, scale = mod_ref[:, 0, :], mod_ref[:, 1, :]
    values = context_ref[...].astype(jnp.float32)
    for spot in range(spots):
        rows = layer_norm(values[:, spot, :], shift, scale)
        for core in range(2):
            parts = [
                rows[:, (2 * chip + core) * depth : (2 * chip + core + 1) * depth]
                for chip in range(chips)
            ]
            at = (core * spots + spot) * prompts
            parts.append(jnp.zeros((prompts, out_ref.shape[1] - width // 2), jnp.bfloat16))
            out_ref[at : at + prompts, :] = jnp.concatenate(parts, axis=1)


def mix_prompts(context, context_mod, chips, columns):
    prompts, spots, width = context.shape
    return pl.pallas_call(
        functools.partial(mixed_kernel, chips),
        grid=(1,),
        in_specs=[pl.BlockSpec(x.shape, lambda i: (0, 0, 0)) for x in (context, context_mod)],
        out_specs=pl.BlockSpec((2 * spots * prompts, columns), lambda i: (0, 0)),
        out_shape=jax.ShapeDtypeStruct((2 * spots * prompts, columns), jnp.bfloat16),
        compiler_params=params(56),
        cost_estimate=cost(),
    )(context, context_mod)


def image_kernel(chips, scalars, x_ref, mod_ref, after_ref, own_ref, give_ref):
    image = layer_norm(x_ref[0].astype(jnp.float32), mod_ref[0, 0:1, :], mod_ref[0, 1:2, :])
    depth = image.shape[1] // (2 * chips)

    def emit(first_ref, second_ref):
        for chip in range(chips):
            start = 2 * chip * depth
            straight = image[:, start : start + 2 * depth]
            turned = jnp.concatenate([straight[:, depth:], straight[:, :depth]], axis=1)
            first_ref[scalars[2 + chip], :, : 2 * depth] = straight
            second_ref[scalars[2 + chip], :, : 2 * depth] = turned

    pl.when(scalars[1] == 0)(lambda: emit(own_ref, give_ref))
    pl.when(scalars[1] == 1)(lambda: emit(give_ref, own_ref))


def modulate_image(scalars, latents, image_mod, chips, after):
    slots, tokens, width = latents.shape
    wide = -(-width // chips // LANES) * LANES
    block = (chips, tokens, wide)
    return pl.pallas_call(
        functools.partial(image_kernel, chips),
        grid_spec=pltpu.PrefetchScalarGridSpec(
            num_scalar_prefetch=1,
            grid=(slots,),
            in_specs=[
                pl.BlockSpec((1, tokens, width), lambda i, s: (i, 0, 0)),
                pl.BlockSpec((1, 2, width), lambda i, s: (i, 0, 0)),
                anywhere(),
            ],
            out_specs=[pl.BlockSpec(block, lambda i, s: (0, i, 0))] * 2,
        ),
        out_shape=[jax.ShapeDtypeStruct((chips, slots * tokens, wide), jnp.bfloat16)] * 2,
        compiler_params=params(32),
        cost_estimate=cost(),
    )(scalars, latents, image_mod, after)


def take_rows(slab, o, depth):
    return jnp.concatenate([part[o, :, :depth] for part in slab], axis=0)


def product_kernel(slots, depth, av_places, b_places, first, others, *refs):
    slabs, refs = refs[:slots], refs[slots:]
    panels = refs[: len(av_places)]
    at = len(av_places)
    pieces = refs[at : at + len(b_places) // 2 + 2 * first]
    out_av, out_b, token_ref = refs[-3:]
    totals = (None, None) if first else refs[-5 - others : -3 - others]
    rows = slabs[0].shape[1]
    columns = out_av.shape[1]
    token_ref[...] = jnp.zeros_like(token_ref)

    def product(slab, places, panel):
        features = jnp.concatenate([take_rows(slab, o, depth) for o in places], axis=1)
        return jnp.dot(features, panel, preferred_element_type=jnp.float32)

    for side, slab in enumerate((slabs[:1], slabs[1:])):
        to = slice(side * rows, (side + 1) * rows)
        if av_places:
            panel = jnp.concatenate([panel[:depth] for panel in panels], axis=0)
            sums = product(slab, av_places, panel)
            out_av[to] = sums if first else totals[0][to] + sums
        elif totals[0] is not out_av:
            out_av[to] = totals[0][to]
        sums = 0.0
        if b_places:
            panel = jnp.concatenate([piece[...] for piece in pieces[2 * first :]], axis=0)
            sums = product(slab, b_places, panel)
        if first:
            features = take_rows(slab, 0, depth)
            half = depth // 2
            for own, part in zip((slice(0, half), slice(half, depth)), pieces):
                sums = sums + jnp.dot(
                    features[:, own], part[:, columns:], preferred_element_type=jnp.float32
                )
            out_b[to] = sums
        else:
            out_b[to] = totals[1][to] + sums


def accumulate(depth, totals, slabs, av_items, b_items, others=()):
    first = totals is None
    slabs = slabs[0] + slabs[1]
    rows, columns = slabs[0].shape[1], 2 * b_items[0][1].shape[1]
    if first:
        columns = 2 * b_items[0][1].shape[1] // 3
    av_places = [o for places, _ in av_items for o in places]
    b_places = [o for places, _ in b_items for o in places]
    operands = slabs + [x for _, x in av_items] + [x for _, x in b_items]
    aliases = {}
    if not first:
        aliases = {len(operands): 0, len(operands) + 1: 1}
        operands += list(totals)
    in_specs = [vmem()] * len(operands) + [anywhere()] * len(others)
    out = pl.pallas_call(
        functools.partial(
            product_kernel, len(slabs), depth, av_places, b_places, first, len(others)
        ),
        in_specs=in_specs,
        out_specs=[vmem()] * 3,
        out_shape=[
            jax.ShapeDtypeStruct((2 * rows, columns), jnp.float32),
            jax.ShapeDtypeStruct((2 * rows, columns // 2), jnp.float32),
            jax.ShapeDtypeStruct((8, LANES), jnp.float32),
        ],
        input_output_aliases=aliases,
        compiler_params=params(20),
        cost_estimate=cost(4 * 10**10),
    )(*operands, *others)
    return out[:2], out[2]


def last_kernel(slots, depth, head_size, av_places, b_places, pieces, *refs):
    slabs, refs = refs[:slots], refs[slots:]
    count = len(av_places) - 1
    panels, (a_far, v_far) = refs[:count], refs[count : count + 2]
    swapped = refs[count + 2 : count + 2 + pieces]
    total_av, total_b, out_a, out_v, out_b, out_far = refs[-6:]
    rows, columns = slabs[0].shape[1], out_a.shape[1]

    def product(slab, places, panel):
        features = jnp.concatenate([take_rows(slab, o, depth) for o in places], axis=1)
        return jnp.dot(features, panel, preferred_element_type=jnp.float32)

    for side, slab in enumerate((slabs[:1], slabs[1:])):
        to = slice(side * rows, (side + 1) * rows)
        for half, far in enumerate((a_far, v_far)):
            lanes = slice(half * columns, (half + 1) * columns)
            parts = [panel[:depth, lanes] for panel in panels] + [far[...]]
            sums = total_av[to, lanes] + product(slab, av_places, jnp.concatenate(parts, axis=0))
            if half == 1:
                out_v[to] = sums.astype(jnp.bfloat16)
                continue
            for pair in range(columns // LANES):
                at = slice(pair * LANES, (pair + 1) * LANES)
                out_a[to, at] = head_pair_norm(sums[:, at], head_size)
        panel = jnp.concatenate([piece[...] for piece in swapped], axis=0)
        out_b[to] = total_b[to] + product(slab, b_places, panel)
        out_far[to, :depth] = take_rows(slab, av_places[-1], depth)


def last_products(depth, head_size, totals, slabs, av_items, far_items, b_items):
    slabs = slabs[0] + slabs[1]
    rows, columns = 2 * slabs[0].shape[1], totals[1].shape[1]
    av_places = [o for places, _ in av_items for o in places] + [far_items[0]]
    b_places = [o for places, _ in b_items for o in places]
    operands = slabs + [x for _, x in av_items] + list(far_items[1:])
    operands += [x for _, x in b_items] + list(totals)
    return pl.pallas_call(
        functools.partial(
            last_kernel, len(slabs), depth, head_size, av_places, b_places, len(b_items)
        ),
        in_specs=[vmem()] * len(operands),
        out_specs=[vmem()] * 4,
        out_shape=[
            jax.ShapeDtypeStruct((rows, columns), jnp.bfloat16),
            jax.ShapeDtypeStruct((rows, columns), jnp.bfloat16),
            jax.ShapeDtypeStruct((rows, columns), jnp.float32),
            jax.ShapeDtypeStruct((rows, slabs[0].shape[2]), jnp.bfloat16),
        ],
        compiler_params=params(20),
        cost_estimate=cost(4 * 10**10),
    )(*operands)


def close_kernel(head_size, total_ref, features_ref, far_ref, out_ref):
    features = features_ref[:, : far_ref.shape[0]]
    sums = jnp.dot(features, far_ref[...], preferred_element_type=jnp.float32) + total_ref[...]
    for pair in range(out_ref.shape[1] // LANES):
        lanes = slice(pair * LANES, (pair + 1) * LANES)
        out_ref[:, lanes] = head_pair_norm(sums[:, lanes], head_size)


def close(total, features, far, head_size):
    return pl.pallas_call(
        functools.partial(close_kernel, head_size),
        in_specs=[vmem()] * 3,
        out_specs=vmem(),
        out_shape=jax.ShapeDtypeStruct(total.shape, jnp.bfloat16),
        compiler_params=params(16),
        cost_estimate=cost(),
    )(total, features, far)


def meet(arrays, others):
    return pl.pallas_call(
        lambda *refs: None,
        in_specs=[anywhere()] * (len(arrays) + len(others)),
        out_specs=[anywhere()] * len(arrays),
        out_shape=[jax.ShapeDtypeStruct(x.shape, x.dtype) for x in arrays],
        input_output_aliases={i: i for i in range(len(arrays))},
        compiler_params=params(4),
        cost_estimate=cost(),
    )(*arrays, *others)


def pick_kernel(ahead_ref, behind_ref, out_ref):
    rows, columns = out_ref.shape[0] // 2, out_ref.shape[1]
    out_ref[:rows] = ahead_ref[:rows]
    out_ref[rows:] = behind_ref[:rows]


def pick(rows, ahead, behind):
    height, columns = ahead.shape[0], ahead.shape[1] // 2
    return pl.pallas_call(
        pick_kernel,
        grid=(1,),
        in_specs=[pl.BlockSpec((height, columns), lambda i: (0, 0))] * 2,
        out_specs=pl.BlockSpec((2 * rows, columns), lambda i: (0, 0)),
        out_shape=jax.ShapeDtypeStruct((2 * rows, columns), jnp.bfloat16),
        compiler_params=params(12),
        cost_estimate=cost(),
    )(ahead, behind)


def pick_last_kernel(ahead_ref, behind_ref, swapped_ref, a_ref, v_ref, ahead_b_ref, behind_b_ref):
    rows = a_ref.shape[0]
    a_ref[...] = ahead_ref[:rows]
    v_ref[...] = behind_ref[:rows]
    ahead_b_ref[...] = swapped_ref[:rows]
    behind_b_ref[...] = swapped_ref[rows:]


def pick_last(rows, ahead, behind, swapped):
    height, columns = ahead.shape[0], ahead.shape[1] // 2
    shape = (rows, columns)
    return pl.pallas_call(
        pick_last_kernel,
        grid=(1,),
        in_specs=[
            pl.BlockSpec((height, columns), lambda i: (0, 0)),
            pl.BlockSpec((height, columns), lambda i: (0, 1)),
            pl.BlockSpec((2 * rows, columns), lambda i: (0, 0)),
        ],
        out_specs=[pl.BlockSpec(shape, lambda i: (0, 0))] * 4,
        out_shape=[jax.ShapeDtypeStruct(shape, jnp.bfloat16)] * 4,
        compiler_params=params(12),
        cost_estimate=cost(),
    )(ahead, behind, swapped)


def join_kernel(scalars, mine_ref, theirs_ref, out_ref):
    columns = mine_ref.shape[1]
    shared = 2 * columns - out_ref.shape[1]

    def emit(low, high):
        out_ref[:, :columns] = low[...]
        out_ref[:, columns:] = high[:, shared:]

    pl.when(scalars[1] == 0)(lambda: emit(mine_ref, theirs_ref))
    pl.when(scalars[1] == 1)(lambda: emit(theirs_ref, mine_ref))


def join(scalars, mine, theirs, inner_width):
    slots, _, tokens = mine.shape
    return pl.pallas_call(
        join_kernel,
        in_specs=[smem(), vmem(), vmem()],
        out_specs=vmem(),
        out_shape=jax.ShapeDtypeStruct((slots, inner_width, tokens), jnp.bfloat16),
        compiler_params=params(8),
        cost_estimate=cost(),
    )(scalars, mine, theirs)


def cut_kernel(k_ref, v_ref, after_ref, out_ref):
    chips, _, span = out_ref.shape
    half = chips // 2
    for chip in range(chips):
        source = k_ref if chip < half else v_ref
        start = (chip % half) * span
        out_ref[chip] = source[:, start : start + span]


def cut_prompt_weights(w_ck, w_cv, chips, after):
    depth, inner_width = w_ck.shape
    span = 2 * inner_width // chips
    return pl.pallas_call(
        cut_kernel,
        grid=(1,),
        in_specs=[pl.BlockSpec(w_ck.shape, lambda i: (0, 0))] * 2 + [anywhere()],
        out_specs=pl.BlockSpec((chips, depth, span), lambda i: (0, 0, 0)),
        out_shape=jax.ShapeDtypeStruct((chips, depth, span), jnp.bfloat16),
        compiler_params=params(56),
        cost_estimate=cost(),
    )(w_ck, w_cv, after)


def prompt_kernel(starts, scalars, after_ref, *refs):
    chips = len(starts)
    blocks, (own_ref, other_ref, out_ref, held_ref) = refs[:chips], refs[chips:]
    depth = own_ref.shape[0]
    half = out_ref.shape[1]
    parts = [
        jnp.concatenate(
            [
                block[start + core * half : start + (core + 1) * half, :depth]
                for start, block in zip(starts, blocks)
            ],
            axis=0,
        )
        for core in range(2)
    ]

    def emit(first, second):
        product = jnp.dot(parts[0], first[...], preferred_element_type=jnp.float32) + jnp.dot(
            parts[1], second[...], preferred_element_type=jnp.float32
        )
        held_ref[...] = product.astype(jnp.bfloat16).reshape(held_ref.shape)

    pl.when(scalars[1] == 0)(lambda: emit(own_ref, other_ref))
    pl.when(scalars[1] == 1)(lambda: emit(other_ref, own_ref))
    for chip in range(chips):
        out_ref[chip] = held_ref[scalars[2 + chip]]


def project_prompts(scalars, blocks, starts, w_own, w_other, after):
    chips, span = len(blocks), w_own.shape[1]
    half = (blocks[0].shape[0] - starts[0]) // 2
    if blocks[0].shape[0] * chips > 4096:
        depth = w_own.shape[0]
        straight = scalars[1] == 0
        weights = [jnp.where(straight, w_own, w_other), jnp.where(straight, w_other, w_own)]
        product = 0.0
        for core, weight in enumerate(weights):
            rows = [
                x[start + core * half : start + (core + 1) * half, :depth]
                for start, x in zip(starts, blocks)
            ]
            rows = jnp.concatenate(rows, axis=0)
            product = product + jnp.dot(rows, weight, preferred_element_type=jnp.float32)
        product = product.astype(jnp.bfloat16).reshape(chips, half, span)
        return jnp.take(product, scalars[2 : 2 + chips], axis=0)
    return pl.pallas_call(
        functools.partial(prompt_kernel, starts),
        in_specs=[smem(), anywhere()] + [vmem()] * (chips + 2),
        out_specs=vmem(),
        out_shape=jax.ShapeDtypeStruct((chips, half, span), jnp.bfloat16),
        scratch_shapes=[pltpu.VMEM((chips, half, span), jnp.bfloat16)],
        compiler_params=params(16),
        cost_estimate=cost(),
    )(scalars, after, *blocks, w_own, w_other)


def route_kernel(spots_here, winner_ref, loser_ref, rows_ref, out_ref):
    tile, count = out_ref.shape[0], rows_ref.shape[0]
    prompts = winner_ref.shape[1]
    row = lax.broadcasted_iota(jnp.int32, (tile, 1), 0) + pl.program_id(0) * tile
    slot = lax.div(row, spots_here)
    reads = (winner_ref[...] == slot) | (loser_ref[...] == slot)
    column = lax.broadcasted_iota(jnp.int32, (prompts, count), 1)
    prompt = lax.broadcasted_iota(jnp.int32, (prompts, count), 0)
    spread = jnp.where(lax.rem(column, prompts) == prompt, 1.0, 0.0).astype(jnp.bfloat16)
    reads = jnp.where(reads, 1.0, 0.0).astype(jnp.bfloat16)
    reads = jnp.dot(reads, spread, preferred_element_type=jnp.float32)
    same_spot = lax.rem(row, spots_here) == lax.div(column[0:1], prompts)
    chosen = jnp.where(same_spot, reads, 0.0).astype(jnp.bfloat16)
    out_ref[...] = jnp.dot(
        chosen, rows_ref[...], preferred_element_type=jnp.float32
    ).astype(jnp.bfloat16)


def route(projected, winner_slot, loser_slot, spots_here):
    count, span = projected.shape
    prompts = winner_slot.shape[0]
    total = 2 * prompts * spots_here
    tile = min(total, 512)
    row = pl.BlockSpec((1, prompts), lambda i: (0, 0))
    return pl.pallas_call(
        functools.partial(route_kernel, spots_here),
        grid=(total // tile,),
        in_specs=[row, row, pl.BlockSpec((count, span), lambda i: (0, 0))],
        out_specs=pl.BlockSpec((tile, span), lambda i: (i, 0)),
        out_shape=jax.ShapeDtypeStruct((total, span), jnp.bfloat16),
        compiler_params=params(32 if count > 1024 else 8),
        cost_estimate=cost(),
    )(winner_slot.reshape(1, prompts), loser_slot.reshape(1, prompts), projected)


def finish_kernel(columns, head_size, scalars, own_ref, other_ref, keys_ref, values_ref):
    devices, rows, span = own_ref.shape
    slots = keys_ref.shape[0] // 2
    each = rows // slots
    inner_width = devices // 2 * span // 2

    def emit(start):
        for side, source in enumerate((own_ref, other_ref)):
            for slot in range(slots):
                at = slice(slot * each, (slot + 1) * each)
                for core in range(2):
                    parts = [source[2 * chip + core, at, :] for chip in range(devices // 2)]
                    whole = jnp.concatenate(parts, axis=1)
                    out = side * slots + slot
                    to = slice(core * each, (core + 1) * each)
                    keys = whole[:, start : start + columns].astype(jnp.float32)
                    for pair in range(columns // LANES):
                        lanes = slice(pair * LANES, (pair + 1) * LANES)
                        keys_ref[out, to, lanes] = head_pair_norm(keys[:, lanes], head_size)
                    first = inner_width + start
                    values_ref[out, to, :] = whole[:, first : first + columns]

    pl.when(scalars[1] == 0)(lambda: emit(0))
    pl.when(scalars[1] == 1)(lambda: emit(inner_width - columns))


def finish_prompts(scalars, own, other, columns, head_size, slots):
    devices, rows, _ = own.shape
    span = 2 * rows // slots
    shape = jax.ShapeDtypeStruct((2 * slots, span, columns), jnp.bfloat16)
    return pl.pallas_call(
        functools.partial(finish_kernel, columns, head_size),
        in_specs=[smem(), vmem(), vmem()],
        out_specs=[vmem()] * 2,
        out_shape=[shape] * 2,
        compiler_params=params(16),
        cost_estimate=cost(),
    )(scalars, own, other)


def attend_kernel(
    head_size,
    spots,
    side,
    scalars,
    winner,
    loser,
    lengths,
    a_ref,
    v_ref,
    b_ref,
    pk_ref,
    pv_ref,
    out_ref,
):
    step = pl.program_id(0)
    count_here = pl.num_programs(0)
    even_group = scalars[0] == 0
    _, columns, tokens = out_ref.shape
    owner = scalars[scalars.shape[0] - 2 + side]
    slot = owner + step

    def count(p, live):
        hit = (winner[p] == slot) | (loser[p] == slot)
        return live + jnp.where(hit, lengths[p], 0)

    live = lax.fori_loop(0, winner.shape[0], count, jnp.int32(0))
    span = pk_ref.shape[1]
    row = lax.broadcasted_iota(jnp.int32, (span, 1), 0)
    rest = lax.rem(row, span // 2)
    position = (2 * lax.div(rest, spots) + lax.div(row, span // 2)) * spots + lax.rem(rest, spots)
    allowed = position < live
    low = lax.broadcasted_iota(jnp.int32, (1, LANES), 1) < head_size
    over_lanes = (((1,), (1,)), ((), ()))
    over_rows = (((0,), (0,)), ((), ()))
    scale = 1.4426950408889634 / head_size**0.5
    here = pl.ds(pl.multiple_of((side * count_here + step) * tokens, tokens), tokens)
    block = side * count_here + step
    for pair in range(columns // LANES):
        lanes = slice(pair * LANES, (pair + 1) * LANES)
        a = a_ref[here, lanes]
        b = b_ref[here, lanes]
        queries = jnp.where(even_group, a, b)
        keys = jnp.where(even_group, b, a)
        values = v_ref[here, lanes]
        prompt_keys = pk_ref[block, :, lanes]
        prompt_values = pv_ref[block, :, lanes]
        for head in range(2):
            side = low if head == 0 else jnp.logical_not(low)
            q = jnp.where(side, queries, jnp.zeros_like(queries))
            s = lax.dot_general(keys, q, over_lanes, preferred_element_type=jnp.float32)
            t = lax.dot_general(prompt_keys, q, over_lanes, preferred_element_type=jnp.float32)
            s = jnp.exp2(s * scale)
            t = jnp.where(allowed, jnp.exp2(t * scale), 0.0)
            total = jnp.sum(s, axis=0, keepdims=True) + jnp.sum(t, axis=0, keepdims=True)
            out = lax.dot_general(
                values, s.astype(jnp.bfloat16), over_rows, preferred_element_type=jnp.float32
            ) + lax.dot_general(
                prompt_values, t.astype(jnp.bfloat16), over_rows, preferred_element_type=jnp.float32
            )
            rows = slice(head * head_size, (head + 1) * head_size)
            to = slice(pair * LANES + head * head_size, pair * LANES + (head + 1) * head_size)
            out_ref[0, to, :] = (out[rows] * (1.0 / total)).astype(jnp.bfloat16)


def attend(side, scalars, routes, rows, prompt_keys, prompt_values, head_size, spots, count):
    tokens = rows[0].shape[0] // (2 * count)
    columns = rows[0].shape[1]
    return pl.pallas_call(
        functools.partial(attend_kernel, head_size, spots, side),
        grid=(count,),
        in_specs=[smem()] * 4 + [vmem()] * 5,
        out_specs=pl.BlockSpec((1, columns, tokens), lambda l: (l, 0, 0)),
        out_shape=jax.ShapeDtypeStruct((count, columns, tokens), jnp.bfloat16),
        compiler_params=params(16),
        cost_estimate=cost(),
    )(scalars, *routes, *rows, prompt_keys, prompt_values)


def ring_order(groups, chips):
    if groups == 2:
        return list(range(0, chips, 2)) + list(range(1, chips, 2))[::-1]
    return list(range(chips))


def solution(mesh):
    groups, dp = mesh.shape["groups"], mesh.shape["dp"]
    chips = dp // 2
    ring = ring_order(groups, chips)
    place = [ring.index(chip) for chip in range(chips)]
    behind_by = np.array(
        [[(place[me] - place[chip]) % chips for chip in range(chips)] for me in range(chips)],
        np.int32,
    )
    forward_pairs = [
        (2 * ring[i] + c, 2 * ring[(i + 1) % chips] + c) for i in range(chips) for c in range(2)
    ]
    backward_pairs = [(b, a) for a, b in forward_pairs]
    core_pairs = [(d, d ^ 1) for d in range(dp)]
    group_pairs = [(g, g ^ 1) for g in range(groups)]
    half_groups = [[2 * chip + c for chip in range(chips)] for c in range(2)]

    def forward(x):
        return lax.ppermute(x, "dp", forward_pairs)

    def backward(x):
        return lax.ppermute(x, "dp", backward_pairs)

    def swap_cores(x):
        return lax.ppermute(x, "dp", core_pairs)

    def swap_groups(x):
        return lax.ppermute(x, "groups", group_pairs)

    def local(
        latents,
        context,
        lengths,
        winner_slot,
        loser_slot,
        image_mod,
        context_mod,
        w_q,
        w_k,
        w_v,
        w_ck,
        w_cv,
    ):
        slot_local, token_count, width = latents.shape
        prompt_count, spot_local, _ = context.shape
        depth, inner_width = w_q.shape
        head_size = inner_width // HEADS
        columns = (HEADS + 1) // 2 * head_size
        me = lax.axis_index("dp")
        my_group = lax.axis_index("groups") % 2
        my_chip, my_core = me // 2, me % 2
        places = lax.dynamic_index_in_dim(jnp.asarray(behind_by), my_chip, 0, keepdims=False)
        first = [my_group, my_core]
        last = [me * slot_local, (me ^ 1) * slot_local]
        scalars = jnp.concatenate([jnp.stack(first), places, jnp.stack(last)]).astype(jnp.int32)

        own_mixed = mix_prompts(context, context_mod, chips, 2 * columns)
        once = [forward(own_mixed), backward(own_mixed)]
        twice = [forward(once[0]), backward(once[1])]
        mixed = {0: (own_mixed, 0)}
        for o, arrived in ((1, once), (2, twice)):
            mixed.setdefault(o % chips, (arrived[0], 0))
            mixed.setdefault(-o % chips, (arrived[1], 0))
        keep, give = split_weights(scalars, w_q, w_k, w_v, columns, own_mixed)
        got = swap_cores(give)
        own_av = [keep[:, : 2 * columns], got[:, : 2 * columns]]
        ahead, behind = [jnp.concatenate(own_av + [x], axis=0) for x in twice]

        own, *give = modulate_image(scalars, latents, image_mod, chips, ahead)

        w_c = cut_prompt_weights(w_ck, w_cv, chips, own_mixed)
        w_c = lax.all_to_all(w_c, "dp", 0, 0, axis_index_groups=half_groups, tiled=True)

        totals = None
        enough = max(1, chips // 8)
        tokens, waiting_av, waiting_b = [w_c], [((0,), ahead)], []
        for o in range(1, chips // 2):
            ahead, behind = meet([forward(ahead), backward(behind)], tokens)
            mixed.setdefault((o + 2) % chips, (ahead, 2 * depth))
            mixed.setdefault((-o - 2) % chips, (behind, 2 * depth))
            if o == 1:
                (w_c,) = meet([w_c], [ahead])
                w_parts = [x.reshape(width // 2, -1) for x in (w_c, swap_cores(w_c))]
            if 4 * o == chips:
                slabs = [[own], [swap_cores(x) for x in meet(give, [ahead])]]
            tokens = []
            if 2 * o + 4 == chips:
                blocks, starts = zip(*[mixed[o] for o in range(chips)])
                projected = project_prompts(scalars, blocks, starts, *w_parts, slabs[1][0])
                projected = projected.reshape(-1, projected.shape[2])
                outgoing = route(projected, winner_slot, loser_slot, chips * spot_local)
                outgoing = outgoing.reshape(dp, -1, outgoing.shape[1])
                arrived = lax.all_to_all(outgoing, "dp", 0, 0, tiled=True)
            last = 2 * o + 2 == chips
            waiting_av += [((o,), ahead), ((chips - o,), behind)]
            if last:
                picked = pick_last(2 * depth, ahead, behind, waiting_b[-1][1])
            else:
                swapped = swap_groups(pick(2 * depth, ahead, behind))
            if len(waiting_b) > 3 * enough or (last and totals is None):
                first = totals is None
                items = [((), keep), ((), got)] if first else waiting_b
                totals, token = accumulate(
                    2 * depth, totals, slabs, waiting_av, items, [outgoing] if last else []
                )
                tokens.append(token)
                waiting_av, waiting_b = [], waiting_b if first else []
            if not last:
                waiting_b.append(((o, chips - o), swapped))
                tokens.append(swapped)
            if 2 * o + 4 == chips:
                tokens.append(outgoing)
        a_far, v_far = meet([forward(picked[0]), backward(picked[1])], tokens)
        o = chips // 2 - 1
        waiting_b += [((o,), forward(picked[2])), ((chips - o,), backward(picked[3]))]
        b_far = swap_groups(a_far)
        rows_a, rows_v, rows_b, features = last_products(
            2 * depth,
            head_size,
            totals,
            slabs,
            waiting_av,
            (chips // 2, a_far, v_far),
            waiting_b,
        )

        (arrived,) = meet([arrived], [rows_v])
        done_rows = (rows_a, rows_v, close(rows_b, features, b_far, head_size))

        prompt_keys, prompt_values = finish_prompts(
            scalars, arrived, swap_cores(arrived), columns, head_size, slot_local
        )

        routes = (winner_slot, loser_slot, lengths)

        def run(side):
            return attend(
                side,
                scalars,
                routes,
                done_rows,
                prompt_keys,
                prompt_values,
                head_size,
                spot_local,
                slot_local,
            )

        theirs = swap_cores(run(1))
        mine = run(0)
        return join(scalars, mine, theirs, inner_width).transpose(0, 2, 1)

    placed = (
        P(("groups", "dp"), None, None),
        P("groups", "dp", None),
        P("groups"),
        P("groups"),
        P("groups"),
        P(("groups", "dp"), None, None),
        P("groups", None, None),
        P("dp", None),
        P("dp", None),
        P("dp", None),
        P("dp", None),
        P("dp", None),
    )
    return jax.shard_map(
        local,
        mesh=mesh,
        in_specs=placed,
        out_specs=P(("groups", "dp"), None, None),
        check_vma=False,
    )
```

```python
import functools

import jax
import jax.numpy as jnp
import numpy as np
from jax import lax
from jax.experimental import pallas as pl
from jax.experimental.pallas import tpu as pltpu
from jax.sharding import PartitionSpec as P

HEADS = 19
LANES = 128


epsilon = 1e-06


def params(mib):
    return pltpu.CompilerParams(vmem_limit_bytes=mib * 2**20)


def cost(flops=1):
    return pl.CostEstimate(flops=flops, bytes_accessed=1, transcendentals=0)


def anywhere():
    return pl.BlockSpec(memory_space=pl.ANY)


def layer_norm(values, shift, scale):
    average = jnp.mean(values, axis=-1, keepdims=True)
    centered = values - average
    variance = jnp.mean(centered * centered, axis=-1, keepdims=True)
    return (centered * lax.rsqrt(variance + epsilon) * (1.0 + scale) + shift).astype(jnp.bfloat16)


def head_pair_norm(x, head_size):
    low = lax.broadcasted_iota(jnp.int32, (1, LANES), 1) < head_size
    squares = x * x
    first = jnp.sum(jnp.where(low, squares, 0.0), axis=-1, keepdims=True)
    second = jnp.sum(jnp.where(low, 0.0, squares), axis=-1, keepdims=True)
    first = lax.rsqrt(first * (1.0 / head_size) + epsilon)
    second = lax.rsqrt(second * (1.0 / head_size) + epsilon)
    return (x * jnp.where(low, first, second)).astype(jnp.bfloat16)


def vmem():
    return pl.BlockSpec(memory_space=pltpu.VMEM)


def smem():
    return pl.BlockSpec(memory_space=pltpu.SMEM)


def split_kernel(columns, scalars, q_ref, k_ref, v_ref, after_ref, keep_ref, give_ref):
    inner_width = q_ref.shape[1]

    def emit(parts, low_ref, high_ref):
        for i, part in enumerate(parts):
            at = slice(i * columns, (i + 1) * columns)
            low_ref[:, at] = part[:, :columns]
            high_ref[:, at] = part[:, inner_width - columns :]

    for group in range(2):
        parts = (q_ref, v_ref, k_ref) if group == 0 else (k_ref, v_ref, q_ref)
        for core in range(2):
            refs = (keep_ref, give_ref) if core == 0 else (give_ref, keep_ref)
            here = (scalars[0] == group) & (scalars[1] == core)
            pl.when(here)(functools.partial(emit, parts, *refs))


def split_weights(scalars, w_q, w_k, w_v, columns, after):
    depth, inner_width = w_q.shape
    shape = jax.ShapeDtypeStruct((depth, 3 * columns), jnp.bfloat16)
    whole = pl.BlockSpec((depth, inner_width), lambda i, s: (0, 0))
    out = pl.BlockSpec((depth, 3 * columns), lambda i, s: (0, 0))
    return pl.pallas_call(
        functools.partial(split_kernel, columns),
        grid_spec=pltpu.PrefetchScalarGridSpec(
            num_scalar_prefetch=1,
            grid=(1,),
            in_specs=[whole] * 3 + [anywhere()],
            out_specs=[out] * 2,
        ),
        out_shape=[shape] * 2,
        compiler_params=params(56),
        cost_estimate=cost(),
    )(scalars, w_q, w_k, w_v, after)


def mixed_kernel(chips, context_ref, mod_ref, out_ref):
    prompts, spots, width = context_ref.shape
    depth = width // (2 * chips)
    shift, scale = mod_ref[:, 0, :], mod_ref[:, 1, :]
    values = context_ref[...].astype(jnp.float32)
    for spot in range(spots):
        rows = layer_norm(values[:, spot, :], shift, scale)
        for core in range(2):
            parts = [
                rows[:, (2 * chip + core) * depth : (2 * chip + core + 1) * depth]
                for chip in range(chips)
            ]
            at = (core * spots + spot) * prompts
            parts.append(jnp.zeros((prompts, out_ref.shape[1] - width // 2), jnp.bfloat16))
            out_ref[at : at + prompts, :] = jnp.concatenate(parts, axis=1)


def mix_prompts(context, context_mod, chips, columns):
    prompts, spots, width = context.shape
    return pl.pallas_call(
        functools.partial(mixed_kernel, chips),
        grid=(1,),
        in_specs=[pl.BlockSpec(x.shape, lambda i: (0, 0, 0)) for x in (context, context_mod)],
        out_specs=pl.BlockSpec((2 * spots * prompts, columns), lambda i: (0, 0)),
        out_shape=jax.ShapeDtypeStruct((2 * spots * prompts, columns), jnp.bfloat16),
        compiler_params=params(56),
        cost_estimate=cost(),
    )(context, context_mod)


def image_kernel(chips, scalars, x_ref, mod_ref, after_ref, own_ref, give_ref):
    image = layer_norm(x_ref[0].astype(jnp.float32), mod_ref[0, 0:1, :], mod_ref[0, 1:2, :])
    depth = image.shape[1] // (2 * chips)

    def emit(first_ref, second_ref):
        for chip in range(chips):
            start = 2 * chip * depth
            straight = image[:, start : start + 2 * depth]
            turned = jnp.concatenate([straight[:, depth:], straight[:, :depth]], axis=1)
            first_ref[scalars[2 + chip], :, : 2 * depth] = straight
            second_ref[scalars[2 + chip], :, : 2 * depth] = turned

    pl.when(scalars[1] == 0)(lambda: emit(own_ref, give_ref))
    pl.when(scalars[1] == 1)(lambda: emit(give_ref, own_ref))


def modulate_image(scalars, latents, image_mod, chips, after):
    slots, tokens, width = latents.shape
    wide = -(-width // chips // LANES) * LANES
    block = (chips, tokens, wide)
    return pl.pallas_call(
        functools.partial(image_kernel, chips),
        grid_spec=pltpu.PrefetchScalarGridSpec(
            num_scalar_prefetch=1,
            grid=(slots,),
            in_specs=[
                pl.BlockSpec((1, tokens, width), lambda i, s: (i, 0, 0)),
                pl.BlockSpec((1, 2, width), lambda i, s: (i, 0, 0)),
                anywhere(),
            ],
            out_specs=[pl.BlockSpec(block, lambda i, s: (0, i, 0))] * 2,
        ),
        out_shape=[jax.ShapeDtypeStruct((chips, slots * tokens, wide), jnp.bfloat16)] * 2,
        compiler_params=params(32),
        cost_estimate=cost(),
    )(scalars, latents, image_mod, after)


def take_rows(slab, o, depth):
    return jnp.concatenate([part[o, :, :depth] for part in slab], axis=0)


def product_kernel(slots, depth, av_places, b_places, first, others, *refs):
    slabs, refs = refs[:slots], refs[slots:]
    panels = refs[: len(av_places)]
    at = len(av_places)
    pieces = refs[at : at + len(b_places) // 2 + 2 * first]
    out_av, out_b, token_ref = refs[-3:]
    totals = (None, None) if first else refs[-5 - others : -3 - others]
    rows = slabs[0].shape[1]
    columns = out_av.shape[1]
    token_ref[...] = jnp.zeros_like(token_ref)

    def product(slab, places, panel):
        features = jnp.concatenate([take_rows(slab, o, depth) for o in places], axis=1)
        return jnp.dot(features, panel, preferred_element_type=jnp.float32)

    for side, slab in enumerate((slabs[:1], slabs[1:])):
        to = slice(side * rows, (side + 1) * rows)
        if av_places:
            panel = jnp.concatenate([panel[:depth] for panel in panels], axis=0)
            sums = product(slab, av_places, panel)
            out_av[to] = sums if first else totals[0][to] + sums
        elif totals[0] is not out_av:
            out_av[to] = totals[0][to]
        sums = 0.0
        if b_places:
            panel = jnp.concatenate([piece[...] for piece in pieces[2 * first :]], axis=0)
            sums = product(slab, b_places, panel)
        if first:
            features = take_rows(slab, 0, depth)
            half = depth // 2
            for own, part in zip((slice(0, half), slice(half, depth)), pieces):
                sums = sums + jnp.dot(
                    features[:, own], part[:, columns:], preferred_element_type=jnp.float32
                )
            out_b[to] = sums
        else:
            out_b[to] = totals[1][to] + sums


def accumulate(depth, totals, slabs, av_items, b_items, others=()):
    first = totals is None
    slabs = slabs[0] + slabs[1]
    rows, columns = slabs[0].shape[1], 2 * b_items[0][1].shape[1]
    if first:
        columns = 2 * b_items[0][1].shape[1] // 3
    av_places = [o for places, _ in av_items for o in places]
    b_places = [o for places, _ in b_items for o in places]
    operands = slabs + [x for _, x in av_items] + [x for _, x in b_items]
    aliases = {}
    if not first:
        aliases = {len(operands): 0, len(operands) + 1: 1}
        operands += list(totals)
    in_specs = [vmem()] * len(operands) + [anywhere()] * len(others)
    out = pl.pallas_call(
        functools.partial(
            product_kernel, len(slabs), depth, av_places, b_places, first, len(others)
        ),
        in_specs=in_specs,
        out_specs=[vmem()] * 3,
        out_shape=[
            jax.ShapeDtypeStruct((2 * rows, columns), jnp.float32),
            jax.ShapeDtypeStruct((2 * rows, columns // 2), jnp.float32),
            jax.ShapeDtypeStruct((8, LANES), jnp.float32),
        ],
        input_output_aliases=aliases,
        compiler_params=params(20),
        cost_estimate=cost(4 * 10**10),
    )(*operands, *others)
    return out[:2], out[2]


def last_kernel(slots, depth, head_size, av_places, b_places, pieces, *refs):
    slabs, refs = refs[:slots], refs[slots:]
    count = len(av_places) - 1
    panels, (a_far, v_far) = refs[:count], refs[count : count + 2]
    swapped = refs[count + 2 : count + 2 + pieces]
    total_av, total_b, out_a, out_v, out_b, out_far = refs[-6:]
    rows, columns = slabs[0].shape[1], out_a.shape[1]

    def product(slab, places, panel):
        features = jnp.concatenate([take_rows(slab, o, depth) for o in places], axis=1)
        return jnp.dot(features, panel, preferred_element_type=jnp.float32)

    for side, slab in enumerate((slabs[:1], slabs[1:])):
        to = slice(side * rows, (side + 1) * rows)
        for half, far in enumerate((a_far, v_far)):
            lanes = slice(half * columns, (half + 1) * columns)
            parts = [panel[:depth, lanes] for panel in panels] + [far[...]]
            sums = total_av[to, lanes] + product(slab, av_places, jnp.concatenate(parts, axis=0))
            if half == 1:
                out_v[to] = sums.astype(jnp.bfloat16)
                continue
            for pair in range(columns // LANES):
                at = slice(pair * LANES, (pair + 1) * LANES)
                out_a[to, at] = head_pair_norm(sums[:, at], head_size)
        panel = jnp.concatenate([piece[...] for piece in swapped], axis=0)
        out_b[to] = total_b[to] + product(slab, b_places, panel)
        out_far[to, :depth] = take_rows(slab, av_places[-1], depth)


def last_products(depth, head_size, totals, slabs, av_items, far_items, b_items):
    slabs = slabs[0] + slabs[1]
    rows, columns = 2 * slabs[0].shape[1], totals[1].shape[1]
    av_places = [o for places, _ in av_items for o in places] + [far_items[0]]
    b_places = [o for places, _ in b_items for o in places]
    operands = slabs + [x for _, x in av_items] + list(far_items[1:])
    operands += [x for _, x in b_items] + list(totals)
    return pl.pallas_call(
        functools.partial(
            last_kernel, len(slabs), depth, head_size, av_places, b_places, len(b_items)
        ),
        in_specs=[vmem()] * len(operands),
        out_specs=[vmem()] * 4,
        out_shape=[
            jax.ShapeDtypeStruct((rows, columns), jnp.bfloat16),
            jax.ShapeDtypeStruct((rows, columns), jnp.bfloat16),
            jax.ShapeDtypeStruct((rows, columns), jnp.float32),
            jax.ShapeDtypeStruct((rows, slabs[0].shape[2]), jnp.bfloat16),
        ],
        compiler_params=params(20),
        cost_estimate=cost(4 * 10**10),
    )(*operands)


def close_kernel(head_size, total_ref, features_ref, far_ref, out_ref):
    features = features_ref[:, : far_ref.shape[0]]
    sums = jnp.dot(features, far_ref[...], preferred_element_type=jnp.float32) + total_ref[...]
    for pair in range(out_ref.shape[1] // LANES):
        lanes = slice(pair * LANES, (pair + 1) * LANES)
        out_ref[:, lanes] = head_pair_norm(sums[:, lanes], head_size)


def close(total, features, far, head_size):
    return pl.pallas_call(
        functools.partial(close_kernel, head_size),
        in_specs=[vmem()] * 3,
        out_specs=vmem(),
        out_shape=jax.ShapeDtypeStruct(total.shape, jnp.bfloat16),
        compiler_params=params(16),
        cost_estimate=cost(),
    )(total, features, far)


def meet(arrays, others):
    return pl.pallas_call(
        lambda *refs: None,
        in_specs=[anywhere()] * (len(arrays) + len(others)),
        out_specs=[anywhere()] * len(arrays),
        out_shape=[jax.ShapeDtypeStruct(x.shape, x.dtype) for x in arrays],
        input_output_aliases={i: i for i in range(len(arrays))},
        compiler_params=params(4),
        cost_estimate=cost(),
    )(*arrays, *others)


def pick_kernel(ahead_ref, behind_ref, out_ref):
    rows, columns = out_ref.shape[0] // 2, out_ref.shape[1]
    out_ref[:rows] = ahead_ref[:rows]
    out_ref[rows:] = behind_ref[:rows]


def pick(rows, ahead, behind):
    height, columns = ahead.shape[0], ahead.shape[1] // 2
    return pl.pallas_call(
        pick_kernel,
        grid=(1,),
        in_specs=[pl.BlockSpec((height, columns), lambda i: (0, 0))] * 2,
        out_specs=pl.BlockSpec((2 * rows, columns), lambda i: (0, 0)),
        out_shape=jax.ShapeDtypeStruct((2 * rows, columns), jnp.bfloat16),
        compiler_params=params(12),
        cost_estimate=cost(),
    )(ahead, behind)


def pick_last_kernel(ahead_ref, behind_ref, swapped_ref, a_ref, v_ref, ahead_b_ref, behind_b_ref):
    rows = a_ref.shape[0]
    a_ref[...] = ahead_ref[:rows]
    v_ref[...] = behind_ref[:rows]
    ahead_b_ref[...] = swapped_ref[:rows]
    behind_b_ref[...] = swapped_ref[rows:]


def pick_last(rows, ahead, behind, swapped):
    height, columns = ahead.shape[0], ahead.shape[1] // 2
    shape = (rows, columns)
    return pl.pallas_call(
        pick_last_kernel,
        grid=(1,),
        in_specs=[
            pl.BlockSpec((height, columns), lambda i: (0, 0)),
            pl.BlockSpec((height, columns), lambda i: (0, 1)),
            pl.BlockSpec((2 * rows, columns), lambda i: (0, 0)),
        ],
        out_specs=[pl.BlockSpec(shape, lambda i: (0, 0))] * 4,
        out_shape=[jax.ShapeDtypeStruct(shape, jnp.bfloat16)] * 4,
        compiler_params=params(12),
        cost_estimate=cost(),
    )(ahead, behind, swapped)


def join_kernel(scalars, mine_ref, theirs_ref, out_ref):
    columns = mine_ref.shape[1]
    shared = 2 * columns - out_ref.shape[1]

    def emit(low, high):
        out_ref[:, :columns] = low[...]
        out_ref[:, columns:] = high[:, shared:]

    pl.when(scalars[1] == 0)(lambda: emit(mine_ref, theirs_ref))
    pl.when(scalars[1] == 1)(lambda: emit(theirs_ref, mine_ref))


def join(scalars, mine, theirs, inner_width):
    slots, _, tokens = mine.shape
    return pl.pallas_call(
        join_kernel,
        in_specs=[smem(), vmem(), vmem()],
        out_specs=vmem(),
        out_shape=jax.ShapeDtypeStruct((slots, inner_width, tokens), jnp.bfloat16),
        compiler_params=params(8),
        cost_estimate=cost(),
    )(scalars, mine, theirs)


def cut_kernel(k_ref, v_ref, after_ref, out_ref):
    chips, _, span = out_ref.shape
    half = chips // 2
    for chip in range(chips):
        source = k_ref if chip < half else v_ref
        start = (chip % half) * span
        out_ref[chip] = source[:, start : start + span]


def cut_prompt_weights(w_ck, w_cv, chips, after):
    depth, inner_width = w_ck.shape
    span = 2 * inner_width // chips
    return pl.pallas_call(
        cut_kernel,
        grid=(1,),
        in_specs=[pl.BlockSpec(w_ck.shape, lambda i: (0, 0))] * 2 + [anywhere()],
        out_specs=pl.BlockSpec((chips, depth, span), lambda i: (0, 0, 0)),
        out_shape=jax.ShapeDtypeStruct((chips, depth, span), jnp.bfloat16),
        compiler_params=params(56),
        cost_estimate=cost(),
    )(w_ck, w_cv, after)


def prompt_kernel(starts, scalars, after_ref, *refs):
    chips = len(starts)
    blocks, (own_ref, other_ref, out_ref, held_ref) = refs[:chips], refs[chips:]
    depth = own_ref.shape[0]
    half = out_ref.shape[1]
    parts = [
        jnp.concatenate(
            [
                block[start + core * half : start + (core + 1) * half, :depth]
                for start, block in zip(starts, blocks)
            ],
            axis=0,
        )
        for core in range(2)
    ]

    def emit(first, second):
        product = jnp.dot(parts[0], first[...], preferred_element_type=jnp.float32) + jnp.dot(
            parts[1], second[...], preferred_element_type=jnp.float32
        )
        held_ref[...] = product.astype(jnp.bfloat16).reshape(held_ref.shape)

    pl.when(scalars[1] == 0)(lambda: emit(own_ref, other_ref))
    pl.when(scalars[1] == 1)(lambda: emit(other_ref, own_ref))
    for chip in range(chips):
        out_ref[chip] = held_ref[scalars[2 + chip]]


def project_prompts(scalars, blocks, starts, w_own, w_other, after):
    chips, span = len(blocks), w_own.shape[1]
    half = (blocks[0].shape[0] - starts[0]) // 2
    if blocks[0].shape[0] * chips > 4096:
        depth = w_own.shape[0]
        straight = scalars[1] == 0
        weights = [jnp.where(straight, w_own, w_other), jnp.where(straight, w_other, w_own)]
        product = 0.0
        for core, weight in enumerate(weights):
            rows = [
                x[start + core * half : start + (core + 1) * half, :depth]
                for start, x in zip(starts, blocks)
            ]
            rows = jnp.concatenate(rows, axis=0)
            product = product + jnp.dot(rows, weight, preferred_element_type=jnp.float32)
        product = product.astype(jnp.bfloat16).reshape(chips, half, span)
        return jnp.take(product, scalars[2 : 2 + chips], axis=0)
    return pl.pallas_call(
        functools.partial(prompt_kernel, starts),
        in_specs=[smem(), anywhere()] + [vmem()] * (chips + 2),
        out_specs=vmem(),
        out_shape=jax.ShapeDtypeStruct((chips, half, span), jnp.bfloat16),
        scratch_shapes=[pltpu.VMEM((chips, half, span), jnp.bfloat16)],
        compiler_params=params(16),
        cost_estimate=cost(),
    )(scalars, after, *blocks, w_own, w_other)


def route_kernel(spots_here, winner_ref, loser_ref, rows_ref, out_ref):
    tile, count = out_ref.shape[0], rows_ref.shape[0]
    prompts = winner_ref.shape[1]
    row = lax.broadcasted_iota(jnp.int32, (tile, 1), 0) + pl.program_id(0) * tile
    slot = lax.div(row, spots_here)
    reads = (winner_ref[...] == slot) | (loser_ref[...] == slot)
    column = lax.broadcasted_iota(jnp.int32, (prompts, count), 1)
    prompt = lax.broadcasted_iota(jnp.int32, (prompts, count), 0)
    spread = jnp.where(lax.rem(column, prompts) == prompt, 1.0, 0.0).astype(jnp.bfloat16)
    reads = jnp.where(reads, 1.0, 0.0).astype(jnp.bfloat16)
    reads = jnp.dot(reads, spread, preferred_element_type=jnp.float32)
    same_spot = lax.rem(row, spots_here) == lax.div(column[0:1], prompts)
    chosen = jnp.where(same_spot, reads, 0.0).astype(jnp.bfloat16)
    out_ref[...] = jnp.dot(
        chosen, rows_ref[...], preferred_element_type=jnp.float32
    ).astype(jnp.bfloat16)


def route(projected, winner_slot, loser_slot, spots_here):
    count, span = projected.shape
    prompts = winner_slot.shape[0]
    total = 2 * prompts * spots_here
    tile = min(total, 512)
    row = pl.BlockSpec((1, prompts), lambda i: (0, 0))
    return pl.pallas_call(
        functools.partial(route_kernel, spots_here),
        grid=(total // tile,),
        in_specs=[row, row, pl.BlockSpec((count, span), lambda i: (0, 0))],
        out_specs=pl.BlockSpec((tile, span), lambda i: (i, 0)),
        out_shape=jax.ShapeDtypeStruct((total, span), jnp.bfloat16),
        compiler_params=params(32 if count > 1024 else 8),
        cost_estimate=cost(),
    )(winner_slot.reshape(1, prompts), loser_slot.reshape(1, prompts), projected)


def side_by_side(parts, start, count):
    span = parts[0].shape[1]
    taken = []
    for i, part in enumerate(parts):
        low, high = max(start - i * span, 0), min(start + count - i * span, span)
        if low < high:
            taken.append(part[:, low:high])
    return jnp.concatenate(taken, axis=1)


def finish_kernel(columns, head_size, scalars, own_ref, other_ref, keys_ref, values_ref):
    devices, rows, span = own_ref.shape
    slots = keys_ref.shape[0] // 2
    each = rows // slots
    inner_width = devices // 2 * span // 2

    def emit(start):
        for side, source in enumerate((own_ref, other_ref)):
            for slot in range(slots):
                at = slice(slot * each, (slot + 1) * each)
                for core in range(2):
                    parts = [source[2 * chip + core, at, :] for chip in range(devices // 2)]
                    out = side * slots + slot
                    to = slice(core * each, (core + 1) * each)
                    keys = side_by_side(parts, start, columns).astype(jnp.float32)
                    for pair in range(columns // LANES):
                        lanes = slice(pair * LANES, (pair + 1) * LANES)
                        keys_ref[out, to, lanes] = head_pair_norm(keys[:, lanes], head_size)
                    first = inner_width + start
                    values_ref[out, to, :] = side_by_side(parts, first, columns)

    pl.when(scalars[1] == 0)(lambda: emit(0))
    pl.when(scalars[1] == 1)(lambda: emit(inner_width - columns))


def finish_prompts(scalars, own, other, columns, head_size, slots):
    devices, rows, _ = own.shape
    span = 2 * rows // slots
    shape = jax.ShapeDtypeStruct((2 * slots, span, columns), jnp.bfloat16)
    return pl.pallas_call(
        functools.partial(finish_kernel, columns, head_size),
        in_specs=[smem(), vmem(), vmem()],
        out_specs=[vmem()] * 2,
        out_shape=[shape] * 2,
        compiler_params=params(16),
        cost_estimate=cost(),
    )(scalars, own, other)


def attend_kernel(
    head_size,
    spots,
    side,
    scalars,
    winner,
    loser,
    lengths,
    a_ref,
    v_ref,
    b_ref,
    pk_ref,
    pv_ref,
    out_ref,
):
    step = pl.program_id(0)
    count_here = pl.num_programs(0)
    even_group = scalars[0] == 0
    _, columns, tokens = out_ref.shape
    owner = scalars[scalars.shape[0] - 2 + side]
    slot = owner + step

    def count(p, live):
        hit = (winner[p] == slot) | (loser[p] == slot)
        return live + jnp.where(hit, lengths[p], 0)

    live = lax.fori_loop(0, winner.shape[0], count, jnp.int32(0))
    span = pk_ref.shape[1]
    row = lax.broadcasted_iota(jnp.int32, (span, 1), 0)
    rest = lax.rem(row, span // 2)
    position = (2 * lax.div(rest, spots) + lax.div(row, span // 2)) * spots + lax.rem(rest, spots)
    allowed = position < live
    low = lax.broadcasted_iota(jnp.int32, (1, LANES), 1) < head_size
    over_lanes = (((1,), (1,)), ((), ()))
    over_rows = (((0,), (0,)), ((), ()))
    scale = 1.4426950408889634 / head_size**0.5
    here = pl.ds(pl.multiple_of((side * count_here + step) * tokens, tokens), tokens)
    block = side * count_here + step
    for pair in range(columns // LANES):
        lanes = slice(pair * LANES, (pair + 1) * LANES)
        a = a_ref[here, lanes]
        b = b_ref[here, lanes]
        queries = jnp.where(even_group, a, b)
        keys = jnp.where(even_group, b, a)
        values = v_ref[here, lanes]
        prompt_keys = pk_ref[block, :, lanes]
        prompt_values = pv_ref[block, :, lanes]
        for head in range(2):
            side = low if head == 0 else jnp.logical_not(low)
            q = jnp.where(side, queries, jnp.zeros_like(queries))
            s = lax.dot_general(keys, q, over_lanes, preferred_element_type=jnp.float32)
            t = lax.dot_general(prompt_keys, q, over_lanes, preferred_element_type=jnp.float32)
            s = jnp.exp2(s * scale)
            t = jnp.where(allowed, jnp.exp2(t * scale), 0.0)
            total = jnp.sum(s, axis=0, keepdims=True) + jnp.sum(t, axis=0, keepdims=True)
            out = lax.dot_general(
                values, s.astype(jnp.bfloat16), over_rows, preferred_element_type=jnp.float32
            ) + lax.dot_general(
                prompt_values, t.astype(jnp.bfloat16), over_rows, preferred_element_type=jnp.float32
            )
            rows = slice(head * head_size, (head + 1) * head_size)
            to = slice(pair * LANES + head * head_size, pair * LANES + (head + 1) * head_size)
            out_ref[0, to, :] = (out[rows] * (1.0 / total)).astype(jnp.bfloat16)


def attend(side, scalars, routes, rows, prompt_keys, prompt_values, head_size, spots, count):
    tokens = rows[0].shape[0] // (2 * count)
    columns = rows[0].shape[1]
    return pl.pallas_call(
        functools.partial(attend_kernel, head_size, spots, side),
        grid=(count,),
        in_specs=[smem()] * 4 + [vmem()] * 5,
        out_specs=pl.BlockSpec((1, columns, tokens), lambda l: (l, 0, 0)),
        out_shape=jax.ShapeDtypeStruct((count, columns, tokens), jnp.bfloat16),
        compiler_params=params(16),
        cost_estimate=cost(),
    )(scalars, *routes, *rows, prompt_keys, prompt_values)


def ring_order(groups, chips):
    if groups == 2:
        return list(range(0, chips, 2)) + list(range(1, chips, 2))[::-1]
    return list(range(chips))


def solution(mesh):
    groups, dp = mesh.shape["groups"], mesh.shape["dp"]
    chips = dp // 2
    ring = ring_order(groups, chips)
    place = [ring.index(chip) for chip in range(chips)]
    behind_by = np.array(
        [[(place[me] - place[chip]) % chips for chip in range(chips)] for me in range(chips)],
        np.int32,
    )
    forward_pairs = [
        (2 * ring[i] + c, 2 * ring[(i + 1) % chips] + c) for i in range(chips) for c in range(2)
    ]
    backward_pairs = [(b, a) for a, b in forward_pairs]
    core_pairs = [(d, d ^ 1) for d in range(dp)]
    group_pairs = [(g, g ^ 1) for g in range(groups)]
    half_groups = [[2 * chip + c for chip in range(chips)] for c in range(2)]

    def forward(x):
        return lax.ppermute(x, "dp", forward_pairs)

    def backward(x):
        return lax.ppermute(x, "dp", backward_pairs)

    def swap_cores(x):
        return lax.ppermute(x, "dp", core_pairs)

    def swap_groups(x):
        return lax.ppermute(x, "groups", group_pairs)

    def local(
        latents,
        context,
        lengths,
        winner_slot,
        loser_slot,
        image_mod,
        context_mod,
        w_q,
        w_k,
        w_v,
        w_ck,
        w_cv,
    ):
        slot_local, token_count, width = latents.shape
        prompt_count, spot_local, _ = context.shape
        depth, inner_width = w_q.shape
        head_size = inner_width // HEADS
        columns = (HEADS + 1) // 2 * head_size
        me = lax.axis_index("dp")
        my_group = lax.axis_index("groups") % 2
        my_chip, my_core = me // 2, me % 2
        places = lax.dynamic_index_in_dim(jnp.asarray(behind_by), my_chip, 0, keepdims=False)
        first = [my_group, my_core]
        last = [me * slot_local, (me ^ 1) * slot_local]
        scalars = jnp.concatenate([jnp.stack(first), places, jnp.stack(last)]).astype(jnp.int32)

        own_mixed = mix_prompts(context, context_mod, chips, 2 * columns)
        once = [forward(own_mixed), backward(own_mixed)]
        twice = [forward(once[0]), backward(once[1])]
        mixed = {0: (own_mixed, 0)}
        for o, arrived in ((1, once), (2, twice)):
            mixed.setdefault(o % chips, (arrived[0], 0))
            mixed.setdefault(-o % chips, (arrived[1], 0))
        keep, give = split_weights(scalars, w_q, w_k, w_v, columns, own_mixed)
        got = swap_cores(give)
        own_av = [keep[:, : 2 * columns], got[:, : 2 * columns]]
        ahead, behind = [jnp.concatenate(own_av + [x], axis=0) for x in twice]

        own, *give = modulate_image(scalars, latents, image_mod, chips, ahead)

        w_c = cut_prompt_weights(w_ck, w_cv, chips, own_mixed)
        w_c = lax.all_to_all(w_c, "dp", 0, 0, axis_index_groups=half_groups, tiled=True)

        totals = None
        enough = max(1, chips // 8)
        tokens, waiting_av, waiting_b = [w_c], [((0,), ahead)], []
        for o in range(1, chips // 2):
            ahead, behind = meet([forward(ahead), backward(behind)], tokens)
            mixed.setdefault((o + 2) % chips, (ahead, 2 * depth))
            mixed.setdefault((-o - 2) % chips, (behind, 2 * depth))
            if o == 1:
                (w_c,) = meet([w_c], [ahead])
                w_parts = [x.reshape(width // 2, -1) for x in (w_c, swap_cores(w_c))]
            if 4 * o == chips:
                slabs = [[own], [swap_cores(x) for x in meet(give, [ahead])]]
            tokens = []
            if 2 * o + 4 == chips:
                blocks, starts = zip(*[mixed[o] for o in range(chips)])
                projected = project_prompts(scalars, blocks, starts, *w_parts, slabs[1][0])
                projected = projected.reshape(-1, projected.shape[2])
                outgoing = route(projected, winner_slot, loser_slot, chips * spot_local)
                outgoing = outgoing.reshape(dp, -1, outgoing.shape[1])
                arrived = lax.all_to_all(outgoing, "dp", 0, 0, tiled=True)
            last = 2 * o + 2 == chips
            waiting_av += [((o,), ahead), ((chips - o,), behind)]
            if last:
                picked = pick_last(2 * depth, ahead, behind, waiting_b[-1][1])
            else:
                swapped = swap_groups(pick(2 * depth, ahead, behind))
            if len(waiting_b) > 3 * enough or (last and totals is None):
                first = totals is None
                items = [((), keep), ((), got)] if first else waiting_b
                totals, token = accumulate(
                    2 * depth, totals, slabs, waiting_av, items, [outgoing] if last else []
                )
                tokens.append(token)
                waiting_av, waiting_b = [], waiting_b if first else []
            if not last:
                waiting_b.append(((o, chips - o), swapped))
                tokens.append(swapped)
            if 2 * o + 4 == chips:
                tokens.append(outgoing)
        a_far, v_far = meet([forward(picked[0]), backward(picked[1])], tokens)
        o = chips // 2 - 1
        waiting_b += [((o,), forward(picked[2])), ((chips - o,), backward(picked[3]))]
        b_far = swap_groups(a_far)
        rows_a, rows_v, rows_b, features = last_products(
            2 * depth,
            head_size,
            totals,
            slabs,
            waiting_av,
            (chips // 2, a_far, v_far),
            waiting_b,
        )

        (arrived,) = meet([arrived], [rows_v])
        done_rows = (rows_a, rows_v, close(rows_b, features, b_far, head_size))

        prompt_keys, prompt_values = finish_prompts(
            scalars, arrived, swap_cores(arrived), columns, head_size, slot_local
        )

        routes = (winner_slot, loser_slot, lengths)

        def run(side):
            return attend(
                side,
                scalars,
                routes,
                done_rows,
                prompt_keys,
                prompt_values,
                head_size,
                spot_local,
                slot_local,
            )

        theirs = swap_cores(run(1))
        mine = run(0)
        return join(scalars, mine, theirs, inner_width).transpose(0, 2, 1)

    placed = (
        P(("groups", "dp"), None, None),
        P("groups", "dp", None),
        P("groups"),
        P("groups"),
        P("groups"),
        P(("groups", "dp"), None, None),
        P("groups", None, None),
        P("dp", None),
        P("dp", None),
        P("dp", None),
        P("dp", None),
        P("dp", None),
    )
    return jax.shard_map(
        local,
        mesh=mesh,
        in_specs=placed,
        out_specs=P(("groups", "dp"), None, None),
        check_vma=False,
    )
```

```python
import functools

import jax
import jax.numpy as jnp
import numpy as np
from jax import lax
from jax.experimental import pallas as pl
from jax.experimental.pallas import tpu as pltpu
from jax.sharding import PartitionSpec as P

HEADS = 19
LANES = 128


epsilon = 1e-06


def params(mib):
    return pltpu.CompilerParams(vmem_limit_bytes=mib * 2**20)


def cost(flops=1):
    return pl.CostEstimate(flops=flops, bytes_accessed=1, transcendentals=0)


def anywhere():
    return pl.BlockSpec(memory_space=pl.ANY)


def layer_norm(values, shift, scale):
    average = jnp.mean(values, axis=-1, keepdims=True)
    centered = values - average
    variance = jnp.mean(centered * centered, axis=-1, keepdims=True)
    return (centered * lax.rsqrt(variance + epsilon) * (1.0 + scale) + shift).astype(jnp.bfloat16)


def head_pair_norm(x, head_size):
    low = lax.broadcasted_iota(jnp.int32, (1, LANES), 1) < head_size
    squares = x * x
    first = jnp.sum(jnp.where(low, squares, 0.0), axis=-1, keepdims=True)
    second = jnp.sum(jnp.where(low, 0.0, squares), axis=-1, keepdims=True)
    first = lax.rsqrt(first * (1.0 / head_size) + epsilon)
    second = lax.rsqrt(second * (1.0 / head_size) + epsilon)
    return (x * jnp.where(low, first, second)).astype(jnp.bfloat16)


def vmem():
    return pl.BlockSpec(memory_space=pltpu.VMEM)


def smem():
    return pl.BlockSpec(memory_space=pltpu.SMEM)


def split_kernel(columns, scalars, q_ref, k_ref, v_ref, after_ref, keep_ref, give_ref):
    inner_width = q_ref.shape[1]

    def emit(parts, low_ref, high_ref):
        for i, part in enumerate(parts):
            at = slice(i * columns, (i + 1) * columns)
            low_ref[:, at] = part[:, :columns]
            high_ref[:, at] = part[:, inner_width - columns :]

    for group in range(2):
        parts = (q_ref, v_ref, k_ref) if group == 0 else (k_ref, v_ref, q_ref)
        for core in range(2):
            refs = (keep_ref, give_ref) if core == 0 else (give_ref, keep_ref)
            here = (scalars[0] == group) & (scalars[1] == core)
            pl.when(here)(functools.partial(emit, parts, *refs))


def split_weights(scalars, w_q, w_k, w_v, columns, after):
    depth, inner_width = w_q.shape
    shape = jax.ShapeDtypeStruct((depth, 3 * columns), jnp.bfloat16)
    whole = pl.BlockSpec((depth, inner_width), lambda i, s: (0, 0))
    out = pl.BlockSpec((depth, 3 * columns), lambda i, s: (0, 0))
    return pl.pallas_call(
        functools.partial(split_kernel, columns),
        grid_spec=pltpu.PrefetchScalarGridSpec(
            num_scalar_prefetch=1,
            grid=(1,),
            in_specs=[whole] * 3 + [anywhere()],
            out_specs=[out] * 2,
        ),
        out_shape=[shape] * 2,
        compiler_params=params(56),
        cost_estimate=cost(),
    )(scalars, w_q, w_k, w_v, after)


def mixed_kernel(chips, context_ref, mod_ref, out_ref):
    prompts, spots, width = context_ref.shape
    depth = width // (2 * chips)
    shift, scale = mod_ref[:, 0, :], mod_ref[:, 1, :]
    values = context_ref[...].astype(jnp.float32)
    for spot in range(spots):
        rows = layer_norm(values[:, spot, :], shift, scale)
        for core in range(2):
            parts = [
                rows[:, (2 * chip + core) * depth : (2 * chip + core + 1) * depth]
                for chip in range(chips)
            ]
            at = (core * spots + spot) * prompts
            parts.append(jnp.zeros((prompts, out_ref.shape[1] - width // 2), jnp.bfloat16))
            out_ref[at : at + prompts, :] = jnp.concatenate(parts, axis=1)


def mix_prompts(context, context_mod, chips, columns):
    prompts, spots, width = context.shape
    return pl.pallas_call(
        functools.partial(mixed_kernel, chips),
        grid=(1,),
        in_specs=[pl.BlockSpec(x.shape, lambda i: (0, 0, 0)) for x in (context, context_mod)],
        out_specs=pl.BlockSpec((2 * spots * prompts, columns), lambda i: (0, 0)),
        out_shape=jax.ShapeDtypeStruct((2 * spots * prompts, columns), jnp.bfloat16),
        compiler_params=params(56),
        cost_estimate=cost(),
    )(context, context_mod)


def image_kernel(chips, scalars, x_ref, mod_ref, after_ref, own_ref, give_ref):
    image = layer_norm(x_ref[0].astype(jnp.float32), mod_ref[0, 0:1, :], mod_ref[0, 1:2, :])
    depth = image.shape[1] // (2 * chips)

    def emit(first_ref, second_ref):
        for chip in range(chips):
            start = 2 * chip * depth
            straight = image[:, start : start + 2 * depth]
            turned = jnp.concatenate([straight[:, depth:], straight[:, :depth]], axis=1)
            first_ref[scalars[2 + chip], :, : 2 * depth] = straight
            second_ref[scalars[2 + chip], :, : 2 * depth] = turned

    pl.when(scalars[1] == 0)(lambda: emit(own_ref, give_ref))
    pl.when(scalars[1] == 1)(lambda: emit(give_ref, own_ref))


def modulate_image(scalars, latents, image_mod, chips, after):
    slots, tokens, width = latents.shape
    wide = -(-width // chips // LANES) * LANES
    block = (chips, tokens, wide)
    return pl.pallas_call(
        functools.partial(image_kernel, chips),
        grid_spec=pltpu.PrefetchScalarGridSpec(
            num_scalar_prefetch=1,
            grid=(slots,),
            in_specs=[
                pl.BlockSpec((1, tokens, width), lambda i, s: (i, 0, 0)),
                pl.BlockSpec((1, 2, width), lambda i, s: (i, 0, 0)),
                anywhere(),
            ],
            out_specs=[pl.BlockSpec(block, lambda i, s: (0, i, 0))] * 2,
        ),
        out_shape=[jax.ShapeDtypeStruct((chips, slots * tokens, wide), jnp.bfloat16)] * 2,
        compiler_params=params(32),
        cost_estimate=cost(),
    )(scalars, latents, image_mod, after)


def take_rows(slab, o, depth):
    return jnp.concatenate([part[o, :, :depth] for part in slab], axis=0)


def product_kernel(slots, depth, av_places, b_places, first, others, *refs):
    slabs, refs = refs[:slots], refs[slots:]
    panels = refs[: len(av_places)]
    at = len(av_places)
    pieces = refs[at : at + len(b_places) // 2 + 2 * first]
    out_av, out_b, token_ref = refs[-3:]
    totals = (None, None) if first else refs[-5 - others : -3 - others]
    rows = slabs[0].shape[1]
    columns = out_av.shape[1]
    token_ref[...] = jnp.zeros_like(token_ref)

    def product(slab, places, panel):
        features = jnp.concatenate([take_rows(slab, o, depth) for o in places], axis=1)
        return jnp.dot(features, panel, preferred_element_type=jnp.float32)

    for side, slab in enumerate((slabs[:1], slabs[1:])):
        to = slice(side * rows, (side + 1) * rows)
        if av_places:
            panel = jnp.concatenate([panel[:depth] for panel in panels], axis=0)
            sums = product(slab, av_places, panel)
            out_av[to] = sums if first else totals[0][to] + sums
        elif totals[0] is not out_av:
            out_av[to] = totals[0][to]
        sums = 0.0
        if b_places:
            panel = jnp.concatenate([piece[...] for piece in pieces[2 * first :]], axis=0)
            sums = product(slab, b_places, panel)
        if first:
            features = take_rows(slab, 0, depth)
            half = depth // 2
            for own, part in zip((slice(0, half), slice(half, depth)), pieces):
                sums = sums + jnp.dot(
                    features[:, own], part[:, columns:], preferred_element_type=jnp.float32
                )
            out_b[to] = sums
        else:
            out_b[to] = totals[1][to] + sums


def accumulate(depth, totals, slabs, av_items, b_items, others=()):
    first = totals is None
    slabs = slabs[0] + slabs[1]
    rows, columns = slabs[0].shape[1], 2 * b_items[0][1].shape[1]
    if first:
        columns = 2 * b_items[0][1].shape[1] // 3
    av_places = [o for places, _ in av_items for o in places]
    b_places = [o for places, _ in b_items for o in places]
    operands = slabs + [x for _, x in av_items] + [x for _, x in b_items]
    aliases = {}
    if not first:
        aliases = {len(operands): 0, len(operands) + 1: 1}
        operands += list(totals)
    in_specs = [vmem()] * len(operands) + [anywhere()] * len(others)
    out = pl.pallas_call(
        functools.partial(
            product_kernel, len(slabs), depth, av_places, b_places, first, len(others)
        ),
        in_specs=in_specs,
        out_specs=[vmem()] * 3,
        out_shape=[
            jax.ShapeDtypeStruct((2 * rows, columns), jnp.float32),
            jax.ShapeDtypeStruct((2 * rows, columns // 2), jnp.float32),
            jax.ShapeDtypeStruct((8, LANES), jnp.float32),
        ],
        input_output_aliases=aliases,
        compiler_params=params(20),
        cost_estimate=cost(4 * 10**10),
    )(*operands, *others)
    return out[:2], out[2]


def last_kernel(slots, depth, head_size, av_places, b_places, pieces, *refs):
    slabs, refs = refs[:slots], refs[slots:]
    count = len(av_places) - 1
    panels, (a_far, v_far) = refs[:count], refs[count : count + 2]
    swapped = refs[count + 2 : count + 2 + pieces]
    total_av, total_b, out_a, out_v, out_b, out_far = refs[-6:]
    rows, columns = slabs[0].shape[1], out_a.shape[1]

    def product(slab, places, panel):
        features = jnp.concatenate([take_rows(slab, o, depth) for o in places], axis=1)
        return jnp.dot(features, panel, preferred_element_type=jnp.float32)

    for side, slab in enumerate((slabs[:1], slabs[1:])):
        to = slice(side * rows, (side + 1) * rows)
        for half, far in enumerate((a_far, v_far)):
            lanes = slice(half * columns, (half + 1) * columns)
            parts = [panel[:depth, lanes] for panel in panels] + [far[...]]
            sums = total_av[to, lanes] + product(slab, av_places, jnp.concatenate(parts, axis=0))
            if half == 1:
                out_v[to] = sums.astype(jnp.bfloat16)
                continue
            for pair in range(columns // LANES):
                at = slice(pair * LANES, (pair + 1) * LANES)
                out_a[to, at] = head_pair_norm(sums[:, at], head_size)
        panel = jnp.concatenate([piece[...] for piece in swapped], axis=0)
        out_b[to] = total_b[to] + product(slab, b_places, panel)
        out_far[to, :depth] = take_rows(slab, av_places[-1], depth)


def last_products(depth, head_size, totals, slabs, av_items, far_items, b_items):
    slabs = slabs[0] + slabs[1]
    rows, columns = 2 * slabs[0].shape[1], totals[1].shape[1]
    av_places = [o for places, _ in av_items for o in places] + [far_items[0]]
    b_places = [o for places, _ in b_items for o in places]
    operands = slabs + [x for _, x in av_items] + list(far_items[1:])
    operands += [x for _, x in b_items] + list(totals)
    return pl.pallas_call(
        functools.partial(
            last_kernel, len(slabs), depth, head_size, av_places, b_places, len(b_items)
        ),
        in_specs=[vmem()] * len(operands),
        out_specs=[vmem()] * 4,
        out_shape=[
            jax.ShapeDtypeStruct((rows, columns), jnp.bfloat16),
            jax.ShapeDtypeStruct((rows, columns), jnp.bfloat16),
            jax.ShapeDtypeStruct((rows, columns), jnp.float32),
            jax.ShapeDtypeStruct((rows, slabs[0].shape[2]), jnp.bfloat16),
        ],
        compiler_params=params(20),
        cost_estimate=cost(4 * 10**10),
    )(*operands)


def close_kernel(head_size, total_ref, features_ref, far_ref, out_ref):
    features = features_ref[:, : far_ref.shape[0]]
    sums = jnp.dot(features, far_ref[...], preferred_element_type=jnp.float32) + total_ref[...]
    for pair in range(out_ref.shape[1] // LANES):
        lanes = slice(pair * LANES, (pair + 1) * LANES)
        out_ref[:, lanes] = head_pair_norm(sums[:, lanes], head_size)


def close(total, features, far, head_size):
    return pl.pallas_call(
        functools.partial(close_kernel, head_size),
        in_specs=[vmem()] * 3,
        out_specs=vmem(),
        out_shape=jax.ShapeDtypeStruct(total.shape, jnp.bfloat16),
        compiler_params=params(16),
        cost_estimate=cost(),
    )(total, features, far)


def meet(arrays, others):
    return pl.pallas_call(
        lambda *refs: None,
        in_specs=[anywhere()] * (len(arrays) + len(others)),
        out_specs=[anywhere()] * len(arrays),
        out_shape=[jax.ShapeDtypeStruct(x.shape, x.dtype) for x in arrays],
        input_output_aliases={i: i for i in range(len(arrays))},
        compiler_params=params(4),
        cost_estimate=cost(),
    )(*arrays, *others)


def pick_kernel(ahead_ref, behind_ref, out_ref):
    rows, columns = out_ref.shape[0] // 2, out_ref.shape[1]
    out_ref[:rows] = ahead_ref[:rows]
    out_ref[rows:] = behind_ref[:rows]


def pick(rows, ahead, behind):
    height, columns = ahead.shape[0], ahead.shape[1] // 2
    return pl.pallas_call(
        pick_kernel,
        grid=(1,),
        in_specs=[pl.BlockSpec((height, columns), lambda i: (0, 0))] * 2,
        out_specs=pl.BlockSpec((2 * rows, columns), lambda i: (0, 0)),
        out_shape=jax.ShapeDtypeStruct((2 * rows, columns), jnp.bfloat16),
        compiler_params=params(12),
        cost_estimate=cost(),
    )(ahead, behind)


def pick_last_kernel(ahead_ref, behind_ref, swapped_ref, a_ref, v_ref, ahead_b_ref, behind_b_ref):
    rows = a_ref.shape[0]
    a_ref[...] = ahead_ref[:rows]
    v_ref[...] = behind_ref[:rows]
    ahead_b_ref[...] = swapped_ref[:rows]
    behind_b_ref[...] = swapped_ref[rows:]


def pick_last(rows, ahead, behind, swapped):
    height, columns = ahead.shape[0], ahead.shape[1] // 2
    shape = (rows, columns)
    return pl.pallas_call(
        pick_last_kernel,
        grid=(1,),
        in_specs=[
            pl.BlockSpec((height, columns), lambda i: (0, 0)),
            pl.BlockSpec((height, columns), lambda i: (0, 1)),
            pl.BlockSpec((2 * rows, columns), lambda i: (0, 0)),
        ],
        out_specs=[pl.BlockSpec(shape, lambda i: (0, 0))] * 4,
        out_shape=[jax.ShapeDtypeStruct(shape, jnp.bfloat16)] * 4,
        compiler_params=params(12),
        cost_estimate=cost(),
    )(ahead, behind, swapped)


def join_kernel(scalars, mine_ref, theirs_ref, out_ref):
    columns = mine_ref.shape[1]
    shared = 2 * columns - out_ref.shape[1]

    def emit(low, high):
        out_ref[:, :columns] = low[...]
        out_ref[:, columns:] = high[:, shared:]

    pl.when(scalars[1] == 0)(lambda: emit(mine_ref, theirs_ref))
    pl.when(scalars[1] == 1)(lambda: emit(theirs_ref, mine_ref))


def join(scalars, mine, theirs, inner_width):
    slots, _, tokens = mine.shape
    return pl.pallas_call(
        join_kernel,
        in_specs=[smem(), vmem(), vmem()],
        out_specs=vmem(),
        out_shape=jax.ShapeDtypeStruct((slots, inner_width, tokens), jnp.bfloat16),
        compiler_params=params(8),
        cost_estimate=cost(),
    )(scalars, mine, theirs)


def cut_kernel(k_ref, v_ref, after_ref, out_ref):
    chips, _, span = out_ref.shape
    half = chips // 2
    for chip in range(chips):
        source = k_ref if chip < half else v_ref
        start = (chip % half) * span
        out_ref[chip] = source[:, start : start + span]


def cut_prompt_weights(w_ck, w_cv, chips, after):
    depth, inner_width = w_ck.shape
    span = 2 * inner_width // chips
    return pl.pallas_call(
        cut_kernel,
        grid=(1,),
        in_specs=[pl.BlockSpec(w_ck.shape, lambda i: (0, 0))] * 2 + [anywhere()],
        out_specs=pl.BlockSpec((chips, depth, span), lambda i: (0, 0, 0)),
        out_shape=jax.ShapeDtypeStruct((chips, depth, span), jnp.bfloat16),
        compiler_params=params(56),
        cost_estimate=cost(),
    )(w_ck, w_cv, after)


def prompt_kernel(starts, scalars, after_ref, *refs):
    chips = len(starts)
    blocks, (own_ref, other_ref, out_ref, held_ref) = refs[:chips], refs[chips:]
    depth = own_ref.shape[0]
    half = out_ref.shape[1]
    parts = [
        jnp.concatenate(
            [
                block[start + core * half : start + (core + 1) * half, :depth]
                for start, block in zip(starts, blocks)
            ],
            axis=0,
        )
        for core in range(2)
    ]

    def emit(first, second):
        product = jnp.dot(parts[0], first[...], preferred_element_type=jnp.float32) + jnp.dot(
            parts[1], second[...], preferred_element_type=jnp.float32
        )
        held_ref[...] = product.astype(jnp.bfloat16).reshape(held_ref.shape)

    pl.when(scalars[1] == 0)(lambda: emit(own_ref, other_ref))
    pl.when(scalars[1] == 1)(lambda: emit(other_ref, own_ref))
    for chip in range(chips):
        out_ref[chip] = held_ref[scalars[2 + chip]]


def project_prompts(scalars, blocks, starts, w_own, w_other, after):
    chips, span = len(blocks), w_own.shape[1]
    half = (blocks[0].shape[0] - starts[0]) // 2
    if blocks[0].shape[0] * chips > 4096:
        depth = w_own.shape[0]
        straight = scalars[1] == 0
        weights = [jnp.where(straight, w_own, w_other), jnp.where(straight, w_other, w_own)]
        product = 0.0
        for core, weight in enumerate(weights):
            rows = [
                x[start + core * half : start + (core + 1) * half, :depth]
                for start, x in zip(starts, blocks)
            ]
            rows = jnp.concatenate(rows, axis=0)
            product = product + jnp.dot(rows, weight, preferred_element_type=jnp.float32)
        product = product.astype(jnp.bfloat16).reshape(chips, half, span)
        return jnp.take(product, scalars[2 : 2 + chips], axis=0)
    return pl.pallas_call(
        functools.partial(prompt_kernel, starts),
        in_specs=[smem(), anywhere()] + [vmem()] * (chips + 2),
        out_specs=vmem(),
        out_shape=jax.ShapeDtypeStruct((chips, half, span), jnp.bfloat16),
        scratch_shapes=[pltpu.VMEM((chips, half, span), jnp.bfloat16)],
        compiler_params=params(16),
        cost_estimate=cost(),
    )(scalars, after, *blocks, w_own, w_other)


def route_kernel(spots_here, winner_ref, loser_ref, rows_ref, out_ref):
    tile, count = out_ref.shape[0], rows_ref.shape[0]
    prompts = winner_ref.shape[1]
    row = lax.broadcasted_iota(jnp.int32, (tile, 1), 0) + pl.program_id(0) * tile
    slot = lax.div(row, spots_here)
    reads = (winner_ref[...] == slot) | (loser_ref[...] == slot)
    column = lax.broadcasted_iota(jnp.int32, (prompts, count), 1)
    prompt = lax.broadcasted_iota(jnp.int32, (prompts, count), 0)
    spread = jnp.where(lax.rem(column, prompts) == prompt, 1.0, 0.0).astype(jnp.bfloat16)
    reads = jnp.where(reads, 1.0, 0.0).astype(jnp.bfloat16)
    reads = jnp.dot(reads, spread, preferred_element_type=jnp.float32)
    same_spot = lax.rem(row, spots_here) == lax.div(column[0:1], prompts)
    chosen = jnp.where(same_spot, reads, 0.0).astype(jnp.bfloat16)
    out_ref[...] = jnp.dot(
        chosen, rows_ref[...], preferred_element_type=jnp.float32
    ).astype(jnp.bfloat16)


def route(projected, winner_slot, loser_slot, spots_here):
    count, span = projected.shape
    prompts = winner_slot.shape[0]
    total = 2 * prompts * spots_here
    tile = min(total, 512)
    row = pl.BlockSpec((1, prompts), lambda i: (0, 0))
    return pl.pallas_call(
        functools.partial(route_kernel, spots_here),
        grid=(total // tile,),
        in_specs=[row, row, pl.BlockSpec((count, span), lambda i: (0, 0))],
        out_specs=pl.BlockSpec((tile, span), lambda i: (i, 0)),
        out_shape=jax.ShapeDtypeStruct((total, span), jnp.bfloat16),
        compiler_params=params(32 if count > 1024 else 8),
        cost_estimate=cost(),
    )(winner_slot.reshape(1, prompts), loser_slot.reshape(1, prompts), projected)


def side_by_side(parts, start, count):
    span = parts[0].shape[1]
    taken = []
    for i, part in enumerate(parts):
        low, high = max(start - i * span, 0), min(start + count - i * span, span)
        if low < high:
            taken.append(part[:, low:high])
    return jnp.concatenate(taken, axis=1)


def finish_kernel(columns, head_size, scalars, own_ref, other_ref, keys_ref, values_ref):
    devices, rows, span = own_ref.shape
    slots = keys_ref.shape[0] // 2
    each = rows // slots
    inner_width = devices // 2 * span // 2

    def emit(start):
        for side, source in enumerate((own_ref, other_ref)):
            for slot in range(slots):
                at = slice(slot * each, (slot + 1) * each)
                for core in range(2):
                    parts = [source[2 * chip + core, at, :] for chip in range(devices // 2)]
                    out = side * slots + slot
                    to = slice(core * each, (core + 1) * each)
                    keys = side_by_side(parts, start, columns).astype(jnp.float32)
                    for pair in range(columns // LANES):
                        lanes = slice(pair * LANES, (pair + 1) * LANES)
                        keys_ref[out, to, lanes] = head_pair_norm(keys[:, lanes], head_size)
                    first = inner_width + start
                    values_ref[out, to, :] = side_by_side(parts, first, columns)

    pl.when(scalars[1] == 0)(lambda: emit(0))
    pl.when(scalars[1] == 1)(lambda: emit(inner_width - columns))


def finish_prompts(scalars, own, other, columns, head_size, slots):
    devices, rows, _ = own.shape
    span = 2 * rows // slots
    shape = jax.ShapeDtypeStruct((2 * slots, span, columns), jnp.bfloat16)
    return pl.pallas_call(
        functools.partial(finish_kernel, columns, head_size),
        in_specs=[smem(), vmem(), vmem()],
        out_specs=[vmem()] * 2,
        out_shape=[shape] * 2,
        compiler_params=params(16),
        cost_estimate=cost(),
    )(scalars, own, other)


def attend_kernel(
    head_size,
    spots,
    side,
    scalars,
    winner,
    loser,
    lengths,
    a_ref,
    v_ref,
    b_ref,
    pk_ref,
    pv_ref,
    out_ref,
):
    step = pl.program_id(0)
    count_here = pl.num_programs(0)
    even_group = scalars[0] == 0
    _, columns, tokens = out_ref.shape
    owner = scalars[scalars.shape[0] - 2 + side]
    slot = owner + step

    def count(p, live):
        hit = (winner[p] == slot) | (loser[p] == slot)
        return live + jnp.where(hit, lengths[p], 0)

    live = lax.fori_loop(0, winner.shape[0], count, jnp.int32(0))
    span = pk_ref.shape[1]
    row = lax.broadcasted_iota(jnp.int32, (span, 1), 0)
    rest = lax.rem(row, span // 2)
    position = (2 * lax.div(rest, spots) + lax.div(row, span // 2)) * spots + lax.rem(rest, spots)
    allowed = position < live
    low = lax.broadcasted_iota(jnp.int32, (1, LANES), 1) < head_size
    over_lanes = (((1,), (1,)), ((), ()))
    over_rows = (((0,), (0,)), ((), ()))
    scale = 1.4426950408889634 / head_size**0.5
    here = pl.ds(pl.multiple_of((side * count_here + step) * tokens, tokens), tokens)
    block = side * count_here + step
    for pair in range(columns // LANES):
        lanes = slice(pair * LANES, (pair + 1) * LANES)
        a = a_ref[here, lanes]
        b = b_ref[here, lanes]
        queries = jnp.where(even_group, a, b)
        keys = jnp.where(even_group, b, a)
        values = v_ref[here, lanes]
        prompt_keys = pk_ref[block, :, lanes]
        prompt_values = pv_ref[block, :, lanes]
        for head in range(2):
            side = low if head == 0 else jnp.logical_not(low)
            q = jnp.where(side, queries, jnp.zeros_like(queries))
            s = lax.dot_general(keys, q, over_lanes, preferred_element_type=jnp.float32)
            t = lax.dot_general(prompt_keys, q, over_lanes, preferred_element_type=jnp.float32)
            s = jnp.exp2(s * scale)
            t = jnp.where(allowed, jnp.exp2(t * scale), 0.0)
            total = jnp.sum(s, axis=0, keepdims=True) + jnp.sum(t, axis=0, keepdims=True)
            out = lax.dot_general(
                values, s.astype(jnp.bfloat16), over_rows, preferred_element_type=jnp.float32
            ) + lax.dot_general(
                prompt_values, t.astype(jnp.bfloat16), over_rows, preferred_element_type=jnp.float32
            )
            rows = slice(head * head_size, (head + 1) * head_size)
            to = slice(pair * LANES + head * head_size, pair * LANES + (head + 1) * head_size)
            out_ref[0, to, :] = (out[rows] * (1.0 / total)).astype(jnp.bfloat16)


def attend(side, scalars, routes, rows, prompt_keys, prompt_values, head_size, spots, count):
    tokens = rows[0].shape[0] // (2 * count)
    columns = rows[0].shape[1]
    return pl.pallas_call(
        functools.partial(attend_kernel, head_size, spots, side),
        grid=(count,),
        in_specs=[smem()] * 4 + [vmem()] * 5,
        out_specs=pl.BlockSpec((1, columns, tokens), lambda l: (l, 0, 0)),
        out_shape=jax.ShapeDtypeStruct((count, columns, tokens), jnp.bfloat16),
        compiler_params=params(16),
        cost_estimate=cost(),
    )(scalars, *routes, *rows, prompt_keys, prompt_values)


def ring_order(groups, chips):
    if groups == 2:
        return list(range(0, chips, 2)) + list(range(1, chips, 2))[::-1]
    return list(range(chips))


def solution(mesh):
    groups, dp = mesh.shape["groups"], mesh.shape["dp"]
    chips = dp // 2
    ring = ring_order(groups, chips)
    place = [ring.index(chip) for chip in range(chips)]
    behind_by = np.array(
        [[(place[me] - place[chip]) % chips for chip in range(chips)] for me in range(chips)],
        np.int32,
    )
    forward_pairs = [
        (2 * ring[i] + c, 2 * ring[(i + 1) % chips] + c) for i in range(chips) for c in range(2)
    ]
    backward_pairs = [(b, a) for a, b in forward_pairs]
    core_pairs = [(d, d ^ 1) for d in range(dp)]
    group_pairs = [(g, g ^ 1) for g in range(groups)]
    half_groups = [[2 * chip + c for chip in range(chips)] for c in range(2)]

    def forward(x):
        return lax.ppermute(x, "dp", forward_pairs)

    def backward(x):
        return lax.ppermute(x, "dp", backward_pairs)

    def swap_cores(x):
        return lax.ppermute(x, "dp", core_pairs)

    def swap_groups(x):
        return lax.ppermute(x, "groups", group_pairs)

    def local(
        latents,
        context,
        lengths,
        winner_slot,
        loser_slot,
        image_mod,
        context_mod,
        w_q,
        w_k,
        w_v,
        w_ck,
        w_cv,
    ):
        slot_local, token_count, width = latents.shape
        prompt_count, spot_local, _ = context.shape
        depth, inner_width = w_q.shape
        head_size = inner_width // HEADS
        columns = (HEADS + 1) // 2 * head_size
        me = lax.axis_index("dp")
        my_group = lax.axis_index("groups") % 2
        my_chip, my_core = me // 2, me % 2
        places = lax.dynamic_index_in_dim(jnp.asarray(behind_by), my_chip, 0, keepdims=False)
        first = [my_group, my_core]
        last = [me * slot_local, (me ^ 1) * slot_local]
        scalars = jnp.concatenate([jnp.stack(first), places, jnp.stack(last)]).astype(jnp.int32)

        own_mixed = mix_prompts(context, context_mod, chips, 2 * columns)
        once = [forward(own_mixed), backward(own_mixed)]
        twice = [forward(once[0]), backward(once[1])]
        mixed = {0: (own_mixed, 0)}
        for o, arrived in ((1, once), (2, twice)):
            mixed.setdefault(o % chips, (arrived[0], 0))
            mixed.setdefault(-o % chips, (arrived[1], 0))
        keep, give = split_weights(scalars, w_q, w_k, w_v, columns, own_mixed)
        got = swap_cores(give)
        own_av = [keep[:, : 2 * columns], got[:, : 2 * columns]]
        blocks = [jnp.concatenate(own_av + [x], axis=0) for x in twice]

        w_c = cut_prompt_weights(w_ck, w_cv, chips, w_q)
        w_c = lax.all_to_all(w_c, "dp", 0, 0, axis_index_groups=half_groups, tiled=True)
        ahead, behind = meet(blocks, [w_c])

        own, *give = modulate_image(scalars, latents, image_mod, chips, ahead)

        totals = None
        enough = max(1, chips // 8)
        tokens, waiting_av, waiting_b = [], [((0,), ahead)], []
        for o in range(1, chips // 2):
            ahead, behind = meet([forward(ahead), backward(behind)], tokens)
            mixed.setdefault((o + 2) % chips, (ahead, 2 * depth))
            mixed.setdefault((-o - 2) % chips, (behind, 2 * depth))
            if o == 1:
                (w_c,) = meet([w_c], [ahead])
                w_parts = [x.reshape(width // 2, -1) for x in (w_c, swap_cores(w_c))]
            if 4 * o == chips:
                slabs = [[own], [swap_cores(x) for x in meet(give, [ahead])]]
            tokens = []
            if 2 * o + 4 == chips:
                blocks, starts = zip(*[mixed[o] for o in range(chips)])
                projected = project_prompts(scalars, blocks, starts, *w_parts, slabs[1][0])
                projected = projected.reshape(-1, projected.shape[2])
                outgoing = route(projected, winner_slot, loser_slot, chips * spot_local)
                outgoing = outgoing.reshape(dp, -1, outgoing.shape[1])
                arrived = lax.all_to_all(outgoing, "dp", 0, 0, tiled=True)
            last = 2 * o + 2 == chips
            waiting_av += [((o,), ahead), ((chips - o,), behind)]
            if last:
                picked = pick_last(2 * depth, ahead, behind, waiting_b[-1][1])
            else:
                swapped = swap_groups(pick(2 * depth, ahead, behind))
            if len(waiting_b) > 3 * enough or (last and totals is None):
                first = totals is None
                items = [((), keep), ((), got)] if first else waiting_b
                totals, token = accumulate(
                    2 * depth, totals, slabs, waiting_av, items, [outgoing] if last else []
                )
                tokens.append(token)
                waiting_av, waiting_b = [], waiting_b if first else []
            if not last:
                waiting_b.append(((o, chips - o), swapped))
                tokens.append(swapped)
            if 2 * o + 4 == chips:
                tokens.append(outgoing)
        a_far, v_far = meet([forward(picked[0]), backward(picked[1])], tokens)
        o = chips // 2 - 1
        waiting_b += [((o,), forward(picked[2])), ((chips - o,), backward(picked[3]))]
        b_far = swap_groups(a_far)
        rows_a, rows_v, rows_b, features = last_products(
            2 * depth,
            head_size,
            totals,
            slabs,
            waiting_av,
            (chips // 2, a_far, v_far),
            waiting_b,
        )

        done_rows = (rows_a, rows_v, close(rows_b, features, b_far, head_size))
        (arrived,) = meet([arrived], [done_rows[2]])

        prompt_keys, prompt_values = finish_prompts(
            scalars, arrived, swap_cores(arrived), columns, head_size, slot_local
        )

        routes = (winner_slot, loser_slot, lengths)

        def run(side):
            return attend(
                side,
                scalars,
                routes,
                done_rows,
                prompt_keys,
                prompt_values,
                head_size,
                spot_local,
                slot_local,
            )

        theirs = swap_cores(run(1))
        mine = run(0)
        return join(scalars, mine, theirs, inner_width).transpose(0, 2, 1)

    placed = (
        P(("groups", "dp"), None, None),
        P("groups", "dp", None),
        P("groups"),
        P("groups"),
        P("groups"),
        P(("groups", "dp"), None, None),
        P("groups", None, None),
        P("dp", None),
        P("dp", None),
        P("dp", None),
        P("dp", None),
        P("dp", None),
    )
    return jax.shard_map(
        local,
        mesh=mesh,
        in_specs=placed,
        out_specs=P(("groups", "dp"), None, None),
        check_vma=False,
    )
```

```python
import functools

import jax
import jax.numpy as jnp
import numpy as np
from jax import lax
from jax.experimental import pallas as pl
from jax.experimental.pallas import tpu as pltpu
from jax.sharding import PartitionSpec as P

HEADS = 19
LANES = 128


epsilon = 1e-06


def params(mib):
    return pltpu.CompilerParams(vmem_limit_bytes=mib * 2**20)


def cost(flops=1):
    return pl.CostEstimate(flops=flops, bytes_accessed=1, transcendentals=0)


def anywhere():
    return pl.BlockSpec(memory_space=pl.ANY)


def layer_norm(values, shift, scale):
    average = jnp.mean(values, axis=-1, keepdims=True)
    centered = values - average
    variance = jnp.mean(centered * centered, axis=-1, keepdims=True)
    return (centered * lax.rsqrt(variance + epsilon) * (1.0 + scale) + shift).astype(jnp.bfloat16)


def head_pair_norm(x, head_size):
    low = lax.broadcasted_iota(jnp.int32, (1, LANES), 1) < head_size
    squares = x * x
    first = jnp.sum(jnp.where(low, squares, 0.0), axis=-1, keepdims=True)
    second = jnp.sum(jnp.where(low, 0.0, squares), axis=-1, keepdims=True)
    first = lax.rsqrt(first * (1.0 / head_size) + epsilon)
    second = lax.rsqrt(second * (1.0 / head_size) + epsilon)
    return (x * jnp.where(low, first, second)).astype(jnp.bfloat16)


def vmem():
    return pl.BlockSpec(memory_space=pltpu.VMEM)


def smem():
    return pl.BlockSpec(memory_space=pltpu.SMEM)


def split_kernel(columns, scalars, q_ref, k_ref, v_ref, after_ref, keep_ref, give_ref):
    inner_width = q_ref.shape[1]

    def emit(parts, low_ref, high_ref):
        for i, part in enumerate(parts):
            at = slice(i * columns, (i + 1) * columns)
            low_ref[:, at] = part[:, :columns]
            high_ref[:, at] = part[:, inner_width - columns :]

    for group in range(2):
        parts = (q_ref, v_ref, k_ref) if group == 0 else (k_ref, v_ref, q_ref)
        for core in range(2):
            refs = (keep_ref, give_ref) if core == 0 else (give_ref, keep_ref)
            here = (scalars[0] == group) & (scalars[1] == core)
            pl.when(here)(functools.partial(emit, parts, *refs))


def split_weights(scalars, w_q, w_k, w_v, columns, after):
    depth, inner_width = w_q.shape
    shape = jax.ShapeDtypeStruct((depth, 3 * columns), jnp.bfloat16)
    whole = pl.BlockSpec((depth, inner_width), lambda i, s: (0, 0))
    out = pl.BlockSpec((depth, 3 * columns), lambda i, s: (0, 0))
    return pl.pallas_call(
        functools.partial(split_kernel, columns),
        grid_spec=pltpu.PrefetchScalarGridSpec(
            num_scalar_prefetch=1,
            grid=(1,),
            in_specs=[whole] * 3 + [anywhere()],
            out_specs=[out] * 2,
        ),
        out_shape=[shape] * 2,
        compiler_params=params(56),
        cost_estimate=cost(),
    )(scalars, w_q, w_k, w_v, after)


def mixed_kernel(chips, context_ref, mod_ref, out_ref):
    prompts, spots, width = context_ref.shape
    depth = width // (2 * chips)
    shift, scale = mod_ref[:, 0, :], mod_ref[:, 1, :]
    values = context_ref[...].astype(jnp.float32)
    for spot in range(spots):
        rows = layer_norm(values[:, spot, :], shift, scale)
        for core in range(2):
            parts = [
                rows[:, (2 * chip + core) * depth : (2 * chip + core + 1) * depth]
                for chip in range(chips)
            ]
            at = (core * spots + spot) * prompts
            parts.append(jnp.zeros((prompts, out_ref.shape[1] - width // 2), jnp.bfloat16))
            out_ref[at : at + prompts, :] = jnp.concatenate(parts, axis=1)


def mix_prompts(context, context_mod, chips, columns):
    prompts, spots, width = context.shape
    return pl.pallas_call(
        functools.partial(mixed_kernel, chips),
        grid=(1,),
        in_specs=[pl.BlockSpec(x.shape, lambda i: (0, 0, 0)) for x in (context, context_mod)],
        out_specs=pl.BlockSpec((2 * spots * prompts, columns), lambda i: (0, 0)),
        out_shape=jax.ShapeDtypeStruct((2 * spots * prompts, columns), jnp.bfloat16),
        compiler_params=params(56),
        cost_estimate=cost(),
    )(context, context_mod)


def image_kernel(chips, scalars, x_ref, mod_ref, after_ref, own_ref, give_ref):
    image = layer_norm(x_ref[0].astype(jnp.float32), mod_ref[0, 0:1, :], mod_ref[0, 1:2, :])
    depth = image.shape[1] // (2 * chips)

    def emit(first_ref, second_ref):
        for chip in range(chips):
            start = 2 * chip * depth
            straight = image[:, start : start + 2 * depth]
            turned = jnp.concatenate([straight[:, depth:], straight[:, :depth]], axis=1)
            first_ref[scalars[2 + chip], :, : 2 * depth] = straight
            second_ref[scalars[2 + chip], :, : 2 * depth] = turned

    pl.when(scalars[1] == 0)(lambda: emit(own_ref, give_ref))
    pl.when(scalars[1] == 1)(lambda: emit(give_ref, own_ref))


def modulate_image(scalars, latents, image_mod, chips, after):
    slots, tokens, width = latents.shape
    wide = -(-width // chips // LANES) * LANES
    block = (chips, tokens, wide)
    return pl.pallas_call(
        functools.partial(image_kernel, chips),
        grid_spec=pltpu.PrefetchScalarGridSpec(
            num_scalar_prefetch=1,
            grid=(slots,),
            in_specs=[
                pl.BlockSpec((1, tokens, width), lambda i, s: (i, 0, 0)),
                pl.BlockSpec((1, 2, width), lambda i, s: (i, 0, 0)),
                anywhere(),
            ],
            out_specs=[pl.BlockSpec(block, lambda i, s: (0, i, 0))] * 2,
        ),
        out_shape=[jax.ShapeDtypeStruct((chips, slots * tokens, wide), jnp.bfloat16)] * 2,
        compiler_params=params(32),
        cost_estimate=cost(),
    )(scalars, latents, image_mod, after)


def take_rows(slab, o, depth):
    return jnp.concatenate([part[o, :, :depth] for part in slab], axis=0)


def product_kernel(slots, depth, av_places, b_places, first, others, *refs):
    slabs, refs = refs[:slots], refs[slots:]
    panels = refs[: len(av_places)]
    at = len(av_places)
    pieces = refs[at : at + len(b_places) // 2 + 2 * first]
    out_av, out_b, token_ref = refs[-3:]
    totals = (None, None) if first else refs[-5 - others : -3 - others]
    rows = slabs[0].shape[1]
    columns = out_av.shape[1]
    token_ref[...] = jnp.zeros_like(token_ref)

    def product(slab, places, panel):
        features = jnp.concatenate([take_rows(slab, o, depth) for o in places], axis=1)
        return jnp.dot(features, panel, preferred_element_type=jnp.float32)

    for side, slab in enumerate((slabs[:1], slabs[1:])):
        to = slice(side * rows, (side + 1) * rows)
        if av_places:
            panel = jnp.concatenate([panel[:depth] for panel in panels], axis=0)
            sums = product(slab, av_places, panel)
            out_av[to] = sums if first else totals[0][to] + sums
        elif totals[0] is not out_av:
            out_av[to] = totals[0][to]
        sums = 0.0
        if b_places:
            panel = jnp.concatenate([piece[...] for piece in pieces[2 * first :]], axis=0)
            sums = product(slab, b_places, panel)
        if first:
            features = take_rows(slab, 0, depth)
            half = depth // 2
            for own, part in zip((slice(0, half), slice(half, depth)), pieces):
                sums = sums + jnp.dot(
                    features[:, own], part[:, columns:], preferred_element_type=jnp.float32
                )
            out_b[to] = sums
        else:
            out_b[to] = totals[1][to] + sums


def accumulate(depth, totals, slabs, av_items, b_items, others=()):
    first = totals is None
    slabs = slabs[0] + slabs[1]
    rows, columns = slabs[0].shape[1], 2 * b_items[0][1].shape[1]
    if first:
        columns = 2 * b_items[0][1].shape[1] // 3
    av_places = [o for places, _ in av_items for o in places]
    b_places = [o for places, _ in b_items for o in places]
    operands = slabs + [x for _, x in av_items] + [x for _, x in b_items]
    aliases = {}
    if not first:
        aliases = {len(operands): 0, len(operands) + 1: 1}
        operands += list(totals)
    in_specs = [vmem()] * len(operands) + [anywhere()] * len(others)
    out = pl.pallas_call(
        functools.partial(
            product_kernel, len(slabs), depth, av_places, b_places, first, len(others)
        ),
        in_specs=in_specs,
        out_specs=[vmem()] * 3,
        out_shape=[
            jax.ShapeDtypeStruct((2 * rows, columns), jnp.float32),
            jax.ShapeDtypeStruct((2 * rows, columns // 2), jnp.float32),
            jax.ShapeDtypeStruct((8, LANES), jnp.float32),
        ],
        input_output_aliases=aliases,
        compiler_params=params(20),
        cost_estimate=cost(4 * 10**10),
    )(*operands, *others)
    return out[:2], out[2]


def last_kernel(slots, depth, head_size, av_places, b_places, pieces, *refs):
    slabs, refs = refs[:slots], refs[slots:]
    count = len(av_places) - 1
    panels, (a_far, v_far) = refs[:count], refs[count : count + 2]
    swapped = refs[count + 2 : count + 2 + pieces]
    total_av, total_b, out_a, out_v, out_b, out_far = refs[-6:]
    rows, columns = slabs[0].shape[1], out_a.shape[1]

    def product(slab, places, panel):
        features = jnp.concatenate([take_rows(slab, o, depth) for o in places], axis=1)
        return jnp.dot(features, panel, preferred_element_type=jnp.float32)

    for side, slab in enumerate((slabs[:1], slabs[1:])):
        to = slice(side * rows, (side + 1) * rows)
        for half, far in enumerate((a_far, v_far)):
            lanes = slice(half * columns, (half + 1) * columns)
            parts = [panel[:depth, lanes] for panel in panels] + [far[...]]
            sums = total_av[to, lanes] + product(slab, av_places, jnp.concatenate(parts, axis=0))
            if half == 1:
                out_v[to] = sums.astype(jnp.bfloat16)
                continue
            for pair in range(columns // LANES):
                at = slice(pair * LANES, (pair + 1) * LANES)
                out_a[to, at] = head_pair_norm(sums[:, at], head_size)
        panel = jnp.concatenate([piece[...] for piece in swapped], axis=0)
        out_b[to] = total_b[to] + product(slab, b_places, panel)
        out_far[to, :depth] = take_rows(slab, av_places[-1], depth)


def last_products(depth, head_size, totals, slabs, av_items, far_items, b_items):
    slabs = slabs[0] + slabs[1]
    rows, columns = 2 * slabs[0].shape[1], totals[1].shape[1]
    av_places = [o for places, _ in av_items for o in places] + [far_items[0]]
    b_places = [o for places, _ in b_items for o in places]
    operands = slabs + [x for _, x in av_items] + list(far_items[1:])
    operands += [x for _, x in b_items] + list(totals)
    return pl.pallas_call(
        functools.partial(
            last_kernel, len(slabs), depth, head_size, av_places, b_places, len(b_items)
        ),
        in_specs=[vmem()] * len(operands),
        out_specs=[vmem()] * 4,
        out_shape=[
            jax.ShapeDtypeStruct((rows, columns), jnp.bfloat16),
            jax.ShapeDtypeStruct((rows, columns), jnp.bfloat16),
            jax.ShapeDtypeStruct((rows, columns), jnp.float32),
            jax.ShapeDtypeStruct((rows, slabs[0].shape[2]), jnp.bfloat16),
        ],
        compiler_params=params(20),
        cost_estimate=cost(4 * 10**10),
    )(*operands)


def close_kernel(head_size, total_ref, features_ref, far_ref, out_ref):
    features = features_ref[:, : far_ref.shape[0]]
    sums = jnp.dot(features, far_ref[...], preferred_element_type=jnp.float32) + total_ref[...]
    for pair in range(out_ref.shape[1] // LANES):
        lanes = slice(pair * LANES, (pair + 1) * LANES)
        out_ref[:, lanes] = head_pair_norm(sums[:, lanes], head_size)


def close(total, features, far, head_size):
    return pl.pallas_call(
        functools.partial(close_kernel, head_size),
        in_specs=[vmem()] * 3,
        out_specs=vmem(),
        out_shape=jax.ShapeDtypeStruct(total.shape, jnp.bfloat16),
        compiler_params=params(16),
        cost_estimate=cost(),
    )(total, features, far)


def meet(arrays, others):
    return pl.pallas_call(
        lambda *refs: None,
        in_specs=[anywhere()] * (len(arrays) + len(others)),
        out_specs=[anywhere()] * len(arrays),
        out_shape=[jax.ShapeDtypeStruct(x.shape, x.dtype) for x in arrays],
        input_output_aliases={i: i for i in range(len(arrays))},
        compiler_params=params(4),
        cost_estimate=cost(),
    )(*arrays, *others)


def pick_kernel(ahead_ref, behind_ref, out_ref):
    rows, columns = out_ref.shape[0] // 2, out_ref.shape[1]
    out_ref[:rows] = ahead_ref[:rows]
    out_ref[rows:] = behind_ref[:rows]


def pick(rows, ahead, behind):
    height, columns = ahead.shape[0], ahead.shape[1] // 2
    return pl.pallas_call(
        pick_kernel,
        grid=(1,),
        in_specs=[pl.BlockSpec((height, columns), lambda i: (0, 0))] * 2,
        out_specs=pl.BlockSpec((2 * rows, columns), lambda i: (0, 0)),
        out_shape=jax.ShapeDtypeStruct((2 * rows, columns), jnp.bfloat16),
        compiler_params=params(12),
        cost_estimate=cost(),
    )(ahead, behind)


def pick_last_kernel(ahead_ref, behind_ref, swapped_ref, a_ref, v_ref, ahead_b_ref, behind_b_ref):
    rows = a_ref.shape[0]
    a_ref[...] = ahead_ref[:rows]
    v_ref[...] = behind_ref[:rows]
    ahead_b_ref[...] = swapped_ref[:rows]
    behind_b_ref[...] = swapped_ref[rows:]


def pick_last(rows, ahead, behind, swapped):
    height, columns = ahead.shape[0], ahead.shape[1] // 2
    shape = (rows, columns)
    return pl.pallas_call(
        pick_last_kernel,
        grid=(1,),
        in_specs=[
            pl.BlockSpec((height, columns), lambda i: (0, 0)),
            pl.BlockSpec((height, columns), lambda i: (0, 1)),
            pl.BlockSpec((2 * rows, columns), lambda i: (0, 0)),
        ],
        out_specs=[pl.BlockSpec(shape, lambda i: (0, 0))] * 4,
        out_shape=[jax.ShapeDtypeStruct(shape, jnp.bfloat16)] * 4,
        compiler_params=params(12),
        cost_estimate=cost(),
    )(ahead, behind, swapped)


def join_kernel(scalars, mine_ref, theirs_ref, out_ref):
    columns = mine_ref.shape[1]
    shared = 2 * columns - out_ref.shape[1]

    def emit(low, high):
        out_ref[:, :columns] = low[...]
        out_ref[:, columns:] = high[:, shared:]

    pl.when(scalars[1] == 0)(lambda: emit(mine_ref, theirs_ref))
    pl.when(scalars[1] == 1)(lambda: emit(theirs_ref, mine_ref))


def join(scalars, mine, theirs, inner_width):
    slots, _, tokens = mine.shape
    return pl.pallas_call(
        join_kernel,
        in_specs=[smem(), vmem(), vmem()],
        out_specs=vmem(),
        out_shape=jax.ShapeDtypeStruct((slots, inner_width, tokens), jnp.bfloat16),
        compiler_params=params(8),
        cost_estimate=cost(),
    )(scalars, mine, theirs)


def cut_kernel(k_ref, v_ref, after_ref, out_ref):
    chips, _, span = out_ref.shape
    half = chips // 2
    for chip in range(chips):
        source = k_ref if chip < half else v_ref
        start = (chip % half) * span
        out_ref[chip] = source[:, start : start + span]


def cut_prompt_weights(w_ck, w_cv, chips, after):
    depth, inner_width = w_ck.shape
    span = 2 * inner_width // chips
    return pl.pallas_call(
        cut_kernel,
        grid=(1,),
        in_specs=[pl.BlockSpec(w_ck.shape, lambda i: (0, 0))] * 2 + [anywhere()],
        out_specs=pl.BlockSpec((chips, depth, span), lambda i: (0, 0, 0)),
        out_shape=jax.ShapeDtypeStruct((chips, depth, span), jnp.bfloat16),
        compiler_params=params(56),
        cost_estimate=cost(),
    )(w_ck, w_cv, after)


def prompt_kernel(starts, scalars, after_ref, *refs):
    chips = len(starts)
    blocks, (own_ref, other_ref, out_ref, held_ref) = refs[:chips], refs[chips:]
    depth = own_ref.shape[0]
    half = out_ref.shape[1]
    parts = [
        jnp.concatenate(
            [
                block[start + core * half : start + (core + 1) * half, :depth]
                for start, block in zip(starts, blocks)
            ],
            axis=0,
        )
        for core in range(2)
    ]

    def emit(first, second):
        product = jnp.dot(parts[0], first[...], preferred_element_type=jnp.float32) + jnp.dot(
            parts[1], second[...], preferred_element_type=jnp.float32
        )
        held_ref[...] = product.astype(jnp.bfloat16).reshape(held_ref.shape)

    pl.when(scalars[1] == 0)(lambda: emit(own_ref, other_ref))
    pl.when(scalars[1] == 1)(lambda: emit(other_ref, own_ref))
    for chip in range(chips):
        out_ref[chip] = held_ref[scalars[2 + chip]]


def project_prompts(scalars, blocks, starts, w_own, w_other, after):
    chips, span = len(blocks), w_own.shape[1]
    half = (blocks[0].shape[0] - starts[0]) // 2
    if blocks[0].shape[0] * chips > 4096:
        depth = w_own.shape[0]
        straight = scalars[1] == 0
        weights = [jnp.where(straight, w_own, w_other), jnp.where(straight, w_other, w_own)]
        product = 0.0
        for core, weight in enumerate(weights):
            rows = [
                x[start + core * half : start + (core + 1) * half, :depth]
                for start, x in zip(starts, blocks)
            ]
            rows = jnp.concatenate(rows, axis=0)
            product = product + jnp.dot(rows, weight, preferred_element_type=jnp.float32)
        product = product.astype(jnp.bfloat16).reshape(chips, half, span)
        return jnp.take(product, scalars[2 : 2 + chips], axis=0)
    return pl.pallas_call(
        functools.partial(prompt_kernel, starts),
        in_specs=[smem(), anywhere()] + [vmem()] * (chips + 2),
        out_specs=vmem(),
        out_shape=jax.ShapeDtypeStruct((chips, half, span), jnp.bfloat16),
        scratch_shapes=[pltpu.VMEM((chips, half, span), jnp.bfloat16)],
        compiler_params=params(16),
        cost_estimate=cost(),
    )(scalars, after, *blocks, w_own, w_other)


def route_kernel(spots_here, winner_ref, loser_ref, rows_ref, out_ref):
    tile, count = out_ref.shape[0], rows_ref.shape[0]
    prompts = winner_ref.shape[1]
    row = lax.broadcasted_iota(jnp.int32, (tile, 1), 0) + pl.program_id(0) * tile
    slot = lax.div(row, spots_here)
    reads = (winner_ref[...] == slot) | (loser_ref[...] == slot)
    column = lax.broadcasted_iota(jnp.int32, (prompts, count), 1)
    prompt = lax.broadcasted_iota(jnp.int32, (prompts, count), 0)
    spread = jnp.where(lax.rem(column, prompts) == prompt, 1.0, 0.0).astype(jnp.bfloat16)
    reads = jnp.where(reads, 1.0, 0.0).astype(jnp.bfloat16)
    reads = jnp.dot(reads, spread, preferred_element_type=jnp.float32)
    same_spot = lax.rem(row, spots_here) == lax.div(column[0:1], prompts)
    chosen = jnp.where(same_spot, reads, 0.0).astype(jnp.bfloat16)
    out_ref[...] = jnp.dot(
        chosen, rows_ref[...], preferred_element_type=jnp.float32
    ).astype(jnp.bfloat16)


def route(projected, winner_slot, loser_slot, spots_here):
    count, span = projected.shape
    prompts = winner_slot.shape[0]
    total = 2 * prompts * spots_here
    tile = min(total, 512)
    row = pl.BlockSpec((1, prompts), lambda i: (0, 0))
    return pl.pallas_call(
        functools.partial(route_kernel, spots_here),
        grid=(total // tile,),
        in_specs=[row, row, pl.BlockSpec((count, span), lambda i: (0, 0))],
        out_specs=pl.BlockSpec((tile, span), lambda i: (i, 0)),
        out_shape=jax.ShapeDtypeStruct((total, span), jnp.bfloat16),
        compiler_params=params(32 if count > 1024 else 8),
        cost_estimate=cost(),
    )(winner_slot.reshape(1, prompts), loser_slot.reshape(1, prompts), projected)


def side_by_side(parts, start, count):
    span = parts[0].shape[1]
    taken = []
    for i, part in enumerate(parts):
        low, high = max(start - i * span, 0), min(start + count - i * span, span)
        if low < high:
            taken.append(part[:, low:high])
    return jnp.concatenate(taken, axis=1)


def finish_kernel(columns, head_size, scalars, own_ref, other_ref, keys_ref, values_ref):
    devices, rows, span = own_ref.shape
    slots = keys_ref.shape[0] // 2
    each = rows // slots
    inner_width = devices // 2 * span // 2

    def emit(start):
        for side, source in enumerate((own_ref, other_ref)):
            for slot in range(slots):
                at = slice(slot * each, (slot + 1) * each)
                for core in range(2):
                    parts = [source[2 * chip + core, at, :] for chip in range(devices // 2)]
                    out = side * slots + slot
                    to = slice(core * each, (core + 1) * each)
                    keys = side_by_side(parts, start, columns).astype(jnp.float32)
                    for pair in range(columns // LANES):
                        lanes = slice(pair * LANES, (pair + 1) * LANES)
                        keys_ref[out, to, lanes] = head_pair_norm(keys[:, lanes], head_size)
                    first = inner_width + start
                    values_ref[out, to, :] = side_by_side(parts, first, columns)

    pl.when(scalars[1] == 0)(lambda: emit(0))
    pl.when(scalars[1] == 1)(lambda: emit(inner_width - columns))


def finish_prompts(scalars, own, other, columns, head_size, slots):
    devices, rows, _ = own.shape
    span = 2 * rows // slots
    shape = jax.ShapeDtypeStruct((2 * slots, span, columns), jnp.bfloat16)
    return pl.pallas_call(
        functools.partial(finish_kernel, columns, head_size),
        in_specs=[smem(), vmem(), vmem()],
        out_specs=[vmem()] * 2,
        out_shape=[shape] * 2,
        compiler_params=params(16),
        cost_estimate=cost(),
    )(scalars, own, other)


def attend_kernel(
    head_size,
    spots,
    side,
    scalars,
    winner,
    loser,
    lengths,
    a_ref,
    v_ref,
    b_ref,
    pk_ref,
    pv_ref,
    out_ref,
):
    step = pl.program_id(0)
    count_here = pl.num_programs(0)
    even_group = scalars[0] == 0
    _, columns, tokens = out_ref.shape
    owner = scalars[scalars.shape[0] - 2 + side]
    slot = owner + step

    def count(p, live):
        hit = (winner[p] == slot) | (loser[p] == slot)
        return live + jnp.where(hit, lengths[p], 0)

    live = lax.fori_loop(0, winner.shape[0], count, jnp.int32(0))
    span = pk_ref.shape[1]
    row = lax.broadcasted_iota(jnp.int32, (span, 1), 0)
    rest = lax.rem(row, span // 2)
    position = (2 * lax.div(rest, spots) + lax.div(row, span // 2)) * spots + lax.rem(rest, spots)
    allowed = position < live
    low = lax.broadcasted_iota(jnp.int32, (1, LANES), 1) < head_size
    over_lanes = (((1,), (1,)), ((), ()))
    over_rows = (((0,), (0,)), ((), ()))
    scale = 1.4426950408889634 / head_size**0.5
    here = pl.ds(pl.multiple_of((side * count_here + step) * tokens, tokens), tokens)
    block = side * count_here + step
    for pair in range(columns // LANES):
        lanes = slice(pair * LANES, (pair + 1) * LANES)
        a = a_ref[here, lanes]
        b = b_ref[here, lanes]
        queries = jnp.where(even_group, a, b)
        keys = jnp.where(even_group, b, a)
        values = v_ref[here, lanes]
        prompt_keys = pk_ref[block, :, lanes]
        prompt_values = pv_ref[block, :, lanes]
        for head in range(2):
            side = low if head == 0 else jnp.logical_not(low)
            q = jnp.where(side, queries, jnp.zeros_like(queries))
            s = lax.dot_general(keys, q, over_lanes, preferred_element_type=jnp.float32)
            t = lax.dot_general(prompt_keys, q, over_lanes, preferred_element_type=jnp.float32)
            s = jnp.exp2(s * scale)
            t = jnp.where(allowed, jnp.exp2(t * scale), 0.0)
            total = jnp.sum(s, axis=0, keepdims=True) + jnp.sum(t, axis=0, keepdims=True)
            out = lax.dot_general(
                values, s.astype(jnp.bfloat16), over_rows, preferred_element_type=jnp.float32
            ) + lax.dot_general(
                prompt_values, t.astype(jnp.bfloat16), over_rows, preferred_element_type=jnp.float32
            )
            rows = slice(head * head_size, (head + 1) * head_size)
            to = slice(pair * LANES + head * head_size, pair * LANES + (head + 1) * head_size)
            out_ref[0, to, :] = (out[rows] * (1.0 / total)).astype(jnp.bfloat16)


def attend(side, scalars, routes, rows, prompt_keys, prompt_values, head_size, spots, count):
    tokens = rows[0].shape[0] // (2 * count)
    columns = rows[0].shape[1]
    return pl.pallas_call(
        functools.partial(attend_kernel, head_size, spots, side),
        grid=(count,),
        in_specs=[smem()] * 4 + [vmem()] * 5,
        out_specs=pl.BlockSpec((1, columns, tokens), lambda l: (l, 0, 0)),
        out_shape=jax.ShapeDtypeStruct((count, columns, tokens), jnp.bfloat16),
        compiler_params=params(16),
        cost_estimate=cost(),
    )(scalars, *routes, *rows, prompt_keys, prompt_values)


def ring_order(groups, chips):
    if groups == 2:
        return list(range(0, chips, 2)) + list(range(1, chips, 2))[::-1]
    return list(range(chips))


def solution(mesh):
    groups, dp = mesh.shape["groups"], mesh.shape["dp"]
    chips = dp // 2
    ring = ring_order(groups, chips)
    place = [ring.index(chip) for chip in range(chips)]
    behind_by = np.array(
        [[(place[me] - place[chip]) % chips for chip in range(chips)] for me in range(chips)],
        np.int32,
    )
    forward_pairs = [
        (2 * ring[i] + c, 2 * ring[(i + 1) % chips] + c) for i in range(chips) for c in range(2)
    ]
    backward_pairs = [(b, a) for a, b in forward_pairs]
    core_pairs = [(d, d ^ 1) for d in range(dp)]
    group_pairs = [(g, g ^ 1) for g in range(groups)]
    half_groups = [[2 * chip + c for chip in range(chips)] for c in range(2)]

    def forward(x):
        return lax.ppermute(x, "dp", forward_pairs)

    def backward(x):
        return lax.ppermute(x, "dp", backward_pairs)

    def swap_cores(x):
        return lax.ppermute(x, "dp", core_pairs)

    def swap_groups(x):
        return lax.ppermute(x, "groups", group_pairs)

    def local(
        latents,
        context,
        lengths,
        winner_slot,
        loser_slot,
        image_mod,
        context_mod,
        w_q,
        w_k,
        w_v,
        w_ck,
        w_cv,
    ):
        slot_local, token_count, width = latents.shape
        prompt_count, spot_local, _ = context.shape
        depth, inner_width = w_q.shape
        head_size = inner_width // HEADS
        columns = (HEADS + 1) // 2 * head_size
        me = lax.axis_index("dp")
        my_group = lax.axis_index("groups") % 2
        my_chip, my_core = me // 2, me % 2
        places = lax.dynamic_index_in_dim(jnp.asarray(behind_by), my_chip, 0, keepdims=False)
        first = [my_group, my_core]
        last = [me * slot_local, (me ^ 1) * slot_local]
        scalars = jnp.concatenate([jnp.stack(first), places, jnp.stack(last)]).astype(jnp.int32)

        own_mixed = mix_prompts(context, context_mod, chips, 2 * columns)
        once = [forward(own_mixed), backward(own_mixed)]
        twice = [forward(once[0]), backward(once[1])]
        mixed = {0: (own_mixed, 0)}
        for o, arrived in ((1, once), (2, twice)):
            mixed.setdefault(o % chips, (arrived[0], 0))
            mixed.setdefault(-o % chips, (arrived[1], 0))
        keep, give = split_weights(scalars, w_q, w_k, w_v, columns, once[0])
        got = swap_cores(give)
        own_av = [keep[:, : 2 * columns], got[:, : 2 * columns]]
        blocks = [jnp.concatenate(own_av + [x], axis=0) for x in twice]

        w_c = cut_prompt_weights(w_ck, w_cv, chips, w_q)
        w_c = lax.all_to_all(w_c, "dp", 0, 0, axis_index_groups=half_groups, tiled=True)
        ahead, behind = meet(blocks, [w_c])

        own, *give = modulate_image(scalars, latents, image_mod, chips, ahead)

        totals = None
        enough = max(1, chips // 8)
        tokens, waiting_av, waiting_b = [], [((0,), ahead)], []
        for o in range(1, chips // 2):
            ahead, behind = meet([forward(ahead), backward(behind)], tokens)
            mixed.setdefault((o + 2) % chips, (ahead, 2 * depth))
            mixed.setdefault((-o - 2) % chips, (behind, 2 * depth))
            if o == 1:
                (w_c,) = meet([w_c], [ahead])
                w_parts = [x.reshape(width // 2, -1) for x in (w_c, swap_cores(w_c))]
            if 4 * o == chips:
                slabs = [[own], [swap_cores(x) for x in meet(give, [ahead])]]
            tokens = []
            if 2 * o + 4 == chips:
                blocks, starts = zip(*[mixed[o] for o in range(chips)])
                projected = project_prompts(scalars, blocks, starts, *w_parts, slabs[1][0])
                projected = projected.reshape(-1, projected.shape[2])
                outgoing = route(projected, winner_slot, loser_slot, chips * spot_local)
                outgoing = outgoing.reshape(dp, -1, outgoing.shape[1])
                arrived = lax.all_to_all(outgoing, "dp", 0, 0, tiled=True)
            last = 2 * o + 2 == chips
            waiting_av += [((o,), ahead), ((chips - o,), behind)]
            if last:
                picked = pick_last(2 * depth, ahead, behind, waiting_b[-1][1])
            else:
                swapped = swap_groups(pick(2 * depth, ahead, behind))
            if len(waiting_b) > 3 * enough or (last and totals is None):
                first = totals is None
                items = [((), keep), ((), got)] if first else waiting_b
                totals, token = accumulate(
                    2 * depth, totals, slabs, waiting_av, items, [outgoing] if last else []
                )
                tokens.append(token)
                waiting_av, waiting_b = [], waiting_b if first else []
            if not last:
                waiting_b.append(((o, chips - o), swapped))
                tokens.append(swapped)
            if 2 * o + 4 == chips:
                tokens.append(outgoing)
        a_far, v_far = meet([forward(picked[0]), backward(picked[1])], tokens)
        o = chips // 2 - 1
        waiting_b += [((o,), forward(picked[2])), ((chips - o,), backward(picked[3]))]
        b_far = swap_groups(a_far)
        rows_a, rows_v, rows_b, features = last_products(
            2 * depth,
            head_size,
            totals,
            slabs,
            waiting_av,
            (chips // 2, a_far, v_far),
            waiting_b,
        )

        done_rows = (rows_a, rows_v, close(rows_b, features, b_far, head_size))
        (arrived,) = meet([arrived], [done_rows[2]])

        prompt_keys, prompt_values = finish_prompts(
            scalars, arrived, swap_cores(arrived), columns, head_size, slot_local
        )

        routes = (winner_slot, loser_slot, lengths)

        def run(side):
            return attend(
                side,
                scalars,
                routes,
                done_rows,
                prompt_keys,
                prompt_values,
                head_size,
                spot_local,
                slot_local,
            )

        theirs = swap_cores(run(1))
        mine = run(0)
        return join(scalars, mine, theirs, inner_width).transpose(0, 2, 1)

    placed = (
        P(("groups", "dp"), None, None),
        P("groups", "dp", None),
        P("groups"),
        P("groups"),
        P("groups"),
        P(("groups", "dp"), None, None),
        P("groups", None, None),
        P("dp", None),
        P("dp", None),
        P("dp", None),
        P("dp", None),
        P("dp", None),
    )
    return jax.shard_map(
        local,
        mesh=mesh,
        in_specs=placed,
        out_specs=P(("groups", "dp"), None, None),
        check_vma=False,
    )
```
